32 devices in a mesh: dp: 16 (over z, x, core), tensor: 2 (over y).
Axes of the slice: x: 2, y: 2, z: 4, core: 2. Of those that a mesh axis runs over, the one named last changes fastest.
Arguments:
- tokens: bfloat16 [64, 502, 768], P('dp', 'tensor'), may hold values from -6 to 6
- slot_position: int32 [64], P('dp'), may hold values from -1 to 3, as said below
- cotangent: bfloat16 [64, 502, 768], P('dp', 'tensor'), may hold values from -6 to 6
- attention: float32 [4, 768, 768], P(None, 'dp', 'tensor'), may hold values from -4 to 4, as said below
- feedforward: float32 [2, 768, 3072], P(None, None, ('dp', 'tensor')), may hold values from -0.21875 to 0.21875
- vectors: float32 [16896], P(('dp', 'tensor')), may hold values from -6 to 6, as said below
- attn_momentum: float32 [4, 768, 768], P(None, 'dp', 'tensor'), may hold values from -2 to 2, as said below
- ffn_momentum: float32 [2, 768, 3072], P(None, None, ('dp', 'tensor')), may hold values from -3 to 3
- vec_momentum: float32 [16896], P(('dp', 'tensor')), may hold values from -3 to 3
- attn_average: float32 [4, 768, 768], P(None, 'dp', 'tensor'), may hold values from -4 to 4, as said below
- ffn_average: float32 [2, 768, 3072], P(None, None, ('dp', 'tensor')), may hold values from -0.21875 to 0.21875
- vec_average: float32 [16896], P(('dp', 'tensor')), may hold values from -6 to 6, as said below
Outputs:
- activations: bfloat16 [64, 502, 768], P('dp', 'tensor')
- token_grad: bfloat16 [64, 502, 768], P('dp', 'tensor')
- momentum_attn: float32 [4, 768, 768], P(None, 'dp', 'tensor')
- momentum_ffn: float32 [2, 768, 3072], P(None, None, ('dp', 'tensor'))
- momentum_vec: float32 [16896], P(('dp', 'tensor'))
- updated_attn: float32 [4, 768, 768], P(None, 'dp', 'tensor')
- updated_ffn: float32 [2, 768, 3072], P(None, None, ('dp', 'tensor'))
- updated_vec: float32 [16896], P(('dp', 'tensor'))
- averaged_attn: float32 [4, 768, 768], P(None, 'dp', 'tensor')
- averaged_ffn: float32 [2, 768, 3072], P(None, None, ('dp', 'tensor'))
- averaged_vec: float32 [16896], P(('dp', 'tensor'))
The draws below stay inside these ranges and needn't reach their ends.
Inputs may be any that keep to these rules, and one draw needn't show every extreme that they name: `slot_position`: each bucket of 4 slots holds whole sequences one after another from its first slot: a slot holds its segment's place in its sequence, a sequence has 2 to 4 segments in consecutive slots starting at place 0, and the slots after a bucket's last sequence hold -1. Some bucket begins with a sequence of 4 segments. `attention`: entries of mean 0; the output projection's entries are larger than the others. `attn_momentum`: no entry is 0. `vectors`: gains near 1, biases of mean 0, initial memory of order one. `attn_average`: drawn by the same law as the attention weights. `vec_average`: drawn by the same law as vectors.
All inputs are finite; a program needn't handle non-finite values.
Results may differ from the reference program's by a relative error of at most 0.023.
Values may be sent and summed in bfloat16 or wider, within the bound.
A program may use at most 256 MiB of HBM per device.

```python
import math
import jax
import jax.numpy as jnp
from jax import lax

D = 768
HEADS = 12
DH = 64
FF = 3072
SEG_TOK = 502
MEM = 10
SLOTS = 4
ROWS = 522
NVEC = 22
SLOTS_ALL = 64
TOTAL_ROWS = 33408
N_DP = 16


def attention_law(key):
    small_scale = D ** (-0.5)
    large_scale = math.sqrt(ROWS / (2.0 * D))
    kind_scale = jnp.array([small_scale, small_scale, small_scale, large_scale], jnp.float32)[:, None, None]
    normal_base = jnp.clip(jax.random.normal(key, (4, D, D), jnp.float32), -6.0, 6.0)
    return normal_base * kind_scale


def vector_law(key):
    normal_base = jnp.clip(jax.random.normal(key, (NVEC, D), jnp.float32), -6.0, 6.0)
    row_index = lax.broadcasted_iota(jnp.int32, (NVEC, D), 0)
    is_gain = (row_index == 3) | (row_index == 6)
    is_memory = row_index >= 8 + FF // D
    row_scale = jnp.where(is_gain, 0.1, jnp.where(is_memory, 1.0, 0.2))
    center = jnp.where(is_gain, 1.0, 0.0)
    return (center + row_scale * normal_base).reshape(NVEC * D)


def draw_attention(key, part):
    return attention_law(jax.random.fold_in(key, 3))


def draw_attn_average(key, part):
    return attention_law(jax.random.fold_in(key, 7))


def draw_vectors(key, part):
    return vector_law(jax.random.fold_in(key, 5))


def draw_vec_average(key, part):
    return vector_law(jax.random.fold_in(key, 11))


def draw_attn_momentum(key, part):
    kind_scale = jnp.array([0.3, 0.3, 1.0, 0.1], jnp.float32)[:, None, None]
    size_part = jnp.exp(jax.random.uniform(jax.random.fold_in(key, 1), (4, D, D), jnp.float32, math.log(0.5), math.log(2.0)))
    sign_flip = jnp.where(jax.random.bernoulli(jax.random.fold_in(key, 2), 0.5, (4, D, D)), 1.0, -1.0)
    return kind_scale * size_part * sign_flip


def draw_slot_position(key, part):
    lengths = jax.random.randint(jax.random.fold_in(key, 1), (N_DP, SLOTS), 2, 5)
    chosen = jax.random.randint(jax.random.fold_in(key, 2), (), 0, N_DP)
    bucket_ids = lax.broadcasted_iota(jnp.int32, (N_DP, SLOTS), 0)
    item_ids = lax.broadcasted_iota(jnp.int32, (N_DP, SLOTS), 1)
    lengths = jnp.where((bucket_ids == chosen) & (item_ids == 0), 4, lengths).astype(jnp.int32)
    starts = jnp.cumsum(lengths, axis=1) - lengths
    ends = starts + lengths
    fitting = ends <= SLOTS
    slot_index = jnp.arange(SLOTS, dtype=jnp.int32)[None, :, None]
    inside = (slot_index >= starts[:, None, :]) & (slot_index < ends[:, None, :]) & fitting[:, None, :]
    position = jnp.sum(jnp.where(inside, slot_index - starts[:, None, :] + 1, 0), axis=2) - 1
    return position.reshape(N_DP * SLOTS).astype(jnp.int32)


def shard_levels(key, extent, split, low, high):
    gain = 1.0
    for axis_at, blocks in split:
        steps = jax.random.uniform(jax.random.fold_in(jax.random.fold_in(key, 6), axis_at), (blocks,), jnp.float32, low / len(split), high / len(split))
        gain = gain * jnp.repeat(jnp.exp(steps), extent[axis_at] // blocks).reshape((-1,) + (1,) * (len(extent) - 1 - axis_at))
    return gain


def gaussian(own_key, extent, scale, bound, pieces=(), kind=jnp.bfloat16):
    gain = shard_levels(own_key, extent, pieces, -0.22, 0.18) if pieces else 1.0
    result = jax.random.normal(own_key, extent, jnp.float32) * scale * gain
    return jnp.minimum(jnp.maximum(result, -bound), bound).astype(kind)


def setup_inputs(seed: int = 0) -> dict:
    splits = jax.random.split(jax.random.key(seed), 13)
    tokens = gaussian(splits[0], (SLOTS_ALL, SEG_TOK, D), 1.0, 6.0, ((0, 16), (1, 2)))
    slot_position = draw_slot_position(jax.random.fold_in(splits[12], 71), 0)
    cotangent = gaussian(splits[2], (SLOTS_ALL, SEG_TOK, D), 1.0, 6.0, ((0, 16), (1, 2)))
    attention = draw_attention(jax.random.fold_in(splits[12], 71), 0)
    feedforward = gaussian(splits[4], (2, D, FF), D ** -0.5, 0.21875, ((2, 32),), jnp.float32)
    vectors = draw_vectors(jax.random.fold_in(splits[12], 71), 0)
    attn_momentum = draw_attn_momentum(jax.random.fold_in(splits[12], 71), 0)
    ffn_momentum = gaussian(splits[7], (2, D, FF), 0.5, 3.0, ((2, 32),), jnp.float32)
    vec_momentum = gaussian(splits[8], (NVEC * D,), 0.5, 3.0, ((0, 32),), jnp.float32)
    attn_average = draw_attn_average(jax.random.fold_in(splits[12], 71), 0)
    ffn_average = gaussian(splits[10], (2, D, FF), D ** -0.5, 0.21875, ((2, 32),), jnp.float32)
    vec_average = draw_vec_average(jax.random.fold_in(splits[12], 71), 0)
    return dict(tokens=tokens, slot_position=slot_position, cotangent=cotangent, attention=attention, feedforward=feedforward, vectors=vectors, attn_momentum=attn_momentum, ffn_momentum=ffn_momentum, vec_momentum=vec_momentum, attn_average=attn_average, ffn_average=ffn_average, vec_average=vec_average)


EPSILON = 1e-05
MOMENTUM = 0.9
AVERAGE_DECAY = 0.75
ATTENTION_RATE = 0.06
FEEDFORWARD_RATE = 0.02
VECTOR_RATE = 0.1
MASK_VALUE = -1e+30

@jax.custom_vjp
def low(v):
    return lax.optimization_barrier(v.astype(jnp.bfloat16)).astype(jnp.float32)

@jax.custom_vjp
def low_back(v):
    return v

def low_keep(v):
    return (low(v), None)

def low_pass(kept, grad):
    return (grad,)

def back_keep(v):
    return (v, None)

def back_low(kept, grad):
    return (low(grad),)
low.defvjp(low_keep, low_pass)
low_back.defvjp(back_keep, back_low)

def product(left, right):
    return jnp.dot(left, right, precision=lax.Precision.HIGHEST)

def layer_norm(rows, norm_gain, norm_shift):
    center = rows - lax.optimization_barrier(jnp.mean(rows, axis=-1, keepdims=True))
    spread = lax.optimization_barrier(jnp.mean(center * center, axis=-1, keepdims=True))
    return center * lax.rsqrt(spread + EPSILON) * norm_gain + norm_shift

def by_heads(block):
    return block.reshape(ROWS, HEADS, DH)

def segment(segment_rows, attention, feedforward, table):
    score_scale = 1.0 / math.sqrt(DH)
    queries = low_back(low(product(segment_rows, attention[0]) + table[0]))
    key_rows = low_back(low(product(segment_rows, attention[1])))
    values = low_back(low(product(segment_rows, attention[2]) + table[1]))
    raw_scores = jnp.einsum('qhd,khd->hqk', by_heads(queries), by_heads(key_rows), precision=lax.Precision.HIGHEST)
    raw_scores = low_back(raw_scores)
    row_ids = lax.broadcasted_iota(jnp.int32, (ROWS, ROWS), 0)
    col_ids = lax.broadcasted_iota(jnp.int32, (ROWS, ROWS), 1)
    causal = row_ids >= col_ids
    scores = jnp.where(causal[None], raw_scores * score_scale, MASK_VALUE)
    row_max = lax.optimization_barrier(jnp.max(scores, axis=-1, keepdims=True))
    exponent = jnp.exp(scores - row_max)
    attend = exponent / lax.optimization_barrier(jnp.sum(exponent, axis=-1, keepdims=True))
    context = jnp.einsum('hqk,khd->qhd', low(attend), by_heads(values), precision=lax.Precision.HIGHEST).reshape(ROWS, D)
    context = low_back(low(context))
    branch = low_back(product(context, attention[3].T) + table[2])
    hidden = low(layer_norm(segment_rows + branch, table[3], table[4]))
    up_bias = table[8:8 + FF // D].reshape(FF)
    upward = low_back(product(hidden, feedforward[0]) + up_bias)
    active = low(jax.nn.gelu(upward, approximate=False))
    downward = low_back(product(active, feedforward[1].T) + table[5])
    return low(layer_norm(hidden + downward, table[6], table[7]))

def bucket(weights, block_tokens, places):
    attention, feedforward, table = weights
    memory_init = table[8 + FF // D:]

    def slot_step(memory, inputs):
        segment_tokens, segment_place = inputs
        memory_in = jnp.where(segment_place == 0, memory_init, memory)
        segment_rows = jnp.concatenate([memory_in, segment_tokens, memory_in], axis=0)
        output = segment(segment_rows, attention, feedforward, table)
        token_rows = jnp.where(segment_place >= 0, output[MEM:MEM + SEG_TOK], 0.0)
        return (output[ROWS - MEM:], token_rows)
    memory_start = jnp.zeros((MEM, D), jnp.float32)
    _, outputs = lax.scan(jax.checkpoint(slot_step), memory_start, (block_tokens, places))
    return outputs

def update(gradient, momentum, weight, average, rate):
    scaled = gradient * (1.0 / math.sqrt(TOTAL_ROWS))
    moment = MOMENTUM * momentum + scaled
    weight_new = weight - rate * (scaled + MOMENTUM * moment)
    return (moment, weight_new, AVERAGE_DECAY * average + (1.0 - AVERAGE_DECAY) * weight_new)

def reference(tokens, slot_position, cotangent, attention, feedforward, vectors, attn_momentum, ffn_momentum, vec_momentum, attn_average, ffn_average, vec_average):
    token_blocks = tokens.astype(jnp.float32).reshape(N_DP, SLOTS, SEG_TOK, D)
    place_blocks = slot_position.reshape(N_DP, SLOTS)
    cot_blocks = cotangent.astype(jnp.float32).reshape(N_DP, SLOTS, SEG_TOK, D)
    params = (attention, feedforward, vectors)

    def per_bucket(totals, inputs):
        block_tokens, block_places, block_cot = inputs

        def forward(weights, token_in):
            rounded = (low(weights[0]), low(weights[1]), low(weights[2]).reshape(NVEC, D))
            return bucket(rounded, token_in, block_places)
        outputs, pull = jax.vjp(forward, params, block_tokens)
        weight_grads, token_grads = pull(block_cot)
        totals = jax.tree.map(jnp.add, totals, weight_grads)
        return (totals, (outputs.astype(jnp.bfloat16), token_grads.astype(jnp.bfloat16)))
    zero_sums = jax.tree.map(jnp.zeros_like, params)
    totals, (outputs, token_grads) = lax.scan(per_bucket, zero_sums, (token_blocks, place_blocks, cot_blocks))
    attn_new = update(totals[0], attn_momentum, attention, attn_average, ATTENTION_RATE)
    ffn_new = update(totals[1], ffn_momentum, feedforward, ffn_average, FEEDFORWARD_RATE)
    vec_new = update(totals[2], vec_momentum, vectors, vec_average, VECTOR_RATE)
    activations = outputs.reshape(SLOTS_ALL, SEG_TOK, D)
    token_grad = token_grads.reshape(SLOTS_ALL, SEG_TOK, D)
    return (activations, token_grad, attn_new[0], ffn_new[0], vec_new[0], attn_new[1], ffn_new[1], vec_new[1], attn_new[2], ffn_new[2], vec_new[2])
```

```python
import functools
import math

import jax
import jax.numpy as jnp
from jax import lax
from jax.experimental import pallas as pl
from jax.experimental.pallas import tpu as pltpu
from jax.sharding import PartitionSpec as P

D = 768
HEADS = 12
DH = 64
FF = 3072
MEM = 10
SLOTS = 4
ROWS = 522
NVEC = 22

HALF = D // 2
SEG = ROWS - MEM
THIN = 16
LOCAL = 2
TILE = 256

EPSILON = 1e-05
MOMENTUM = 0.9
AVERAGE_DECAY = 0.75
ATTENTION_RATE = 0.06
FEEDFORWARD_RATE = 0.02
VECTOR_RATE = 0.1
MASK_VALUE = -1e30
SCALE = 1.0 / math.sqrt(DH)

F32 = jnp.float32
BF16 = jnp.bfloat16
MIB = 1 << 20

QUERY_BIAS, VALUE_BIAS, OUT_BIAS, GAIN1, SHIFT1, DOWN_BIAS, GAIN2, SHIFT2, UP_BIAS = range(9)
FIRST_MEMORY = UP_BIAS + FF // D


def nn(a, b):
    return lax.dot_general(a, b, (((1,), (0,)), ((), ())), preferred_element_type=F32)


def nt(a, b):
    return lax.dot_general(a, b, (((1,), (1,)), ((), ())), preferred_element_type=F32)


def tn(a, b):
    return lax.dot_general(a, b, (((0,), (0,)), ((), ())), preferred_element_type=F32)


def normalized(rows):
    center = rows - jnp.mean(rows, axis=-1, keepdims=True)
    spread = jnp.mean(center * center, axis=-1, keepdims=True)
    inverse = lax.rsqrt(spread + EPSILON)
    return center * inverse, inverse


def normalized_back(grad, unit, inverse):
    mean_grad = jnp.mean(grad, axis=-1, keepdims=True)
    mean_along = jnp.mean(grad * unit, axis=-1, keepdims=True)
    return inverse * (grad - mean_grad - unit * mean_along)


def gelu_parts(u):
    size = jnp.abs(u)
    t = 1.0 / (1.0 + (0.3275911 / math.sqrt(2.0)) * size)
    bell = jnp.exp(-0.5 * u * u)
    poly = t * (
        0.5 * 0.254829592
        + t
        * (
            0.5 * -0.284496736
            + t * (0.5 * 1.421413741 + t * (0.5 * -1.453152027 + t * (0.5 * 1.061405429)))
        )
    )
    tail = poly * bell
    cdf = jnp.where(u < 0, tail, 1.0 - tail)
    return u * cdf, cdf + (u * (1.0 / math.sqrt(2.0 * math.pi))) * bell


def row_sum(block):
    return jnp.sum(block, axis=0, keepdims=True)


def params(limit=60, **more):
    return pltpu.CompilerParams(vmem_limit_bytes=limit * MIB, **more)


def once(shape, index):
    return pl.BlockSpec(shape, lambda *_: index, pipeline_mode=pl.Buffered(1))


ANY = pl.BlockSpec(memory_space=pl.ANY)
SMEM = pl.BlockSpec(memory_space=pltpu.SMEM)
VMEM = pl.BlockSpec(memory_space=pltpu.VMEM)


def sds(shape, dtype):
    return jax.ShapeDtypeStruct(shape, dtype)


def project_kernel(x_ref, w_ref, table_ref, q_ref, k_ref, v_ref):
    x = x_ref[0]
    for side in range(2):
        cols = slice(HALF * side, HALF * (side + 1))
        query = nn(x, w_ref[side, 0]) + table_ref[QUERY_BIAS : QUERY_BIAS + 1, cols]
        q_ref[0, :, cols] = (query * SCALE).astype(BF16)
        k_ref[0, :, cols] = nn(x, w_ref[side, 1]).astype(BF16)
        value = nn(x, w_ref[side, 2]) + table_ref[VALUE_BIAS : VALUE_BIAS + 1, cols]
        v_ref[0, :, cols] = value.astype(BF16)


def project(x, attn, table):
    rows = pl.BlockSpec((1, TILE, D), lambda s, i: (s, i, 0))
    return pl.pallas_call(
        project_kernel,
        grid=(LOCAL, SEG // TILE),
        in_specs=[rows, once((2, 3, D, HALF), (0, 0, 0, 0)), once((NVEC, D), (0, 0))],
        out_specs=[rows] * 3,
        out_shape=[sds((LOCAL, SEG, D), BF16)] * 3,
        compiler_params=params(),
    )(x, attn, table)


def head_masks():
    feature_head = lax.broadcasted_iota(jnp.int32, (1, D), 1) // DH
    return [feature_head == h for h in range(HEADS)]


def by_head(rows16, masks):
    zero = jnp.zeros_like(rows16)
    return jnp.concatenate([jnp.where(m, rows16, zero) for m in masks], axis=0)


def own_columns(blocks, masks):
    total = jnp.zeros((THIN, D), blocks.dtype)
    for h, m in enumerate(masks):
        total = jnp.where(m, blocks[THIN * h : THIN * (h + 1)], total)
    return total


def copies_of(key_mask_shape):
    row = lax.rem(lax.broadcasted_iota(jnp.int32, key_mask_shape, 0), THIN)
    key = lax.broadcasted_iota(jnp.int32, key_mask_shape, 1)
    return jnp.where((key < MEM) & (key <= row), 2.0, 1.0)


def chain_kernel(
    place_ref,
    flag_ref,
    start_ref,
    table_ref,
    attn_ref,
    ffn_ref,
    x_in,
    q_in,
    k_in,
    v_in,
    saved_d_in,
    saved_f_in,
    saved_s_in,
    x_ref,
    q_ref,
    k_ref,
    v_ref,
    saved_d_ref,
    saved_f_ref,
    saved_s_ref,
    memory_ref,
    wa,
    wf,
    xb,
    qb,
    kb,
    vb,
    save_d,
    save_f,
    save_s,
    sem_w,
    sem_x,
    sem_kv,
    sem_out,
):
    del x_in, q_in, k_in, v_in, saved_d_in, saved_f_in, saved_s_in
    active = flag_ref[0] > 0
    memory_ref[...] = start_ref[...]

    @pl.when(active)
    def _():
        loads = [
            pltpu.make_async_copy(attn_ref, wa, sem_w.at[0]),
            pltpu.make_async_copy(ffn_ref.at[0], wf.at[0], sem_w.at[1]),
            pltpu.make_async_copy(ffn_ref.at[1], wf.at[1], sem_w.at[2]),
        ]
        tiles = [
            pltpu.make_async_copy(x_ref.at[s, pl.ds(0, THIN)], xb.at[s], sem_x.at[s])
            for s in range(LOCAL)
        ]
        keys = [
            pltpu.make_async_copy(src.at[s], dst.at[s], sem_kv.at[2 * s + i])
            for s in range(LOCAL)
            for i, (src, dst) in enumerate(((k_ref, kb), (v_ref, vb)))
        ]
        for c in tiles + loads[:1] + keys + loads[1:]:
            c.start()
        masks = head_masks()
        memory_row = lax.broadcasted_iota(jnp.int32, (THIN, 1), 0) < MEM
        first = table_ref[FIRST_MEMORY:NVEC, :]
        first = jnp.concatenate([first, jnp.zeros((THIN - MEM, D), F32)], axis=0)
        row = lambda r: table_ref[r : r + 1, :]
        for s in range(LOCAL):
            tiles[s].wait()
            if s == 0:
                loads[0].wait()
            keys[2 * s].wait()
            keys[2 * s + 1].wait()
            memory = jnp.where(place_ref[s] == 0, first, memory_ref[...].astype(F32))
            x16 = jnp.where(memory_row, memory, xb[s].astype(F32)).astype(BF16)
            xb[s] = x16
            for side in range(2):
                cols = slice(HALF * side, HALF * (side + 1))
                query = nn(x16, wa[side, 0]) + table_ref[QUERY_BIAS : QUERY_BIAS + 1, cols]
                qb[s, :, cols] = (query * SCALE).astype(BF16)
                kb[s, 0:THIN, cols] = nn(x16, wa[side, 1]).astype(BF16)
                value = nn(x16, wa[side, 2]) + table_ref[VALUE_BIAS : VALUE_BIAS + 1, cols]
                vb[s, 0:THIN, cols] = value.astype(BF16)
            outs = [
                pltpu.make_async_copy(xb.at[s], x_ref.at[s, pl.ds(0, THIN)], sem_out.at[4 * s]),
                pltpu.make_async_copy(qb.at[s], q_ref.at[s, pl.ds(0, THIN)], sem_out.at[4 * s + 1]),
                pltpu.make_async_copy(
                    kb.at[s, pl.ds(0, THIN)], k_ref.at[s, pl.ds(0, THIN)], sem_out.at[4 * s + 2]
                ),
                pltpu.make_async_copy(
                    vb.at[s, pl.ds(0, THIN)], v_ref.at[s, pl.ds(0, THIN)], sem_out.at[4 * s + 3]
                ),
            ]
            for c in outs:
                c.start()

            def rest(s=s):
                q_heads = by_head(qb[s], masks)
                score = nt(q_heads, kb[s])
                top = jnp.max(score, axis=-1, keepdims=True)
                weight = jnp.exp(score - top) * copies_of(score.shape)
                total = jnp.sum(weight, axis=-1, keepdims=True)
                share = (weight / total).astype(BF16)
                log_total = top + jnp.log(total)
                context = own_columns(nn(share, vb[s]), masks).astype(BF16)
                branch = nt(context[:, :HALF], wa[0, 3]) + nt(context[:, HALF:], wa[1, 3])
                unit1, inverse1 = normalized(xb[s].astype(F32) + branch + row(OUT_BIAS))
                hidden = (unit1 * row(GAIN1) + row(SHIFT1)).astype(BF16)
                if s == 0:
                    loads[1].wait()
                up = nt(hidden, wf[0])
                up_bias = jnp.concatenate([row(UP_BIAS + i) for i in range(FF // D)], axis=1)
                active16, slope = gelu_parts(up + up_bias)
                active16 = active16.astype(BF16)
                if s == 0:
                    loads[2].wait()
                second = hidden.astype(F32) + nn(active16, wf[1]) + row(DOWN_BIAS)
                unit2, inverse2 = normalized(second)
                memory_ref[...] = (unit2 * row(GAIN2) + row(SHIFT2)).astype(BF16)
                save_d[s, 0] = hidden
                save_d[s, 1] = unit1.astype(BF16)
                save_d[s, 2] = unit2.astype(BF16)
                save_d[s, 3] = context
                save_f[s, 0] = active16
                save_f[s, 1] = slope.astype(BF16)
                wide = lambda v: jnp.broadcast_to(v, (v.shape[0], 128))
                save_s[s, 0 : HEADS * THIN] = wide(log_total)
                save_s[s, HEADS * THIN : HEADS * THIN + THIN] = wide(inverse1)
                save_s[s, HEADS * THIN + THIN :] = wide(inverse2)

            if s == LOCAL - 1:
                last_needed = flag_ref[1] > 0

                @pl.when(last_needed)
                def _():
                    rest()

                @pl.when(jnp.logical_not(last_needed))
                def _():
                    loads_done = (s != 0)
                    del loads_done
                    save_d[s] = jnp.zeros_like(save_d[s])
                    save_f[s] = jnp.zeros_like(save_f[s])
                    save_s[s] = jnp.zeros_like(save_s[s])
            else:
                rest()
            for c in outs:
                c.wait()
        saves = [
            pltpu.make_async_copy(save_d, saved_d_ref, sem_out.at[0]),
            pltpu.make_async_copy(save_f, saved_f_ref, sem_out.at[1]),
            pltpu.make_async_copy(save_s, saved_s_ref, sem_out.at[2]),
        ]
        for c in saves:
            c.start()
        for c in saves:
            c.wait()


SAVED = (
    sds((LOCAL, 4, THIN, D), BF16),
    sds((LOCAL, 2, THIN, FF), BF16),
    sds((LOCAL, HEADS * THIN + 2 * THIN, 128), F32),
)


def chain(place, flag, start, table, attn, ffn, x, q, k, v, saved):
    whole = sds((LOCAL, SEG, D), BF16)
    outs = pl.pallas_call(
        chain_kernel,
        in_specs=[SMEM, SMEM, VMEM, VMEM] + [ANY] * 9,
        out_specs=[ANY] * 7 + [VMEM],
        out_shape=[whole] * 4 + list(SAVED) + [sds((THIN, D), BF16)],
        input_output_aliases={6 + i: i for i in range(7)},
        scratch_shapes=[
            pltpu.VMEM((2, 4, D, HALF), BF16),
            pltpu.VMEM((2, FF, D), BF16),
            pltpu.VMEM((LOCAL, THIN, D), BF16),
            pltpu.VMEM((LOCAL, THIN, D), BF16),
            pltpu.VMEM((LOCAL, SEG, D), BF16),
            pltpu.VMEM((LOCAL, SEG, D), BF16),
            pltpu.VMEM((LOCAL, 4, THIN, D), BF16),
            pltpu.VMEM((LOCAL, 2, THIN, FF), BF16),
            pltpu.VMEM((LOCAL, HEADS * THIN + 2 * THIN, 128), F32),
            pltpu.SemaphoreType.DMA((3,)),
            pltpu.SemaphoreType.DMA((LOCAL,)),
            pltpu.SemaphoreType.DMA((2 * LOCAL,)),
            pltpu.SemaphoreType.DMA((4 * LOCAL,)),
        ],
        compiler_params=params(),
    )(place, flag, start, table, attn, ffn, x, q, k, v, *saved)
    return outs[:4], outs[4:7], outs[7]


def own_lanes(block, head):
    lane = lax.broadcasted_iota(jnp.int32, block.shape, 1)
    return jnp.where((lane < DH) == (head == 0), block, jnp.zeros_like(block))


def seen(score, first_query):
    key = lax.broadcasted_iota(jnp.int32, score.shape, 0)
    query = lax.broadcasted_iota(jnp.int32, score.shape, 1) + first_query
    return key <= query


def attend_kernel(q_ref, k_ref, v_ref, c_ref, log_ref):
    for part in range(SEG // TILE):
        rows = slice(TILE * part, TILE * (part + 1))
        keys = slice(0, TILE * (part + 1))
        contexts = []
        for head in range(2):
            score = nt(own_lanes(k_ref[0, keys], head), q_ref[0, rows])
            score = jnp.where(seen(score, TILE * part), score, MASK_VALUE)
            top = jnp.max(score, axis=0, keepdims=True)
            weight = jnp.exp(score - top)
            total = jnp.sum(weight, axis=0, keepdims=True)
            share = (weight * (1.0 / total)).astype(BF16)
            log_ref[0, 0, head : head + 1, rows] = top + jnp.log(total)
            contexts.append(tn(share, v_ref[0, keys]))
        lane = lax.broadcasted_iota(jnp.int32, contexts[0].shape, 1)
        c_ref[0, rows] = jnp.where(lane < DH, contexts[0], contexts[1]).astype(BF16)


PAIR = pl.BlockSpec((1, SEG, 2 * DH), lambda s, h: (s, 0, h))
PAIR_LOG = pl.BlockSpec((1, 1, 2, SEG), lambda s, h: (s, h, 0, 0))


def attend(q, k, v):
    return pl.pallas_call(
        attend_kernel,
        grid=(LOCAL, HEADS // 2),
        in_specs=[PAIR] * 3,
        out_specs=[PAIR, PAIR_LOG],
        out_shape=[sds((LOCAL, SEG, D), BF16), sds((LOCAL, HEADS // 2, 2, SEG), F32)],
        compiler_params=params(),
    )(q, k, v)


def attend_back_kernel(q_ref, k_ref, v_ref, dc_ref, log_ref, dq_ref, dk_ref, dv_ref):
    last = SEG // TILE
    key_terms, value_terms = [], []
    for head in range(2):
        key_sum, value_sum = [], []
        query_parts = []
        for part in range(last):
            rows = slice(TILE * part, TILE * (part + 1))
            keys = slice(0, TILE * (part + 1))
            q, dc = q_ref[0, rows], dc_ref[0, rows]
            k = k_ref[0, keys]
            score = nt(own_lanes(k, head), q)
            share = jnp.exp(score - log_ref[0, 0, head : head + 1, rows])
            share = jnp.where(seen(score, TILE * part), share, 0.0)
            share_grad = nt(own_lanes(v_ref[0, keys], head), dc)
            inner = jnp.sum(share_grad * share, axis=0, keepdims=True)
            score_grad = (share * (share_grad - inner)).astype(BF16)
            value_sum.append(nn(share.astype(BF16), dc))
            key_sum.append(nn(score_grad, q))
            query_parts.append(tn(score_grad, k))
        key_terms.append(key_sum)
        value_terms.append(value_sum)
        if head == 0:
            first_queries = query_parts
    for part in range(last):
        rows = slice(TILE * part, TILE * (part + 1))
        lane = lax.broadcasted_iota(jnp.int32, (TILE, 2 * DH), 1)
        pick = lambda a, b: jnp.where(lane < DH, a, b)
        dq_ref[0, rows] = (pick(first_queries[part], query_parts[part]) * SCALE).astype(BF16)
        for terms, out in ((key_terms, dk_ref), (value_terms, dv_ref)):
            total = None
            for later in range(part, last):
                term = pick(terms[0][later][rows], terms[1][later][rows])
                total = term if total is None else total + term
            out[0, rows] = total.astype(BF16)


def attend_back(q, k, v, dc, log_total):
    return pl.pallas_call(
        attend_back_kernel,
        grid=(LOCAL, HEADS // 2),
        in_specs=[PAIR] * 4 + [PAIR_LOG],
        out_specs=[PAIR] * 3,
        out_shape=[sds((LOCAL, SEG, D), BF16)] * 3,
        compiler_params=params(),
    )(q, k, v, dc, log_total)


def rows_kernel(
    x_ref,
    c_ref,
    cot_ref,
    wo_ref,
    wf_ref,
    table_ref,
    y_ref,
    h_ref,
    g_ref,
    du_ref,
    df_ref,
    da_ref,
    dc_ref,
    sums_ref,
    slope_ref,
):
    row = lambda r: table_ref[r : r + 1, :]

    @pl.when((pl.program_id(0) == 0) & (pl.program_id(1) == 0))
    def _():
        sums_ref[...] = jnp.zeros_like(sums_ref)

    def add(r, value):
        sums_ref[r : r + 1, :] += value

    c = c_ref[0]
    branch = nt(c[:, :HALF], wo_ref[0, 0]) + nt(c[:, HALF:], wo_ref[1, 0])
    unit1, inverse1 = normalized(x_ref[0].astype(F32) + branch + row(OUT_BIAS))
    hidden = (unit1 * row(GAIN1) + row(SHIFT1)).astype(BF16)
    h_ref[0] = hidden
    second = hidden.astype(F32) + row(DOWN_BIAS)
    for i in range(FF // D):
        cols = slice(D * i, D * (i + 1))
        up = nt(hidden, wf_ref[0, cols]) + row(UP_BIAS + i)
        active, slope = gelu_parts(up)
        active = active.astype(BF16)
        g_ref[0, :, cols] = active
        slope_ref[:, cols] = slope.astype(BF16)
        second = second + nn(active, wf_ref[1, cols])
    unit2, inverse2 = normalized(second)
    y_ref[0] = (unit2 * row(GAIN2) + row(SHIFT2)).astype(BF16)

    grad = cot_ref[0].astype(F32)
    add(GAIN2, row_sum(grad * unit2))
    add(SHIFT2, row_sum(grad))
    second_grad = normalized_back(grad * row(GAIN2), unit2, inverse2)
    down_grad = second_grad.astype(BF16)
    df_ref[0] = down_grad
    add(DOWN_BIAS, row_sum(down_grad.astype(F32)))
    hidden_grad = second_grad
    for i in range(FF // D):
        cols = slice(D * i, D * (i + 1))
        up_grad = (nt(down_grad, wf_ref[1, cols]) * slope_ref[:, cols].astype(F32)).astype(BF16)
        du_ref[0, :, cols] = up_grad
        add(UP_BIAS + i, row_sum(up_grad.astype(F32)))
        hidden_grad = hidden_grad + nn(up_grad, wf_ref[0, cols])
    add(GAIN1, row_sum(hidden_grad * unit1))
    add(SHIFT1, row_sum(hidden_grad))
    branch_grad = normalized_back(hidden_grad * row(GAIN1), unit1, inverse1).astype(BF16)
    da_ref[0] = branch_grad
    add(OUT_BIAS, row_sum(branch_grad.astype(F32)))
    for side in range(2):
        dc_ref[0, :, HALF * side : HALF * (side + 1)] = nn(branch_grad, wo_ref[side, 0]).astype(BF16)


def rows_part(x, c, cot, attn, ffn, table):
    rows = pl.BlockSpec((1, TILE, D), lambda s, i: (s, i, 0))
    wide = pl.BlockSpec((1, TILE, FF), lambda s, i: (s, i, 0))
    whole, whole_wide = sds((LOCAL, SEG, D), BF16), sds((LOCAL, SEG, FF), BF16)
    return pl.pallas_call(
        rows_kernel,
        grid=(LOCAL, SEG // TILE),
        in_specs=[rows] * 3
        + [once((2, 1, D, HALF), (0, 3, 0, 0)), once((2, FF, D), (0, 0, 0)), once((NVEC, D), (0, 0))],
        out_specs=[rows, rows, wide, wide, rows, rows, rows, once((THIN, D), (0, 0))],
        out_shape=[whole, whole, whole_wide, whole_wide, whole, whole, whole, sds((THIN, D), F32)],
        scratch_shapes=[pltpu.VMEM((TILE, FF), BF16)],
        compiler_params=params(),
    )(x, c, cot, attn, ffn, table)


def chain_back_kernel(
    place_ref,
    flag_ref,
    start_ref,
    table_ref,
    attn_ref,
    ffn_ref,
    q_ref,
    k_ref,
    v_ref,
    saved_d_ref,
    saved_f_ref,
    saved_s_ref,
    dk_in,
    dv_in,
    thin_d_in,
    thin_f_in,
    sums_in,
    dk_ref,
    dv_ref,
    thin_d_ref,
    thin_f_ref,
    sums_ref,
    grad_ref,
    wa,
    wf,
    qb,
    kb,
    vb,
    dkb,
    dvb,
    save_d,
    save_f,
    save_s,
    thin_d,
    thin_f,
    sums,
    sem_w,
    sem_in,
    sem_out,
):
    del dk_in, dv_in, thin_d_in, thin_f_in, sums_in
    grad_ref[...] = start_ref[...]

    @pl.when(flag_ref[0] > 0)
    def _():
        loads = [
            pltpu.make_async_copy(attn_ref, wa, sem_w.at[0]),
            pltpu.make_async_copy(ffn_ref.at[0], wf.at[0], sem_w.at[1]),
            pltpu.make_async_copy(ffn_ref.at[1], wf.at[1], sem_w.at[2]),
        ]
        reads = [
            pltpu.make_async_copy(q_ref.at[:, pl.ds(0, THIN)], qb, sem_in.at[0]),
            pltpu.make_async_copy(k_ref, kb, sem_in.at[1]),
            pltpu.make_async_copy(v_ref, vb, sem_in.at[2]),
            pltpu.make_async_copy(dk_ref, dkb, sem_in.at[3]),
            pltpu.make_async_copy(dv_ref, dvb, sem_in.at[4]),
            pltpu.make_async_copy(saved_d_ref, save_d, sem_in.at[5]),
            pltpu.make_async_copy(saved_f_ref, save_f, sem_in.at[6]),
            pltpu.make_async_copy(saved_s_ref, save_s, sem_in.at[7]),
        ]
        for c in reads + [loads[2], loads[1], loads[0]]:
            c.start()
        sums[...] = jnp.zeros_like(sums)
        masks = head_masks()
        memory_row = lax.broadcasted_iota(jnp.int32, (THIN, 1), 0) < MEM
        row = lambda r: table_ref[r : r + 1, :]

        def add(r, value):
            sums[r : r + 1, :] += value

        for c in reads:
            c.wait()
        loads[2].wait()
        loads[1].wait()
        loads[0].wait()
        for s in reversed(range(LOCAL)):
            after = flag_ref[2] if s == LOCAL - 1 else place_ref[s + 1]

            def through(s=s, after=after):
                grad = jnp.where(memory_row & (after > 0), grad_ref[...], 0.0)
                unit1, unit2 = save_d[s, 1].astype(F32), save_d[s, 2].astype(F32)
                base = HEADS * THIN
                log_total = save_s[s, 0:base, 0:1]
                inverse1 = save_s[s, base : base + THIN, 0:1]
                inverse2 = save_s[s, base + THIN :, 0:1]
                add(GAIN2, row_sum(grad * unit2))
                add(SHIFT2, row_sum(grad))
                second_grad = normalized_back(grad * row(GAIN2), unit2, inverse2)
                down_grad = second_grad.astype(BF16)
                add(DOWN_BIAS, row_sum(down_grad.astype(F32)))
                up_grad = (nt(down_grad, wf[1]) * save_f[s, 1].astype(F32)).astype(BF16)
                up_sum = row_sum(up_grad.astype(F32))
                for i in range(FF // D):
                    add(UP_BIAS + i, up_sum[:, D * i : D * (i + 1)])
                hidden_grad = second_grad + nn(up_grad, wf[0])
                add(GAIN1, row_sum(hidden_grad * unit1))
                add(SHIFT1, row_sum(hidden_grad))
                pre_grad = normalized_back(hidden_grad * row(GAIN1), unit1, inverse1)
                branch_grad = pre_grad.astype(BF16)
                add(OUT_BIAS, row_sum(branch_grad.astype(F32)))
                context_grad = jnp.concatenate(
                    [nn(branch_grad, wa[0, 3]), nn(branch_grad, wa[1, 3])], axis=1
                ).astype(BF16)
                dc_heads = by_head(context_grad, masks)
                q_heads = by_head(qb[s], masks)
                score = nt(q_heads, kb[s])
                share = jnp.exp(score - log_total) * copies_of(score.shape)
                share_grad = nt(dc_heads, vb[s])
                inner = jnp.sum(share_grad * share, axis=-1, keepdims=True)
                score_grad = (share * (share_grad - inner)).astype(BF16)
                query_grad = (own_columns(nn(score_grad, kb[s]), masks) * SCALE).astype(BF16)
                dkb[s] = (dkb[s].astype(F32) + tn(score_grad, q_heads)).astype(BF16)
                dvb[s] = (dvb[s].astype(F32) + tn(share.astype(BF16), dc_heads)).astype(BF16)
                thin_d[s, 0] = down_grad
                thin_d[s, 1] = branch_grad
                thin_d[s, 2] = query_grad
                thin_d[s, 3] = save_d[s, 0]
                thin_d[s, 4] = save_d[s, 3]
                thin_f[s, 0] = up_grad
                thin_f[s, 1] = save_f[s, 0]
                grad_ref[...] = (
                    pre_grad
                    + nt(query_grad[:, :HALF], wa[0, 0])
                    + nt(query_grad[:, HALF:], wa[1, 0])
                )

            if s == LOCAL - 1:

                @pl.when(flag_ref[1] > 0)
                def _():
                    through()

                @pl.when(flag_ref[1] == 0)
                def _():
                    thin_d[s] = jnp.zeros_like(thin_d[s])
                    thin_f[s] = jnp.zeros_like(thin_f[s])
                    grad_ref[...] = jnp.zeros_like(grad_ref)
            else:
                through()
            grad = grad_ref[...]
            for side in range(2):
                cols = slice(HALF * side, HALF * (side + 1))
                grad = grad + nt(dkb[s, 0:THIN, cols], wa[side, 1])
                grad = grad + nt(dvb[s, 0:THIN, cols], wa[side, 2])
            grad_ref[...] = grad
            first = jnp.where(place_ref[s] == 0, grad, 0.0)
            sums[FIRST_MEMORY : FIRST_MEMORY + THIN, :] += first
        writes = [
            pltpu.make_async_copy(dkb, dk_ref, sem_out.at[0]),
            pltpu.make_async_copy(dvb, dv_ref, sem_out.at[1]),
            pltpu.make_async_copy(thin_d, thin_d_ref, sem_out.at[2]),
            pltpu.make_async_copy(thin_f, thin_f_ref, sem_out.at[3]),
            pltpu.make_async_copy(sums, sums_ref, sem_out.at[4]),
        ]
        for c in writes:
            c.start()
        for c in writes:
            c.wait()


THIN_SHAPES = (
    sds((LOCAL, 5, THIN, D), BF16),
    sds((LOCAL, 2, THIN, FF), BF16),
    sds((FIRST_MEMORY + THIN, D), F32),
)


def chain_back(place, flag, start, table, attn, ffn, q, k, v, saved, dk, dv, thin):
    whole = sds((LOCAL, SEG, D), BF16)
    outs = pl.pallas_call(
        chain_back_kernel,
        in_specs=[SMEM, SMEM, VMEM, VMEM] + [ANY] * 13,
        out_specs=[ANY] * 5 + [VMEM],
        out_shape=[whole] * 2 + list(THIN_SHAPES) + [sds((THIN, D), F32)],
        input_output_aliases={12 + i: i for i in range(5)},
        scratch_shapes=[
            pltpu.VMEM((2, 4, D, HALF), BF16),
            pltpu.VMEM((2, FF, D), BF16),
            pltpu.VMEM((LOCAL, THIN, D), BF16),
        ]
        + [pltpu.VMEM((LOCAL, SEG, D), BF16)] * 4
        + [pltpu.VMEM(s.shape, s.dtype) for s in SAVED + THIN_SHAPES]
        + [
            pltpu.SemaphoreType.DMA((3,)),
            pltpu.SemaphoreType.DMA((8,)),
            pltpu.SemaphoreType.DMA((5,)),
        ],
        compiler_params=params(),
    )(place, flag, start, table, attn, ffn, q, k, v, *saved, dk, dv, *thin)
    return outs[:2], outs[2:5], outs[5]


def token_grad_kernel(da_ref, dq_ref, dk_ref, dv_ref, w_ref, out_ref):
    total = da_ref[0].astype(F32)
    for side in range(2):
        cols = slice(HALF * side, HALF * (side + 1))
        for i, ref in enumerate((dq_ref, dk_ref, dv_ref)):
            total = total + nt(ref[0, :, cols], w_ref[side, i])
    out_ref[0] = total.astype(BF16)


def token_gradient(da, dq, dk, dv, attn):
    rows = pl.BlockSpec((1, TILE, D), lambda s, i: (s, i, 0))
    return pl.pallas_call(
        token_grad_kernel,
        grid=(LOCAL, SEG // TILE),
        in_specs=[rows] * 4 + [once((2, 3, D, HALF), (0, 0, 0, 0))],
        out_specs=rows,
        out_shape=sds((LOCAL, SEG, D), BF16),
        compiler_params=params(),
    )(da, dq, dk, dv, attn)


def flat(ref):
    return ref[...].reshape(LOCAL * ref.shape[1], ref.shape[2])


def ffn_grad_kernel(g_ref, du_ref, df_ref, h_ref, thin_f_ref, thin_d_ref, out_ref):
    up = tn(flat(du_ref), flat(h_ref))
    down = tn(flat(g_ref), flat(df_ref))
    for s in range(LOCAL):
        up = up + tn(thin_f_ref[s, 0], thin_d_ref[s, 3])
        down = down + tn(thin_f_ref[s, 1], thin_d_ref[s, 0])
    out_ref[0] = up.astype(BF16)
    out_ref[1] = down.astype(BF16)


def ffn_gradient(g, du, df, h, thin_d, thin_f, chunk=256):
    hidden = pl.BlockSpec((LOCAL, SEG, chunk), lambda i: (0, 0, i))
    full = once((LOCAL, SEG, D), (0, 0, 0))
    return pl.pallas_call(
        ffn_grad_kernel,
        grid=(FF // chunk,),
        in_specs=[
            hidden,
            hidden,
            full,
            full,
            pl.BlockSpec((LOCAL, 2, THIN, chunk), lambda i: (0, 0, 0, i)),
            once(THIN_SHAPES[0].shape, (0, 0, 0, 0)),
        ],
        out_specs=pl.BlockSpec((2, chunk, D), lambda i: (0, i, 0)),
        out_shape=sds((2, FF, D), BF16),
        compiler_params=params(),
    )(g, du, df, h, thin_f, thin_d)


def attn_grad_kernel(x_ref, da_ref, dq_ref, dk_ref, dv_ref, c_ref, thin_d_ref, out_ref, bias_ref):
    thin_c = pl.ds(pl.multiple_of(pl.program_id(0) * HALF, HALF), HALF)
    x = flat(x_ref)
    dq, dk, dv = flat(dq_ref), flat(dk_ref), flat(dv_ref)
    query = tn(x, dq)
    query_bias = row_sum(dq.astype(F32))
    output = tn(flat(da_ref), flat(c_ref))
    for s in range(LOCAL):
        dq16 = thin_d_ref[s, 2, :, thin_c]
        query = query + tn(x_ref[s, 0:THIN], dq16)
        query_bias = query_bias + row_sum(dq16.astype(F32))
        output = output + tn(thin_d_ref[s, 1], thin_d_ref[s, 4, :, thin_c])
    out_ref[0, 0] = query.astype(BF16)
    out_ref[0, 1] = tn(x, dk).astype(BF16)
    out_ref[0, 2] = tn(x, dv).astype(BF16)
    out_ref[0, 3] = output.astype(BF16)
    bias_ref[0] = jnp.concatenate(
        [query_bias, row_sum(dv.astype(F32)), jnp.zeros((6, HALF), F32)], axis=0
    )


def attn_gradient(x, da, dq, dk, dv, c, thin_d):
    half = pl.BlockSpec((LOCAL, SEG, HALF), lambda i: (0, 0, i))
    full = once((LOCAL, SEG, D), (0, 0, 0))
    return pl.pallas_call(
        attn_grad_kernel,
        grid=(2,),
        in_specs=[full, full, half, half, half, half, once(THIN_SHAPES[0].shape, (0, 0, 0, 0))],
        out_specs=[
            pl.BlockSpec((1, 4, D, HALF), lambda i: (i, 0, 0, 0)),
            pl.BlockSpec((1, 8, HALF), lambda i: (i, 0, 0)),
        ],
        out_shape=[sds((2, 4, D, HALF), BF16), sds((2, 8, HALF), F32)],
        compiler_params=params(),
    )(x, da, dq, dk, dv, c, thin_d)


def update(gradient, momentum, weight, average, rate, grad_scale):
    scaled = gradient * grad_scale
    moment = MOMENTUM * momentum + scaled
    weight_new = weight - rate * (scaled + MOMENTUM * moment)
    return (moment, weight_new, AVERAGE_DECAY * average + (1.0 - AVERAGE_DECAY) * weight_new)


def gather_weights(attention, feedforward, vectors):
    attn = lax.all_gather(attention.astype(BF16), "dp", axis=1, tiled=True)
    attn = lax.all_gather(attn, "tensor", axis=0)
    hidden_major = jnp.swapaxes(feedforward.astype(BF16), 1, 2)
    ffn = lax.all_gather(hidden_major, ("dp", "tensor"), axis=1, tiled=True)
    table = lax.all_gather(vectors.astype(BF16), ("dp", "tensor"), axis=0, tiled=True)
    return attn, ffn, table.reshape(NVEC, D).astype(F32)


def swap(value):
    return lax.ppermute(value, "tensor", [(0, 1), (1, 0)])


def whole_rows(halves, side):
    mine = lax.dynamic_slice_in_dim(halves, LOCAL * side, LOCAL, 0)
    other = swap(lax.dynamic_slice_in_dim(halves, LOCAL * (1 - side), LOCAL, 0))
    first = jnp.where(side == 0, mine, other)
    second = jnp.where(side == 0, other, mine)
    return jnp.concatenate([jnp.zeros((LOCAL, MEM, D), halves.dtype), first, second], axis=1)


def half_rows(rows, side):
    half = (SEG - MEM) // 2
    first, second = rows[:, MEM : MEM + half], rows[:, MEM + half :]
    mine = jnp.where(side == 0, first, second)
    other = swap(jnp.where(side == 0, second, first))
    return jnp.concatenate(
        [jnp.where(side == 0, mine, other), jnp.where(side == 0, other, mine)], axis=0
    )


def on_device(
    tokens,
    slot_position,
    cotangent,
    attention,
    feedforward,
    vectors,
    attn_momentum,
    ffn_momentum,
    vec_momentum,
    attn_average,
    ffn_average,
    vec_average,
):
    side = lax.axis_index("tensor")
    first_side = side == 0
    attn, ffn, table = gather_weights(attention, feedforward, vectors)
    place = lax.dynamic_slice_in_dim(slot_position, LOCAL * side, LOCAL, 0)
    live = (place >= 0)[:, None, None]

    x = whole_rows(tokens, side)
    cot = jnp.where(live, whole_rows(cotangent, side), 0)
    q, k, v = project(x, attn, table)

    on = lambda flag: flag.astype(jnp.int32)
    saved = tuple(jnp.zeros(s.shape, s.dtype) for s in SAVED)
    start = jnp.zeros((THIN, D), BF16)
    flag = jnp.stack([on(first_side), jnp.int32(1)])
    (x, q, k, v), saved, memory = chain(place, flag, start, table, attn, ffn, x, q, k, v, saved)
    memory = lax.ppermute(memory, "tensor", [(0, 1)])
    flag = jnp.stack([on(~first_side), jnp.int32(0)])
    (x, q, k, v), saved, _ = chain(place, flag, memory, table, attn, ffn, x, q, k, v, saved)

    c, log_total = attend(q, k, v)
    y, h, g, du, df, da, dc, sums = rows_part(x, c, cot, attn, ffn, table)
    dq, dk, dv = attend_back(q, k, v, dc, log_total)

    thin = tuple(jnp.zeros(s.shape, s.dtype) for s in THIN_SHAPES)
    back = functools.partial(chain_back, place)
    flag = jnp.stack([on(~first_side), jnp.int32(0), jnp.int32(-1)])
    start = jnp.zeros((THIN, D), F32)
    (dk, dv), thin, grad = back(flag, start, table, attn, ffn, q, k, v, saved, dk, dv, thin)
    grad = lax.ppermute(grad, "tensor", [(1, 0)])
    flag = jnp.stack([on(first_side), jnp.int32(1), slot_position[LOCAL]])
    (dk, dv), thin, _ = back(flag, grad, table, attn, ffn, q, k, v, saved, dk, dv, thin)
    thin_d, thin_f, thin_sums = thin

    token_grad = token_gradient(da, dq, dk, dv, attn)
    ffn_terms = ffn_gradient(g, du, df, h, thin_d, thin_f)
    attn_terms, bias_terms = attn_gradient(x, da, dq, dk, dv, c, thin_d)

    activations = half_rows(jnp.where(live, y, 0), side)
    token_grad = half_rows(jnp.where(live, token_grad, 0), side)

    bias_rows = jnp.concatenate([bias_terms[0, :2], bias_terms[1, :2]], axis=1)
    leading = jnp.concatenate([bias_rows, sums[2:FIRST_MEMORY], jnp.zeros((MEM, D), F32)], axis=0)
    vec_terms = leading + thin_sums[:NVEC]

    attn_grad = lax.psum_scatter(attn_terms, "tensor", scatter_dimension=0, tiled=False)
    attn_grad = lax.psum_scatter(attn_grad, "dp", scatter_dimension=1, tiled=True).astype(F32)
    ffn_grad = lax.psum_scatter(ffn_terms, ("dp", "tensor"), scatter_dimension=1, tiled=True)
    ffn_grad = jnp.swapaxes(ffn_grad, 1, 2).astype(F32)
    vec_grad = lax.psum_scatter(
        vec_terms.reshape(-1), ("dp", "tensor"), scatter_dimension=0, tiled=True
    )
    grad_scale = 1.0 / math.sqrt(lax.axis_size("dp") * SLOTS * ROWS)
    attn_new = update(attn_grad, attn_momentum, attention, attn_average, ATTENTION_RATE, grad_scale)
    ffn_new = update(ffn_grad, ffn_momentum, feedforward, ffn_average, FEEDFORWARD_RATE, grad_scale)
    vec_new = update(vec_grad, vec_momentum, vectors, vec_average, VECTOR_RATE, grad_scale)
    return (
        activations,
        token_grad,
        attn_new[0],
        ffn_new[0],
        vec_new[0],
        attn_new[1],
        ffn_new[1],
        vec_new[1],
        attn_new[2],
        ffn_new[2],
        vec_new[2],
    )


def solution(mesh):
    attn_spec = P(None, "dp", "tensor")
    ffn_spec = P(None, None, ("dp", "tensor"))
    vec_spec = P(("dp", "tensor"))
    rows_spec = P("dp", "tensor", None)
    states = (attn_spec, ffn_spec, vec_spec)
    return jax.shard_map(
        on_device,
        mesh=mesh,
        in_specs=(rows_spec, P("dp"), rows_spec) + states * 3,
        out_specs=(rows_spec, rows_spec) + states * 3,
        check_vma=False,
    )
```

```python
import functools
import math

import jax
import jax.numpy as jnp
from jax import lax
from jax.experimental import pallas as pl
from jax.experimental.pallas import tpu as pltpu
from jax.sharding import PartitionSpec as P

D = 768
HEADS = 12
DH = 64
FF = 3072
MEM = 10
SLOTS = 4
ROWS = 522
NVEC = 22

HALF = D // 2
SEG = ROWS - MEM
THIN = 16
LOCAL = 2
TILE = 256

EPSILON = 1e-05
MOMENTUM = 0.9
AVERAGE_DECAY = 0.75
ATTENTION_RATE = 0.06
FEEDFORWARD_RATE = 0.02
VECTOR_RATE = 0.1
MASK_VALUE = -1e30
SCALE = 1.0 / math.sqrt(DH)

F32 = jnp.float32
BF16 = jnp.bfloat16
MIB = 1 << 20

QUERY_BIAS, VALUE_BIAS, OUT_BIAS, GAIN1, SHIFT1, DOWN_BIAS, GAIN2, SHIFT2, UP_BIAS = range(9)
FIRST_MEMORY = UP_BIAS + FF // D


def nn(a, b):
    return lax.dot_general(a, b, (((1,), (0,)), ((), ())), preferred_element_type=F32)


def nt(a, b):
    return lax.dot_general(a, b, (((1,), (1,)), ((), ())), preferred_element_type=F32)


def tn(a, b):
    return lax.dot_general(a, b, (((0,), (0,)), ((), ())), preferred_element_type=F32)


def normalized(rows):
    center = rows - jnp.mean(rows, axis=-1, keepdims=True)
    spread = jnp.mean(center * center, axis=-1, keepdims=True)
    inverse = lax.rsqrt(spread + EPSILON)
    return center * inverse, inverse


def normalized_back(grad, unit, inverse):
    mean_grad = jnp.mean(grad, axis=-1, keepdims=True)
    mean_along = jnp.mean(grad * unit, axis=-1, keepdims=True)
    return inverse * (grad - mean_grad - unit * mean_along)


def gelu_parts(u):
    size = jnp.abs(u)
    t = 1.0 / (1.0 + (0.3275911 / math.sqrt(2.0)) * size)
    bell = jnp.exp(-0.5 * u * u)
    poly = t * (
        0.5 * 0.254829592
        + t
        * (
            0.5 * -0.284496736
            + t * (0.5 * 1.421413741 + t * (0.5 * -1.453152027 + t * (0.5 * 1.061405429)))
        )
    )
    tail = poly * bell
    cdf = jnp.where(u < 0, tail, 1.0 - tail)
    return u * cdf, cdf + (u * (1.0 / math.sqrt(2.0 * math.pi))) * bell


def row_sum(block):
    return jnp.sum(block, axis=0, keepdims=True)


def params(limit=60, **more):
    return pltpu.CompilerParams(vmem_limit_bytes=limit * MIB, **more)


def once(shape, index):
    return pl.BlockSpec(shape, lambda *_: index, pipeline_mode=pl.Buffered(1))


ANY = pl.BlockSpec(memory_space=pl.ANY)
SMEM = pl.BlockSpec(memory_space=pltpu.SMEM)
VMEM = pl.BlockSpec(memory_space=pltpu.VMEM)


def sds(shape, dtype):
    return jax.ShapeDtypeStruct(shape, dtype)


def my_place():
    dp = lax.axis_index("dp")
    return dp // 4, (dp // 2) % 2, dp % 2, lax.axis_index("tensor")


def device(z, x, c, y):
    return {"dp": (z * 2 + x) * 2 + c, "tensor": y}


def entry_barrier(nz):
    z, x, c, y = my_place()
    barrier = pltpu.get_barrier_semaphore()
    signal = lambda d: pl.semaphore_signal(
        barrier, inc=1, device_id=d, device_id_type=pl.DeviceIdType.MESH
    )
    signal(device(z, 1 - x, c, y))
    signal(device(z, x, 1 - c, y))
    signal(device(z, x, c, 1 - y))

    @pl.when(z > 0)
    def _():
        signal(device(z - 1, x, c, y))

    @pl.when(z < nz - 1)
    def _():
        signal(device(z + 1, x, c, y))

    up = lax.convert_element_type(z < nz - 1, jnp.int32)
    down = lax.convert_element_type(z > 0, jnp.int32)
    pl.semaphore_wait(barrier, 3 + up + down)


def attn_view(ref, z, x, c, y):
    return ref.at[y, :, z, x, c]


def ffn_view(ref, z, x, c, y):
    return ref.at[:, z, x, c, y]


def vec_view(ref, z, x, c, y):
    return ref.at[z, x, c, y]


def partners(place):
    _, x, c, y = place
    first = (x + (1 - c) * (1 - 2 * x), y + c * (1 - 2 * y))
    second = (x + c * (1 - 2 * x), y + (1 - c) * (1 - 2 * y))
    return first, second, (1 - x, 1 - y)


COLUMN, FIRST, SECOND, BOTH, CORE = 0, 1, 2, 3, 4
UP, DOWN = 0, 8


def gather_kernel(nz, views, *refs):
    n = len(views)
    srcs, outs = refs[:n], refs[n : 2 * n]
    send_sem, recv_sem, own_sem = refs[2 * n :]
    place = z, x, c, y = my_place()
    first, second, both = partners(place)
    own = [
        pltpu.make_async_copy(src, view(out, *place), own_sem.at[i])
        for i, (src, out, view) in enumerate(zip(srcs, outs, views))
    ]
    for copy in own:
        copy.start()
    entry_barrier(nz)
    for copy in own:
        copy.wait()
    to_first = device(z, first[0], c, first[1])
    to_second = device(z, second[0], c, second[1])
    to_core = device(z, x, 1 - c, y)

    def copies(send, recv, shard, target):
        return [
            pltpu.make_async_remote_copy(
                src_ref=view(out, *shard),
                dst_ref=view(out, *shard),
                send_sem=send_sem.at[send, shard[0], i],
                recv_sem=recv_sem.at[recv, shard[0], i],
                device_id=target,
                device_id_type=pl.DeviceIdType.MESH,
            )
            for i, (out, view) in enumerate(zip(outs, views))
        ]

    def start(*args):
        for copy in copies(*args):
            copy.start()

    def arrived(*args):
        for copy in copies(*args):
            copy.wait_recv()

    def sent(*args):
        for copy in copies(*args):
            copy.wait_send()

    def column(zz):
        return (zz, x, c, y)

    def of_first(zz):
        return (zz, first[0], c, first[1])

    def of_second(zz):
        return (zz, second[0], c, second[1])

    def of_both(zz):
        return (zz, both[0], c, both[1])

    core_first, core_second = CORE + 2 - c, CORE + 1 + c

    def move_up(zz):
        return (UP, COLUMN, column(zz), device(z + 1, x, c, y))

    def move_down(zz):
        return (DOWN, COLUMN, column(zz), device(z - 1, x, c, y))

    def stage0(zz, rising, falling, wait):
        if wait:
            arrived(UP, COLUMN, column(zz), to_core)
        if rising:

            @pl.when(z < nz - 1)
            def _():
                start(*move_up(zz))

        if falling:

            @pl.when(z > 0)
            def _():
                start(*move_down(zz))

        start(FIRST, FIRST, column(zz), to_first)
        start(SECOND, SECOND, column(zz), to_second)
        start(CORE, CORE, column(zz), to_core)

    def stage1(zz):
        arrived(FIRST, FIRST, of_first(zz), to_first)
        start(BOTH, BOTH, of_first(zz), to_second)
        start(core_first, core_first, of_first(zz), to_core)

    def stage2(zz):
        arrived(SECOND, SECOND, of_second(zz), to_second)
        start(core_second, core_second, of_second(zz), to_core)
        arrived(BOTH, BOTH, of_both(zz), to_second)
        start(CORE + 3, CORE + 3, of_both(zz), to_core)

    stage0(z, True, True, False)

    def step(t, carry):
        @pl.when((t < nz) & (z - t >= 0))
        def _():
            stage0(z - t, True, False, True)

        @pl.when((t < nz) & (z + t < nz))
        def _():
            stage0(z + t, False, True, True)

        for lag, stage in ((1, stage1), (2, stage2)):
            late = t - lag

            @pl.when((late >= 0) & (late < nz) & (z - late >= 0))
            def _():
                stage(z - late)

            @pl.when((late > 0) & (late < nz) & (z + late < nz))
            def _():
                stage(z + late)

        return carry

    lax.fori_loop(1, nz + 2, step, 0)

    def finish(zz, carry):
        @pl.when((zz <= z) & (z < nz - 1))
        def _():
            sent(*move_up(zz))

        @pl.when((zz >= z) & (z > 0))
        def _():
            sent(*move_down(zz))

        sent(FIRST, FIRST, column(zz), to_first)
        sent(SECOND, SECOND, column(zz), to_second)
        sent(BOTH, BOTH, of_first(zz), to_second)
        sent(CORE, CORE, column(zz), to_core)
        sent(core_first, core_first, of_first(zz), to_core)
        sent(core_second, core_second, of_second(zz), to_core)
        sent(CORE + 3, CORE + 3, of_both(zz), to_core)
        for fx in range(2):
            for fy in range(2):
                kind = CORE + 2 * fx + fy
                shard = (zz, x + fx * (1 - 2 * x), 1 - c, y + fy * (1 - 2 * y))
                arrived(kind, kind, shard, to_core)
        return carry

    lax.fori_loop(0, nz, finish, 0)


def gather(nz, collective_id, parts):
    shards, shapes, views = zip(*parts)
    n = len(parts)
    return pl.pallas_call(
        functools.partial(gather_kernel, nz, views),
        in_specs=[ANY] * n,
        out_specs=[ANY] * n,
        out_shape=[sds(shape, shard.dtype) for shard, shape in zip(shards, shapes)],
        scratch_shapes=[
            pltpu.SemaphoreType.DMA((9, nz, n)),
            pltpu.SemaphoreType.DMA((8, nz, n)),
            pltpu.SemaphoreType.DMA((n,)),
        ],
        compiler_params=params(16, collective_id=collective_id, has_side_effects=True),
    )(*shards)


def scatter_kernel(nz, views, *refs):
    n = len(views)
    terms, outs = refs[:n], refs[n : 2 * n]
    mine, from_core, from_second, from_first, from_below, from_above = (
        refs[2 * n + i * n : 3 * n + i * n] for i in range(6)
    )
    send_sem, recv_sem, own_sem = refs[8 * n :]
    place = z, x, c, y = my_place()
    first, second, both = partners(place)
    to_first = device(z, first[0], c, first[1])
    to_second = device(z, second[0], c, second[1])
    to_core = device(z, x, 1 - c, y)

    def copies(srcs, dsts, send, recv, zz, target):
        return [
            pltpu.make_async_remote_copy(
                src_ref=srcs[i],
                dst_ref=dsts[i],
                send_sem=send_sem.at[send, zz, i],
                recv_sem=recv_sem.at[recv, zz, i],
                device_id=target,
                device_id_type=pl.DeviceIdType.MESH,
            )
            for i in range(n)
        ]

    def slots(bufs, *index):
        return [b.at[index] for b in bufs]

    def pick(refs_, *index):
        return [b[index] for b in refs_]

    flips = [(fx, fy) for fx in range(2) for fy in range(2)]

    def at(fx, fy):
        return x + fx * (1 - 2 * x), y + fy * (1 - 2 * y)

    def core_copies(zz, f):
        fx, fy = flips[f]
        xx, yy = at(fx, fy)
        return copies(
            [view(t, zz, xx, 1 - c, yy) for t, view in zip(terms, views)],
            slots(from_core, zz, f),
            f,
            f,
            zz,
            to_core,
        )

    def own_copies(zz, f):
        fx, fy = flips[f]
        xx, yy = at(fx, fy)
        return [
            pltpu.make_async_copy(
                view(t, zz, xx, c, yy), mine[i].at[zz, f], own_sem.at[f, zz, i]
            )
            for i, (t, view) in enumerate(zip(terms, views))
        ]

    f_first, f_second = 2 - c, 1 + c

    def second_copies(zz, across):
        return copies(
            slots(from_core, zz, 3 if across else f_second),
            slots(from_second, zz, 1 if across else 0),
            4 + across,
            4 + across,
            zz,
            to_second,
        )

    def first_copies(zz):
        return copies(slots(from_second, zz, 1), slots(from_first, zz), 6, 6, zz, to_first)

    def up_copies(zz):
        return copies(slots(from_first, zz), slots(from_below, zz), 7, 7, zz, device(z + 1, x, c, y))

    def down_copies(zz):
        return copies(slots(from_first, zz), slots(from_above, zz), 8, 8, zz, device(z - 1, x, c, y))

    def run(group, what):
        for copy in group:
            getattr(copy, what)()

    def add(into, index, other, other_index):
        for i in range(n):
            a, b = into[i].at[index], other[i].at[other_index]
            a[...] = (a[...].astype(F32) + b[...].astype(F32)).astype(a.dtype)

    def by_distance(t, do):
        @pl.when((t >= 0) & (t < nz) & (z - t >= 0))
        def _():
            do(z - t)

        @pl.when((t > 0) & (t < nz) & (z + t < nz))
        def _():
            do(z + t)

    def start_own(zz):
        for f in range(4):
            run(own_copies(zz, f), "start")

    def start_core(zz):
        for f in (3, 1, 2, 0):
            run(core_copies(zz, f), "start")

    def stage0(zz):
        for f in (3, 1, 2, 0):
            run(core_copies(zz, f), "wait_recv")
            run(own_copies(zz, f), "wait")
            add(from_core, (zz, f), mine, (zz, f))
        run(second_copies(zz, 1), "start")
        run(second_copies(zz, 0), "start")

    def stage1(zz):
        run(second_copies(zz, 1), "wait_recv")
        add(from_second, (zz, 1), from_core, (zz, f_first))
        run(first_copies(zz), "start")

    def stage2(zz):
        run(second_copies(zz, 0), "wait_recv")
        add(from_second, (zz, 0), from_core, (zz, 0))
        run(first_copies(zz), "wait_recv")
        add(from_first, (zz,), from_second, (zz, 0))

        @pl.when(zz > z)
        def _():
            @pl.when(z > 0)
            def _():
                run(up_copies(zz), "wait_recv")
                add(from_first, (zz,), from_below, (zz,))

            run(up_copies(zz), "start")

        @pl.when(zz < z)
        def _():
            @pl.when(z < nz - 1)
            def _():
                run(down_copies(zz), "wait_recv")
                add(from_first, (zz,), from_above, (zz,))

            run(down_copies(zz), "start")

    entry_barrier(nz)

    def begin(k, carry):
        by_distance(nz - 1 - k, start_core)
        by_distance(nz - 1 - k, start_own)
        return carry

    lax.fori_loop(0, nz, begin, 0)

    def step(k, carry):
        t = nz - 1 - k
        by_distance(t, stage0)
        by_distance(t + 1, stage1)
        by_distance(t + 2, stage2)
        return carry

    lax.fori_loop(0, nz + 2, step, 0)

    @pl.when(z > 0)
    def _():
        run(up_copies(z), "wait_recv")
        add(from_first, (z,), from_below, (z,))

    @pl.when(z < nz - 1)
    def _():
        run(down_copies(z), "wait_recv")
        add(from_first, (z,), from_above, (z,))

    for i in range(n):
        outs[i][...] = from_first[i][z]

    def finish(zz, carry):
        for f in range(4):
            run(core_copies(zz, f), "wait_send")
        run(second_copies(zz, 1), "wait_send")
        run(second_copies(zz, 0), "wait_send")
        run(first_copies(zz), "wait_send")

        @pl.when(zz > z)
        def _():
            run(up_copies(zz), "wait_send")

        @pl.when(zz < z)
        def _():
            run(down_copies(zz), "wait_send")

        return carry

    lax.fori_loop(0, nz, finish, 0)


def scatter(nz, collective_id, parts):
    terms, shapes, views = zip(*parts)
    n = len(parts)
    dtypes = [t.dtype for t in terms]

    def bufs(*lead):
        return [pltpu.VMEM((*lead, *shape), d) for shape, d in zip(shapes, dtypes)]

    return pl.pallas_call(
        functools.partial(scatter_kernel, nz, views),
        in_specs=[ANY] * n,
        out_specs=[VMEM] * n,
        out_shape=[sds(shape, d) for shape, d in zip(shapes, dtypes)],
        scratch_shapes=[
            *bufs(nz, 4),
            *bufs(nz, 4),
            *bufs(nz, 2),
            *bufs(nz),
            *bufs(nz),
            *bufs(nz),
            pltpu.SemaphoreType.DMA((9, nz, n)),
            pltpu.SemaphoreType.DMA((9, nz, n)),
            pltpu.SemaphoreType.DMA((4, nz, n)),
        ],
        compiler_params=params(62, collective_id=collective_id, has_side_effects=True),
    )(*terms)


def project_kernel(x_ref, w_ref, table_ref, q_ref, k_ref, v_ref):
    x = x_ref[0]
    for side in range(2):
        cols = slice(HALF * side, HALF * (side + 1))
        query = nn(x, w_ref[side, 0]) + table_ref[QUERY_BIAS : QUERY_BIAS + 1, cols]
        q_ref[0, :, cols] = (query * SCALE).astype(BF16)
        k_ref[0, :, cols] = nn(x, w_ref[side, 1]).astype(BF16)
        value = nn(x, w_ref[side, 2]) + table_ref[VALUE_BIAS : VALUE_BIAS + 1, cols]
        v_ref[0, :, cols] = value.astype(BF16)


def project(x, attn, table):
    rows = pl.BlockSpec((1, TILE, D), lambda s, i: (s, i, 0))
    return pl.pallas_call(
        project_kernel,
        grid=(LOCAL, SEG // TILE),
        in_specs=[rows, once((2, 3, D, HALF), (0, 0, 0, 0)), once((NVEC, D), (0, 0))],
        out_specs=[rows] * 3,
        out_shape=[sds((LOCAL, SEG, D), BF16)] * 3,
        compiler_params=params(),
    )(x, attn, table)


def head_masks():
    feature_head = lax.broadcasted_iota(jnp.int32, (1, D), 1) // DH
    return [feature_head == h for h in range(HEADS)]


def by_head(rows16, masks):
    zero = jnp.zeros_like(rows16)
    return jnp.concatenate([jnp.where(m, rows16, zero) for m in masks], axis=0)


def own_columns(blocks, masks):
    total = jnp.zeros((THIN, D), blocks.dtype)
    for h, m in enumerate(masks):
        total = jnp.where(m, blocks[THIN * h : THIN * (h + 1)], total)
    return total


def copies_of(key_mask_shape):
    row = lax.rem(lax.broadcasted_iota(jnp.int32, key_mask_shape, 0), THIN)
    key = lax.broadcasted_iota(jnp.int32, key_mask_shape, 1)
    return jnp.where((key < MEM) & (key <= row), 2.0, 1.0)


def chain_kernel(
    place_ref,
    flag_ref,
    start_ref,
    table_ref,
    attn_ref,
    ffn_ref,
    x_in,
    q_in,
    k_in,
    v_in,
    saved_d_in,
    saved_f_in,
    saved_s_in,
    x_ref,
    q_ref,
    k_ref,
    v_ref,
    saved_d_ref,
    saved_f_ref,
    saved_s_ref,
    memory_ref,
    wa,
    wf,
    xb,
    qb,
    kb,
    vb,
    save_d,
    save_f,
    save_s,
    sem_w,
    sem_x,
    sem_kv,
    sem_out,
):
    del x_in, q_in, k_in, v_in, saved_d_in, saved_f_in, saved_s_in
    active = flag_ref[0] > 0
    memory_ref[...] = start_ref[...]

    @pl.when(active)
    def _():
        loads = [
            pltpu.make_async_copy(attn_ref, wa, sem_w.at[0]),
            pltpu.make_async_copy(ffn_ref.at[0], wf.at[0], sem_w.at[1]),
            pltpu.make_async_copy(ffn_ref.at[1], wf.at[1], sem_w.at[2]),
        ]
        tiles = [
            pltpu.make_async_copy(x_ref.at[s, pl.ds(0, THIN)], xb.at[s], sem_x.at[s])
            for s in range(LOCAL)
        ]
        keys = [
            pltpu.make_async_copy(src.at[s], dst.at[s], sem_kv.at[2 * s + i])
            for s in range(LOCAL)
            for i, (src, dst) in enumerate(((k_ref, kb), (v_ref, vb)))
        ]
        for c in tiles + loads[:1] + keys + loads[1:]:
            c.start()
        masks = head_masks()
        memory_row = lax.broadcasted_iota(jnp.int32, (THIN, 1), 0) < MEM
        first = table_ref[FIRST_MEMORY:NVEC, :]
        first = jnp.concatenate([first, jnp.zeros((THIN - MEM, D), F32)], axis=0)
        row = lambda r: table_ref[r : r + 1, :]
        for s in range(LOCAL):
            tiles[s].wait()
            if s == 0:
                loads[0].wait()
            keys[2 * s].wait()
            keys[2 * s + 1].wait()
            memory = jnp.where(place_ref[s] == 0, first, memory_ref[...].astype(F32))
            x16 = jnp.where(memory_row, memory, xb[s].astype(F32)).astype(BF16)
            xb[s] = x16
            for side in range(2):
                cols = slice(HALF * side, HALF * (side + 1))
                query = nn(x16, wa[side, 0]) + table_ref[QUERY_BIAS : QUERY_BIAS + 1, cols]
                qb[s, :, cols] = (query * SCALE).astype(BF16)
                kb[s, 0:THIN, cols] = nn(x16, wa[side, 1]).astype(BF16)
                value = nn(x16, wa[side, 2]) + table_ref[VALUE_BIAS : VALUE_BIAS + 1, cols]
                vb[s, 0:THIN, cols] = value.astype(BF16)
            outs = [
                pltpu.make_async_copy(xb.at[s], x_ref.at[s, pl.ds(0, THIN)], sem_out.at[4 * s]),
                pltpu.make_async_copy(qb.at[s], q_ref.at[s, pl.ds(0, THIN)], sem_out.at[4 * s + 1]),
                pltpu.make_async_copy(
                    kb.at[s, pl.ds(0, THIN)], k_ref.at[s, pl.ds(0, THIN)], sem_out.at[4 * s + 2]
                ),
                pltpu.make_async_copy(
                    vb.at[s, pl.ds(0, THIN)], v_ref.at[s, pl.ds(0, THIN)], sem_out.at[4 * s + 3]
                ),
            ]
            for c in outs:
                c.start()

            def rest(s=s):
                q_heads = by_head(qb[s], masks)
                score = nt(q_heads, kb[s])
                top = jnp.max(score, axis=-1, keepdims=True)
                weight = jnp.exp(score - top) * copies_of(score.shape)
                total = jnp.sum(weight, axis=-1, keepdims=True)
                share = (weight / total).astype(BF16)
                log_total = top + jnp.log(total)
                context = own_columns(nn(share, vb[s]), masks).astype(BF16)
                branch = nt(context[:, :HALF], wa[0, 3]) + nt(context[:, HALF:], wa[1, 3])
                unit1, inverse1 = normalized(xb[s].astype(F32) + branch + row(OUT_BIAS))
                hidden = (unit1 * row(GAIN1) + row(SHIFT1)).astype(BF16)
                if s == 0:
                    loads[1].wait()
                up = nt(hidden, wf[0])
                up_bias = jnp.concatenate([row(UP_BIAS + i) for i in range(FF // D)], axis=1)
                active16, slope = gelu_parts(up + up_bias)
                active16 = active16.astype(BF16)
                if s == 0:
                    loads[2].wait()
                second = hidden.astype(F32) + nn(active16, wf[1]) + row(DOWN_BIAS)
                unit2, inverse2 = normalized(second)
                memory_ref[...] = (unit2 * row(GAIN2) + row(SHIFT2)).astype(BF16)
                save_d[s, 0] = hidden
                save_d[s, 1] = unit1.astype(BF16)
                save_d[s, 2] = unit2.astype(BF16)
                save_d[s, 3] = context
                save_f[s, 0] = active16
                save_f[s, 1] = slope.astype(BF16)
                wide = lambda v: jnp.broadcast_to(v, (v.shape[0], 128))
                save_s[s, 0 : HEADS * THIN] = wide(log_total)
                save_s[s, HEADS * THIN : HEADS * THIN + THIN] = wide(inverse1)
                save_s[s, HEADS * THIN + THIN :] = wide(inverse2)

            if s == LOCAL - 1:
                last_needed = flag_ref[1] > 0

                @pl.when(last_needed)
                def _():
                    rest()

                @pl.when(jnp.logical_not(last_needed))
                def _():
                    loads_done = (s != 0)
                    del loads_done
                    save_d[s] = jnp.zeros_like(save_d[s])
                    save_f[s] = jnp.zeros_like(save_f[s])
                    save_s[s] = jnp.zeros_like(save_s[s])
            else:
                rest()
            for c in outs:
                c.wait()
        saves = [
            pltpu.make_async_copy(save_d, saved_d_ref, sem_out.at[0]),
            pltpu.make_async_copy(save_f, saved_f_ref, sem_out.at[1]),
            pltpu.make_async_copy(save_s, saved_s_ref, sem_out.at[2]),
        ]
        for c in saves:
            c.start()
        for c in saves:
            c.wait()


SAVED = (
    sds((LOCAL, 4, THIN, D), BF16),
    sds((LOCAL, 2, THIN, FF), BF16),
    sds((LOCAL, HEADS * THIN + 2 * THIN, 128), F32),
)


def chain(place, flag, start, table, attn, ffn, x, q, k, v, saved):
    whole = sds((LOCAL, SEG, D), BF16)
    outs = pl.pallas_call(
        chain_kernel,
        in_specs=[SMEM, SMEM, VMEM, VMEM] + [ANY] * 9,
        out_specs=[ANY] * 7 + [VMEM],
        out_shape=[whole] * 4 + list(SAVED) + [sds((THIN, D), BF16)],
        input_output_aliases={6 + i: i for i in range(7)},
        scratch_shapes=[
            pltpu.VMEM((2, 4, D, HALF), BF16),
            pltpu.VMEM((2, FF, D), BF16),
            pltpu.VMEM((LOCAL, THIN, D), BF16),
            pltpu.VMEM((LOCAL, THIN, D), BF16),
            pltpu.VMEM((LOCAL, SEG, D), BF16),
            pltpu.VMEM((LOCAL, SEG, D), BF16),
            pltpu.VMEM((LOCAL, 4, THIN, D), BF16),
            pltpu.VMEM((LOCAL, 2, THIN, FF), BF16),
            pltpu.VMEM((LOCAL, HEADS * THIN + 2 * THIN, 128), F32),
            pltpu.SemaphoreType.DMA((3,)),
            pltpu.SemaphoreType.DMA((LOCAL,)),
            pltpu.SemaphoreType.DMA((2 * LOCAL,)),
            pltpu.SemaphoreType.DMA((4 * LOCAL,)),
        ],
        compiler_params=params(),
    )(place, flag, start, table, attn, ffn, x, q, k, v, *saved)
    return outs[:4], outs[4:7], outs[7]


def own_lanes(block, head):
    lane = lax.broadcasted_iota(jnp.int32, block.shape, 1)
    return jnp.where((lane < DH) == (head == 0), block, jnp.zeros_like(block))


def seen(score, first_query):
    key = lax.broadcasted_iota(jnp.int32, score.shape, 0)
    query = lax.broadcasted_iota(jnp.int32, score.shape, 1) + first_query
    return key <= query


def attend_kernel(q_ref, k_ref, v_ref, c_ref, log_ref):
    for part in range(SEG // TILE):
        rows = slice(TILE * part, TILE * (part + 1))
        keys = slice(0, TILE * (part + 1))
        contexts = []
        for head in range(2):
            score = nt(own_lanes(k_ref[0, keys], head), q_ref[0, rows])
            score = jnp.where(seen(score, TILE * part), score, MASK_VALUE)
            top = jnp.max(score, axis=0, keepdims=True)
            weight = jnp.exp(score - top)
            total = jnp.sum(weight, axis=0, keepdims=True)
            share = (weight * (1.0 / total)).astype(BF16)
            log_ref[0, 0, head : head + 1, rows] = top + jnp.log(total)
            contexts.append(tn(share, v_ref[0, keys]))
        lane = lax.broadcasted_iota(jnp.int32, contexts[0].shape, 1)
        c_ref[0, rows] = jnp.where(lane < DH, contexts[0], contexts[1]).astype(BF16)


PAIR = pl.BlockSpec((1, SEG, 2 * DH), lambda s, h: (s, 0, h))
PAIR_LOG = pl.BlockSpec((1, 1, 2, SEG), lambda s, h: (s, h, 0, 0))


def attend(q, k, v):
    return pl.pallas_call(
        attend_kernel,
        grid=(LOCAL, HEADS // 2),
        in_specs=[PAIR] * 3,
        out_specs=[PAIR, PAIR_LOG],
        out_shape=[sds((LOCAL, SEG, D), BF16), sds((LOCAL, HEADS // 2, 2, SEG), F32)],
        compiler_params=params(),
    )(q, k, v)


def attend_back_kernel(q_ref, k_ref, v_ref, dc_ref, log_ref, dq_ref, dk_ref, dv_ref):
    last = SEG // TILE
    key_terms, value_terms = [], []
    for head in range(2):
        key_sum, value_sum = [], []
        query_parts = []
        for part in range(last):
            rows = slice(TILE * part, TILE * (part + 1))
            keys = slice(0, TILE * (part + 1))
            q, dc = q_ref[0, rows], dc_ref[0, rows]
            k = k_ref[0, keys]
            score = nt(own_lanes(k, head), q)
            share = jnp.exp(score - log_ref[0, 0, head : head + 1, rows])
            share = jnp.where(seen(score, TILE * part), share, 0.0)
            share_grad = nt(own_lanes(v_ref[0, keys], head), dc)
            inner = jnp.sum(share_grad * share, axis=0, keepdims=True)
            score_grad = (share * (share_grad - inner)).astype(BF16)
            value_sum.append(nn(share.astype(BF16), dc))
            key_sum.append(nn(score_grad, q))
            query_parts.append(tn(score_grad, k))
        key_terms.append(key_sum)
        value_terms.append(value_sum)
        if head == 0:
            first_queries = query_parts
    for part in range(last):
        rows = slice(TILE * part, TILE * (part + 1))
        lane = lax.broadcasted_iota(jnp.int32, (TILE, 2 * DH), 1)
        pick = lambda a, b: jnp.where(lane < DH, a, b)
        dq_ref[0, rows] = (pick(first_queries[part], query_parts[part]) * SCALE).astype(BF16)
        for terms, out in ((key_terms, dk_ref), (value_terms, dv_ref)):
            total = None
            for later in range(part, last):
                term = pick(terms[0][later][rows], terms[1][later][rows])
                total = term if total is None else total + term
            out[0, rows] = total.astype(BF16)


def attend_back(q, k, v, dc, log_total):
    return pl.pallas_call(
        attend_back_kernel,
        grid=(LOCAL, HEADS // 2),
        in_specs=[PAIR] * 4 + [PAIR_LOG],
        out_specs=[PAIR] * 3,
        out_shape=[sds((LOCAL, SEG, D), BF16)] * 3,
        compiler_params=params(),
    )(q, k, v, dc, log_total)


def rows_kernel(
    x_ref,
    c_ref,
    cot_ref,
    wo_ref,
    wf_ref,
    table_ref,
    y_ref,
    h_ref,
    g_ref,
    du_ref,
    df_ref,
    da_ref,
    dc_ref,
    sums_ref,
    slope_ref,
):
    row = lambda r: table_ref[r : r + 1, :]

    @pl.when((pl.program_id(0) == 0) & (pl.program_id(1) == 0))
    def _():
        sums_ref[...] = jnp.zeros_like(sums_ref)

    def add(r, value):
        sums_ref[r : r + 1, :] += value

    c = c_ref[0]
    branch = nt(c[:, :HALF], wo_ref[0, 0]) + nt(c[:, HALF:], wo_ref[1, 0])
    unit1, inverse1 = normalized(x_ref[0].astype(F32) + branch + row(OUT_BIAS))
    hidden = (unit1 * row(GAIN1) + row(SHIFT1)).astype(BF16)
    h_ref[0] = hidden
    second = hidden.astype(F32) + row(DOWN_BIAS)
    for i in range(FF // D):
        cols = slice(D * i, D * (i + 1))
        up = nt(hidden, wf_ref[0, cols]) + row(UP_BIAS + i)
        active, slope = gelu_parts(up)
        active = active.astype(BF16)
        g_ref[0, :, cols] = active
        slope_ref[:, cols] = slope.astype(BF16)
        second = second + nn(active, wf_ref[1, cols])
    unit2, inverse2 = normalized(second)
    y_ref[0] = (unit2 * row(GAIN2) + row(SHIFT2)).astype(BF16)

    grad = cot_ref[0].astype(F32)
    add(GAIN2, row_sum(grad * unit2))
    add(SHIFT2, row_sum(grad))
    second_grad = normalized_back(grad * row(GAIN2), unit2, inverse2)
    down_grad = second_grad.astype(BF16)
    df_ref[0] = down_grad
    add(DOWN_BIAS, row_sum(down_grad.astype(F32)))
    hidden_grad = second_grad
    for i in range(FF // D):
        cols = slice(D * i, D * (i + 1))
        up_grad = (nt(down_grad, wf_ref[1, cols]) * slope_ref[:, cols].astype(F32)).astype(BF16)
        du_ref[0, :, cols] = up_grad
        add(UP_BIAS + i, row_sum(up_grad.astype(F32)))
        hidden_grad = hidden_grad + nn(up_grad, wf_ref[0, cols])
    add(GAIN1, row_sum(hidden_grad * unit1))
    add(SHIFT1, row_sum(hidden_grad))
    branch_grad = normalized_back(hidden_grad * row(GAIN1), unit1, inverse1).astype(BF16)
    da_ref[0] = branch_grad
    add(OUT_BIAS, row_sum(branch_grad.astype(F32)))
    for side in range(2):
        dc_ref[0, :, HALF * side : HALF * (side + 1)] = nn(branch_grad, wo_ref[side, 0]).astype(BF16)


def rows_part(x, c, cot, attn, ffn, table):
    rows = pl.BlockSpec((1, TILE, D), lambda s, i: (s, i, 0))
    wide = pl.BlockSpec((1, TILE, FF), lambda s, i: (s, i, 0))
    whole, whole_wide = sds((LOCAL, SEG, D), BF16), sds((LOCAL, SEG, FF), BF16)
    return pl.pallas_call(
        rows_kernel,
        grid=(LOCAL, SEG // TILE),
        in_specs=[rows] * 3
        + [once((2, 1, D, HALF), (0, 3, 0, 0)), once((2, FF, D), (0, 0, 0)), once((NVEC, D), (0, 0))],
        out_specs=[rows, rows, wide, wide, rows, rows, rows, once((THIN, D), (0, 0))],
        out_shape=[whole, whole, whole_wide, whole_wide, whole, whole, whole, sds((THIN, D), F32)],
        scratch_shapes=[pltpu.VMEM((TILE, FF), BF16)],
        compiler_params=params(),
    )(x, c, cot, attn, ffn, table)


def chain_back_kernel(
    place_ref,
    flag_ref,
    start_ref,
    table_ref,
    attn_ref,
    ffn_ref,
    q_ref,
    k_ref,
    v_ref,
    saved_d_ref,
    saved_f_ref,
    saved_s_ref,
    dk_in,
    dv_in,
    thin_d_in,
    thin_f_in,
    sums_in,
    dk_ref,
    dv_ref,
    thin_d_ref,
    thin_f_ref,
    sums_ref,
    grad_ref,
    wa,
    wf,
    qb,
    kb,
    vb,
    dkb,
    dvb,
    save_d,
    save_f,
    save_s,
    thin_d,
    thin_f,
    sums,
    sem_w,
    sem_in,
    sem_out,
):
    del dk_in, dv_in, thin_d_in, thin_f_in, sums_in
    grad_ref[...] = start_ref[...]

    @pl.when(flag_ref[0] > 0)
    def _():
        loads = [
            pltpu.make_async_copy(attn_ref, wa, sem_w.at[0]),
            pltpu.make_async_copy(ffn_ref.at[0], wf.at[0], sem_w.at[1]),
            pltpu.make_async_copy(ffn_ref.at[1], wf.at[1], sem_w.at[2]),
        ]
        reads = [
            pltpu.make_async_copy(q_ref.at[:, pl.ds(0, THIN)], qb, sem_in.at[0]),
            pltpu.make_async_copy(k_ref, kb, sem_in.at[1]),
            pltpu.make_async_copy(v_ref, vb, sem_in.at[2]),
            pltpu.make_async_copy(dk_ref, dkb, sem_in.at[3]),
            pltpu.make_async_copy(dv_ref, dvb, sem_in.at[4]),
            pltpu.make_async_copy(saved_d_ref, save_d, sem_in.at[5]),
            pltpu.make_async_copy(saved_f_ref, save_f, sem_in.at[6]),
            pltpu.make_async_copy(saved_s_ref, save_s, sem_in.at[7]),
        ]
        for c in reads + [loads[2], loads[1], loads[0]]:
            c.start()
        sums[...] = jnp.zeros_like(sums)
        masks = head_masks()
        memory_row = lax.broadcasted_iota(jnp.int32, (THIN, 1), 0) < MEM
        row = lambda r: table_ref[r : r + 1, :]

        def add(r, value):
            sums[r : r + 1, :] += value

        for c in reads:
            c.wait()
        loads[2].wait()
        loads[1].wait()
        loads[0].wait()
        for s in reversed(range(LOCAL)):
            after = flag_ref[2] if s == LOCAL - 1 else place_ref[s + 1]

            def through(s=s, after=after):
                grad = jnp.where(memory_row & (after > 0), grad_ref[...], 0.0)
                unit1, unit2 = save_d[s, 1].astype(F32), save_d[s, 2].astype(F32)
                base = HEADS * THIN
                log_total = save_s[s, 0:base, 0:1]
                inverse1 = save_s[s, base : base + THIN, 0:1]
                inverse2 = save_s[s, base + THIN :, 0:1]
                add(GAIN2, row_sum(grad * unit2))
                add(SHIFT2, row_sum(grad))
                second_grad = normalized_back(grad * row(GAIN2), unit2, inverse2)
                down_grad = second_grad.astype(BF16)
                add(DOWN_BIAS, row_sum(down_grad.astype(F32)))
                up_grad = (nt(down_grad, wf[1]) * save_f[s, 1].astype(F32)).astype(BF16)
                up_sum = row_sum(up_grad.astype(F32))
                for i in range(FF // D):
                    add(UP_BIAS + i, up_sum[:, D * i : D * (i + 1)])
                hidden_grad = second_grad + nn(up_grad, wf[0])
                add(GAIN1, row_sum(hidden_grad * unit1))
                add(SHIFT1, row_sum(hidden_grad))
                pre_grad = normalized_back(hidden_grad * row(GAIN1), unit1, inverse1)
                branch_grad = pre_grad.astype(BF16)
                add(OUT_BIAS, row_sum(branch_grad.astype(F32)))
                context_grad = jnp.concatenate(
                    [nn(branch_grad, wa[0, 3]), nn(branch_grad, wa[1, 3])], axis=1
                ).astype(BF16)
                dc_heads = by_head(context_grad, masks)
                q_heads = by_head(qb[s], masks)
                score = nt(q_heads, kb[s])
                share = jnp.exp(score - log_total) * copies_of(score.shape)
                share_grad = nt(dc_heads, vb[s])
                inner = jnp.sum(share_grad * share, axis=-1, keepdims=True)
                score_grad = (share * (share_grad - inner)).astype(BF16)
                query_grad = (own_columns(nn(score_grad, kb[s]), masks) * SCALE).astype(BF16)
                dkb[s] = (dkb[s].astype(F32) + tn(score_grad, q_heads)).astype(BF16)
                dvb[s] = (dvb[s].astype(F32) + tn(share.astype(BF16), dc_heads)).astype(BF16)
                thin_d[s, 0] = down_grad
                thin_d[s, 1] = branch_grad
                thin_d[s, 2] = query_grad
                thin_d[s, 3] = save_d[s, 0]
                thin_d[s, 4] = save_d[s, 3]
                thin_f[s, 0] = up_grad
                thin_f[s, 1] = save_f[s, 0]
                grad_ref[...] = (
                    pre_grad
                    + nt(query_grad[:, :HALF], wa[0, 0])
                    + nt(query_grad[:, HALF:], wa[1, 0])
                )

            if s == LOCAL - 1:

                @pl.when(flag_ref[1] > 0)
                def _():
                    through()

                @pl.when(flag_ref[1] == 0)
                def _():
                    thin_d[s] = jnp.zeros_like(thin_d[s])
                    thin_f[s] = jnp.zeros_like(thin_f[s])
                    grad_ref[...] = jnp.zeros_like(grad_ref)
            else:
                through()
            grad = grad_ref[...]
            for side in range(2):
                cols = slice(HALF * side, HALF * (side + 1))
                grad = grad + nt(dkb[s, 0:THIN, cols], wa[side, 1])
                grad = grad + nt(dvb[s, 0:THIN, cols], wa[side, 2])
            grad_ref[...] = grad
            first = jnp.where(place_ref[s] == 0, grad, 0.0)
            sums[FIRST_MEMORY : FIRST_MEMORY + THIN, :] += first
        writes = [
            pltpu.make_async_copy(dkb, dk_ref, sem_out.at[0]),
            pltpu.make_async_copy(dvb, dv_ref, sem_out.at[1]),
            pltpu.make_async_copy(thin_d, thin_d_ref, sem_out.at[2]),
            pltpu.make_async_copy(thin_f, thin_f_ref, sem_out.at[3]),
            pltpu.make_async_copy(sums, sums_ref, sem_out.at[4]),
        ]
        for c in writes:
            c.start()
        for c in writes:
            c.wait()


THIN_SHAPES = (
    sds((LOCAL, 5, THIN, D), BF16),
    sds((LOCAL, 2, THIN, FF), BF16),
    sds((FIRST_MEMORY + THIN, D), F32),
)


def chain_back(place, flag, start, table, attn, ffn, q, k, v, saved, dk, dv, thin):
    whole = sds((LOCAL, SEG, D), BF16)
    outs = pl.pallas_call(
        chain_back_kernel,
        in_specs=[SMEM, SMEM, VMEM, VMEM] + [ANY] * 13,
        out_specs=[ANY] * 5 + [VMEM],
        out_shape=[whole] * 2 + list(THIN_SHAPES) + [sds((THIN, D), F32)],
        input_output_aliases={12 + i: i for i in range(5)},
        scratch_shapes=[
            pltpu.VMEM((2, 4, D, HALF), BF16),
            pltpu.VMEM((2, FF, D), BF16),
            pltpu.VMEM((LOCAL, THIN, D), BF16),
        ]
        + [pltpu.VMEM((LOCAL, SEG, D), BF16)] * 4
        + [pltpu.VMEM(s.shape, s.dtype) for s in SAVED + THIN_SHAPES]
        + [
            pltpu.SemaphoreType.DMA((3,)),
            pltpu.SemaphoreType.DMA((8,)),
            pltpu.SemaphoreType.DMA((5,)),
        ],
        compiler_params=params(),
    )(place, flag, start, table, attn, ffn, q, k, v, *saved, dk, dv, *thin)
    return outs[:2], outs[2:5], outs[5]


def token_grad_kernel(da_ref, dq_ref, dk_ref, dv_ref, w_ref, out_ref):
    total = da_ref[0].astype(F32)
    for side in range(2):
        cols = slice(HALF * side, HALF * (side + 1))
        for i, ref in enumerate((dq_ref, dk_ref, dv_ref)):
            total = total + nt(ref[0, :, cols], w_ref[side, i])
    out_ref[0] = total.astype(BF16)


def token_gradient(da, dq, dk, dv, attn):
    rows = pl.BlockSpec((1, TILE, D), lambda s, i: (s, i, 0))
    return pl.pallas_call(
        token_grad_kernel,
        grid=(LOCAL, SEG // TILE),
        in_specs=[rows] * 4 + [once((2, 3, D, HALF), (0, 0, 0, 0))],
        out_specs=rows,
        out_shape=sds((LOCAL, SEG, D), BF16),
        compiler_params=params(),
    )(da, dq, dk, dv, attn)


def flat(ref):
    return ref[...].reshape(LOCAL * ref.shape[1], ref.shape[2])


def ffn_grad_kernel(g_ref, du_ref, df_ref, h_ref, thin_f_ref, thin_d_ref, out_ref):
    up = tn(flat(du_ref), flat(h_ref))
    down = tn(flat(g_ref), flat(df_ref))
    for s in range(LOCAL):
        up = up + tn(thin_f_ref[s, 0], thin_d_ref[s, 3])
        down = down + tn(thin_f_ref[s, 1], thin_d_ref[s, 0])
    out_ref[0] = up.astype(BF16)
    out_ref[1] = down.astype(BF16)


def ffn_gradient(g, du, df, h, thin_d, thin_f, chunk=256):
    hidden = pl.BlockSpec((LOCAL, SEG, chunk), lambda i: (0, 0, i))
    full = once((LOCAL, SEG, D), (0, 0, 0))
    return pl.pallas_call(
        ffn_grad_kernel,
        grid=(FF // chunk,),
        in_specs=[
            hidden,
            hidden,
            full,
            full,
            pl.BlockSpec((LOCAL, 2, THIN, chunk), lambda i: (0, 0, 0, i)),
            once(THIN_SHAPES[0].shape, (0, 0, 0, 0)),
        ],
        out_specs=pl.BlockSpec((2, chunk, D), lambda i: (0, i, 0)),
        out_shape=sds((2, FF, D), BF16),
        compiler_params=params(),
    )(g, du, df, h, thin_f, thin_d)


def attn_grad_kernel(x_ref, da_ref, dq_ref, dk_ref, dv_ref, c_ref, thin_d_ref, out_ref, bias_ref):
    thin_c = pl.ds(pl.multiple_of(pl.program_id(0) * HALF, HALF), HALF)
    x = flat(x_ref)
    dq, dk, dv = flat(dq_ref), flat(dk_ref), flat(dv_ref)
    query = tn(x, dq)
    query_bias = row_sum(dq.astype(F32))
    output = tn(flat(da_ref), flat(c_ref))
    for s in range(LOCAL):
        dq16 = thin_d_ref[s, 2, :, thin_c]
        query = query + tn(x_ref[s, 0:THIN], dq16)
        query_bias = query_bias + row_sum(dq16.astype(F32))
        output = output + tn(thin_d_ref[s, 1], thin_d_ref[s, 4, :, thin_c])
    out_ref[0, 0] = query.astype(BF16)
    out_ref[0, 1] = tn(x, dk).astype(BF16)
    out_ref[0, 2] = tn(x, dv).astype(BF16)
    out_ref[0, 3] = output.astype(BF16)
    bias_ref[0] = jnp.concatenate(
        [query_bias, row_sum(dv.astype(F32)), jnp.zeros((6, HALF), F32)], axis=0
    )


def attn_gradient(x, da, dq, dk, dv, c, thin_d):
    half = pl.BlockSpec((LOCAL, SEG, HALF), lambda i: (0, 0, i))
    full = once((LOCAL, SEG, D), (0, 0, 0))
    return pl.pallas_call(
        attn_grad_kernel,
        grid=(2,),
        in_specs=[full, full, half, half, half, half, once(THIN_SHAPES[0].shape, (0, 0, 0, 0))],
        out_specs=[
            pl.BlockSpec((1, 4, D, HALF), lambda i: (i, 0, 0, 0)),
            pl.BlockSpec((1, 8, HALF), lambda i: (i, 0, 0)),
        ],
        out_shape=[sds((2, 4, D, HALF), BF16), sds((2, 8, HALF), F32)],
        compiler_params=params(),
    )(x, da, dq, dk, dv, c, thin_d)


def update(gradient, momentum, weight, average, rate, grad_scale):
    scaled = gradient * grad_scale
    moment = MOMENTUM * momentum + scaled
    weight_new = weight - rate * (scaled + MOMENTUM * moment)
    return (moment, weight_new, AVERAGE_DECAY * average + (1.0 - AVERAGE_DECAY) * weight_new)


VEC_TILE = (8, 128)


def in_tiles(rows):
    size = VEC_TILE[0] * VEC_TILE[1]
    padded = jnp.pad(rows, [(0, 0)] * (rows.ndim - 1) + [(0, size - rows.shape[-1])])
    return padded.reshape(*rows.shape[:-1], *VEC_TILE)


def gather_weights(attention, feedforward, vectors):
    nz = lax.axis_size("dp") // 4
    rows, hidden, entries = attention.shape[1], feedforward.shape[2], vectors.shape[0]
    attn, ffn, table = gather(
        nz,
        0,
        [
            (attention.astype(BF16), (2, 4, nz, 2, 2, rows, HALF), attn_view),
            (jnp.swapaxes(feedforward.astype(BF16), 1, 2), (2, nz, 2, 2, 2, hidden, D), ffn_view),
            (in_tiles(vectors.astype(BF16).astype(F32)), (nz, 2, 2, 2, *VEC_TILE), vec_view),
        ],
    )
    table = table.reshape(nz * 8, VEC_TILE[0] * VEC_TILE[1])[:, :entries].reshape(NVEC, D)
    return attn.reshape(2, 4, D, HALF), ffn.reshape(2, FF, D), table


def scatter_gradients(attn_terms, ffn_terms, vec_terms, shapes):
    nz = lax.axis_size("dp") // 4
    rows, hidden, entries = shapes
    attn, ffn, vec = scatter(
        nz,
        1,
        [
            (attn_terms.reshape(2, 4, nz, 2, 2, rows, HALF), (4, rows, HALF), attn_view),
            (ffn_terms.reshape(2, nz, 2, 2, 2, hidden, D), (2, hidden, D), ffn_view),
            (in_tiles(vec_terms.reshape(nz, 2, 2, 2, entries)), VEC_TILE, vec_view),
        ],
    )
    return attn.astype(F32), jnp.swapaxes(ffn, 1, 2).astype(F32), vec.reshape(-1)[:entries]


def swap(value):
    return lax.ppermute(value, "tensor", [(0, 1), (1, 0)])


def whole_rows(halves, side):
    mine = lax.dynamic_slice_in_dim(halves, LOCAL * side, LOCAL, 0)
    other = swap(lax.dynamic_slice_in_dim(halves, LOCAL * (1 - side), LOCAL, 0))
    first = jnp.where(side == 0, mine, other)
    second = jnp.where(side == 0, other, mine)
    return jnp.concatenate([jnp.zeros((LOCAL, MEM, D), halves.dtype), first, second], axis=1)


def half_rows(rows, side):
    half = (SEG - MEM) // 2
    first, second = rows[:, MEM : MEM + half], rows[:, MEM + half :]
    mine = jnp.where(side == 0, first, second)
    other = swap(jnp.where(side == 0, second, first))
    return jnp.concatenate(
        [jnp.where(side == 0, mine, other), jnp.where(side == 0, other, mine)], axis=0
    )


def on_device(
    tokens,
    slot_position,
    cotangent,
    attention,
    feedforward,
    vectors,
    attn_momentum,
    ffn_momentum,
    vec_momentum,
    attn_average,
    ffn_average,
    vec_average,
):
    side = lax.axis_index("tensor")
    first_side = side == 0
    attn, ffn, table = gather_weights(attention, feedforward, vectors)
    place = lax.dynamic_slice_in_dim(slot_position, LOCAL * side, LOCAL, 0)
    live = (place >= 0)[:, None, None]

    x = whole_rows(tokens, side)
    cot = jnp.where(live, whole_rows(cotangent, side), 0)
    q, k, v = project(x, attn, table)

    on = lambda flag: flag.astype(jnp.int32)
    saved = tuple(jnp.zeros(s.shape, s.dtype) for s in SAVED)
    start = jnp.zeros((THIN, D), BF16)
    flag = jnp.stack([on(first_side), jnp.int32(1)])
    (x, q, k, v), saved, memory = chain(place, flag, start, table, attn, ffn, x, q, k, v, saved)
    memory = lax.ppermute(memory, "tensor", [(0, 1)])
    flag = jnp.stack([on(~first_side), jnp.int32(0)])
    (x, q, k, v), saved, _ = chain(place, flag, memory, table, attn, ffn, x, q, k, v, saved)

    c, log_total = attend(q, k, v)
    y, h, g, du, df, da, dc, sums = rows_part(x, c, cot, attn, ffn, table)
    dq, dk, dv = attend_back(q, k, v, dc, log_total)

    thin = tuple(jnp.zeros(s.shape, s.dtype) for s in THIN_SHAPES)
    back = functools.partial(chain_back, place)
    flag = jnp.stack([on(~first_side), jnp.int32(0), jnp.int32(-1)])
    start = jnp.zeros((THIN, D), F32)
    (dk, dv), thin, grad = back(flag, start, table, attn, ffn, q, k, v, saved, dk, dv, thin)
    grad = lax.ppermute(grad, "tensor", [(1, 0)])
    flag = jnp.stack([on(first_side), jnp.int32(1), slot_position[LOCAL]])
    (dk, dv), thin, _ = back(flag, grad, table, attn, ffn, q, k, v, saved, dk, dv, thin)
    thin_d, thin_f, thin_sums = thin

    token_grad = token_gradient(da, dq, dk, dv, attn)
    ffn_terms = ffn_gradient(g, du, df, h, thin_d, thin_f)
    attn_terms, bias_terms = attn_gradient(x, da, dq, dk, dv, c, thin_d)

    activations = half_rows(jnp.where(live, y, 0), side)
    token_grad = half_rows(jnp.where(live, token_grad, 0), side)

    bias_rows = jnp.concatenate([bias_terms[0, :2], bias_terms[1, :2]], axis=1)
    leading = jnp.concatenate([bias_rows, sums[2:FIRST_MEMORY], jnp.zeros((MEM, D), F32)], axis=0)
    vec_terms = leading + thin_sums[:NVEC]

    attn_grad, ffn_grad, vec_grad = scatter_gradients(
        attn_terms,
        ffn_terms,
        vec_terms,
        (attention.shape[1], feedforward.shape[2], vectors.shape[0]),
    )
    grad_scale = 1.0 / math.sqrt(lax.axis_size("dp") * SLOTS * ROWS)
    attn_new = update(attn_grad, attn_momentum, attention, attn_average, ATTENTION_RATE, grad_scale)
    ffn_new = update(ffn_grad, ffn_momentum, feedforward, ffn_average, FEEDFORWARD_RATE, grad_scale)
    vec_new = update(vec_grad, vec_momentum, vectors, vec_average, VECTOR_RATE, grad_scale)
    return (
        activations,
        token_grad,
        attn_new[0],
        ffn_new[0],
        vec_new[0],
        attn_new[1],
        ffn_new[1],
        vec_new[1],
        attn_new[2],
        ffn_new[2],
        vec_new[2],
    )


def solution(mesh):
    attn_spec = P(None, "dp", "tensor")
    ffn_spec = P(None, None, ("dp", "tensor"))
    vec_spec = P(("dp", "tensor"))
    rows_spec = P("dp", "tensor", None)
    states = (attn_spec, ffn_spec, vec_spec)
    return jax.shard_map(
        on_device,
        mesh=mesh,
        in_specs=(rows_spec, P("dp"), rows_spec) + states * 3,
        out_specs=(rows_spec, rows_spec) + states * 3,
        check_vma=False,
    )
```

```python
import functools
import math

import jax
import jax.numpy as jnp
from jax import lax
from jax.experimental import pallas as pl
from jax.experimental.pallas import tpu as pltpu
from jax.sharding import PartitionSpec as P

D = 768
HEADS = 12
DH = 64
FF = 3072
MEM = 10
SLOTS = 4
ROWS = 522
NVEC = 22

HALF = D // 2
SEG = ROWS - MEM
THIN = 16
LOCAL = 2
TILE = 256

EPSILON = 1e-05
MOMENTUM = 0.9
AVERAGE_DECAY = 0.75
ATTENTION_RATE = 0.06
FEEDFORWARD_RATE = 0.02
VECTOR_RATE = 0.1
MASK_VALUE = -1e30
SCALE = 1.0 / math.sqrt(DH)

F32 = jnp.float32
BF16 = jnp.bfloat16
MIB = 1 << 20

QUERY_BIAS, VALUE_BIAS, OUT_BIAS, GAIN1, SHIFT1, DOWN_BIAS, GAIN2, SHIFT2, UP_BIAS = range(9)
FIRST_MEMORY = UP_BIAS + FF // D


def nn(a, b):
    return lax.dot_general(a, b, (((1,), (0,)), ((), ())), preferred_element_type=F32)


def nt(a, b):
    return lax.dot_general(a, b, (((1,), (1,)), ((), ())), preferred_element_type=F32)


def tn(a, b):
    return lax.dot_general(a, b, (((0,), (0,)), ((), ())), preferred_element_type=F32)


def normalized(rows):
    center = rows - jnp.mean(rows, axis=-1, keepdims=True)
    spread = jnp.mean(center * center, axis=-1, keepdims=True)
    inverse = lax.rsqrt(spread + EPSILON)
    return center * inverse, inverse


def normalized_back(grad, unit, inverse):
    mean_grad = jnp.mean(grad, axis=-1, keepdims=True)
    mean_along = jnp.mean(grad * unit, axis=-1, keepdims=True)
    return inverse * (grad - mean_grad - unit * mean_along)


def gelu_parts(u):
    size = jnp.abs(u)
    t = 1.0 / (1.0 + (0.3275911 / math.sqrt(2.0)) * size)
    bell = jnp.exp(-0.5 * u * u)
    poly = t * (
        0.5 * 0.254829592
        + t
        * (
            0.5 * -0.284496736
            + t * (0.5 * 1.421413741 + t * (0.5 * -1.453152027 + t * (0.5 * 1.061405429)))
        )
    )
    tail = poly * bell
    cdf = jnp.where(u < 0, tail, 1.0 - tail)
    return u * cdf, cdf + (u * (1.0 / math.sqrt(2.0 * math.pi))) * bell


def row_sum(block):
    return jnp.sum(block, axis=0, keepdims=True)


def params(limit=60, **more):
    return pltpu.CompilerParams(vmem_limit_bytes=limit * MIB, **more)


def once(shape, index):
    return pl.BlockSpec(shape, lambda *_: index, pipeline_mode=pl.Buffered(1))


ANY = pl.BlockSpec(memory_space=pltpu.HBM)
SMEM = pl.BlockSpec(memory_space=pltpu.SMEM)
VMEM = pl.BlockSpec(memory_space=pltpu.VMEM)


def sds(shape, dtype):
    return jax.ShapeDtypeStruct(shape, dtype)


def my_place():
    dp = lax.axis_index("dp")
    return dp // 4, (dp // 2) % 2, dp % 2, lax.axis_index("tensor")


def device(z, x, c, y):
    return {"dp": (z * 2 + x) * 2 + c, "tensor": y}


def entry_barrier(nz):
    z, x, c, y = my_place()
    barrier = pltpu.get_barrier_semaphore()
    signal = lambda d: pl.semaphore_signal(
        barrier, inc=1, device_id=d, device_id_type=pl.DeviceIdType.MESH
    )
    signal(device(z, 1 - x, c, y))
    signal(device(z, x, 1 - c, y))
    signal(device(z, x, c, 1 - y))

    @pl.when(z > 0)
    def _():
        signal(device(z - 1, x, c, y))

    @pl.when(z < nz - 1)
    def _():
        signal(device(z + 1, x, c, y))

    up = lax.convert_element_type(z < nz - 1, jnp.int32)
    down = lax.convert_element_type(z > 0, jnp.int32)
    pl.semaphore_wait(barrier, 3 + up + down)


def attn_view(ref, z, x, c, y):
    return ref.at[:, z, x, c, :, pl.ds(pl.multiple_of(y * HALF, HALF), HALF)]


def ffn_view(ref, z, x, c, y):
    return ref.at[:, z, x, c, y]


def vec_view(ref, z, x, c, y):
    return ref.at[z, x, c, y]


def partners(place, lead):
    _, x, _, y = place
    first = (x + (1 - lead) * (1 - 2 * x), y + lead * (1 - 2 * y))
    second = (x + lead * (1 - 2 * x), y + (1 - lead) * (1 - 2 * y))
    return first, second, (1 - x, 1 - y)


COLUMN, FIRST, SECOND, BOTH, CORE = 0, 1, 2, 3, 4
UP, DOWN = 0, 8


def remote(src, dst, send_sem, recv_sem, target):
    return pltpu.make_async_remote_copy(
        src_ref=src,
        dst_ref=dst,
        send_sem=send_sem,
        recv_sem=recv_sem,
        device_id=target,
        device_id_type=pl.DeviceIdType.MESH,
    )


def gather_steps(nz, place, lead, pieces, send_sem, recv_sem):
    z, x, c, y = place
    first, second, both = partners(place, lead)
    to_first = device(z, first[0], c, first[1])
    to_second = device(z, second[0], c, second[1])
    to_core = device(z, x, 1 - c, y)

    def copies(send, recv, shard, target):
        return [
            remote(
                view(out, *shard),
                view(out, *shard),
                send_sem.at[send, shard[0], i],
                recv_sem.at[recv, shard[0], i],
                target,
            )
            for i, out, view in pieces
        ]

    def start(*args):
        for copy in copies(*args):
            copy.start()

    def arrived(*args):
        for copy in copies(*args):
            copy.wait_recv()

    def sent(*args):
        for copy in copies(*args):
            copy.wait_send()

    def column(zz):
        return (zz, x, c, y)

    def of_first(zz):
        return (zz, first[0], c, first[1])

    def of_second(zz):
        return (zz, second[0], c, second[1])

    def of_both(zz):
        return (zz, both[0], c, both[1])

    core_first, core_second = CORE + 2 - lead, CORE + 1 + lead

    def move_up(zz):
        return (UP, COLUMN, column(zz), device(z + 1, x, c, y))

    def move_down(zz):
        return (DOWN, COLUMN, column(zz), device(z - 1, x, c, y))

    def stage0(zz, rising, falling, wait):
        if wait:
            arrived(UP, COLUMN, column(zz), to_core)
        if rising:

            @pl.when(z < nz - 1)
            def _():
                start(*move_up(zz))

        if falling:

            @pl.when(z > 0)
            def _():
                start(*move_down(zz))

        start(FIRST, FIRST, column(zz), to_first)
        start(SECOND, SECOND, column(zz), to_second)
        start(CORE, CORE, column(zz), to_core)

    def stage1(zz):
        arrived(FIRST, FIRST, of_first(zz), to_first)
        start(BOTH, BOTH, of_first(zz), to_second)
        start(core_first, core_first, of_first(zz), to_core)

    def stage2(zz):
        arrived(SECOND, SECOND, of_second(zz), to_second)
        start(core_second, core_second, of_second(zz), to_core)
        arrived(BOTH, BOTH, of_both(zz), to_second)
        start(CORE + 3, CORE + 3, of_both(zz), to_core)

    def begin():
        stage0(z, True, True, False)

    def step(t):
        @pl.when((t < nz) & (z - t >= 0))
        def _():
            stage0(z - t, True, False, True)

        @pl.when((t < nz) & (z + t < nz))
        def _():
            stage0(z + t, False, True, True)

        for lag, stage in ((1, stage1), (2, stage2)):
            late = t - lag

            @pl.when((late >= 0) & (late < nz) & (z - late >= 0))
            def _():
                stage(z - late)

            @pl.when((late > 0) & (late < nz) & (z + late < nz))
            def _():
                stage(z + late)

    def all_arrived(zz, carry):
        for fx in range(2):
            for fy in range(2):
                kind = CORE + 2 * fx + fy
                shard = (zz, x + fx * (1 - 2 * x), 1 - c, y + fy * (1 - 2 * y))
                arrived(kind, kind, shard, to_core)
        return carry

    def all_sent(zz, carry):
        @pl.when((zz <= z) & (z < nz - 1))
        def _():
            sent(*move_up(zz))

        @pl.when((zz >= z) & (z > 0))
        def _():
            sent(*move_down(zz))

        sent(FIRST, FIRST, column(zz), to_first)
        sent(SECOND, SECOND, column(zz), to_second)
        sent(BOTH, BOTH, of_first(zz), to_second)
        sent(CORE, CORE, column(zz), to_core)
        sent(core_first, core_first, of_first(zz), to_core)
        sent(core_second, core_second, of_second(zz), to_core)
        sent(CORE + 3, CORE + 3, of_both(zz), to_core)
        return carry

    def end_arrive():
        lax.fori_loop(0, nz, all_arrived, 0)

    def end_send():
        lax.fori_loop(0, nz, all_sent, 0)

    return begin, step, end_arrive, end_send


def swap_halves(place, rows, other, sem):
    z, x, c, y = place
    return remote(
        rows.at[pl.ds(LOCAL * (1 - y), LOCAL)],
        other,
        sem.at[0],
        sem.at[1],
        device(z, x, c, 1 - y),
    )


def gather_kernel(nz, views, *refs):
    n = len(views)
    srcs, tokens, outs, other = refs[:n], refs[n], refs[n + 1 : 2 * n + 1], refs[2 * n + 1]
    send_sem, recv_sem, own_sem, swap_sem = refs[2 * n + 2 :]
    place = my_place()
    halves = swap_halves(place, tokens, other, swap_sem)
    own = [
        pltpu.make_async_copy(src, view(out, *place), own_sem.at[i])
        for i, (src, out, view) in enumerate(zip(srcs, outs, views))
    ]
    for copy in own:
        copy.start()
    entry_barrier(nz)
    halves.start()
    for copy in own:
        copy.wait()
    pieces = [(i, out, view) for i, (out, view) in enumerate(zip(outs, views))]
    begin, step, end_arrive, end_send = gather_steps(
        nz, place, place[2], pieces, send_sem, recv_sem
    )
    begin()

    def loop(t, carry):
        step(t)
        return carry

    lax.fori_loop(1, nz + 2, loop, 0)
    end_send()
    end_arrive()
    halves.wait()


def gather(nz, collective_id, parts, tokens):
    shards, shapes, views = zip(*parts)
    n = len(parts)
    return pl.pallas_call(
        functools.partial(gather_kernel, nz, views),
        in_specs=[ANY] * (n + 1),
        out_specs=[ANY] * (n + 1),
        out_shape=[sds(shape, shard.dtype) for shard, shape in zip(shards, shapes)]
        + [sds((LOCAL, *tokens.shape[1:]), tokens.dtype)],
        scratch_shapes=[
            pltpu.SemaphoreType.DMA((9, nz, n)),
            pltpu.SemaphoreType.DMA((8, nz, n)),
            pltpu.SemaphoreType.DMA((n,)),
            pltpu.SemaphoreType.DMA((2,)),
        ],
        name="gather",
        compiler_params=params(collective_id=collective_id, has_side_effects=True),
    )(*shards, tokens)


def scatter_kernel(nz, views, *refs):
    n = len(views)
    terms, outs = refs[:n], refs[n : 2 * n]
    mine, from_core, from_second, from_first, from_below, from_above = (
        refs[2 * n + i * n : 3 * n + i * n] for i in range(6)
    )
    send_sem, recv_sem, own_sem = refs[8 * n :]
    place = z, x, c, y = my_place()
    first, second, both = partners(place, place[2])
    to_first = device(z, first[0], c, first[1])
    to_second = device(z, second[0], c, second[1])
    to_core = device(z, x, 1 - c, y)

    def copies(srcs, dsts, send, recv, zz, target):
        return [
            pltpu.make_async_remote_copy(
                src_ref=srcs[i],
                dst_ref=dsts[i],
                send_sem=send_sem.at[send, zz, i],
                recv_sem=recv_sem.at[recv, zz, i],
                device_id=target,
                device_id_type=pl.DeviceIdType.MESH,
            )
            for i in range(n)
        ]

    def slots(bufs, *index):
        return [b.at[index] for b in bufs]

    def pick(refs_, *index):
        return [b[index] for b in refs_]

    flips = [(fx, fy) for fx in range(2) for fy in range(2)]

    def at(fx, fy):
        return x + fx * (1 - 2 * x), y + fy * (1 - 2 * y)

    def core_copies(zz, f):
        fx, fy = flips[f]
        xx, yy = at(fx, fy)
        return copies(
            [view(t, zz, xx, 1 - c, yy) for t, view in zip(terms, views)],
            slots(from_core, zz, f),
            f,
            f,
            zz,
            to_core,
        )

    def own_copies(zz, f):
        fx, fy = flips[f]
        xx, yy = at(fx, fy)
        return [
            pltpu.make_async_copy(
                view(t, zz, xx, c, yy), mine[i].at[zz, f], own_sem.at[f, zz, i]
            )
            for i, (t, view) in enumerate(zip(terms, views))
        ]

    f_first, f_second = 2 - c, 1 + c

    def second_copies(zz, across):
        return copies(
            slots(from_core, zz, 3 if across else f_second),
            slots(from_second, zz, 1 if across else 0),
            4 + across,
            4 + across,
            zz,
            to_second,
        )

    def first_copies(zz):
        return copies(slots(from_second, zz, 1), slots(from_first, zz), 6, 6, zz, to_first)

    def up_copies(zz):
        return copies(slots(from_first, zz), slots(from_below, zz), 7, 7, zz, device(z + 1, x, c, y))

    def down_copies(zz):
        return copies(slots(from_first, zz), slots(from_above, zz), 8, 8, zz, device(z - 1, x, c, y))

    def run(group, what):
        for copy in group:
            getattr(copy, what)()

    def add(into, index, other, other_index):
        for i in range(n):
            a, b = into[i].at[index], other[i].at[other_index]
            a[...] = (a[...].astype(F32) + b[...].astype(F32)).astype(a.dtype)

    def by_distance(t, do):
        @pl.when((t >= 0) & (t < nz) & (z - t >= 0))
        def _():
            do(z - t)

        @pl.when((t > 0) & (t < nz) & (z + t < nz))
        def _():
            do(z + t)

    def start_own(zz):
        for f in range(4):
            run(own_copies(zz, f), "start")

    def start_core(zz):
        for f in (3, 1, 2, 0):
            run(core_copies(zz, f), "start")

    def stage0(zz):
        for f in (3, 1, 2, 0):
            run(core_copies(zz, f), "wait_recv")
            run(own_copies(zz, f), "wait")
            add(from_core, (zz, f), mine, (zz, f))
        run(second_copies(zz, 1), "start")
        run(second_copies(zz, 0), "start")

    def stage1(zz):
        run(second_copies(zz, 1), "wait_recv")
        add(from_second, (zz, 1), from_core, (zz, f_first))
        run(first_copies(zz), "start")

    def stage2(zz):
        run(second_copies(zz, 0), "wait_recv")
        add(from_second, (zz, 0), from_core, (zz, 0))
        run(first_copies(zz), "wait_recv")
        add(from_first, (zz,), from_second, (zz, 0))

        @pl.when(zz > z)
        def _():
            @pl.when(z > 0)
            def _():
                run(up_copies(zz), "wait_recv")
                add(from_first, (zz,), from_below, (zz,))

            run(up_copies(zz), "start")

        @pl.when(zz < z)
        def _():
            @pl.when(z < nz - 1)
            def _():
                run(down_copies(zz), "wait_recv")
                add(from_first, (zz,), from_above, (zz,))

            run(down_copies(zz), "start")

    entry_barrier(nz)

    def begin(k, carry):
        by_distance(nz - 1 - k, start_core)
        by_distance(nz - 1 - k, start_own)
        return carry

    lax.fori_loop(0, nz, begin, 0)

    def step(k, carry):
        t = nz - 1 - k
        by_distance(t, stage0)
        by_distance(t + 1, stage1)
        by_distance(t + 2, stage2)
        return carry

    lax.fori_loop(0, nz + 2, step, 0)

    @pl.when(z > 0)
    def _():
        run(up_copies(z), "wait_recv")
        add(from_first, (z,), from_below, (z,))

    @pl.when(z < nz - 1)
    def _():
        run(down_copies(z), "wait_recv")
        add(from_first, (z,), from_above, (z,))

    for i in range(n):
        outs[i][...] = from_first[i][z]

    def finish(zz, carry):
        for f in range(4):
            run(core_copies(zz, f), "wait_send")
        run(second_copies(zz, 1), "wait_send")
        run(second_copies(zz, 0), "wait_send")
        run(first_copies(zz), "wait_send")

        @pl.when(zz > z)
        def _():
            run(up_copies(zz), "wait_send")

        @pl.when(zz < z)
        def _():
            run(down_copies(zz), "wait_send")

        return carry

    lax.fori_loop(0, nz, finish, 0)


def scatter(nz, collective_id, parts):
    terms, shapes, views = zip(*parts)
    n = len(parts)
    dtypes = [t.dtype for t in terms]

    def bufs(*lead):
        return [pltpu.VMEM((*lead, *shape), d) for shape, d in zip(shapes, dtypes)]

    return pl.pallas_call(
        functools.partial(scatter_kernel, nz, views),
        in_specs=[ANY] * n,
        out_specs=[VMEM] * n,
        out_shape=[sds(shape, d) for shape, d in zip(shapes, dtypes)],
        scratch_shapes=[
            *bufs(nz, 4),
            *bufs(nz, 4),
            *bufs(nz, 2),
            *bufs(nz),
            *bufs(nz),
            *bufs(nz),
            pltpu.SemaphoreType.DMA((9, nz, n)),
            pltpu.SemaphoreType.DMA((9, nz, n)),
            pltpu.SemaphoreType.DMA((4, nz, n)),
        ],
        name="scatter",
        compiler_params=params(62, collective_id=collective_id, has_side_effects=True),
    )(*terms)


def whole_rows(side, mine, other):
    mine, other = mine.astype(F32), other.astype(F32)
    first = jnp.where(side == 0, mine, other)
    second = jnp.where(side == 0, other, mine)
    return jnp.concatenate([jnp.zeros((MEM, D), F32), first, second], axis=0)


def split_rows(side, rows):
    half = (SEG - MEM) // 2
    first, second = rows[MEM : MEM + half], rows[MEM + half :]
    keep = jnp.where(side == 0, first, second)
    send = jnp.where(side == 0, second, first)
    return keep, send


def project_kernel(mine_ref, other_ref, w_ref, table_ref, x_ref, q_ref, k_ref, v_ref):
    side = lax.axis_index("tensor")
    mine = mine_ref[LOCAL * side + pl.program_id(0)]
    x = whole_rows(side, mine, other_ref[0]).astype(BF16)
    x_ref[0] = x
    query = nn(x, w_ref[0]) + table_ref[QUERY_BIAS : QUERY_BIAS + 1, :]
    q_ref[0] = (query * SCALE).astype(BF16)
    k_ref[0] = nn(x, w_ref[1]).astype(BF16)
    v_ref[0] = (nn(x, w_ref[2]) + table_ref[VALUE_BIAS : VALUE_BIAS + 1, :]).astype(BF16)


def slot_rows(width=D):
    return pl.BlockSpec((1, SEG, width), lambda s: (s, 0, 0))


def half_rows(half):
    return pl.BlockSpec((1, half, D), lambda s: (s, 0, 0))


def project(tokens, other, attn, table):
    return pl.pallas_call(
        project_kernel,
        grid=(LOCAL,),
        in_specs=[
            once(tokens.shape, (0, 0, 0)),
            half_rows(tokens.shape[1]),
            once((3, D, D), (0, 0, 0)),
            once((NVEC, D), (0, 0)),
        ],
        out_specs=[slot_rows()] * 4,
        out_shape=[sds((LOCAL, SEG, D), BF16)] * 4,
        name="project",
        compiler_params=params(),
    )(tokens, other, attn, table)


def head_masks():
    feature_head = lax.broadcasted_iota(jnp.int32, (1, D), 1) // DH
    return [feature_head == h for h in range(HEADS)]


def by_head(rows16, masks):
    zero = jnp.zeros_like(rows16)
    return jnp.concatenate([jnp.where(m, rows16, zero) for m in masks], axis=0)


def own_columns(blocks, masks):
    total = jnp.zeros((THIN, D), blocks.dtype)
    for h, m in enumerate(masks):
        total = jnp.where(m, blocks[THIN * h : THIN * (h + 1)], total)
    return total


def copies_of(key_mask_shape):
    row = lax.rem(lax.broadcasted_iota(jnp.int32, key_mask_shape, 0), THIN)
    key = lax.broadcasted_iota(jnp.int32, key_mask_shape, 1)
    return jnp.where((key < MEM) & (key <= row), 2.0, 1.0)


def chain_kernel(turn, *refs):
    n_in = 8 if turn == 0 else 12
    place_ref, table_ref, attn_ref, ffn_ref = refs[:4]
    start_ref = refs[8] if turn else None
    (
        x_ref,
        q_ref,
        k_ref,
        v_ref,
        saved_d_ref,
        saved_f_ref,
        saved_s_ref,
        memory_ref,
        wa,
        wf,
        xb,
        qb,
        kb,
        vb,
        save_d,
        save_f,
        save_s,
        sem_w,
        sem_x,
        sem_kv,
        sem_out,
    ) = refs[n_in:]

    @pl.when(lax.axis_index("tensor") == turn)
    def _():
        loads = [
            pltpu.make_async_copy(attn_ref, wa, sem_w.at[0]),
            pltpu.make_async_copy(ffn_ref.at[0], wf.at[0], sem_w.at[1]),
            pltpu.make_async_copy(ffn_ref.at[1], wf.at[1], sem_w.at[2]),
        ]
        tiles = [
            pltpu.make_async_copy(x_ref.at[s, pl.ds(0, THIN)], xb.at[s], sem_x.at[s])
            for s in range(LOCAL)
        ]
        keys = [
            pltpu.make_async_copy(src.at[s], dst.at[s], sem_kv.at[2 * s + i])
            for s in range(LOCAL)
            for i, (src, dst) in enumerate(((k_ref, kb), (v_ref, vb)))
        ]
        for c in tiles + loads[:1] + keys + loads[1:]:
            c.start()
        masks = head_masks()
        memory_row = lax.broadcasted_iota(jnp.int32, (THIN, 1), 0) < MEM
        first = table_ref[FIRST_MEMORY:NVEC, :]
        first = jnp.concatenate([first, jnp.zeros((THIN - MEM, D), F32)], axis=0)
        row = lambda r: table_ref[r : r + 1, :]
        memory = None if start_ref is None else start_ref[...].astype(F32)
        for s in range(LOCAL):
            tiles[s].wait()
            if s == 0:
                loads[0].wait()
            keys[2 * s].wait()
            keys[2 * s + 1].wait()
            if memory is None:
                memory = first
            else:
                memory = jnp.where(place_ref[LOCAL * turn + s] == 0, first, memory)
            x16 = jnp.where(memory_row, memory, xb[s].astype(F32)).astype(BF16)
            xb[s] = x16
            qb[s] = ((nn(x16, wa[0]) + row(QUERY_BIAS)) * SCALE).astype(BF16)
            kb[s, 0:THIN] = nn(x16, wa[1]).astype(BF16)
            vb[s, 0:THIN] = (nn(x16, wa[2]) + row(VALUE_BIAS)).astype(BF16)
            outs = [
                pltpu.make_async_copy(xb.at[s], x_ref.at[s, pl.ds(0, THIN)], sem_out.at[4 * s]),
                pltpu.make_async_copy(qb.at[s], q_ref.at[s, pl.ds(0, THIN)], sem_out.at[4 * s + 1]),
                pltpu.make_async_copy(
                    kb.at[s, pl.ds(0, THIN)], k_ref.at[s, pl.ds(0, THIN)], sem_out.at[4 * s + 2]
                ),
                pltpu.make_async_copy(
                    vb.at[s, pl.ds(0, THIN)], v_ref.at[s, pl.ds(0, THIN)], sem_out.at[4 * s + 3]
                ),
            ]
            for c in outs:
                c.start()
            if turn == 1 and s == LOCAL - 1:
                save_d[s] = jnp.zeros_like(save_d[s])
                save_f[s] = jnp.zeros_like(save_f[s])
                save_s[s] = jnp.zeros_like(save_s[s])
            else:
                q_heads = by_head(qb[s], masks)
                score = nt(q_heads, kb[s])
                top = jnp.max(score, axis=-1, keepdims=True)
                weight = jnp.exp(score - top) * copies_of(score.shape)
                total = jnp.sum(weight, axis=-1, keepdims=True)
                share = (weight / total).astype(BF16)
                log_total = top + jnp.log(total)
                context = own_columns(nn(share, vb[s]), masks).astype(BF16)
                unit1, inverse1 = normalized(
                    x16.astype(F32) + nt(context, wa[3]) + row(OUT_BIAS)
                )
                hidden = (unit1 * row(GAIN1) + row(SHIFT1)).astype(BF16)
                if s == 0:
                    loads[1].wait()
                up = nt(hidden, wf[0])
                up_bias = jnp.concatenate([row(UP_BIAS + i) for i in range(FF // D)], axis=1)
                active16, slope = gelu_parts(up + up_bias)
                active16 = active16.astype(BF16)
                if s == 0:
                    loads[2].wait()
                second = hidden.astype(F32) + nn(active16, wf[1]) + row(DOWN_BIAS)
                unit2, inverse2 = normalized(second)
                output = (unit2 * row(GAIN2) + row(SHIFT2)).astype(BF16)
                memory = output.astype(F32)
                memory_ref[...] = output
                save_d[s, 0] = hidden
                save_d[s, 1] = unit1.astype(BF16)
                save_d[s, 2] = unit2.astype(BF16)
                save_d[s, 3] = context
                save_f[s, 0] = active16
                save_f[s, 1] = slope.astype(BF16)
                wide = lambda v: jnp.broadcast_to(v, (v.shape[0], 128))
                save_s[s, 0 : HEADS * THIN] = wide(log_total)
                save_s[s, HEADS * THIN : HEADS * THIN + THIN] = wide(inverse1)
                save_s[s, HEADS * THIN + THIN :] = wide(inverse2)
            for c in outs:
                c.wait()
        saves = [
            pltpu.make_async_copy(save_d, saved_d_ref, sem_out.at[0]),
            pltpu.make_async_copy(save_f, saved_f_ref, sem_out.at[1]),
            pltpu.make_async_copy(save_s, saved_s_ref, sem_out.at[2]),
        ]
        for c in saves:
            c.start()
        for c in saves:
            c.wait()


SAVED = (
    sds((LOCAL, 4, THIN, D), BF16),
    sds((LOCAL, 2, THIN, FF), BF16),
    sds((LOCAL, HEADS * THIN + 2 * THIN, 128), F32),
)


def chain(turn, place, table, attn, ffn, x, q, k, v, start=None, saved=()):
    whole = sds((LOCAL, SEG, D), BF16)
    aliases = {4 + i: i for i in range(4)}
    more, specs = (), []
    if turn:
        more, specs = (start, *saved), [VMEM] + [ANY] * 3
        aliases.update({9 + i: 4 + i for i in range(3)})
    outs = pl.pallas_call(
        functools.partial(chain_kernel, turn),
        in_specs=[SMEM, VMEM] + [ANY] * 6 + specs,
        out_specs=[ANY] * 7 + [VMEM],
        out_shape=[whole] * 4 + list(SAVED) + [sds((THIN, D), BF16)],
        input_output_aliases=aliases,
        scratch_shapes=[
            pltpu.VMEM((4, D, D), BF16),
            pltpu.VMEM((2, FF, D), BF16),
            pltpu.VMEM((LOCAL, THIN, D), BF16),
            pltpu.VMEM((LOCAL, THIN, D), BF16),
            pltpu.VMEM((LOCAL, SEG, D), BF16),
            pltpu.VMEM((LOCAL, SEG, D), BF16),
            pltpu.VMEM((LOCAL, 4, THIN, D), BF16),
            pltpu.VMEM((LOCAL, 2, THIN, FF), BF16),
            pltpu.VMEM((LOCAL, HEADS * THIN + 2 * THIN, 128), F32),
            pltpu.SemaphoreType.DMA((3,)),
            pltpu.SemaphoreType.DMA((LOCAL,)),
            pltpu.SemaphoreType.DMA((2 * LOCAL,)),
            pltpu.SemaphoreType.DMA((4 * LOCAL,)),
        ],
        name="chain",
        compiler_params=params(),
    )(place, table, attn, ffn, x, q, k, v, *more)
    return outs[:4], outs[4:7], outs[7]


def own_lanes(block, head):
    lane = lax.broadcasted_iota(jnp.int32, block.shape, 1)
    return jnp.where((lane < DH) == (head == 0), block, jnp.zeros_like(block))


def seen(score, first_query):
    key = lax.broadcasted_iota(jnp.int32, score.shape, 0)
    query = lax.broadcasted_iota(jnp.int32, score.shape, 1) + first_query
    return key <= query


def attend_pair(q, k, v):
    contexts_of, logs_of = [], [[], []]
    for part in range(SEG // TILE):
        rows = slice(TILE * part, TILE * (part + 1))
        keys = slice(0, TILE * (part + 1))
        contexts = []
        for head in range(2):
            score = nt(own_lanes(k[keys], head), q[rows])
            key = lax.broadcasted_iota(jnp.int32, score.shape, 0)
            allowed = seen(score, TILE * part) & (key >= MEM)
            score = jnp.where(allowed, score, MASK_VALUE)
            top = jnp.max(score, axis=0, keepdims=True)
            weight = jnp.exp(score - top)
            total = jnp.sum(weight, axis=0, keepdims=True)
            share = (weight * (1.0 / total)).astype(BF16)
            logs_of[head].append(top + jnp.log(total))
            contexts.append(tn(share, v[keys]))
        lane = lax.broadcasted_iota(jnp.int32, contexts[0].shape, 1)
        contexts_of.append(jnp.where(lane < DH, contexts[0], contexts[1]).astype(BF16))
    return jnp.concatenate(contexts_of, axis=0), [jnp.concatenate(l, axis=1) for l in logs_of]


def attend_kernel(q_ref, k_ref, v_ref, c_ref, log_ref):
    context, logs = attend_pair(q_ref[0], k_ref[0], v_ref[0])
    c_ref[0] = context
    for head in range(2):
        log_ref[0, 0, head : head + 1] = logs[head]


def with_memory(q, k16, v16, context, log_tokens):
    masks = head_masks()
    score = nt(by_head(k16, masks), q).reshape(HEADS, THIN, SEG)
    key = lax.broadcasted_iota(jnp.int32, score.shape, 1)
    score = jnp.where(key < MEM, score, MASK_VALUE)
    top = jnp.maximum(jnp.max(score, axis=1), log_tokens)
    weight = jnp.exp(score - top[:, None])
    old = jnp.exp(log_tokens - top)
    total = jnp.sum(weight, axis=1) + old
    share = (weight * (1.0 / total)[:, None]).reshape(HEADS * THIN, SEG).astype(BF16)
    kept = old / total
    coarse = kept.astype(BF16)
    fine = (kept - coarse.astype(F32)).astype(BF16)
    pad = jnp.zeros((4, SEG), BF16)
    head = lax.rem(lax.broadcasted_iota(jnp.int32, (2 * THIN, D), 0), THIN)
    spread = jnp.where(head == lax.broadcasted_iota(jnp.int32, (2 * THIN, D), 1) // DH, 1.0, 0.0)
    factor = tn(jnp.concatenate([coarse, pad, fine, pad], axis=0), spread.astype(BF16))
    context = factor * context.astype(F32) + tn(share, by_head(v16, masks))
    return context.astype(BF16), top + jnp.log(total)


PAIR = pl.BlockSpec((1, SEG, 2 * DH), lambda s, h: (s, 0, h))
PAIR_LOG = pl.BlockSpec((1, 1, 2, SEG), lambda s, h: (s, h, 0, 0))


def attend(q, k, v):
    return pl.pallas_call(
        attend_kernel,
        grid=(LOCAL, HEADS // 2),
        in_specs=[PAIR] * 3,
        out_specs=[PAIR, PAIR_LOG],
        out_shape=[sds((LOCAL, SEG, D), BF16), sds((LOCAL, HEADS // 2, 2, SEG), F32)],
        name="attend",
        compiler_params=params(),
    )(q, k, v)


def attend_back_kernel(q_ref, k_ref, v_ref, dc_ref, log_ref, dq_ref, dk_ref, dv_ref):
    last = SEG // TILE
    key_terms, value_terms = [], []
    for head in range(2):
        key_sum, value_sum = [], []
        query_parts = []
        for part in range(last):
            rows = slice(TILE * part, TILE * (part + 1))
            keys = slice(0, TILE * (part + 1))
            q, dc = q_ref[0, rows], dc_ref[0, rows]
            k = k_ref[0, keys]
            score = nt(own_lanes(k, head), q)
            share = jnp.exp(score - log_ref[0, 0, head : head + 1, rows])
            share = jnp.where(seen(score, TILE * part), share, 0.0)
            share_grad = nt(own_lanes(v_ref[0, keys], head), dc)
            inner = jnp.sum(share_grad * share, axis=0, keepdims=True)
            score_grad = (share * (share_grad - inner)).astype(BF16)
            value_sum.append(nn(share.astype(BF16), dc))
            key_sum.append(nn(score_grad, q))
            query_parts.append(tn(score_grad, k))
        key_terms.append(key_sum)
        value_terms.append(value_sum)
        if head == 0:
            first_queries = query_parts
    for part in range(last):
        rows = slice(TILE * part, TILE * (part + 1))
        lane = lax.broadcasted_iota(jnp.int32, (TILE, 2 * DH), 1)
        pick = lambda a, b: jnp.where(lane < DH, a, b)
        dq_ref[0, rows] = (pick(first_queries[part], query_parts[part]) * SCALE).astype(BF16)
        for terms, out in ((key_terms, dk_ref), (value_terms, dv_ref)):
            total = None
            for later in range(part, last):
                term = pick(terms[0][later][rows], terms[1][later][rows])
                total = term if total is None else total + term
            out[0, rows] = total.astype(BF16)


def attend_back(q, k, v, dc, log_total):
    return pl.pallas_call(
        attend_back_kernel,
        grid=(LOCAL, HEADS // 2),
        in_specs=[PAIR] * 4 + [PAIR_LOG],
        out_specs=[PAIR] * 3,
        out_shape=[sds((LOCAL, SEG, D), BF16)] * 3,
        name="attend_back",
        compiler_params=params(),
    )(q, k, v, dc, log_total)


def rows_kernel(
    place_ref,
    x_ref,
    q_ref,
    k16_ref,
    v16_ref,
    tokens_c_ref,
    tokens_log_ref,
    mine_ref,
    other_ref,
    wo_ref,
    wf_ref,
    table_ref,
    keep_ref,
    send_ref,
    h_ref,
    g_ref,
    du_ref,
    df_ref,
    da_ref,
    dc_ref,
    c_ref,
    log_ref,
    sums_ref,
    slope_ref,
):
    row = lambda r: table_ref[r : r + 1, :]
    slot = pl.program_id(0)
    side = lax.axis_index("tensor")
    live = place_ref[LOCAL * side + slot] >= 0

    @pl.when(slot == 0)
    def _():
        sums_ref[...] = jnp.zeros_like(sums_ref)

    def add(r, value):
        sums_ref[r : r + 1, :] += value

    log_tokens = jnp.concatenate([tokens_log_ref[0, h] for h in range(HEADS // 2)], axis=0)
    context, log_total = with_memory(
        q_ref[0], k16_ref[0], v16_ref[0], tokens_c_ref[0], log_tokens
    )
    c_ref[0] = context
    for h in range(HEADS // 2):
        log_ref[0, h] = log_total[2 * h : 2 * h + 2]
    unit1, inverse1 = normalized(x_ref[0].astype(F32) + nt(context, wo_ref[0]) + row(OUT_BIAS))
    hidden = (unit1 * row(GAIN1) + row(SHIFT1)).astype(BF16)
    h_ref[0] = hidden
    second = hidden.astype(F32) + row(DOWN_BIAS)
    for i in range(FF // D):
        cols = slice(D * i, D * (i + 1))
        up = nt(hidden, wf_ref[0, cols]) + row(UP_BIAS + i)
        active, slope = gelu_parts(up)
        active = active.astype(BF16)
        g_ref[0, :, cols] = active
        slope_ref[:, cols] = slope.astype(BF16)
        second = second + nn(active, wf_ref[1, cols])
    unit2, inverse2 = normalized(second)
    output = jnp.where(live, unit2 * row(GAIN2) + row(SHIFT2), 0.0)
    keep, send = split_rows(side, output)
    keep_ref[0] = keep.astype(BF16)
    send_ref[0] = send.astype(BF16)

    grad = whole_rows(side, mine_ref[LOCAL * side + slot], other_ref[0])
    grad = jnp.where(live, grad, 0.0)
    add(GAIN2, row_sum(grad * unit2))
    add(SHIFT2, row_sum(grad))
    second_grad = normalized_back(grad * row(GAIN2), unit2, inverse2)
    down_grad = second_grad.astype(BF16)
    df_ref[0] = down_grad
    add(DOWN_BIAS, row_sum(down_grad.astype(F32)))
    hidden_grad = second_grad
    for i in range(FF // D):
        cols = slice(D * i, D * (i + 1))
        up_grad = (nt(down_grad, wf_ref[1, cols]) * slope_ref[:, cols].astype(F32)).astype(BF16)
        du_ref[0, :, cols] = up_grad
        add(UP_BIAS + i, row_sum(up_grad.astype(F32)))
        hidden_grad = hidden_grad + nn(up_grad, wf_ref[0, cols])
    add(GAIN1, row_sum(hidden_grad * unit1))
    add(SHIFT1, row_sum(hidden_grad))
    branch_grad = normalized_back(hidden_grad * row(GAIN1), unit1, inverse1).astype(BF16)
    da_ref[0] = branch_grad
    add(OUT_BIAS, row_sum(branch_grad.astype(F32)))
    dc_ref[0] = nn(branch_grad, wo_ref[0]).astype(BF16)


def rows_part(place, x, q, k, v, c, log_tokens, cot, other, attn, ffn, table):
    half = cot.shape[1]
    whole, whole_wide = sds((LOCAL, SEG, D), BF16), sds((LOCAL, SEG, FF), BF16)
    part, logs = sds((LOCAL, half, D), BF16), sds((LOCAL, HEADS // 2, 2, SEG), F32)
    rows, wide = slot_rows(), slot_rows(FF)
    thin = pl.BlockSpec((1, THIN, D), lambda s: (s, 0, 0))
    log_rows = pl.BlockSpec((1, HEADS // 2, 2, SEG), lambda s: (s, 0, 0, 0))
    return pl.pallas_call(
        rows_kernel,
        grid=(LOCAL,),
        in_specs=[SMEM, rows, rows, thin, thin, rows, log_rows]
        + [once(cot.shape, (0, 0, 0)), half_rows(half)]
        + [once((1, D, D), (3, 0, 0)), once((2, FF, D), (0, 0, 0)), once((NVEC, D), (0, 0))],
        out_specs=[half_rows(half)] * 2
        + [rows, wide, wide, rows, rows, rows, rows, log_rows, once((THIN, D), (0, 0))],
        out_shape=[part] * 2
        + [whole, whole_wide, whole_wide, whole, whole, whole, whole, logs, sds((THIN, D), F32)],
        scratch_shapes=[pltpu.VMEM((SEG, FF), BF16)],
        name="rows_part",
        compiler_params=params(),
    )(place, x, q, k, v, c, log_tokens, cot, other, attn, ffn, table)


def chain_back_kernel(turn, *refs):
    n_in = 12 if turn else 16
    place_ref, table_ref, attn_ref, ffn_ref, q_ref, k_ref, v_ref = refs[:7]
    saved_d_ref, saved_f_ref, saved_s_ref = refs[7:10]
    start_ref = None if turn else refs[12]
    (
        dk_ref,
        dv_ref,
        thin_d_ref,
        thin_f_ref,
        sums_ref,
        grad_ref,
        wa,
        wf,
        qb,
        kb,
        vb,
        dkb,
        dvb,
        save_d,
        save_f,
        save_s,
        thin_d,
        thin_f,
        sums,
        sem_w,
        sem_in,
        sem_out,
    ) = refs[n_in:]

    @pl.when(lax.axis_index("tensor") == turn)
    def _():
        loads = [
            pltpu.make_async_copy(attn_ref, wa, sem_w.at[0]),
            pltpu.make_async_copy(ffn_ref.at[0], wf.at[0], sem_w.at[1]),
            pltpu.make_async_copy(ffn_ref.at[1], wf.at[1], sem_w.at[2]),
        ]
        reads = [
            pltpu.make_async_copy(q_ref.at[:, pl.ds(0, THIN)], qb, sem_in.at[0]),
            pltpu.make_async_copy(k_ref, kb, sem_in.at[1]),
            pltpu.make_async_copy(v_ref, vb, sem_in.at[2]),
            pltpu.make_async_copy(dk_ref, dkb, sem_in.at[3]),
            pltpu.make_async_copy(dv_ref, dvb, sem_in.at[4]),
            pltpu.make_async_copy(saved_d_ref, save_d, sem_in.at[5]),
            pltpu.make_async_copy(saved_f_ref, save_f, sem_in.at[6]),
            pltpu.make_async_copy(saved_s_ref, save_s, sem_in.at[7]),
        ]
        order = reads[5:] + [loads[2], loads[1], loads[0]] + reads[:5]
        if turn:
            order = reads[3:5] + [loads[0]] + reads[5:] + [loads[2], loads[1]] + reads[:3]
        for c in order:
            c.start()
        waited = set()

        def need(*copies):
            for c in copies:
                if id(c) not in waited:
                    waited.add(id(c))
                    c.wait()

        sums[...] = jnp.zeros_like(sums)
        masks = head_masks()
        memory_row = lax.broadcasted_iota(jnp.int32, (THIN, 1), 0) < MEM
        row = lambda r: table_ref[r : r + 1, :]

        def add(r, value):
            sums[r : r + 1, :] += value

        grad = None if turn else start_ref[...]
        for s in reversed(range(LOCAL)):
            if turn and s == LOCAL - 1:
                thin_d[s] = jnp.zeros_like(thin_d[s])
                thin_f[s] = jnp.zeros_like(thin_f[s])
                grad = jnp.zeros((THIN, D), F32)
            else:
                after = place_ref[LOCAL * turn + s + 1]
                grad = jnp.where(memory_row & (after > 0), grad, 0.0)
                need(*reads[5:])
                unit1, unit2 = save_d[s, 1].astype(F32), save_d[s, 2].astype(F32)
                base = HEADS * THIN
                log_total = save_s[s, 0:base, 0:1]
                inverse1 = save_s[s, base : base + THIN, 0:1]
                inverse2 = save_s[s, base + THIN :, 0:1]
                add(GAIN2, row_sum(grad * unit2))
                add(SHIFT2, row_sum(grad))
                second_grad = normalized_back(grad * row(GAIN2), unit2, inverse2)
                down_grad = second_grad.astype(BF16)
                add(DOWN_BIAS, row_sum(down_grad.astype(F32)))
                need(loads[2])
                up_grad = (nt(down_grad, wf[1]) * save_f[s, 1].astype(F32)).astype(BF16)
                up_sum = row_sum(up_grad.astype(F32))
                for i in range(FF // D):
                    add(UP_BIAS + i, up_sum[:, D * i : D * (i + 1)])
                need(loads[1])
                hidden_grad = second_grad + nn(up_grad, wf[0])
                add(GAIN1, row_sum(hidden_grad * unit1))
                add(SHIFT1, row_sum(hidden_grad))
                pre_grad = normalized_back(hidden_grad * row(GAIN1), unit1, inverse1)
                branch_grad = pre_grad.astype(BF16)
                add(OUT_BIAS, row_sum(branch_grad.astype(F32)))
                need(loads[0])
                context_grad = nn(branch_grad, wa[3]).astype(BF16)
                dc_heads = by_head(context_grad, masks)
                need(*reads[:5])
                q_heads = by_head(qb[s], masks)
                score = nt(q_heads, kb[s])
                share = jnp.exp(score - log_total) * copies_of(score.shape)
                share_grad = nt(dc_heads, vb[s])
                inner = jnp.sum(share_grad * share, axis=-1, keepdims=True)
                score_grad = (share * (share_grad - inner)).astype(BF16)
                query_grad = (own_columns(nn(score_grad, kb[s]), masks) * SCALE).astype(BF16)
                dkb[s] = (dkb[s].astype(F32) + tn(score_grad, q_heads)).astype(BF16)
                dvb[s] = (dvb[s].astype(F32) + tn(share.astype(BF16), dc_heads)).astype(BF16)
                thin_d[s, 0] = down_grad
                thin_d[s, 1] = branch_grad
                thin_d[s, 2] = query_grad
                thin_d[s, 3] = save_d[s, 0]
                thin_d[s, 4] = save_d[s, 3]
                thin_f[s, 0] = up_grad
                thin_f[s, 1] = save_f[s, 0]
                grad = pre_grad + nt(query_grad, wa[0])
            need(loads[0], reads[3], reads[4])
            grad = grad + nt(dkb[s, 0:THIN], wa[1]) + nt(dvb[s, 0:THIN], wa[2])
            first = jnp.where(place_ref[LOCAL * turn + s] == 0, grad, 0.0)
            sums[FIRST_MEMORY : FIRST_MEMORY + THIN, :] += first
        grad_ref[...] = grad
        writes = [
            pltpu.make_async_copy(dkb, dk_ref, sem_out.at[0]),
            pltpu.make_async_copy(dvb, dv_ref, sem_out.at[1]),
            pltpu.make_async_copy(thin_d, thin_d_ref, sem_out.at[2]),
            pltpu.make_async_copy(thin_f, thin_f_ref, sem_out.at[3]),
            pltpu.make_async_copy(sums, sums_ref, sem_out.at[4]),
        ]
        for c in writes:
            c.start()
        for c in writes:
            c.wait()


THIN_SHAPES = (
    sds((LOCAL, 5, THIN, D), BF16),
    sds((LOCAL, 2, THIN, FF), BF16),
    sds((FIRST_MEMORY + THIN, D), F32),
)


def chain_back(turn, place, table, attn, ffn, q, k, v, saved, dk, dv, start=None, thin=()):
    whole = sds((LOCAL, SEG, D), BF16)
    aliases = {10: 0, 11: 1}
    more, specs = (), []
    if turn == 0:
        more, specs = (start, *thin), [VMEM] + [ANY] * 3
        aliases.update({13 + i: 2 + i for i in range(3)})
    outs = pl.pallas_call(
        functools.partial(chain_back_kernel, turn),
        in_specs=[SMEM, VMEM] + [ANY] * 10 + specs,
        out_specs=[ANY] * 5 + [VMEM],
        out_shape=[whole] * 2 + list(THIN_SHAPES) + [sds((THIN, D), F32)],
        input_output_aliases=aliases,
        scratch_shapes=[
            pltpu.VMEM((4, D, D), BF16),
            pltpu.VMEM((2, FF, D), BF16),
            pltpu.VMEM((LOCAL, THIN, D), BF16),
        ]
        + [pltpu.VMEM((LOCAL, SEG, D), BF16)] * 4
        + [pltpu.VMEM(s.shape, s.dtype) for s in SAVED + THIN_SHAPES]
        + [
            pltpu.SemaphoreType.DMA((3,)),
            pltpu.SemaphoreType.DMA((8,)),
            pltpu.SemaphoreType.DMA((5,)),
        ],
        name="chain_back",
        compiler_params=params(),
    )(place, table, attn, ffn, q, k, v, *saved, dk, dv, *more)
    return outs[:2], outs[2:5], outs[5]


def table_row(ref, index, entries):
    blocks = []
    lane = lax.broadcasted_iota(jnp.int32, (1, 128), 1)
    for block in range(D // 128):
        at, end = index * D + 128 * block, index * D + 128 * (block + 1)
        target, value = 0, jnp.zeros((1, 128), F32)
        while at < end:
            shard, inner = at // entries, at % entries
            count = min(end - at, entries - inner, 128 - inner % 128)
            place = (shard // 8, shard // 4 % 2, shard // 2 % 2, shard % 2)
            source = ref[place][inner // 128 : inner // 128 + 1]
            shift = (target - inner) % 128
            if shift:
                source = pltpu.roll(source, shift, 1)
            value = jnp.where((lane >= target) & (lane < target + count), source, value)
            at, target = at + count, target + count
        blocks.append(value)
    return jnp.concatenate(blocks, axis=1)


def head_kernel(
    nz,
    entries,
    attn_src,
    ffn_src,
    vec_src,
    tokens,
    attn_ref,
    ffn_ref,
    vec_ref,
    x_ref,
    q_ref,
    k_ref,
    v_ref,
    c_ref,
    log_ref,
    wa,
    vec,
    mine,
    other,
    xb,
    qb,
    kb,
    vb,
    cb,
    logs,
    send_sem,
    recv_sem,
    own_sem,
    swap_sem,
    out_sem,
):
    place = my_place()
    side = place[3]
    halves = swap_halves(place, tokens, other, swap_sem)
    own = [
        pltpu.make_async_copy(attn_src, attn_view(wa, *place), own_sem.at[0]),
        pltpu.make_async_copy(vec_src, vec_view(vec, *place), own_sem.at[1]),
        pltpu.make_async_copy(ffn_src, ffn_view(ffn_ref, *place), own_sem.at[2]),
        pltpu.make_async_copy(tokens.at[pl.ds(LOCAL * side, LOCAL)], mine, own_sem.at[3]),
    ]
    for copy in own:
        copy.start()
    entry_barrier(nz)
    halves.start()
    steps = functools.partial(gather_steps, nz, place, send_sem=send_sem, recv_sem=recv_sem)
    begin, step, end_arrive, end_send = steps(
        1, [(0, wa, attn_view), (1, vec, vec_view)]
    )
    begin2, step2, end_arrive2, end_send2 = steps(place[2], [(2, ffn_ref, ffn_view)])
    own[0].wait()
    own[1].wait()
    begin()

    def loop(t, carry):
        step(t)
        return carry

    lax.fori_loop(1, nz + 2, loop, 0)
    own[2].wait()
    begin2()
    own[3].wait()
    halves.wait()
    end_arrive()
    outs = [
        pltpu.make_async_copy(wa, attn_ref, out_sem.at[0]),
        pltpu.make_async_copy(vec, vec_ref, out_sem.at[1]),
    ]
    for copy in outs:
        copy.start()

    weight = lambda i: wa[i].reshape(D, D)

    def project_slot(s):
        x = whole_rows(side, mine[s], other[s]).astype(BF16)
        xb[s] = x
        qb[s] = ((nn(x, weight(0)) + table_row(vec, QUERY_BIAS, entries)) * SCALE).astype(BF16)
        kb[s] = nn(x, weight(1)).astype(BF16)
        vb[s] = (nn(x, weight(2)) + table_row(vec, VALUE_BIAS, entries)).astype(BF16)
        for i, (buf, out) in enumerate(((xb, x_ref), (qb, q_ref), (kb, k_ref), (vb, v_ref))):
            outs.append(pltpu.make_async_copy(buf.at[s], out.at[s], out_sem.at[2 + 4 * s + i]))
            outs[-1].start()

    def attend_at(i, carry):
        s, h = i // (HEADS // 2), i % (HEADS // 2)
        lanes = pl.ds(pl.multiple_of(h * 2 * DH, 2 * DH), 2 * DH)
        context, log_rows = attend_pair(qb[s, :, lanes], kb[s, :, lanes], vb[s, :, lanes])
        cb[s, :, lanes] = context
        for head in range(2):
            logs[s, h, head : head + 1] = log_rows[head]
        return carry

    project_slot(0)
    project_slot(1)
    pairs = LOCAL * HEADS // 2
    done = 0
    for t in range(1, nz + 2):
        step2(t)
        upto = pairs * t // (nz + 1)
        lax.fori_loop(done, upto, attend_at, 0)
        done = upto
    outs.append(pltpu.make_async_copy(cb, c_ref, out_sem.at[2 + 4 * LOCAL]))
    outs.append(pltpu.make_async_copy(logs, log_ref, out_sem.at[3 + 4 * LOCAL]))
    outs[-1].start()
    outs[-2].start()
    end_send()
    end_send2()
    end_arrive2()
    for copy in outs:
        copy.wait()


def head(nz, attention, hidden_major, vec, tokens, entries):
    rows, hidden = attention.shape[1], hidden_major.shape[1]
    whole = sds((LOCAL, SEG, D), BF16)
    logs = (LOCAL, HEADS // 2, 2, SEG)
    attn_shape, vec_shape = (4, nz, 2, 2, rows, D), (nz, 2, 2, 2, *VEC_TILE)
    half = pltpu.VMEM((LOCAL, *tokens.shape[1:]), BF16)
    return pl.pallas_call(
        functools.partial(head_kernel, nz, entries),
        in_specs=[ANY] * 4,
        out_specs=[ANY] * 9,
        out_shape=[
            sds(attn_shape, BF16),
            sds((2, nz, 2, 2, 2, hidden, D), BF16),
            sds(vec_shape, F32),
            *[whole] * 5,
            sds(logs, F32),
        ],
        scratch_shapes=[
            pltpu.VMEM(attn_shape, BF16),
            pltpu.VMEM(vec_shape, F32),
            half,
            half,
            *[pltpu.VMEM(whole.shape, BF16)] * 5,
            pltpu.VMEM(logs, F32),
            pltpu.SemaphoreType.DMA((9, nz, 3)),
            pltpu.SemaphoreType.DMA((8, nz, 3)),
            pltpu.SemaphoreType.DMA((4,)),
            pltpu.SemaphoreType.DMA((2,)),
            pltpu.SemaphoreType.DMA((4 + 4 * LOCAL,)),
        ],
        name="head",
        compiler_params=params(collective_id=0, has_side_effects=True),
    )(attention, hidden_major, vec, tokens)


def token_grad_kernel(place_ref, da_ref, dq_ref, dk_ref, dv_ref, w_ref, keep_ref, send_ref):
    side = lax.axis_index("tensor")
    total = da_ref[0].astype(F32)
    for i, ref in enumerate((dq_ref, dk_ref, dv_ref)):
        total = total + nt(ref[0], w_ref[i])
    live = place_ref[LOCAL * side + pl.program_id(0)] >= 0
    keep, send = split_rows(side, jnp.where(live, total, 0.0))
    keep_ref[0] = keep.astype(BF16)
    send_ref[0] = send.astype(BF16)


def token_gradient(place, da, dq, dk, dv, attn):
    half = (SEG - MEM) // 2
    return pl.pallas_call(
        token_grad_kernel,
        grid=(LOCAL,),
        in_specs=[SMEM] + [slot_rows()] * 4 + [once((3, D, D), (0, 0, 0))],
        out_specs=[half_rows(half)] * 2,
        out_shape=[sds((LOCAL, half, D), BF16)] * 2,
        name="token_gradient",
        compiler_params=params(),
    )(place, da, dq, dk, dv, attn)


def flat(ref):
    return ref[...].reshape(LOCAL * ref.shape[1], ref.shape[2])


def ffn_grad_kernel(g_ref, du_ref, df_ref, h_ref, thin_f_ref, thin_d_ref, out_ref):
    up = tn(flat(du_ref), flat(h_ref))
    down = tn(flat(g_ref), flat(df_ref))
    for s in range(LOCAL):
        up = up + tn(thin_f_ref[s, 0], thin_d_ref[s, 3])
        down = down + tn(thin_f_ref[s, 1], thin_d_ref[s, 0])
    out_ref[0] = up.astype(BF16)
    out_ref[1] = down.astype(BF16)


def ffn_gradient(g, du, df, h, thin_d, thin_f, chunk=768):
    hidden = pl.BlockSpec((LOCAL, SEG, chunk), lambda i: (0, 0, i))
    full = once((LOCAL, SEG, D), (0, 0, 0))
    return pl.pallas_call(
        ffn_grad_kernel,
        grid=(FF // chunk,),
        in_specs=[
            hidden,
            hidden,
            full,
            full,
            pl.BlockSpec((LOCAL, 2, THIN, chunk), lambda i: (0, 0, 0, i)),
            once(THIN_SHAPES[0].shape, (0, 0, 0, 0)),
        ],
        out_specs=pl.BlockSpec((2, chunk, D), lambda i: (0, i, 0)),
        out_shape=sds((2, FF, D), BF16),
        name="ffn_gradient",
        compiler_params=params(),
    )(g, du, df, h, thin_f, thin_d)


def attn_grad_kernel(
    x_ref, da_ref, dq_ref, dk_ref, dv_ref, c_ref, thin_d_ref, thin_c_ref, sums_ref, thin_sums_ref,
    out_ref, vec_ref
):
    x = flat(x_ref)
    dq, dk, dv = flat(dq_ref), flat(dk_ref), flat(dv_ref)
    query = tn(x, dq)
    query_bias = row_sum(dq.astype(F32))
    output = tn(flat(da_ref), flat(c_ref))
    for s in range(LOCAL):
        dq16 = thin_c_ref[s, 2]
        query = query + tn(x_ref[s, 0:THIN], dq16)
        query_bias = query_bias + row_sum(dq16.astype(F32))
        output = output + tn(thin_d_ref[s, 1], thin_c_ref[s, 4])
    out_ref[0] = query.astype(BF16)
    out_ref[1] = tn(x, dk).astype(BF16)
    out_ref[2] = tn(x, dv).astype(BF16)
    out_ref[3] = output.astype(BF16)
    vec_ref[...] = thin_sums_ref[...]
    vec_ref[0:FIRST_MEMORY] = thin_sums_ref[0:FIRST_MEMORY] + sums_ref[0:FIRST_MEMORY]
    vec_ref[QUERY_BIAS : QUERY_BIAS + 1] = query_bias
    vec_ref[VALUE_BIAS : VALUE_BIAS + 1] = row_sum(dv.astype(F32))


def attn_gradient(x, da, dq, dk, dv, c, thin_d, sums, thin_sums, chunk=256):
    part = pl.BlockSpec((LOCAL, SEG, chunk), lambda i: (0, 0, i))
    full = once((LOCAL, SEG, D), (0, 0, 0))
    lanes = lambda rows: pl.BlockSpec((rows, chunk), lambda i: (0, i))
    return pl.pallas_call(
        attn_grad_kernel,
        grid=(D // chunk,),
        in_specs=[
            full,
            full,
            part,
            part,
            part,
            part,
            once(THIN_SHAPES[0].shape, (0, 0, 0, 0)),
            pl.BlockSpec((LOCAL, 5, THIN, chunk), lambda i: (0, 0, 0, i)),
            lanes(THIN),
            lanes(FIRST_MEMORY + THIN),
        ],
        out_specs=[
            pl.BlockSpec((4, D, chunk), lambda i: (0, 0, i)),
            lanes(FIRST_MEMORY + THIN),
        ],
        out_shape=[sds((4, D, D), BF16), sds((FIRST_MEMORY + THIN, D), F32)],
        name="attn_gradient",
        compiler_params=params(),
    )(x, da, dq, dk, dv, c, thin_d, thin_d, sums, thin_sums)


def update(gradient, momentum, weight, average, rate, grad_scale):
    scaled = gradient * grad_scale
    moment = MOMENTUM * momentum + scaled
    weight_new = weight - rate * (scaled + MOMENTUM * moment)
    return (moment, weight_new, AVERAGE_DECAY * average + (1.0 - AVERAGE_DECAY) * weight_new)


VEC_TILE = (8, 128)


def in_tiles(rows):
    size = VEC_TILE[0] * VEC_TILE[1]
    padded = jnp.pad(rows, [(0, 0)] * (rows.ndim - 1) + [(0, size - rows.shape[-1])])
    return padded.reshape(*rows.shape[:-1], *VEC_TILE)


def start(attention, feedforward, vectors, tokens):
    nz = lax.axis_size("dp") // 4
    rows, hidden, entries = attention.shape[1], feedforward.shape[2], vectors.shape[0]
    attention = attention.astype(BF16)
    hidden_major = jnp.swapaxes(feedforward.astype(BF16), 1, 2)
    vec = in_tiles(vectors.astype(BF16).astype(F32))
    aligned = rows % THIN == 0
    if aligned:
        attn, ffn, table, *work = head(nz, attention, hidden_major, vec, tokens, entries)
    else:
        attn, ffn, table, other = gather(
            nz,
            0,
            [
                (attention, (4, nz, 2, 2, rows, D), attn_view),
                (hidden_major, (2, nz, 2, 2, 2, hidden, D), ffn_view),
                (vec, (nz, 2, 2, 2, *VEC_TILE), vec_view),
            ],
            tokens,
        )
    attn, ffn = attn.reshape(4, D, D), ffn.reshape(2, FF, D)
    table = table.reshape(nz * 8, VEC_TILE[0] * VEC_TILE[1])[:, :entries].reshape(NVEC, D)
    if not aligned:
        work = project(tokens, other, attn, table)
        work = [*work, *attend(*work[1:])]
    return attn, ffn, table, work


def scatter_gradients(attn_terms, ffn_terms, vec_terms, shapes):
    nz = lax.axis_size("dp") // 4
    rows, hidden, entries = shapes
    attn, ffn, vec = scatter(
        nz,
        1,
        [
            (attn_terms.reshape(4, nz, 2, 2, rows, D), (4, rows, HALF), attn_view),
            (ffn_terms.reshape(2, nz, 2, 2, 2, hidden, D), (2, hidden, D), ffn_view),
            (in_tiles(vec_terms.reshape(nz, 2, 2, 2, entries)), VEC_TILE, vec_view),
        ],
    )
    return attn.astype(F32), jnp.swapaxes(ffn, 1, 2).astype(F32), vec.reshape(-1)[:entries]


def swap(value):
    return lax.ppermute(value, "tensor", [(0, 1), (1, 0)])


def joined_kernel(keep_ref, other_ref, out_ref, sem):
    side = lax.axis_index("tensor")
    copies = [
        pltpu.make_async_copy(keep_ref, out_ref.at[pl.ds(LOCAL * side, LOCAL)], sem.at[0]),
        pltpu.make_async_copy(other_ref, out_ref.at[pl.ds(LOCAL * (1 - side), LOCAL)], sem.at[1]),
    ]
    for c in copies:
        c.start()
    for c in copies:
        c.wait()


def joined(keep, other):
    return pl.pallas_call(
        joined_kernel,
        in_specs=[ANY] * 2,
        out_specs=ANY,
        out_shape=sds((2 * LOCAL, *keep.shape[1:]), keep.dtype),
        scratch_shapes=[pltpu.SemaphoreType.DMA((2,))],
        name="joined",
        compiler_params=params(16),
    )(keep, other)


def on_device(
    tokens,
    slot_position,
    cotangent,
    attention,
    feedforward,
    vectors,
    attn_momentum,
    ffn_momentum,
    vec_momentum,
    attn_average,
    ffn_average,
    vec_average,
):
    place = slot_position
    attn, ffn, table, work = start(attention, feedforward, vectors, tokens)
    x, q, k, v, c, log_tokens = work

    cot_sent, _ = lax.optimization_barrier((cotangent, log_tokens))
    side = lax.axis_index("tensor")
    cot_other = swap(lax.dynamic_slice_in_dim(cot_sent, LOCAL * (1 - side), LOCAL, 0))

    (x, q, k, v), saved, memory = chain(0, place, table, attn, ffn, x, q, k, v)
    memory = lax.ppermute(memory, "tensor", [(0, 1)])
    (x, q, k, v), saved, _ = chain(1, place, table, attn, ffn, x, q, k, v, memory, saved)

    keep, send, h, g, du, df, da, dc, c, log_total, sums = rows_part(
        place, x, q, k, v, c, log_tokens, cotangent, cot_other, attn, ffn, table
    )
    activations = joined(keep, swap(send))
    dq, dk, dv = attend_back(q, k, v, dc, log_total)

    back = functools.partial(chain_back, place=place, table=table, attn=attn, ffn=ffn)
    back = functools.partial(back, q=q, k=k, v=v, saved=saved)
    (dk, dv), thin, grad = back(1, dk=dk, dv=dv)
    grad = lax.ppermute(grad, "tensor", [(1, 0)])
    (dk, dv), thin, _ = back(0, dk=dk, dv=dv, start=grad, thin=thin)
    thin_d, thin_f, thin_sums = thin

    keep, send = token_gradient(place, da, dq, dk, dv, attn)
    token_grad = joined(keep, swap(send))
    ffn_terms = ffn_gradient(g, du, df, h, thin_d, thin_f)
    attn_terms, vec_terms = attn_gradient(x, da, dq, dk, dv, c, thin_d, sums, thin_sums)
    vec_terms = vec_terms[:NVEC]

    attn_grad, ffn_grad, vec_grad = scatter_gradients(
        attn_terms,
        ffn_terms,
        vec_terms,
        (attention.shape[1], feedforward.shape[2], vectors.shape[0]),
    )
    grad_scale = 1.0 / math.sqrt(lax.axis_size("dp") * SLOTS * ROWS)
    attn_new = update(attn_grad, attn_momentum, attention, attn_average, ATTENTION_RATE, grad_scale)
    ffn_new = update(ffn_grad, ffn_momentum, feedforward, ffn_average, FEEDFORWARD_RATE, grad_scale)
    vec_new = update(vec_grad, vec_momentum, vectors, vec_average, VECTOR_RATE, grad_scale)
    return (
        activations,
        token_grad,
        attn_new[0],
        ffn_new[0],
        vec_new[0],
        attn_new[1],
        ffn_new[1],
        vec_new[1],
        attn_new[2],
        ffn_new[2],
        vec_new[2],
    )


def solution(mesh):
    attn_spec = P(None, "dp", "tensor")
    ffn_spec = P(None, None, ("dp", "tensor"))
    vec_spec = P(("dp", "tensor"))
    rows_spec = P("dp", "tensor", None)
    states = (attn_spec, ffn_spec, vec_spec)
    return jax.shard_map(
        on_device,
        mesh=mesh,
        in_specs=(rows_spec, P("dp"), rows_spec) + states * 3,
        out_specs=(rows_spec, rows_spec) + states * 3,
        check_vma=False,
    )
```

```python
import functools
import math

import jax
import jax.numpy as jnp
from jax import lax
from jax.experimental import pallas as pl
from jax.experimental.pallas import tpu as pltpu
from jax.sharding import PartitionSpec as P

D = 768
HEADS = 12
DH = 64
FF = 3072
MEM = 10
SLOTS = 4
ROWS = 522
NVEC = 22

HALF = D // 2
SEG = ROWS - MEM
THIN = 16
LOCAL = 2
TILE = 256

EPSILON = 1e-05
MOMENTUM = 0.9
AVERAGE_DECAY = 0.75
ATTENTION_RATE = 0.06
FEEDFORWARD_RATE = 0.02
VECTOR_RATE = 0.1
MASK_VALUE = -1e30
SCALE = 1.0 / math.sqrt(DH)

F32 = jnp.float32
BF16 = jnp.bfloat16
MIB = 1 << 20

QUERY_BIAS, VALUE_BIAS, OUT_BIAS, GAIN1, SHIFT1, DOWN_BIAS, GAIN2, SHIFT2, UP_BIAS = range(9)
FIRST_MEMORY = UP_BIAS + FF // D


def nn(a, b):
    return lax.dot_general(a, b, (((1,), (0,)), ((), ())), preferred_element_type=F32)


def nt(a, b):
    return lax.dot_general(a, b, (((1,), (1,)), ((), ())), preferred_element_type=F32)


def tn(a, b):
    return lax.dot_general(a, b, (((0,), (0,)), ((), ())), preferred_element_type=F32)


def normalized(rows):
    center = rows - jnp.mean(rows, axis=-1, keepdims=True)
    spread = jnp.mean(center * center, axis=-1, keepdims=True)
    inverse = lax.rsqrt(spread + EPSILON)
    return center * inverse, inverse


def normalized_back(grad, unit, inverse):
    mean_grad = jnp.mean(grad, axis=-1, keepdims=True)
    mean_along = jnp.mean(grad * unit, axis=-1, keepdims=True)
    return inverse * (grad - mean_grad - unit * mean_along)


def gelu_parts(u):
    size = jnp.abs(u)
    t = 1.0 / (1.0 + (0.3275911 / math.sqrt(2.0)) * size)
    bell = jnp.exp(-0.5 * u * u)
    poly = t * (
        0.5 * 0.254829592
        + t
        * (
            0.5 * -0.284496736
            + t * (0.5 * 1.421413741 + t * (0.5 * -1.453152027 + t * (0.5 * 1.061405429)))
        )
    )
    tail = poly * bell
    cdf = jnp.where(u < 0, tail, 1.0 - tail)
    return u * cdf, cdf + (u * (1.0 / math.sqrt(2.0 * math.pi))) * bell


def row_sum(block):
    return jnp.sum(block, axis=0, keepdims=True)


def params(limit=60, **more):
    return pltpu.CompilerParams(vmem_limit_bytes=limit * MIB, **more)


def once(shape, index):
    return pl.BlockSpec(shape, lambda *_: index, pipeline_mode=pl.Buffered(1))


ANY = pl.BlockSpec(memory_space=pltpu.HBM)
SMEM = pl.BlockSpec(memory_space=pltpu.SMEM)
VMEM = pl.BlockSpec(memory_space=pltpu.VMEM)


def sds(shape, dtype):
    return jax.ShapeDtypeStruct(shape, dtype)


def my_place():
    dp = lax.axis_index("dp")
    return dp // 4, (dp // 2) % 2, dp % 2, lax.axis_index("tensor")


def device(z, x, c, y):
    return {"dp": (z * 2 + x) * 2 + c, "tensor": y}


def entry_barrier(nz):
    z, x, c, y = my_place()
    barrier = pltpu.get_barrier_semaphore()
    signal = lambda d: pl.semaphore_signal(
        barrier, inc=1, device_id=d, device_id_type=pl.DeviceIdType.MESH
    )
    signal(device(z, 1 - x, c, y))
    signal(device(z, x, 1 - c, y))
    signal(device(z, x, c, 1 - y))

    @pl.when(z > 0)
    def _():
        signal(device(z - 1, x, c, y))

    @pl.when(z < nz - 1)
    def _():
        signal(device(z + 1, x, c, y))

    up = lax.convert_element_type(z < nz - 1, jnp.int32)
    down = lax.convert_element_type(z > 0, jnp.int32)
    pl.semaphore_wait(barrier, 3 + up + down)


def attn_view(ref, z, x, c, y):
    return ref.at[:, z, x, c, :, pl.ds(pl.multiple_of(y * HALF, HALF), HALF)]


def ffn_view(ref, z, x, c, y):
    return ref.at[:, z, x, c, y]


def vec_view(ref, z, x, c, y):
    return ref.at[z, x, c, y]


def hidden_view(ref, z, x, c, y):
    return ref.at[z, x, c, y]


def partners(place, lead):
    _, x, _, y = place
    first = (x + (1 - lead) * (1 - 2 * x), y + lead * (1 - 2 * y))
    second = (x + lead * (1 - 2 * x), y + (1 - lead) * (1 - 2 * y))
    return first, second, (1 - x, 1 - y)


COLUMN, FIRST, SECOND, BOTH, CORE = 0, 1, 2, 3, 4
UP, DOWN, UP_FIRST, DOWN_FIRST = 0, 8, 9, 10


def remote(src, dst, send_sem, recv_sem, target):
    return pltpu.make_async_remote_copy(
        src_ref=src,
        dst_ref=dst,
        send_sem=send_sem,
        recv_sem=recv_sem,
        device_id=target,
        device_id_type=pl.DeviceIdType.MESH,
    )


def gather_steps(nz, place, lead, z_second, pieces, send_sem, recv_sem):
    z, x, c, y = place
    first, second, both = partners(place, lead)
    to_first = device(z, first[0], c, first[1])
    to_second = device(z, second[0], c, second[1])
    to_core = device(z, x, 1 - c, y)

    def copies(send, recv, shard, target):
        return [
            remote(
                view(out, *shard),
                view(out, *shard),
                send_sem.at[send, shard[0], i],
                recv_sem.at[recv, shard[0], i],
                target,
            )
            for i, out, view in pieces
        ]

    def start(*args):
        for copy in copies(*args):
            copy.start()

    def arrived(*args):
        for copy in copies(*args):
            copy.wait_recv()

    def sent(*args):
        for copy in copies(*args):
            copy.wait_send()

    def column(zz):
        return (zz, x, c, y)

    def of_first(zz):
        return (zz, first[0], c, first[1])

    def of_second(zz):
        return (zz, second[0], c, second[1])

    def of_both(zz):
        return (zz, both[0], c, both[1])

    core_first, core_second = CORE + 2 - lead, CORE + 1 + lead

    def move_up(zz):
        return (UP, COLUMN, column(zz), device(z + 1, x, c, y))

    def move_down(zz):
        return (DOWN, COLUMN, column(zz), device(z - 1, x, c, y))

    def first_up(zz):
        return (UP_FIRST, FIRST, of_first(zz), device(z + 1, x, c, y))

    def first_down(zz):
        return (DOWN_FIRST, FIRST, of_first(zz), device(z - 1, x, c, y))

    def along(zz, rising, falling, up, down):
        if rising:

            @pl.when(z < nz - 1)
            def _():
                start(*up(zz))

        if falling:

            @pl.when(z > 0)
            def _():
                start(*down(zz))

    def stage0(zz, rising, falling, wait):
        if wait:
            arrived(UP, COLUMN, column(zz), to_core)
        if z_second and not wait:
            start(FIRST, FIRST, column(zz), to_first)
        along(zz, rising, falling, move_up, move_down)
        if not z_second:
            start(FIRST, FIRST, column(zz), to_first)
        start(SECOND, SECOND, column(zz), to_second)
        start(CORE, CORE, column(zz), to_core)

    def stage1(zz, rising, falling):
        arrived(FIRST, FIRST, of_first(zz), to_first)
        if z_second:
            along(zz, rising, falling, first_up, first_down)
        start(BOTH, BOTH, of_first(zz), to_second)
        start(core_first, core_first, of_first(zz), to_core)

    def stage2(zz, rising, falling):
        arrived(SECOND, SECOND, of_second(zz), to_second)
        start(core_second, core_second, of_second(zz), to_core)
        arrived(BOTH, BOTH, of_both(zz), to_second)
        start(CORE + 3, CORE + 3, of_both(zz), to_core)

    def begin():
        stage0(z, True, True, False)

    def step(t):
        @pl.when((t < nz) & (z - t >= 0))
        def _():
            stage0(z - t, True, False, True)

        @pl.when((t < nz) & (z + t < nz))
        def _():
            stage0(z + t, False, True, True)

        for lag, stage in ((1, stage1), (2, stage2)):
            late = t - lag

            @pl.when(late == 0)
            def _():
                stage(z, True, True)

            @pl.when((late > 0) & (late < nz) & (z - late >= 0))
            def _():
                stage(z - late, True, False)

            @pl.when((late > 0) & (late < nz) & (z + late < nz))
            def _():
                stage(z + late, False, True)

    def all_arrived(zz, carry):
        for fx in range(2):
            for fy in range(2):
                kind = CORE + 2 * fx + fy
                shard = (zz, x + fx * (1 - 2 * x), 1 - c, y + fy * (1 - 2 * y))
                arrived(kind, kind, shard, to_core)
        return carry

    def all_sent(zz, carry):
        @pl.when((zz <= z) & (z < nz - 1))
        def _():
            sent(*move_up(zz))

        @pl.when((zz >= z) & (z > 0))
        def _():
            sent(*move_down(zz))

        if z_second:

            @pl.when((zz <= z) & (z < nz - 1))
            def _():
                sent(*first_up(zz))

            @pl.when((zz >= z) & (z > 0))
            def _():
                sent(*first_down(zz))

            @pl.when(zz == z)
            def _():
                sent(FIRST, FIRST, column(zz), to_first)

        else:
            sent(FIRST, FIRST, column(zz), to_first)
        sent(SECOND, SECOND, column(zz), to_second)
        sent(BOTH, BOTH, of_first(zz), to_second)
        sent(CORE, CORE, column(zz), to_core)
        sent(core_first, core_first, of_first(zz), to_core)
        sent(core_second, core_second, of_second(zz), to_core)
        sent(CORE + 3, CORE + 3, of_both(zz), to_core)
        return carry

    def end_arrive():
        lax.fori_loop(0, nz, all_arrived, 0)

    def end_send():
        lax.fori_loop(0, nz, all_sent, 0)

    return begin, step, end_arrive, end_send


def swap_halves(place, rows, other, sem):
    z, x, c, y = place
    return remote(
        rows.at[pl.ds(LOCAL * (1 - y), LOCAL)],
        other,
        sem.at[0],
        sem.at[1],
        device(z, x, c, 1 - y),
    )


def gather_kernel(nz, views, *refs):
    n = len(views)
    srcs, tokens, outs, other = refs[:n], refs[n], refs[n + 1 : 2 * n + 1], refs[2 * n + 1]
    send_sem, recv_sem, own_sem, swap_sem = refs[2 * n + 2 :]
    place = my_place()
    halves = swap_halves(place, tokens, other, swap_sem)
    own = [
        pltpu.make_async_copy(src, view(out, *place), own_sem.at[i])
        for i, (src, out, view) in enumerate(zip(srcs, outs, views))
    ]
    for copy in own:
        copy.start()
    entry_barrier(nz)
    halves.start()
    for copy in own:
        copy.wait()
    pieces = [(i, out, view) for i, (out, view) in enumerate(zip(outs, views))]
    begin, step, end_arrive, end_send = gather_steps(
        nz, place, place[2], False, pieces, send_sem, recv_sem
    )
    begin()

    def loop(t, carry):
        step(t)
        return carry

    lax.fori_loop(1, nz + 2, loop, 0)
    end_send()
    end_arrive()
    halves.wait()


def gather(nz, collective_id, parts, tokens):
    shards, shapes, views = zip(*parts)
    n = len(parts)
    return pl.pallas_call(
        functools.partial(gather_kernel, nz, views),
        in_specs=[ANY] * (n + 1),
        out_specs=[ANY] * (n + 1),
        out_shape=[sds(shape, shard.dtype) for shard, shape in zip(shards, shapes)]
        + [sds((LOCAL, *tokens.shape[1:]), tokens.dtype)],
        scratch_shapes=[
            pltpu.SemaphoreType.DMA((11, nz, n)),
            pltpu.SemaphoreType.DMA((8, nz, n)),
            pltpu.SemaphoreType.DMA((n,)),
            pltpu.SemaphoreType.DMA((2,)),
        ],
        name="gather",
        compiler_params=params(collective_id=collective_id, has_side_effects=True),
    )(*shards, tokens)


def scatter_kernel(nz, views, *refs):
    n = len(views)
    terms, outs = refs[:n], refs[n : 2 * n]
    mine, from_core, from_second, from_first, from_below, from_above = (
        refs[2 * n + i * n : 3 * n + i * n] for i in range(6)
    )
    send_sem, recv_sem, own_sem = refs[8 * n :]
    place = z, x, c, y = my_place()
    first, second, both = partners(place, place[2])
    to_first = device(z, first[0], c, first[1])
    to_second = device(z, second[0], c, second[1])
    to_core = device(z, x, 1 - c, y)

    def copies(srcs, dsts, send, recv, zz, target):
        return [
            pltpu.make_async_remote_copy(
                src_ref=srcs[i],
                dst_ref=dsts[i],
                send_sem=send_sem.at[send, zz, i],
                recv_sem=recv_sem.at[recv, zz, i],
                device_id=target,
                device_id_type=pl.DeviceIdType.MESH,
            )
            for i in range(n)
        ]

    def slots(bufs, *index):
        return [b.at[index] for b in bufs]

    def pick(refs_, *index):
        return [b[index] for b in refs_]

    flips = [(fx, fy) for fx in range(2) for fy in range(2)]

    def at(fx, fy):
        return x + fx * (1 - 2 * x), y + fy * (1 - 2 * y)

    def core_copies(zz, f):
        fx, fy = flips[f]
        xx, yy = at(fx, fy)
        return copies(
            [view(t, zz, xx, 1 - c, yy) for t, view in zip(terms, views)],
            slots(from_core, zz, f),
            f,
            f,
            zz,
            to_core,
        )

    def own_copies(zz, f):
        fx, fy = flips[f]
        xx, yy = at(fx, fy)
        return [
            pltpu.make_async_copy(
                view(t, zz, xx, c, yy), mine[i].at[zz, f], own_sem.at[f, zz, i]
            )
            for i, (t, view) in enumerate(zip(terms, views))
        ]

    f_first, f_second = 2 - c, 1 + c

    def second_copies(zz, across):
        return copies(
            slots(from_core, zz, 3 if across else f_second),
            slots(from_second, zz, 1 if across else 0),
            4 + across,
            4 + across,
            zz,
            to_second,
        )

    def first_copies(zz):
        return copies(slots(from_second, zz, 1), slots(from_first, zz), 6, 6, zz, to_first)

    def up_copies(zz):
        return copies(slots(from_first, zz), slots(from_below, zz), 7, 7, zz, device(z + 1, x, c, y))

    def down_copies(zz):
        return copies(slots(from_first, zz), slots(from_above, zz), 8, 8, zz, device(z - 1, x, c, y))

    def run(group, what):
        for copy in group:
            getattr(copy, what)()

    def add(into, index, other, other_index):
        for i in range(n):
            a, b = into[i].at[index], other[i].at[other_index]
            a[...] = (a[...].astype(F32) + b[...].astype(F32)).astype(a.dtype)

    def by_distance(t, do):
        @pl.when((t >= 0) & (t < nz) & (z - t >= 0))
        def _():
            do(z - t)

        @pl.when((t > 0) & (t < nz) & (z + t < nz))
        def _():
            do(z + t)

    def start_own(zz):
        for f in range(4):
            run(own_copies(zz, f), "start")

    def start_core(zz):
        for f in (3, 1, 2, 0):
            run(core_copies(zz, f), "start")

    def stage0(zz):
        for f in (3, 1, 2, 0):
            run(core_copies(zz, f), "wait_recv")
            run(own_copies(zz, f), "wait")
            add(from_core, (zz, f), mine, (zz, f))
        run(second_copies(zz, 1), "start")
        run(second_copies(zz, 0), "start")

    def stage1(zz):
        run(second_copies(zz, 1), "wait_recv")
        add(from_second, (zz, 1), from_core, (zz, f_first))
        run(first_copies(zz), "start")

    def stage2(zz):
        run(second_copies(zz, 0), "wait_recv")
        add(from_second, (zz, 0), from_core, (zz, 0))
        run(first_copies(zz), "wait_recv")
        add(from_first, (zz,), from_second, (zz, 0))

        @pl.when(zz > z)
        def _():
            @pl.when(z > 0)
            def _():
                run(up_copies(zz), "wait_recv")
                add(from_first, (zz,), from_below, (zz,))

            run(up_copies(zz), "start")

        @pl.when(zz < z)
        def _():
            @pl.when(z < nz - 1)
            def _():
                run(down_copies(zz), "wait_recv")
                add(from_first, (zz,), from_above, (zz,))

            run(down_copies(zz), "start")

    entry_barrier(nz)

    def begin(k, carry):
        by_distance(nz - 1 - k, start_core)
        by_distance(nz - 1 - k, start_own)
        return carry

    lax.fori_loop(0, nz, begin, 0)

    def step(k, carry):
        t = nz - 1 - k
        by_distance(t, stage0)
        by_distance(t + 1, stage1)
        by_distance(t + 2, stage2)
        return carry

    lax.fori_loop(0, nz + 2, step, 0)

    @pl.when(z > 0)
    def _():
        run(up_copies(z), "wait_recv")
        add(from_first, (z,), from_below, (z,))

    @pl.when(z < nz - 1)
    def _():
        run(down_copies(z), "wait_recv")
        add(from_first, (z,), from_above, (z,))

    for i in range(n):
        outs[i][...] = from_first[i][z]

    def finish(zz, carry):
        for f in range(4):
            run(core_copies(zz, f), "wait_send")
        run(second_copies(zz, 1), "wait_send")
        run(second_copies(zz, 0), "wait_send")
        run(first_copies(zz), "wait_send")

        @pl.when(zz > z)
        def _():
            run(up_copies(zz), "wait_send")

        @pl.when(zz < z)
        def _():
            run(down_copies(zz), "wait_send")

        return carry

    lax.fori_loop(0, nz, finish, 0)


def scatter(nz, collective_id, parts):
    terms, shapes, views = zip(*parts)
    n = len(parts)
    dtypes = [t.dtype for t in terms]

    def bufs(*lead):
        return [pltpu.VMEM((*lead, *shape), d) for shape, d in zip(shapes, dtypes)]

    return pl.pallas_call(
        functools.partial(scatter_kernel, nz, views),
        in_specs=[ANY] * n,
        out_specs=[VMEM] * n,
        out_shape=[sds(shape, d) for shape, d in zip(shapes, dtypes)],
        scratch_shapes=[
            *bufs(nz, 4),
            *bufs(nz, 4),
            *bufs(nz, 2),
            *bufs(nz),
            *bufs(nz),
            *bufs(nz),
            pltpu.SemaphoreType.DMA((9, nz, n)),
            pltpu.SemaphoreType.DMA((9, nz, n)),
            pltpu.SemaphoreType.DMA((4, nz, n)),
        ],
        name="scatter",
        compiler_params=params(62, collective_id=collective_id, has_side_effects=True),
    )(*terms)


def whole_rows(side, mine, other):
    mine, other = mine.astype(F32), other.astype(F32)
    first = jnp.where(side == 0, mine, other)
    second = jnp.where(side == 0, other, mine)
    return jnp.concatenate([jnp.zeros((MEM, D), F32), first, second], axis=0)


def split_rows(side, rows):
    half = (SEG - MEM) // 2
    first, second = rows[MEM : MEM + half], rows[MEM + half :]
    keep = jnp.where(side == 0, first, second)
    send = jnp.where(side == 0, second, first)
    return keep, send


def project_kernel(mine_ref, other_ref, w_ref, table_ref, x_ref, q_ref, k_ref, v_ref):
    side = lax.axis_index("tensor")
    mine = mine_ref[LOCAL * side + pl.program_id(0)]
    x = whole_rows(side, mine, other_ref[0]).astype(BF16)
    x_ref[0] = x
    query = nn(x, w_ref[0]) + table_ref[QUERY_BIAS : QUERY_BIAS + 1, :]
    q_ref[0] = (query * SCALE).astype(BF16)
    k_ref[0] = nn(x, w_ref[1]).astype(BF16)
    v_ref[0] = (nn(x, w_ref[2]) + table_ref[VALUE_BIAS : VALUE_BIAS + 1, :]).astype(BF16)


def slot_rows(width=D):
    return pl.BlockSpec((1, SEG, width), lambda s: (s, 0, 0))


def half_rows(half):
    return pl.BlockSpec((1, half, D), lambda s: (s, 0, 0))


def project(tokens, other, attn, table):
    return pl.pallas_call(
        project_kernel,
        grid=(LOCAL,),
        in_specs=[
            once(tokens.shape, (0, 0, 0)),
            half_rows(tokens.shape[1]),
            once((3, D, D), (0, 0, 0)),
            once((NVEC, D), (0, 0)),
        ],
        out_specs=[slot_rows()] * 4,
        out_shape=[sds((LOCAL, SEG, D), BF16)] * 4,
        name="project",
        compiler_params=params(),
    )(tokens, other, attn, table)


def head_masks():
    feature_head = lax.broadcasted_iota(jnp.int32, (1, D), 1) // DH
    return [feature_head == h for h in range(HEADS)]


def by_head(rows16, masks):
    zero = jnp.zeros_like(rows16)
    return jnp.concatenate([jnp.where(m, rows16, zero) for m in masks], axis=0)


def own_columns(blocks, masks):
    total = jnp.zeros((THIN, D), blocks.dtype)
    for h, m in enumerate(masks):
        total = jnp.where(m, blocks[THIN * h : THIN * (h + 1)], total)
    return total


def copies_of(key_mask_shape):
    row = lax.rem(lax.broadcasted_iota(jnp.int32, key_mask_shape, 0), THIN)
    key = lax.broadcasted_iota(jnp.int32, key_mask_shape, 1)
    return jnp.where((key < MEM) & (key <= row), 2.0, 1.0)


def pair_barrier(place):
    z, x, c, y = place
    barrier = pltpu.get_barrier_semaphore()
    pl.semaphore_signal(
        barrier,
        inc=1,
        device_id=device(z, x, c, 1 - y),
        device_id_type=pl.DeviceIdType.MESH,
    )
    pl.semaphore_wait(barrier, 1)


def chain_kernel(
    place_ref,
    table_ref,
    attn_ref,
    ffn_ref,
    x_in,
    q_in,
    k_in,
    v_in,
    cot_ref,
    x_ref,
    q_ref,
    k_ref,
    v_ref,
    saved_d_ref,
    saved_f_ref,
    saved_s_ref,
    cot_other_ref,
    wa,
    wf,
    xb,
    qb,
    kb,
    vb,
    save_d,
    save_f,
    save_s,
    left,
    given,
    sem_w,
    sem_x,
    sem_kv,
    sem_out,
    sem_memory,
    sem_cot,
):
    del x_in, q_in, k_in, v_in
    place = z, x, c, y = my_place()
    loads = [
        pltpu.make_async_copy(attn_ref, wa, sem_w.at[0]),
        pltpu.make_async_copy(ffn_ref.at[0], wf.at[0], sem_w.at[1]),
        pltpu.make_async_copy(ffn_ref.at[1], wf.at[1], sem_w.at[2]),
    ]
    tiles = [
        pltpu.make_async_copy(x_ref.at[s, pl.ds(0, THIN)], xb.at[s], sem_x.at[s])
        for s in range(LOCAL)
    ]
    keys = [
        pltpu.make_async_copy(src.at[s], dst.at[s], sem_kv.at[2 * s + i])
        for s in range(LOCAL)
        for i, (src, dst) in enumerate(((k_ref, kb), (v_ref, vb)))
    ]
    for copy in tiles + loads[:1] + keys + loads[1:]:
        copy.start()
    pair_barrier(place)
    cot_swap = swap_halves(place, cot_ref, cot_other_ref, sem_cot)
    cot_swap.start()
    handed = remote(left, given, sem_memory.at[0], sem_memory.at[1], device(z, x, c, 1 - y))

    masks = head_masks()
    memory_row = lax.broadcasted_iota(jnp.int32, (THIN, 1), 0) < MEM
    first = table_ref[FIRST_MEMORY:NVEC, :]
    first = jnp.concatenate([first, jnp.zeros((THIN - MEM, D), F32)], axis=0)
    row = lambda r: table_ref[r : r + 1, :]

    def slots(turn, memory):
        for s in range(LOCAL):
            tiles[s].wait()
            if s == 0:
                loads[0].wait()
            keys[2 * s].wait()
            keys[2 * s + 1].wait()
            if memory is None:
                memory = first
            else:
                memory = jnp.where(place_ref[LOCAL * turn + s] == 0, first, memory)
            x16 = jnp.where(memory_row, memory, xb[s].astype(F32)).astype(BF16)
            xb[s] = x16
            qb[s] = ((nn(x16, wa[0]) + row(QUERY_BIAS)) * SCALE).astype(BF16)
            kb[s, 0:THIN] = nn(x16, wa[1]).astype(BF16)
            vb[s, 0:THIN] = (nn(x16, wa[2]) + row(VALUE_BIAS)).astype(BF16)
            outs = [
                pltpu.make_async_copy(
                    src.at[s, pl.ds(0, THIN)], dst.at[s, pl.ds(0, THIN)], sem_out.at[4 * s + i]
                )
                for i, (src, dst) in enumerate(
                    ((xb, x_ref), (qb, q_ref), (kb, k_ref), (vb, v_ref))
                )
            ]
            for copy in outs:
                copy.start()
            if turn == 1 and s == LOCAL - 1:
                save_d[s] = jnp.zeros_like(save_d[s])
                save_f[s] = jnp.zeros_like(save_f[s])
                save_s[s] = jnp.zeros_like(save_s[s])
            else:
                q_heads = by_head(qb[s], masks)
                score = nt(q_heads, kb[s])
                top = jnp.max(score, axis=-1, keepdims=True)
                weight = jnp.exp(score - top) * copies_of(score.shape)
                total = jnp.sum(weight, axis=-1, keepdims=True)
                share = (weight / total).astype(BF16)
                log_total = top + jnp.log(total)
                context = own_columns(nn(share, vb[s]), masks).astype(BF16)
                unit1, inverse1 = normalized(
                    x16.astype(F32) + nt(context, wa[3]) + row(OUT_BIAS)
                )
                hidden = (unit1 * row(GAIN1) + row(SHIFT1)).astype(BF16)
                if s == 0:
                    loads[1].wait()
                up = nt(hidden, wf[0])
                up_bias = jnp.concatenate([row(UP_BIAS + i) for i in range(FF // D)], axis=1)
                active16, slope = gelu_parts(up + up_bias)
                active16 = active16.astype(BF16)
                if s == 0:
                    loads[2].wait()
                second = hidden.astype(F32) + nn(active16, wf[1]) + row(DOWN_BIAS)
                unit2, inverse2 = normalized(second)
                output = (unit2 * row(GAIN2) + row(SHIFT2)).astype(BF16)
                memory = output.astype(F32)
                if turn == 0 and s == LOCAL - 1:
                    left[...] = output
                    handed.start()
                save_d[s, 0] = hidden
                save_d[s, 1] = unit1.astype(BF16)
                save_d[s, 2] = unit2.astype(BF16)
                save_d[s, 3] = context
                save_f[s, 0] = active16
                save_f[s, 1] = slope.astype(BF16)
                wide = lambda v: jnp.broadcast_to(v, (v.shape[0], 128))
                save_s[s, 0 : HEADS * THIN] = wide(log_total)
                save_s[s, HEADS * THIN : HEADS * THIN + THIN] = wide(inverse1)
                save_s[s, HEADS * THIN + THIN :] = wide(inverse2)
            for copy in outs:
                copy.wait()

    @pl.when(y == 0)
    def _():
        slots(0, None)
        handed.wait_send()

    @pl.when(y == 1)
    def _():
        handed.wait_recv()
        slots(1, given[...].astype(F32))

    saves = [
        pltpu.make_async_copy(save_d, saved_d_ref, sem_out.at[0]),
        pltpu.make_async_copy(save_f, saved_f_ref, sem_out.at[1]),
        pltpu.make_async_copy(save_s, saved_s_ref, sem_out.at[2]),
    ]
    for copy in saves:
        copy.start()
    for copy in saves:
        copy.wait()
    cot_swap.wait()


SAVED = (
    sds((LOCAL, 4, THIN, D), BF16),
    sds((LOCAL, 2, THIN, FF), BF16),
    sds((LOCAL, HEADS * THIN + 2 * THIN, 128), F32),
)


def chain(place, table, attn, ffn, x, q, k, v, cot):
    whole = sds((LOCAL, SEG, D), BF16)
    outs = pl.pallas_call(
        chain_kernel,
        in_specs=[SMEM, VMEM] + [ANY] * 7,
        out_specs=[ANY] * 8,
        out_shape=[whole] * 4 + list(SAVED) + [sds((LOCAL, *cot.shape[1:]), BF16)],
        input_output_aliases={4 + i: i for i in range(4)},
        scratch_shapes=[
            pltpu.VMEM((4, D, D), BF16),
            pltpu.VMEM((2, FF, D), BF16),
            pltpu.VMEM((LOCAL, THIN, D), BF16),
            pltpu.VMEM((LOCAL, THIN, D), BF16),
            pltpu.VMEM((LOCAL, SEG, D), BF16),
            pltpu.VMEM((LOCAL, SEG, D), BF16),
            *[pltpu.VMEM(s.shape, s.dtype) for s in SAVED],
            pltpu.VMEM((THIN, D), BF16),
            pltpu.VMEM((THIN, D), BF16),
            pltpu.SemaphoreType.DMA((3,)),
            pltpu.SemaphoreType.DMA((LOCAL,)),
            pltpu.SemaphoreType.DMA((2 * LOCAL,)),
            pltpu.SemaphoreType.DMA((4 * LOCAL,)),
            pltpu.SemaphoreType.DMA((2,)),
            pltpu.SemaphoreType.DMA((2,)),
        ],
        name="chain",
        compiler_params=params(collective_id=2, has_side_effects=True),
    )(place, table, attn, ffn, x, q, k, v, cot)
    return outs[:4], outs[4:7], outs[7]


def own_lanes(block, head):
    lane = lax.broadcasted_iota(jnp.int32, block.shape, 1)
    return jnp.where((lane < DH) == (head == 0), block, jnp.zeros_like(block))


def seen(score, first_query):
    key = lax.broadcasted_iota(jnp.int32, score.shape, 0)
    query = lax.broadcasted_iota(jnp.int32, score.shape, 1) + first_query
    return key <= query


def attend_pair(q, k, v):
    contexts_of, logs_of = [], [[], []]
    for part in range(SEG // TILE):
        rows = slice(TILE * part, TILE * (part + 1))
        keys = slice(0, TILE * (part + 1))
        contexts = []
        for head in range(2):
            score = nt(own_lanes(k[keys], head), q[rows])
            key = lax.broadcasted_iota(jnp.int32, score.shape, 0)
            allowed = seen(score, TILE * part) & (key >= MEM)
            score = jnp.where(allowed, score, MASK_VALUE)
            top = jnp.max(score, axis=0, keepdims=True)
            weight = jnp.exp(score - top)
            total = jnp.sum(weight, axis=0, keepdims=True)
            share = (weight * (1.0 / total)).astype(BF16)
            logs_of[head].append(top + jnp.log(total))
            contexts.append(tn(share, v[keys]))
        lane = lax.broadcasted_iota(jnp.int32, contexts[0].shape, 1)
        contexts_of.append(jnp.where(lane < DH, contexts[0], contexts[1]).astype(BF16))
    return jnp.concatenate(contexts_of, axis=0), [jnp.concatenate(l, axis=1) for l in logs_of]


def attend_kernel(q_ref, k_ref, v_ref, c_ref, log_ref):
    context, logs = attend_pair(q_ref[0], k_ref[0], v_ref[0])
    c_ref[0] = context
    for head in range(2):
        log_ref[0, 0, head : head + 1] = logs[head]


def with_memory(q, k16, v16, context, log_tokens):
    masks = head_masks()
    score = nt(by_head(k16, masks), q).reshape(HEADS, THIN, SEG)
    key = lax.broadcasted_iota(jnp.int32, score.shape, 1)
    score = jnp.where(key < MEM, score, MASK_VALUE)
    top = jnp.maximum(jnp.max(score, axis=1), log_tokens)
    weight = jnp.exp(score - top[:, None])
    old = jnp.exp(log_tokens - top)
    total = jnp.sum(weight, axis=1) + old
    share = (weight * (1.0 / total)[:, None]).reshape(HEADS * THIN, SEG).astype(BF16)
    kept = old / total
    coarse = kept.astype(BF16)
    fine = (kept - coarse.astype(F32)).astype(BF16)
    pad = jnp.zeros((4, SEG), BF16)
    head = lax.rem(lax.broadcasted_iota(jnp.int32, (2 * THIN, D), 0), THIN)
    spread = jnp.where(head == lax.broadcasted_iota(jnp.int32, (2 * THIN, D), 1) // DH, 1.0, 0.0)
    factor = tn(jnp.concatenate([coarse, pad, fine, pad], axis=0), spread.astype(BF16))
    context = factor * context.astype(F32) + tn(share, by_head(v16, masks))
    return context.astype(BF16), top + jnp.log(total)


PAIR = pl.BlockSpec((1, SEG, 2 * DH), lambda s, h: (s, 0, h))
PAIR_LOG = pl.BlockSpec((1, 1, 2, SEG), lambda s, h: (s, h, 0, 0))


def attend(q, k, v):
    return pl.pallas_call(
        attend_kernel,
        grid=(LOCAL, HEADS // 2),
        in_specs=[PAIR] * 3,
        out_specs=[PAIR, PAIR_LOG],
        out_shape=[sds((LOCAL, SEG, D), BF16), sds((LOCAL, HEADS // 2, 2, SEG), F32)],
        name="attend",
        compiler_params=params(),
    )(q, k, v)


def attend_back_kernel(q_ref, k_ref, v_ref, dc_ref, log_ref, dq_ref, dk_ref, dv_ref):
    last = SEG // TILE
    key_terms, value_terms = [], []
    for head in range(2):
        key_sum, value_sum = [], []
        query_parts = []
        for part in range(last):
            rows = slice(TILE * part, TILE * (part + 1))
            keys = slice(0, TILE * (part + 1))
            q, dc = q_ref[0, rows], dc_ref[0, rows]
            k = k_ref[0, keys]
            score = nt(own_lanes(k, head), q)
            share = jnp.exp(score - log_ref[0, 0, head : head + 1, rows])
            share = jnp.where(seen(score, TILE * part), share, 0.0)
            share_grad = nt(own_lanes(v_ref[0, keys], head), dc)
            inner = jnp.sum(share_grad * share, axis=0, keepdims=True)
            score_grad = (share * (share_grad - inner)).astype(BF16)
            value_sum.append(nn(share.astype(BF16), dc))
            key_sum.append(nn(score_grad, q))
            query_parts.append(tn(score_grad, k))
        key_terms.append(key_sum)
        value_terms.append(value_sum)
        if head == 0:
            first_queries = query_parts
    for part in range(last):
        rows = slice(TILE * part, TILE * (part + 1))
        lane = lax.broadcasted_iota(jnp.int32, (TILE, 2 * DH), 1)
        pick = lambda a, b: jnp.where(lane < DH, a, b)
        dq_ref[0, rows] = (pick(first_queries[part], query_parts[part]) * SCALE).astype(BF16)
        for terms, out in ((key_terms, dk_ref), (value_terms, dv_ref)):
            total = None
            for later in range(part, last):
                term = pick(terms[0][later][rows], terms[1][later][rows])
                total = term if total is None else total + term
            out[0, rows] = total.astype(BF16)


def attend_back(q, k, v, dc, log_total):
    return pl.pallas_call(
        attend_back_kernel,
        grid=(LOCAL, HEADS // 2),
        in_specs=[PAIR] * 4 + [PAIR_LOG],
        out_specs=[PAIR] * 3,
        out_shape=[sds((LOCAL, SEG, D), BF16)] * 3,
        name="attend_back",
        compiler_params=params(),
    )(q, k, v, dc, log_total)


def rows_kernel(
    place_ref,
    x_ref,
    q_ref,
    k16_ref,
    v16_ref,
    tokens_c_ref,
    tokens_log_ref,
    mine_ref,
    other_ref,
    wo_ref,
    wf_ref,
    table_ref,
    keep_ref,
    send_ref,
    h_ref,
    g_ref,
    du_ref,
    df_ref,
    da_ref,
    dc_ref,
    c_ref,
    log_ref,
    sums_ref,
    slope_ref,
):
    row = lambda r: table_ref[r : r + 1, :]
    slot = pl.program_id(0)
    side = lax.axis_index("tensor")
    live = place_ref[LOCAL * side + slot] >= 0

    @pl.when(slot == 0)
    def _():
        sums_ref[...] = jnp.zeros_like(sums_ref)

    def add(r, value):
        sums_ref[r : r + 1, :] += value

    log_tokens = jnp.concatenate([tokens_log_ref[0, h] for h in range(HEADS // 2)], axis=0)
    context, log_total = with_memory(
        q_ref[0], k16_ref[0], v16_ref[0], tokens_c_ref[0], log_tokens
    )
    c_ref[0] = context
    for h in range(HEADS // 2):
        log_ref[0, h] = log_total[2 * h : 2 * h + 2]
    unit1, inverse1 = normalized(x_ref[0].astype(F32) + nt(context, wo_ref[0]) + row(OUT_BIAS))
    hidden = (unit1 * row(GAIN1) + row(SHIFT1)).astype(BF16)
    h_ref[0] = hidden
    second = hidden.astype(F32) + row(DOWN_BIAS)
    for i in range(FF // D):
        cols = slice(D * i, D * (i + 1))
        up = nt(hidden, wf_ref[0, cols]) + row(UP_BIAS + i)
        active, slope = gelu_parts(up)
        active = active.astype(BF16)
        g_ref[0, :, cols] = active
        slope_ref[:, cols] = slope.astype(BF16)
        second = second + nn(active, wf_ref[1, cols])
    unit2, inverse2 = normalized(second)
    output = jnp.where(live, unit2 * row(GAIN2) + row(SHIFT2), 0.0)
    keep, send = split_rows(side, output)
    keep_ref[0] = keep.astype(BF16)
    send_ref[0] = send.astype(BF16)

    grad = whole_rows(side, mine_ref[LOCAL * side + slot], other_ref[0])
    grad = jnp.where(live, grad, 0.0)
    add(GAIN2, row_sum(grad * unit2))
    add(SHIFT2, row_sum(grad))
    second_grad = normalized_back(grad * row(GAIN2), unit2, inverse2)
    down_grad = second_grad.astype(BF16)
    df_ref[0] = down_grad
    add(DOWN_BIAS, row_sum(down_grad.astype(F32)))
    hidden_grad = second_grad
    for i in range(FF // D):
        cols = slice(D * i, D * (i + 1))
        up_grad = (nt(down_grad, wf_ref[1, cols]) * slope_ref[:, cols].astype(F32)).astype(BF16)
        du_ref[0, :, cols] = up_grad
        add(UP_BIAS + i, row_sum(up_grad.astype(F32)))
        hidden_grad = hidden_grad + nn(up_grad, wf_ref[0, cols])
    add(GAIN1, row_sum(hidden_grad * unit1))
    add(SHIFT1, row_sum(hidden_grad))
    branch_grad = normalized_back(hidden_grad * row(GAIN1), unit1, inverse1).astype(BF16)
    da_ref[0] = branch_grad
    add(OUT_BIAS, row_sum(branch_grad.astype(F32)))
    dc_ref[0] = nn(branch_grad, wo_ref[0]).astype(BF16)


def rows_part(place, x, q, k, v, c, log_tokens, cot, other, attn, ffn, table):
    half = cot.shape[1]
    whole, whole_wide = sds((LOCAL, SEG, D), BF16), sds((LOCAL, SEG, FF), BF16)
    part, logs = sds((LOCAL, half, D), BF16), sds((LOCAL, HEADS // 2, 2, SEG), F32)
    rows, wide = slot_rows(), slot_rows(FF)
    thin = pl.BlockSpec((1, THIN, D), lambda s: (s, 0, 0))
    log_rows = pl.BlockSpec((1, HEADS // 2, 2, SEG), lambda s: (s, 0, 0, 0))
    return pl.pallas_call(
        rows_kernel,
        grid=(LOCAL,),
        in_specs=[SMEM, rows, rows, thin, thin, rows, log_rows]
        + [once(cot.shape, (0, 0, 0)), half_rows(half)]
        + [once((1, D, D), (3, 0, 0)), once((2, FF, D), (0, 0, 0)), once((NVEC, D), (0, 0))],
        out_specs=[half_rows(half)] * 2
        + [rows, wide, wide, rows, rows, rows, rows, log_rows, once((THIN, D), (0, 0))],
        out_shape=[part] * 2
        + [whole, whole_wide, whole_wide, whole, whole, whole, whole, logs, sds((THIN, D), F32)],
        scratch_shapes=[pltpu.VMEM((SEG, FF), BF16)],
        name="rows_part",
        compiler_params=params(),
    )(place, x, q, k, v, c, log_tokens, cot, other, attn, ffn, table)


CHUNK = 768


def chain_back_kernel(
    place_ref,
    table_ref,
    attn_ref,
    ffn_ref,
    q_ref,
    k_ref,
    v_ref,
    saved_d_ref,
    saved_f_ref,
    saved_s_ref,
    g_ref,
    du_ref,
    df_ref,
    h_ref,
    send_ref,
    dk_in,
    dv_in,
    da_in,
    dq_in,
    c_in,
    dk_ref,
    dv_ref,
    da_ref,
    dq_ref,
    c_ref,
    thin_d_ref,
    thin_f_ref,
    sums_ref,
    terms_ref,
    received_ref,
    wa,
    wf,
    qb,
    kb,
    vb,
    dkb,
    dvb,
    tiles,
    df,
    hid,
    gb,
    dub,
    staged,
    save_d,
    save_f,
    save_s,
    thin_d,
    thin_f,
    sums,
    left,
    given,
    sem_w,
    sem_in,
    sem_ff,
    sem_chunk,
    sem_out,
    sem_stage,
    sem_grad,
    sem_swap,
):
    del dk_in, dv_in, da_in, dq_in, c_in
    place = z, x, c, y = my_place()
    loads = [
        pltpu.make_async_copy(attn_ref, wa, sem_w.at[0]),
        pltpu.make_async_copy(ffn_ref.at[0], wf.at[0], sem_w.at[1]),
        pltpu.make_async_copy(ffn_ref.at[1], wf.at[1], sem_w.at[2]),
    ]
    first_rows = lambda ref: ref.at[:, pl.ds(0, THIN)]
    grads = [
        pltpu.make_async_copy(dk_ref, dkb, sem_in.at[0]),
        pltpu.make_async_copy(dv_ref, dvb, sem_in.at[1]),
    ]
    saved = [
        pltpu.make_async_copy(saved_d_ref, save_d, sem_in.at[2]),
        pltpu.make_async_copy(saved_f_ref, save_f, sem_in.at[3]),
        pltpu.make_async_copy(saved_s_ref, save_s, sem_in.at[4]),
    ]
    reads = [
        pltpu.make_async_copy(first_rows(q_ref), qb, sem_in.at[5]),
        pltpu.make_async_copy(k_ref, kb, sem_in.at[6]),
        pltpu.make_async_copy(v_ref, vb, sem_in.at[7]),
    ]
    merged = (da_ref, dq_ref, c_ref)
    tile_reads = [
        pltpu.make_async_copy(first_rows(ref), tiles.at[i], sem_in.at[8 + i])
        for i, ref in enumerate(merged)
    ]
    rows_in = [
        pltpu.make_async_copy(df_ref, df, sem_ff.at[0]),
        pltpu.make_async_copy(h_ref, hid, sem_ff.at[1]),
    ]

    def chunk_reads(i):
        lanes = pl.ds(CHUNK * i, CHUNK)
        return [
            pltpu.make_async_copy(src.at[:, :, lanes], dst.at[i % 2], sem_chunk.at[i % 2, j])
            for j, (src, dst) in enumerate(((g_ref, gb), (du_ref, dub)))
        ]

    @pl.when(y == 1)
    def _():
        for copy in grads + loads[:1] + saved + loads[:0:-1] + reads + tile_reads:
            copy.start()
        for copy in rows_in + chunk_reads(0) + chunk_reads(1):
            copy.start()

    @pl.when(y == 0)
    def _():
        for copy in rows_in + chunk_reads(0) + chunk_reads(1):
            copy.start()
        for copy in grads + loads[:1] + saved + loads[:0:-1] + reads + tile_reads:
            copy.start()

    pair_barrier(place)
    swap = remote(
        send_ref, received_ref, sem_swap.at[0], sem_swap.at[1], device(z, x, c, 1 - y)
    )
    swap.start()
    handed = remote(left, given, sem_grad.at[0], sem_grad.at[1], device(z, x, c, 1 - y))

    sums[...] = jnp.zeros_like(sums)
    thin_d[...] = jnp.zeros_like(thin_d)
    thin_f[...] = jnp.zeros_like(thin_f)
    masks = head_masks()
    memory_row = lax.broadcasted_iota(jnp.int32, (THIN, 1), 0) < MEM
    row = lambda r: table_ref[r : r + 1, :]

    def add(r, value):
        sums[r : r + 1, :] += value

    def slots(turn, grad):
        waited = set()

        def need(*copies):
            for copy in copies:
                if id(copy) not in waited:
                    waited.add(id(copy))
                    copy.wait()

        for s in reversed(range(LOCAL)):
            if turn == 1 and s == LOCAL - 1:
                grad = jnp.zeros((THIN, D), F32)
            else:
                after = place_ref[LOCAL * turn + s + 1]
                grad = jnp.where(memory_row, jnp.where(after > 0, grad, 0.0), 0.0)
                need(*saved)
                unit1, unit2 = save_d[s, 1].astype(F32), save_d[s, 2].astype(F32)
                base = HEADS * THIN
                log_total = save_s[s, 0:base, 0:1]
                inverse1 = save_s[s, base : base + THIN, 0:1]
                inverse2 = save_s[s, base + THIN :, 0:1]
                add(GAIN2, row_sum(grad * unit2))
                add(SHIFT2, row_sum(grad))
                second_grad = normalized_back(grad * row(GAIN2), unit2, inverse2)
                down_grad = second_grad.astype(BF16)
                add(DOWN_BIAS, row_sum(down_grad.astype(F32)))
                need(loads[2])
                up_grad = (nt(down_grad, wf[1]) * save_f[s, 1].astype(F32)).astype(BF16)
                up_sum = row_sum(up_grad.astype(F32))
                for i in range(FF // D):
                    add(UP_BIAS + i, up_sum[:, D * i : D * (i + 1)])
                need(loads[1])
                hidden_grad = second_grad + nn(up_grad, wf[0])
                add(GAIN1, row_sum(hidden_grad * unit1))
                add(SHIFT1, row_sum(hidden_grad))
                pre_grad = normalized_back(hidden_grad * row(GAIN1), unit1, inverse1)
                branch_grad = pre_grad.astype(BF16)
                add(OUT_BIAS, row_sum(branch_grad.astype(F32)))
                need(loads[0])
                context_grad = nn(branch_grad, wa[3]).astype(BF16)
                dc_heads = by_head(context_grad, masks)
                need(*reads)
                q_heads = by_head(qb[s], masks)
                score = nt(q_heads, kb[s])
                share = jnp.exp(score - log_total) * copies_of(score.shape)
                share_grad = nt(dc_heads, vb[s])
                inner = jnp.sum(share_grad * share, axis=-1, keepdims=True)
                score_grad = (share * (share_grad - inner)).astype(BF16)
                query_grad = (own_columns(nn(score_grad, kb[s]), masks) * SCALE).astype(BF16)
                need(*grads)
                dkb[s] = (dkb[s].astype(F32) + tn(score_grad, q_heads)).astype(BF16)
                dvb[s] = (dvb[s].astype(F32) + tn(share.astype(BF16), dc_heads)).astype(BF16)
                thin_d[s, 0] = down_grad
                thin_d[s, 1] = save_d[s, 0]
                thin_f[s, 0] = up_grad
                thin_f[s, 1] = save_f[s, 0]
                need(*tile_reads)
                for i, value in enumerate((branch_grad, query_grad, save_d[s, 3])):
                    tiles[i, s] = jnp.where(memory_row, value, tiles[i, s])
                grad = pre_grad + nt(query_grad, wa[0])
            need(loads[0], *grads)
            grad = grad + nt(dkb[s, 0:THIN], wa[1]) + nt(dvb[s, 0:THIN], wa[2])
            first = jnp.where(place_ref[LOCAL * turn + s] == 0, grad, 0.0)
            sums[FIRST_MEMORY : FIRST_MEMORY + THIN, :] += first
        return grad

    @pl.when(y == 1)
    def _():
        left[...] = slots(1, None)
        handed.start()

    for copy in rows_in:
        copy.wait()
    for s in range(LOCAL):
        df[s, 0:THIN] = jnp.where(memory_row, thin_d[s, 0], df[s, 0:THIN])
        hid[s, 0:THIN] = jnp.where(memory_row, thin_d[s, 1], hid[s, 0:THIN])
    chunks = FF // CHUNK
    stores = [
        pltpu.make_async_copy(
            staged.at[i % 2], terms_ref.at[:, pl.ds(CHUNK * i, CHUNK)], sem_stage.at[i % 2]
        )
        for i in range(chunks)
    ]
    for i in range(chunks):
        for copy in chunk_reads(i):
            copy.wait()
        lanes = slice(CHUNK * i, CHUNK * (i + 1))
        for s in range(LOCAL):
            for j, buf in ((1, gb), (0, dub)):
                old = buf[i % 2, s, 0:THIN]
                buf[i % 2, s, 0:THIN] = jnp.where(memory_row, thin_f[s, j, :, lanes], old)
        if i >= 2:
            stores[i - 2].wait()
        for j, (buf, rows) in enumerate(((dub, hid), (gb, df))):
            terms = tn(
                buf[i % 2].reshape(LOCAL * SEG, CHUNK), rows[...].reshape(LOCAL * SEG, D)
            )
            staged[i % 2, j] = terms.astype(BF16)
        stores[i].start()
        if i + 2 < chunks:
            for copy in chunk_reads(i + 2):
                copy.start()

    @pl.when(y == 0)
    def _():
        handed.wait_recv()
        slots(0, given[...])

    @pl.when(y == 1)
    def _():
        handed.wait_send()

    writes = [
        pltpu.make_async_copy(dkb, dk_ref, sem_out.at[0]),
        pltpu.make_async_copy(dvb, dv_ref, sem_out.at[1]),
        pltpu.make_async_copy(thin_d, thin_d_ref, sem_out.at[2]),
        pltpu.make_async_copy(thin_f, thin_f_ref, sem_out.at[3]),
        pltpu.make_async_copy(sums, sums_ref, sem_out.at[4]),
        *[
            pltpu.make_async_copy(tiles.at[i], first_rows(ref), sem_out.at[5 + i])
            for i, ref in enumerate(merged)
        ],
    ]
    for copy in writes:
        copy.start()
    for copy in writes + stores[-2:]:
        copy.wait()
    swap.wait()


THIN_SHAPES = (
    sds((LOCAL, 2, THIN, D), BF16),
    sds((LOCAL, 2, THIN, FF), BF16),
    sds((FIRST_MEMORY + THIN, D), F32),
)


def chain_back(place, table, attn, ffn, q, k, v, saved, g, du, df, h, send, dk, dv, da, dq, c):
    whole = sds((LOCAL, SEG, D), BF16)
    rows = pltpu.VMEM(whole.shape, BF16)
    tile = pltpu.VMEM((LOCAL, THIN, D), BF16)
    dma = lambda *shape: pltpu.SemaphoreType.DMA(shape)
    outs = pl.pallas_call(
        chain_back_kernel,
        in_specs=[SMEM, VMEM] + [ANY] * 18,
        out_specs=[ANY] * 10,
        out_shape=[whole] * 5
        + list(THIN_SHAPES)
        + [sds((2, FF, D), BF16), sds(send.shape, BF16)],
        input_output_aliases={15 + i: i for i in range(5)},
        scratch_shapes=[
            pltpu.VMEM((4, D, D), BF16),
            pltpu.VMEM((2, FF, D), BF16),
            tile,
            rows,
            rows,
            rows,
            rows,
            pltpu.VMEM((3, LOCAL, THIN, D), BF16),
            rows,
            rows,
            pltpu.VMEM((2, LOCAL, SEG, CHUNK), BF16),
            pltpu.VMEM((2, LOCAL, SEG, CHUNK), BF16),
            pltpu.VMEM((2, 2, CHUNK, D), BF16),
            *[pltpu.VMEM(s.shape, s.dtype) for s in SAVED + THIN_SHAPES],
            pltpu.VMEM((THIN, D), F32),
            pltpu.VMEM((THIN, D), F32),
            dma(3),
            dma(11),
            dma(2),
            dma(2, 2),
            dma(8),
            dma(2),
            dma(2),
            dma(2),
        ],
        name="chain_back",
        compiler_params=params(collective_id=3, has_side_effects=True),
    )(place, table, attn, ffn, q, k, v, *saved, g, du, df, h, send, dk, dv, da, dq, c)
    return outs[:5], outs[5:8], outs[8], outs[9]


def table_row(ref, index, entries):
    blocks = []
    lane = lax.broadcasted_iota(jnp.int32, (1, 128), 1)
    for block in range(D // 128):
        at, end = index * D + 128 * block, index * D + 128 * (block + 1)
        target, value = 0, jnp.zeros((1, 128), F32)
        while at < end:
            shard, inner = at // entries, at % entries
            count = min(end - at, entries - inner, 128 - inner % 128)
            place = (shard // 8, shard // 4 % 2, shard // 2 % 2, shard % 2)
            source = ref[place][inner // 128 : inner // 128 + 1]
            shift = (target - inner) % 128
            if shift:
                source = pltpu.roll(source, shift, 1)
            value = jnp.where((lane >= target) & (lane < target + count), source, value)
            at, target = at + count, target + count
        blocks.append(value)
    return jnp.concatenate(blocks, axis=1)


def head_kernel(
    nz,
    entries,
    attn_src,
    ffn_src,
    vec_src,
    tokens,
    attn_ref,
    ffn_ref,
    vec_ref,
    x_ref,
    q_ref,
    k_ref,
    v_ref,
    c_ref,
    log_ref,
    wa,
    vec,
    mine,
    other,
    xb,
    qb,
    kb,
    vb,
    cb,
    logs,
    send_sem,
    recv_sem,
    own_sem,
    swap_sem,
    out_sem,
):
    place = my_place()
    side = place[3]
    halves = swap_halves(place, tokens, other, swap_sem)
    own = [
        pltpu.make_async_copy(attn_src, attn_view(wa, *place), own_sem.at[0]),
        pltpu.make_async_copy(vec_src, vec_view(vec, *place), own_sem.at[1]),
        pltpu.make_async_copy(ffn_src, ffn_view(ffn_ref, *place), own_sem.at[2]),
        pltpu.make_async_copy(tokens.at[pl.ds(LOCAL * side, LOCAL)], mine, own_sem.at[3]),
    ]
    for copy in own:
        copy.start()
    entry_barrier(nz)
    steps = functools.partial(gather_steps, nz, place, send_sem=send_sem, recv_sem=recv_sem)
    begin, step, end_arrive, end_send = steps(
        1, True, [(0, wa, attn_view), (1, vec, vec_view)]
    )
    late = [
        steps(place[2], bool(i), [(2 + i, ffn_ref.at[i], hidden_view)]) for i in range(2)
    ]
    own[0].wait()
    own[1].wait()
    begin()
    halves.start()

    def loop(t, carry):
        step(t)
        return carry

    lax.fori_loop(1, nz + 2, loop, 0)
    own[2].wait()
    for begin2, _, _, _ in late:
        begin2()
    own[3].wait()
    halves.wait()
    end_arrive()
    outs = [
        pltpu.make_async_copy(wa, attn_ref, out_sem.at[0]),
        pltpu.make_async_copy(vec, vec_ref, out_sem.at[1]),
    ]
    for copy in outs:
        copy.start()

    weight = lambda i: wa[i].reshape(D, D)

    def project_slot(s):
        x = whole_rows(side, mine[s], other[s]).astype(BF16)
        xb[s] = x
        qb[s] = ((nn(x, weight(0)) + table_row(vec, QUERY_BIAS, entries)) * SCALE).astype(BF16)
        kb[s] = nn(x, weight(1)).astype(BF16)
        vb[s] = (nn(x, weight(2)) + table_row(vec, VALUE_BIAS, entries)).astype(BF16)
        for i, (buf, out) in enumerate(((xb, x_ref), (qb, q_ref), (kb, k_ref), (vb, v_ref))):
            outs.append(pltpu.make_async_copy(buf.at[s], out.at[s], out_sem.at[2 + 4 * s + i]))
            outs[-1].start()

    def attend_at(i, carry):
        s, h = i // (HEADS // 2), i % (HEADS // 2)
        lanes = pl.ds(pl.multiple_of(h * 2 * DH, 2 * DH), 2 * DH)
        context, log_rows = attend_pair(qb[s, :, lanes], kb[s, :, lanes], vb[s, :, lanes])
        cb[s, :, lanes] = context
        for head in range(2):
            logs[s, h, head : head + 1] = log_rows[head]
        return carry

    project_slot(0)
    project_slot(1)
    pairs = LOCAL * HEADS // 2
    done = 0
    for t in range(1, nz + 2):
        for _, step2, _, _ in late:
            step2(t)
        upto = pairs * t // (nz + 1)
        lax.fori_loop(done, upto, attend_at, 0)
        done = upto
    outs.append(pltpu.make_async_copy(cb, c_ref, out_sem.at[2 + 4 * LOCAL]))
    outs.append(pltpu.make_async_copy(logs, log_ref, out_sem.at[3 + 4 * LOCAL]))
    outs[-1].start()
    outs[-2].start()
    end_send()
    for _, _, end_arrive2, end_send2 in late:
        end_send2()
        end_arrive2()
    for copy in outs:
        copy.wait()


def head(nz, attention, hidden_major, vec, tokens, entries):
    rows, hidden = attention.shape[1], hidden_major.shape[1]
    whole = sds((LOCAL, SEG, D), BF16)
    logs = (LOCAL, HEADS // 2, 2, SEG)
    attn_shape, vec_shape = (4, nz, 2, 2, rows, D), (nz, 2, 2, 2, *VEC_TILE)
    half = pltpu.VMEM((LOCAL, *tokens.shape[1:]), BF16)
    return pl.pallas_call(
        functools.partial(head_kernel, nz, entries),
        in_specs=[ANY] * 4,
        out_specs=[ANY] * 9,
        out_shape=[
            sds(attn_shape, BF16),
            sds((2, nz, 2, 2, 2, hidden, D), BF16),
            sds(vec_shape, F32),
            *[whole] * 5,
            sds(logs, F32),
        ],
        scratch_shapes=[
            pltpu.VMEM(attn_shape, BF16),
            pltpu.VMEM(vec_shape, F32),
            half,
            half,
            *[pltpu.VMEM(whole.shape, BF16)] * 5,
            pltpu.VMEM(logs, F32),
            pltpu.SemaphoreType.DMA((11, nz, 4)),
            pltpu.SemaphoreType.DMA((8, nz, 4)),
            pltpu.SemaphoreType.DMA((4,)),
            pltpu.SemaphoreType.DMA((2,)),
            pltpu.SemaphoreType.DMA((4 + 4 * LOCAL,)),
        ],
        name="head",
        compiler_params=params(collective_id=0, has_side_effects=True),
    )(attention, hidden_major, vec, tokens)


def token_grad_kernel(place_ref, da_ref, dq_ref, dk_ref, dv_ref, w_ref, keep_ref, send_ref):
    side = lax.axis_index("tensor")
    total = da_ref[0].astype(F32)
    for i, ref in enumerate((dq_ref, dk_ref, dv_ref)):
        total = total + nt(ref[0], w_ref[i])
    live = place_ref[LOCAL * side + pl.program_id(0)] >= 0
    keep, send = split_rows(side, jnp.where(live, total, 0.0))
    keep_ref[0] = keep.astype(BF16)
    send_ref[0] = send.astype(BF16)


def token_gradient(place, da, dq, dk, dv, attn):
    half = (SEG - MEM) // 2
    return pl.pallas_call(
        token_grad_kernel,
        grid=(LOCAL,),
        in_specs=[SMEM] + [slot_rows()] * 4 + [once((3, D, D), (0, 0, 0))],
        out_specs=[half_rows(half)] * 2,
        out_shape=[sds((LOCAL, half, D), BF16)] * 2,
        name="token_gradient",
        compiler_params=params(),
    )(place, da, dq, dk, dv, attn)


def flat(ref):
    return ref[...].reshape(LOCAL * ref.shape[1], ref.shape[2])


def attn_grad_kernel(
    x_ref, da_ref, dq_ref, dk_ref, dv_ref, c_ref, sums_ref, thin_sums_ref, out_ref, vec_ref
):
    x = flat(x_ref)
    dq, dv = flat(dq_ref), flat(dv_ref)
    out_ref[0] = tn(x, dq).astype(BF16)
    out_ref[1] = tn(x, flat(dk_ref)).astype(BF16)
    out_ref[2] = tn(x, dv).astype(BF16)
    out_ref[3] = tn(flat(da_ref), flat(c_ref)).astype(BF16)
    vec_ref[...] = thin_sums_ref[...]
    vec_ref[0:FIRST_MEMORY] = thin_sums_ref[0:FIRST_MEMORY] + sums_ref[0:FIRST_MEMORY]
    vec_ref[QUERY_BIAS : QUERY_BIAS + 1] = row_sum(dq.astype(F32))
    vec_ref[VALUE_BIAS : VALUE_BIAS + 1] = row_sum(dv.astype(F32))


def attn_gradient(x, da, dq, dk, dv, c, sums, thin_sums, chunk=256):
    part = pl.BlockSpec((LOCAL, SEG, chunk), lambda i: (0, 0, i))
    full = once((LOCAL, SEG, D), (0, 0, 0))
    lanes = lambda rows: pl.BlockSpec((rows, chunk), lambda i: (0, i))
    return pl.pallas_call(
        attn_grad_kernel,
        grid=(D // chunk,),
        in_specs=[full, full, part, part, part, part, lanes(THIN), lanes(FIRST_MEMORY + THIN)],
        out_specs=[
            pl.BlockSpec((4, D, chunk), lambda i: (0, 0, i)),
            lanes(FIRST_MEMORY + THIN),
        ],
        out_shape=[sds((4, D, D), BF16), sds((FIRST_MEMORY + THIN, D), F32)],
        name="attn_gradient",
        compiler_params=params(),
    )(x, da, dq, dk, dv, c, sums, thin_sums)


def add_thin_kernel(thin_f_ref, thin_d_ref, terms_ref, out_ref):
    out_ref[...] = terms_ref[...]

    @pl.when(lax.axis_index("tensor") == 0)
    def _():
        for j, (a, b) in enumerate(((0, 1), (1, 0))):
            left = jnp.concatenate([thin_f_ref[s, a] for s in range(LOCAL)], axis=0)
            right = jnp.concatenate([thin_d_ref[s, b] for s in range(LOCAL)], axis=0)
            out_ref[j] = (terms_ref[j].astype(F32) + tn(left, right)).astype(BF16)


def add_thin(terms, thin_d, thin_f):
    block = pl.BlockSpec((2, CHUNK, D), lambda i: (0, i, 0))
    return pl.pallas_call(
        add_thin_kernel,
        grid=(FF // CHUNK,),
        in_specs=[
            pl.BlockSpec((LOCAL, 2, THIN, CHUNK), lambda i: (0, 0, 0, i)),
            once(thin_d.shape, (0, 0, 0, 0)),
            block,
        ],
        out_specs=block,
        out_shape=sds((2, FF, D), BF16),
        name="add_thin",
        compiler_params=params(),
    )(thin_f, thin_d, terms)


def update(gradient, momentum, weight, average, rate, grad_scale):
    scaled = gradient * grad_scale
    moment = MOMENTUM * momentum + scaled
    weight_new = weight - rate * (scaled + MOMENTUM * moment)
    return (moment, weight_new, AVERAGE_DECAY * average + (1.0 - AVERAGE_DECAY) * weight_new)


VEC_TILE = (8, 128)


def in_tiles(rows):
    size = VEC_TILE[0] * VEC_TILE[1]
    padded = jnp.pad(rows, [(0, 0)] * (rows.ndim - 1) + [(0, size - rows.shape[-1])])
    return padded.reshape(*rows.shape[:-1], *VEC_TILE)


def start(attention, feedforward, vectors, tokens):
    nz = lax.axis_size("dp") // 4
    rows, hidden, entries = attention.shape[1], feedforward.shape[2], vectors.shape[0]
    attention = attention.astype(BF16)
    hidden_major = jnp.swapaxes(feedforward.astype(BF16), 1, 2)
    vec = in_tiles(vectors.astype(BF16).astype(F32))
    aligned = rows % THIN == 0
    if aligned:
        attn, ffn, table, *work = head(nz, attention, hidden_major, vec, tokens, entries)
    else:
        attn, ffn, table, other = gather(
            nz,
            0,
            [
                (attention, (4, nz, 2, 2, rows, D), attn_view),
                (hidden_major, (2, nz, 2, 2, 2, hidden, D), ffn_view),
                (vec, (nz, 2, 2, 2, *VEC_TILE), vec_view),
            ],
            tokens,
        )
    attn, ffn = attn.reshape(4, D, D), ffn.reshape(2, FF, D)
    table = table.reshape(nz * 8, VEC_TILE[0] * VEC_TILE[1])[:, :entries].reshape(NVEC, D)
    if not aligned:
        work = project(tokens, other, attn, table)
        work = [*work, *attend(*work[1:])]
    return attn, ffn, table, work


def scatter_gradients(attn_terms, ffn_terms, vec_terms, shapes):
    nz = lax.axis_size("dp") // 4
    rows, hidden, entries = shapes
    attn, ffn, vec = scatter(
        nz,
        1,
        [
            (attn_terms.reshape(4, nz, 2, 2, rows, D), (4, rows, HALF), attn_view),
            (ffn_terms.reshape(2, nz, 2, 2, 2, hidden, D), (2, hidden, D), ffn_view),
            (in_tiles(vec_terms.reshape(nz, 2, 2, 2, entries)), VEC_TILE, vec_view),
        ],
    )
    return attn.astype(F32), jnp.swapaxes(ffn, 1, 2).astype(F32), vec.reshape(-1)[:entries]


def swap(value):
    return lax.ppermute(value, "tensor", [(0, 1), (1, 0)])


def joined_kernel(keep_ref, other_ref, out_ref, sem):
    side = lax.axis_index("tensor")
    copies = [
        pltpu.make_async_copy(keep_ref, out_ref.at[pl.ds(LOCAL * side, LOCAL)], sem.at[0]),
        pltpu.make_async_copy(other_ref, out_ref.at[pl.ds(LOCAL * (1 - side), LOCAL)], sem.at[1]),
    ]
    for c in copies:
        c.start()
    for c in copies:
        c.wait()


def joined(keep, other):
    return pl.pallas_call(
        joined_kernel,
        in_specs=[ANY] * 2,
        out_specs=ANY,
        out_shape=sds((2 * LOCAL, *keep.shape[1:]), keep.dtype),
        scratch_shapes=[pltpu.SemaphoreType.DMA((2,))],
        name="joined",
        compiler_params=params(16),
    )(keep, other)


def on_device(
    tokens,
    slot_position,
    cotangent,
    attention,
    feedforward,
    vectors,
    attn_momentum,
    ffn_momentum,
    vec_momentum,
    attn_average,
    ffn_average,
    vec_average,
):
    place = slot_position
    attn, ffn, table, work = start(attention, feedforward, vectors, tokens)
    x, q, k, v, c, log_tokens = work

    (x, q, k, v), saved, cot_other = chain(place, table, attn, ffn, x, q, k, v, cotangent)
    keep, send, h, g, du, df, da, dc, c, log_total, sums = rows_part(
        place, x, q, k, v, c, log_tokens, cotangent, cot_other, attn, ffn, table
    )
    dq, dk, dv = attend_back(q, k, v, dc, log_total)
    (dk, dv, da, dq, c), thin, ffn_terms, received = chain_back(
        place, table, attn, ffn, q, k, v, saved, g, du, df, h, send, dk, dv, da, dq, c
    )
    thin_d, thin_f, thin_sums = thin
    activations = joined(keep, received)

    keep, send = token_gradient(place, da, dq, dk, dv, attn)
    token_grad = joined(keep, swap(send))
    ffn_terms = add_thin(ffn_terms, thin_d, thin_f)
    attn_terms, vec_terms = attn_gradient(x, da, dq, dk, dv, c, sums, thin_sums)
    vec_terms = vec_terms[:NVEC]

    attn_grad, ffn_grad, vec_grad = scatter_gradients(
        attn_terms,
        ffn_terms,
        vec_terms,
        (attention.shape[1], feedforward.shape[2], vectors.shape[0]),
    )
    grad_scale = 1.0 / math.sqrt(lax.axis_size("dp") * SLOTS * ROWS)
    attn_new = update(attn_grad, attn_momentum, attention, attn_average, ATTENTION_RATE, grad_scale)
    ffn_new = update(ffn_grad, ffn_momentum, feedforward, ffn_average, FEEDFORWARD_RATE, grad_scale)
    vec_new = update(vec_grad, vec_momentum, vectors, vec_average, VECTOR_RATE, grad_scale)
    return (
        activations,
        token_grad,
        attn_new[0],
        ffn_new[0],
        vec_new[0],
        attn_new[1],
        ffn_new[1],
        vec_new[1],
        attn_new[2],
        ffn_new[2],
        vec_new[2],
    )


def solution(mesh):
    attn_spec = P(None, "dp", "tensor")
    ffn_spec = P(None, None, ("dp", "tensor"))
    vec_spec = P(("dp", "tensor"))
    rows_spec = P("dp", "tensor", None)
    states = (attn_spec, ffn_spec, vec_spec)
    return jax.shard_map(
        on_device,
        mesh=mesh,
        in_specs=(rows_spec, P("dp"), rows_spec) + states * 3,
        out_specs=(rows_spec, rows_spec) + states * 3,
        check_vma=False,
    )
```

```python
import functools
import math

import jax
import jax.numpy as jnp
from jax import lax
from jax.experimental import pallas as pl
from jax.experimental.pallas import tpu as pltpu
from jax.sharding import PartitionSpec as P

D = 768
HEADS = 12
DH = 64
FF = 3072
MEM = 10
SLOTS = 4
ROWS = 522
NVEC = 22

HALF = D // 2
SEG = ROWS - MEM
THIN = 16
LOCAL = 2
TILE = 256

EPSILON = 1e-05
MOMENTUM = 0.9
AVERAGE_DECAY = 0.75
ATTENTION_RATE = 0.06
FEEDFORWARD_RATE = 0.02
VECTOR_RATE = 0.1
MASK_VALUE = -1e30
SCALE = 1.0 / math.sqrt(DH)

F32 = jnp.float32
BF16 = jnp.bfloat16
MIB = 1 << 20

QUERY_BIAS, VALUE_BIAS, OUT_BIAS, GAIN1, SHIFT1, DOWN_BIAS, GAIN2, SHIFT2, UP_BIAS = range(9)
FIRST_MEMORY = UP_BIAS + FF // D


def nn(a, b):
    return lax.dot_general(a, b, (((1,), (0,)), ((), ())), preferred_element_type=F32)


def nt(a, b):
    return lax.dot_general(a, b, (((1,), (1,)), ((), ())), preferred_element_type=F32)


def tn(a, b):
    return lax.dot_general(a, b, (((0,), (0,)), ((), ())), preferred_element_type=F32)


def normalized(rows):
    center = rows - jnp.mean(rows, axis=-1, keepdims=True)
    spread = jnp.mean(center * center, axis=-1, keepdims=True)
    inverse = lax.rsqrt(spread + EPSILON)
    return center * inverse, inverse


def normalized_back(grad, unit, inverse):
    mean_grad = jnp.mean(grad, axis=-1, keepdims=True)
    mean_along = jnp.mean(grad * unit, axis=-1, keepdims=True)
    return inverse * (grad - mean_grad - unit * mean_along)


def gelu_parts(u):
    size = jnp.abs(u)
    t = 1.0 / (1.0 + (0.3275911 / math.sqrt(2.0)) * size)
    bell = jnp.exp(-0.5 * u * u)
    poly = t * (
        0.5 * 0.254829592
        + t
        * (
            0.5 * -0.284496736
            + t * (0.5 * 1.421413741 + t * (0.5 * -1.453152027 + t * (0.5 * 1.061405429)))
        )
    )
    tail = poly * bell
    cdf = jnp.where(u < 0, tail, 1.0 - tail)
    return u * cdf, cdf + (u * (1.0 / math.sqrt(2.0 * math.pi))) * bell


def row_sum(block):
    return jnp.sum(block, axis=0, keepdims=True)


def params(limit=60, **more):
    return pltpu.CompilerParams(vmem_limit_bytes=limit * MIB, **more)


def once(shape, index):
    return pl.BlockSpec(shape, lambda *_: index, pipeline_mode=pl.Buffered(1))


ANY = pl.BlockSpec(memory_space=pltpu.HBM)
SMEM = pl.BlockSpec(memory_space=pltpu.SMEM)
VMEM = pl.BlockSpec(memory_space=pltpu.VMEM)


def sds(shape, dtype):
    return jax.ShapeDtypeStruct(shape, dtype)


def my_place():
    dp = lax.axis_index("dp")
    return dp // 4, (dp // 2) % 2, dp % 2, lax.axis_index("tensor")


def device(z, x, c, y):
    return {"dp": (z * 2 + x) * 2 + c, "tensor": y}


def entry_barrier(nz):
    z, x, c, y = my_place()
    barrier = pltpu.get_barrier_semaphore()
    signal = lambda d: pl.semaphore_signal(
        barrier, inc=1, device_id=d, device_id_type=pl.DeviceIdType.MESH
    )
    signal(device(z, 1 - x, c, y))
    signal(device(z, x, 1 - c, y))
    signal(device(z, x, c, 1 - y))

    @pl.when(z > 0)
    def _():
        signal(device(z - 1, x, c, y))

    @pl.when(z < nz - 1)
    def _():
        signal(device(z + 1, x, c, y))

    up = lax.convert_element_type(z < nz - 1, jnp.int32)
    down = lax.convert_element_type(z > 0, jnp.int32)
    pl.semaphore_wait(barrier, 3 + up + down)


def attn_view(ref, z, x, c, y):
    return ref.at[:, z, x, c, :, pl.ds(pl.multiple_of(y * HALF, HALF), HALF)]


def ffn_view(ref, z, x, c, y):
    return ref.at[:, z, x, c, y]


def vec_view(ref, z, x, c, y):
    return ref.at[z, x, c, y]


def hidden_view(ref, z, x, c, y):
    return ref.at[z, x, c, y]


def partners(place, lead):
    _, x, _, y = place
    first = (x + (1 - lead) * (1 - 2 * x), y + lead * (1 - 2 * y))
    second = (x + lead * (1 - 2 * x), y + (1 - lead) * (1 - 2 * y))
    return first, second, (1 - x, 1 - y)


COLUMN, FIRST, SECOND, BOTH, CORE = 0, 1, 2, 3, 4
UP, DOWN, UP_FIRST, DOWN_FIRST = 0, 8, 9, 10


def remote(src, dst, send_sem, recv_sem, target):
    return pltpu.make_async_remote_copy(
        src_ref=src,
        dst_ref=dst,
        send_sem=send_sem,
        recv_sem=recv_sem,
        device_id=target,
        device_id_type=pl.DeviceIdType.MESH,
    )


def gather_steps(nz, place, lead, z_second, pieces, send_sem, recv_sem):
    z, x, c, y = place
    first, second, both = partners(place, lead)
    to_first = device(z, first[0], c, first[1])
    to_second = device(z, second[0], c, second[1])
    to_core = device(z, x, 1 - c, y)

    def copies(send, recv, shard, target):
        return [
            remote(
                view(out, *shard),
                view(out, *shard),
                send_sem.at[send, shard[0], i],
                recv_sem.at[recv, shard[0], i],
                target,
            )
            for i, out, view in pieces
        ]

    def start(*args):
        for copy in copies(*args):
            copy.start()

    def arrived(*args):
        for copy in copies(*args):
            copy.wait_recv()

    def sent(*args):
        for copy in copies(*args):
            copy.wait_send()

    def column(zz):
        return (zz, x, c, y)

    def of_first(zz):
        return (zz, first[0], c, first[1])

    def of_second(zz):
        return (zz, second[0], c, second[1])

    def of_both(zz):
        return (zz, both[0], c, both[1])

    core_first, core_second = CORE + 2 - lead, CORE + 1 + lead

    def move_up(zz):
        return (UP, COLUMN, column(zz), device(z + 1, x, c, y))

    def move_down(zz):
        return (DOWN, COLUMN, column(zz), device(z - 1, x, c, y))

    def first_up(zz):
        return (UP_FIRST, FIRST, of_first(zz), device(z + 1, x, c, y))

    def first_down(zz):
        return (DOWN_FIRST, FIRST, of_first(zz), device(z - 1, x, c, y))

    def along(zz, rising, falling, up, down):
        if rising:

            @pl.when(z < nz - 1)
            def _():
                start(*up(zz))

        if falling:

            @pl.when(z > 0)
            def _():
                start(*down(zz))

    def stage0(zz, rising, falling, wait):
        if wait:
            arrived(UP, COLUMN, column(zz), to_core)
        if z_second and not wait:
            start(FIRST, FIRST, column(zz), to_first)
        along(zz, rising, falling, move_up, move_down)
        if not z_second:
            start(FIRST, FIRST, column(zz), to_first)
        start(SECOND, SECOND, column(zz), to_second)
        start(CORE, CORE, column(zz), to_core)

    def stage1(zz, rising, falling):
        arrived(FIRST, FIRST, of_first(zz), to_first)
        if z_second:
            along(zz, rising, falling, first_up, first_down)
        start(BOTH, BOTH, of_first(zz), to_second)
        start(core_first, core_first, of_first(zz), to_core)

    def stage2(zz, rising, falling):
        arrived(SECOND, SECOND, of_second(zz), to_second)
        start(core_second, core_second, of_second(zz), to_core)
        arrived(BOTH, BOTH, of_both(zz), to_second)
        start(CORE + 3, CORE + 3, of_both(zz), to_core)

    def begin():
        stage0(z, True, True, False)

    def step(t):
        @pl.when((t < nz) & (z - t >= 0))
        def _():
            stage0(z - t, True, False, True)

        @pl.when((t < nz) & (z + t < nz))
        def _():
            stage0(z + t, False, True, True)

        for lag, stage in ((1, stage1), (2, stage2)):
            late = t - lag

            @pl.when(late == 0)
            def _():
                stage(z, True, True)

            @pl.when((late > 0) & (late < nz) & (z - late >= 0))
            def _():
                stage(z - late, True, False)

            @pl.when((late > 0) & (late < nz) & (z + late < nz))
            def _():
                stage(z + late, False, True)

    def all_arrived(zz, carry):
        for fx in range(2):
            for fy in range(2):
                kind = CORE + 2 * fx + fy
                shard = (zz, x + fx * (1 - 2 * x), 1 - c, y + fy * (1 - 2 * y))
                arrived(kind, kind, shard, to_core)
        return carry

    def all_sent(zz, carry):
        @pl.when((zz <= z) & (z < nz - 1))
        def _():
            sent(*move_up(zz))

        @pl.when((zz >= z) & (z > 0))
        def _():
            sent(*move_down(zz))

        if z_second:

            @pl.when((zz <= z) & (z < nz - 1))
            def _():
                sent(*first_up(zz))

            @pl.when((zz >= z) & (z > 0))
            def _():
                sent(*first_down(zz))

            @pl.when(zz == z)
            def _():
                sent(FIRST, FIRST, column(zz), to_first)

        else:
            sent(FIRST, FIRST, column(zz), to_first)
        sent(SECOND, SECOND, column(zz), to_second)
        sent(BOTH, BOTH, of_first(zz), to_second)
        sent(CORE, CORE, column(zz), to_core)
        sent(core_first, core_first, of_first(zz), to_core)
        sent(core_second, core_second, of_second(zz), to_core)
        sent(CORE + 3, CORE + 3, of_both(zz), to_core)
        return carry

    def end_arrive():
        lax.fori_loop(0, nz, all_arrived, 0)

    def end_send():
        lax.fori_loop(0, nz, all_sent, 0)

    return begin, step, end_arrive, end_send


def swap_halves(place, rows, other, sem):
    z, x, c, y = place
    return remote(
        rows.at[pl.ds(LOCAL * (1 - y), LOCAL)],
        other,
        sem.at[0],
        sem.at[1],
        device(z, x, c, 1 - y),
    )


def place_rows(place, keep, send, out, sem):
    z, x, c, y = place
    own = out.at[pl.ds(LOCAL * y, LOCAL)]
    return [
        pltpu.make_async_copy(keep, own, sem.at[2]),
        remote(send, own, sem.at[0], sem.at[1], device(z, x, c, 1 - y)),
    ]


def gather_kernel(nz, views, *refs):
    n = len(views)
    srcs, tokens, outs, other = refs[:n], refs[n], refs[n + 1 : 2 * n + 1], refs[2 * n + 1]
    send_sem, recv_sem, own_sem, swap_sem = refs[2 * n + 2 :]
    place = my_place()
    halves = swap_halves(place, tokens, other, swap_sem)
    own = [
        pltpu.make_async_copy(src, view(out, *place), own_sem.at[i])
        for i, (src, out, view) in enumerate(zip(srcs, outs, views))
    ]
    for copy in own:
        copy.start()
    entry_barrier(nz)
    halves.start()
    for copy in own:
        copy.wait()
    pieces = [(i, out, view) for i, (out, view) in enumerate(zip(outs, views))]
    begin, step, end_arrive, end_send = gather_steps(
        nz, place, place[2], False, pieces, send_sem, recv_sem
    )
    begin()

    def loop(t, carry):
        step(t)
        return carry

    lax.fori_loop(1, nz + 2, loop, 0)
    end_send()
    end_arrive()
    halves.wait()


def gather(nz, collective_id, parts, tokens):
    shards, shapes, views = zip(*parts)
    n = len(parts)
    return pl.pallas_call(
        functools.partial(gather_kernel, nz, views),
        in_specs=[ANY] * (n + 1),
        out_specs=[ANY] * (n + 1),
        out_shape=[sds(shape, shard.dtype) for shard, shape in zip(shards, shapes)]
        + [sds((LOCAL, *tokens.shape[1:]), tokens.dtype)],
        scratch_shapes=[
            pltpu.SemaphoreType.DMA((11, nz, n)),
            pltpu.SemaphoreType.DMA((8, nz, n)),
            pltpu.SemaphoreType.DMA((n,)),
            pltpu.SemaphoreType.DMA((2,)),
        ],
        name="gather",
        compiler_params=params(collective_id=collective_id, has_side_effects=True),
    )(*shards, tokens)


def scatter_kernel(nz, views, *refs):
    n = len(views)
    terms, outs = refs[:n], refs[n : 2 * n]
    mine, from_core, from_second, from_first, from_below, from_above = (
        refs[2 * n + i * n : 3 * n + i * n] for i in range(6)
    )
    send_sem, recv_sem, own_sem = refs[8 * n :]
    place = z, x, c, y = my_place()
    first, second, both = partners(place, place[2])
    to_first = device(z, first[0], c, first[1])
    to_second = device(z, second[0], c, second[1])
    to_core = device(z, x, 1 - c, y)

    def copies(srcs, dsts, send, recv, zz, target):
        return [
            pltpu.make_async_remote_copy(
                src_ref=srcs[i],
                dst_ref=dsts[i],
                send_sem=send_sem.at[send, zz, i],
                recv_sem=recv_sem.at[recv, zz, i],
                device_id=target,
                device_id_type=pl.DeviceIdType.MESH,
            )
            for i in range(n)
        ]

    def slots(bufs, *index):
        return [b.at[index] for b in bufs]

    def pick(refs_, *index):
        return [b[index] for b in refs_]

    flips = [(fx, fy) for fx in range(2) for fy in range(2)]

    def at(fx, fy):
        return x + fx * (1 - 2 * x), y + fy * (1 - 2 * y)

    def core_copies(zz, f):
        fx, fy = flips[f]
        xx, yy = at(fx, fy)
        return copies(
            [view(t, zz, xx, 1 - c, yy) for t, view in zip(terms, views)],
            slots(from_core, zz, f),
            f,
            f,
            zz,
            to_core,
        )

    def own_copies(zz, f):
        fx, fy = flips[f]
        xx, yy = at(fx, fy)
        return [
            pltpu.make_async_copy(
                view(t, zz, xx, c, yy), mine[i].at[zz, f], own_sem.at[f, zz, i]
            )
            for i, (t, view) in enumerate(zip(terms, views))
        ]

    f_first, f_second = 2 - c, 1 + c

    def second_copies(zz, across):
        return copies(
            slots(from_core, zz, 3 if across else f_second),
            slots(from_second, zz, 1 if across else 0),
            4 + across,
            4 + across,
            zz,
            to_second,
        )

    def first_copies(zz):
        return copies(slots(from_second, zz, 1), slots(from_first, zz), 6, 6, zz, to_first)

    def up_copies(zz):
        return copies(slots(from_first, zz), slots(from_below, zz), 7, 7, zz, device(z + 1, x, c, y))

    def down_copies(zz):
        return copies(slots(from_first, zz), slots(from_above, zz), 8, 8, zz, device(z - 1, x, c, y))

    def run(group, what):
        for copy in group:
            getattr(copy, what)()

    def add(into, index, other, other_index):
        for i in range(n):
            a, b = into[i].at[index], other[i].at[other_index]
            a[...] = (a[...].astype(F32) + b[...].astype(F32)).astype(a.dtype)

    def by_distance(t, do):
        @pl.when((t >= 0) & (t < nz) & (z - t >= 0))
        def _():
            do(z - t)

        @pl.when((t > 0) & (t < nz) & (z + t < nz))
        def _():
            do(z + t)

    def start_own(zz):
        for f in range(4):
            run(own_copies(zz, f), "start")

    def start_core(zz):
        for f in (3, 1, 2, 0):
            run(core_copies(zz, f), "start")

    def stage0(zz):
        for f in (3, 1, 2, 0):
            run(core_copies(zz, f), "wait_recv")
            run(own_copies(zz, f), "wait")
            add(from_core, (zz, f), mine, (zz, f))
        run(second_copies(zz, 1), "start")
        run(second_copies(zz, 0), "start")

    def stage1(zz):
        run(second_copies(zz, 1), "wait_recv")
        add(from_second, (zz, 1), from_core, (zz, f_first))
        run(first_copies(zz), "start")

    def stage2(zz):
        run(second_copies(zz, 0), "wait_recv")
        add(from_second, (zz, 0), from_core, (zz, 0))
        run(first_copies(zz), "wait_recv")
        add(from_first, (zz,), from_second, (zz, 0))

        @pl.when(zz > z)
        def _():
            @pl.when(z > 0)
            def _():
                run(up_copies(zz), "wait_recv")
                add(from_first, (zz,), from_below, (zz,))

            run(up_copies(zz), "start")

        @pl.when(zz < z)
        def _():
            @pl.when(z < nz - 1)
            def _():
                run(down_copies(zz), "wait_recv")
                add(from_first, (zz,), from_above, (zz,))

            run(down_copies(zz), "start")

    entry_barrier(nz)

    def begin(k, carry):
        by_distance(nz - 1 - k, start_core)
        by_distance(nz - 1 - k, start_own)
        return carry

    lax.fori_loop(0, nz, begin, 0)

    def step(k, carry):
        t = nz - 1 - k
        by_distance(t, stage0)
        by_distance(t + 1, stage1)
        by_distance(t + 2, stage2)
        return carry

    lax.fori_loop(0, nz + 2, step, 0)

    @pl.when(z > 0)
    def _():
        run(up_copies(z), "wait_recv")
        add(from_first, (z,), from_below, (z,))

    @pl.when(z < nz - 1)
    def _():
        run(down_copies(z), "wait_recv")
        add(from_first, (z,), from_above, (z,))

    for i in range(n):
        outs[i][...] = from_first[i][z]

    def finish(zz, carry):
        for f in range(4):
            run(core_copies(zz, f), "wait_send")
        run(second_copies(zz, 1), "wait_send")
        run(second_copies(zz, 0), "wait_send")
        run(first_copies(zz), "wait_send")

        @pl.when(zz > z)
        def _():
            run(up_copies(zz), "wait_send")

        @pl.when(zz < z)
        def _():
            run(down_copies(zz), "wait_send")

        return carry

    lax.fori_loop(0, nz, finish, 0)


def scatter(nz, collective_id, parts):
    terms, shapes, views = zip(*parts)
    n = len(parts)
    dtypes = [t.dtype for t in terms]

    def bufs(*lead):
        return [pltpu.VMEM((*lead, *shape), d) for shape, d in zip(shapes, dtypes)]

    return pl.pallas_call(
        functools.partial(scatter_kernel, nz, views),
        in_specs=[ANY] * n,
        out_specs=[VMEM] * n,
        out_shape=[sds(shape, d) for shape, d in zip(shapes, dtypes)],
        scratch_shapes=[
            *bufs(nz, 4),
            *bufs(nz, 4),
            *bufs(nz, 2),
            *bufs(nz),
            *bufs(nz),
            *bufs(nz),
            pltpu.SemaphoreType.DMA((9, nz, n)),
            pltpu.SemaphoreType.DMA((9, nz, n)),
            pltpu.SemaphoreType.DMA((4, nz, n)),
        ],
        name="scatter",
        compiler_params=params(62, collective_id=collective_id, has_side_effects=True),
    )(*terms)


def whole_rows(side, mine, other):
    mine, other = mine.astype(F32), other.astype(F32)
    first = jnp.where(side == 0, mine, other)
    second = jnp.where(side == 0, other, mine)
    return jnp.concatenate([jnp.zeros((MEM, D), F32), first, second], axis=0)


def split_rows(side, rows):
    half = (SEG - MEM) // 2
    first, second = rows[MEM : MEM + half], rows[MEM + half :]
    keep = jnp.where(side == 0, first, second)
    send = jnp.where(side == 0, second, first)
    return keep, send


def project_kernel(mine_ref, other_ref, w_ref, table_ref, x_ref, q_ref, k_ref, v_ref):
    side = lax.axis_index("tensor")
    mine = mine_ref[LOCAL * side + pl.program_id(0)]
    x = whole_rows(side, mine, other_ref[0]).astype(BF16)
    x_ref[0] = x
    query = nn(x, w_ref[0]) + table_ref[QUERY_BIAS : QUERY_BIAS + 1, :]
    q_ref[0] = (query * SCALE).astype(BF16)
    k_ref[0] = nn(x, w_ref[1]).astype(BF16)
    v_ref[0] = (nn(x, w_ref[2]) + table_ref[VALUE_BIAS : VALUE_BIAS + 1, :]).astype(BF16)


def slot_rows(width=D):
    return pl.BlockSpec((1, SEG, width), lambda s: (s, 0, 0))


def half_rows(half):
    return pl.BlockSpec((1, half, D), lambda s: (s, 0, 0))


def project(tokens, other, attn, table):
    return pl.pallas_call(
        project_kernel,
        grid=(LOCAL,),
        in_specs=[
            once(tokens.shape, (0, 0, 0)),
            half_rows(tokens.shape[1]),
            once((3, D, D), (0, 0, 0)),
            once((NVEC, D), (0, 0)),
        ],
        out_specs=[slot_rows()] * 4,
        out_shape=[sds((LOCAL, SEG, D), BF16)] * 4,
        name="project",
        compiler_params=params(),
    )(tokens, other, attn, table)


def head_masks():
    feature_head = lax.broadcasted_iota(jnp.int32, (1, D), 1) // DH
    return [feature_head == h for h in range(HEADS)]


def by_head(rows16, masks):
    zero = jnp.zeros_like(rows16)
    return jnp.concatenate([jnp.where(m, rows16, zero) for m in masks], axis=0)


def own_columns(blocks, masks):
    total = jnp.zeros((THIN, D), blocks.dtype)
    for h, m in enumerate(masks):
        total = jnp.where(m, blocks[THIN * h : THIN * (h + 1)], total)
    return total


def copies_of(key_mask_shape):
    row = lax.rem(lax.broadcasted_iota(jnp.int32, key_mask_shape, 0), THIN)
    key = lax.broadcasted_iota(jnp.int32, key_mask_shape, 1)
    return jnp.where((key < MEM) & (key <= row), 2.0, 1.0)


def pair_barrier(place):
    z, x, c, y = place
    barrier = pltpu.get_barrier_semaphore()
    pl.semaphore_signal(
        barrier,
        inc=1,
        device_id=device(z, x, c, 1 - y),
        device_id_type=pl.DeviceIdType.MESH,
    )
    pl.semaphore_wait(barrier, 1)


def chain_kernel(
    place_ref,
    table_ref,
    attn_ref,
    ffn_ref,
    x_in,
    q_in,
    k_in,
    v_in,
    cot_ref,
    x_ref,
    q_ref,
    k_ref,
    v_ref,
    saved_d_ref,
    saved_f_ref,
    saved_s_ref,
    cot_other_ref,
    wa,
    wf,
    xb,
    qb,
    kb,
    vb,
    save_d,
    save_f,
    save_s,
    left,
    given,
    sem_w,
    sem_x,
    sem_kv,
    sem_out,
    sem_memory,
    sem_cot,
):
    del x_in, q_in, k_in, v_in
    place = z, x, c, y = my_place()
    loads = [
        pltpu.make_async_copy(attn_ref, wa, sem_w.at[0]),
        pltpu.make_async_copy(ffn_ref.at[0], wf.at[0], sem_w.at[1]),
        pltpu.make_async_copy(ffn_ref.at[1], wf.at[1], sem_w.at[2]),
    ]
    tiles = [
        pltpu.make_async_copy(x_ref.at[s, pl.ds(0, THIN)], xb.at[s], sem_x.at[s])
        for s in range(LOCAL)
    ]
    keys = [
        pltpu.make_async_copy(src.at[s], dst.at[s], sem_kv.at[2 * s + i])
        for s in range(LOCAL)
        for i, (src, dst) in enumerate(((k_ref, kb), (v_ref, vb)))
    ]
    for copy in tiles + loads[:1] + keys + loads[1:]:
        copy.start()
    pair_barrier(place)
    cot_swap = swap_halves(place, cot_ref, cot_other_ref, sem_cot)
    cot_swap.start()
    handed = remote(left, given, sem_memory.at[0], sem_memory.at[1], device(z, x, c, 1 - y))

    masks = head_masks()
    memory_row = lax.broadcasted_iota(jnp.int32, (THIN, 1), 0) < MEM
    first = table_ref[FIRST_MEMORY:NVEC, :]
    first = jnp.concatenate([first, jnp.zeros((THIN - MEM, D), F32)], axis=0)
    row = lambda r: table_ref[r : r + 1, :]

    def slots(turn, memory):
        for s in range(LOCAL):
            tiles[s].wait()
            if s == 0:
                loads[0].wait()
            keys[2 * s].wait()
            keys[2 * s + 1].wait()
            if memory is None:
                memory = first
            else:
                memory = jnp.where(place_ref[LOCAL * turn + s] == 0, first, memory)
            x16 = jnp.where(memory_row, memory, xb[s].astype(F32)).astype(BF16)
            xb[s] = x16
            qb[s] = ((nn(x16, wa[0]) + row(QUERY_BIAS)) * SCALE).astype(BF16)
            kb[s, 0:THIN] = nn(x16, wa[1]).astype(BF16)
            vb[s, 0:THIN] = (nn(x16, wa[2]) + row(VALUE_BIAS)).astype(BF16)
            outs = [
                pltpu.make_async_copy(
                    src.at[s, pl.ds(0, THIN)], dst.at[s, pl.ds(0, THIN)], sem_out.at[4 * s + i]
                )
                for i, (src, dst) in enumerate(
                    ((xb, x_ref), (qb, q_ref), (kb, k_ref), (vb, v_ref))
                )
            ]
            for copy in outs:
                copy.start()
            if turn == 1 and s == LOCAL - 1:
                save_d[s] = jnp.zeros_like(save_d[s])
                save_f[s] = jnp.zeros_like(save_f[s])
                save_s[s] = jnp.zeros_like(save_s[s])
            else:
                q_heads = by_head(qb[s], masks)
                score = nt(q_heads, kb[s])
                top = jnp.max(score, axis=-1, keepdims=True)
                weight = jnp.exp(score - top) * copies_of(score.shape)
                total = jnp.sum(weight, axis=-1, keepdims=True)
                share = (weight / total).astype(BF16)
                log_total = top + jnp.log(total)
                context = own_columns(nn(share, vb[s]), masks).astype(BF16)
                unit1, inverse1 = normalized(
                    x16.astype(F32) + nt(context, wa[3]) + row(OUT_BIAS)
                )
                hidden = (unit1 * row(GAIN1) + row(SHIFT1)).astype(BF16)
                if s == 0:
                    loads[1].wait()
                up = nt(hidden, wf[0])
                up_bias = jnp.concatenate([row(UP_BIAS + i) for i in range(FF // D)], axis=1)
                active16, slope = gelu_parts(up + up_bias)
                active16 = active16.astype(BF16)
                if s == 0:
                    loads[2].wait()
                second = hidden.astype(F32) + nn(active16, wf[1]) + row(DOWN_BIAS)
                unit2, inverse2 = normalized(second)
                output = (unit2 * row(GAIN2) + row(SHIFT2)).astype(BF16)
                memory = output.astype(F32)
                if turn == 0 and s == LOCAL - 1:
                    left[...] = output
                    handed.start()
                save_d[s, 0] = hidden
                save_d[s, 1] = unit1.astype(BF16)
                save_d[s, 2] = unit2.astype(BF16)
                save_d[s, 3] = context
                save_f[s, 0] = active16
                save_f[s, 1] = slope.astype(BF16)
                wide = lambda v: jnp.broadcast_to(v, (v.shape[0], 128))
                save_s[s, 0 : HEADS * THIN] = wide(log_total)
                save_s[s, HEADS * THIN : HEADS * THIN + THIN] = wide(inverse1)
                save_s[s, HEADS * THIN + THIN :] = wide(inverse2)
            for copy in outs:
                copy.wait()

    @pl.when(y == 0)
    def _():
        slots(0, None)
        handed.wait_send()

    @pl.when(y == 1)
    def _():
        handed.wait_recv()
        slots(1, given[...].astype(F32))

    saves = [
        pltpu.make_async_copy(save_d, saved_d_ref, sem_out.at[0]),
        pltpu.make_async_copy(save_f, saved_f_ref, sem_out.at[1]),
        pltpu.make_async_copy(save_s, saved_s_ref, sem_out.at[2]),
    ]
    for copy in saves:
        copy.start()
    for copy in saves:
        copy.wait()
    cot_swap.wait()


SAVED = (
    sds((LOCAL, 4, THIN, D), BF16),
    sds((LOCAL, 2, THIN, FF), BF16),
    sds((LOCAL, HEADS * THIN + 2 * THIN, 128), F32),
)


def chain(place, table, attn, ffn, x, q, k, v, cot):
    whole = sds((LOCAL, SEG, D), BF16)
    outs = pl.pallas_call(
        chain_kernel,
        in_specs=[SMEM, VMEM] + [ANY] * 7,
        out_specs=[ANY] * 8,
        out_shape=[whole] * 4 + list(SAVED) + [sds((LOCAL, *cot.shape[1:]), BF16)],
        input_output_aliases={4 + i: i for i in range(4)},
        scratch_shapes=[
            pltpu.VMEM((4, D, D), BF16),
            pltpu.VMEM((2, FF, D), BF16),
            pltpu.VMEM((LOCAL, THIN, D), BF16),
            pltpu.VMEM((LOCAL, THIN, D), BF16),
            pltpu.VMEM((LOCAL, SEG, D), BF16),
            pltpu.VMEM((LOCAL, SEG, D), BF16),
            *[pltpu.VMEM(s.shape, s.dtype) for s in SAVED],
            pltpu.VMEM((THIN, D), BF16),
            pltpu.VMEM((THIN, D), BF16),
            pltpu.SemaphoreType.DMA((3,)),
            pltpu.SemaphoreType.DMA((LOCAL,)),
            pltpu.SemaphoreType.DMA((2 * LOCAL,)),
            pltpu.SemaphoreType.DMA((4 * LOCAL,)),
            pltpu.SemaphoreType.DMA((2,)),
            pltpu.SemaphoreType.DMA((2,)),
        ],
        name="chain",
        compiler_params=params(collective_id=2, has_side_effects=True),
    )(place, table, attn, ffn, x, q, k, v, cot)
    return outs[:4], outs[4:7], outs[7]


def own_lanes(block, head):
    lane = lax.broadcasted_iota(jnp.int32, block.shape, 1)
    return jnp.where((lane < DH) == (head == 0), block, jnp.zeros_like(block))


def seen(score, first_query):
    key = lax.broadcasted_iota(jnp.int32, score.shape, 0)
    query = lax.broadcasted_iota(jnp.int32, score.shape, 1) + first_query
    return key <= query


def attend_pair(q, k, v):
    contexts_of, logs_of = [], [[], []]
    for part in range(SEG // TILE):
        rows = slice(TILE * part, TILE * (part + 1))
        keys = slice(0, TILE * (part + 1))
        contexts = []
        for head in range(2):
            score = nt(own_lanes(k[keys], head), q[rows])
            key = lax.broadcasted_iota(jnp.int32, score.shape, 0)
            allowed = seen(score, TILE * part) & (key >= MEM)
            score = jnp.where(allowed, score, MASK_VALUE)
            top = jnp.max(score, axis=0, keepdims=True)
            weight = jnp.exp(score - top)
            total = jnp.sum(weight, axis=0, keepdims=True)
            share = (weight * (1.0 / total)).astype(BF16)
            logs_of[head].append(top + jnp.log(total))
            contexts.append(tn(share, v[keys]))
        lane = lax.broadcasted_iota(jnp.int32, contexts[0].shape, 1)
        contexts_of.append(jnp.where(lane < DH, contexts[0], contexts[1]).astype(BF16))
    return jnp.concatenate(contexts_of, axis=0), [jnp.concatenate(l, axis=1) for l in logs_of]


def attend_kernel(q_ref, k_ref, v_ref, c_ref, log_ref):
    context, logs = attend_pair(q_ref[0], k_ref[0], v_ref[0])
    c_ref[0] = context
    for head in range(2):
        log_ref[0, 0, head : head + 1] = logs[head]


def with_memory(q, k16, v16, context, log_tokens):
    masks = head_masks()
    score = nt(by_head(k16, masks), q).reshape(HEADS, THIN, SEG)
    key = lax.broadcasted_iota(jnp.int32, score.shape, 1)
    score = jnp.where(key < MEM, score, MASK_VALUE)
    top = jnp.maximum(jnp.max(score, axis=1), log_tokens)
    weight = jnp.exp(score - top[:, None])
    old = jnp.exp(log_tokens - top)
    total = jnp.sum(weight, axis=1) + old
    share = (weight * (1.0 / total)[:, None]).reshape(HEADS * THIN, SEG).astype(BF16)
    kept = old / total
    coarse = kept.astype(BF16)
    fine = (kept - coarse.astype(F32)).astype(BF16)
    pad = jnp.zeros((4, SEG), BF16)
    head = lax.rem(lax.broadcasted_iota(jnp.int32, (2 * THIN, D), 0), THIN)
    spread = jnp.where(head == lax.broadcasted_iota(jnp.int32, (2 * THIN, D), 1) // DH, 1.0, 0.0)
    factor = tn(jnp.concatenate([coarse, pad, fine, pad], axis=0), spread.astype(BF16))
    context = factor * context.astype(F32) + tn(share, by_head(v16, masks))
    return context.astype(BF16), top + jnp.log(total)


PAIR = pl.BlockSpec((1, SEG, 2 * DH), lambda s, h: (s, 0, h))
PAIR_LOG = pl.BlockSpec((1, 1, 2, SEG), lambda s, h: (s, h, 0, 0))


def attend(q, k, v):
    return pl.pallas_call(
        attend_kernel,
        grid=(LOCAL, HEADS // 2),
        in_specs=[PAIR] * 3,
        out_specs=[PAIR, PAIR_LOG],
        out_shape=[sds((LOCAL, SEG, D), BF16), sds((LOCAL, HEADS // 2, 2, SEG), F32)],
        name="attend",
        compiler_params=params(),
    )(q, k, v)


def attend_back_pair(q, k, v, dc, logs):
    last = SEG // TILE
    key_terms, value_terms, query_terms = [], [], []
    for head in range(2):
        key_sum, value_sum, query_parts = [], [], []
        for part in range(last):
            rows = slice(TILE * part, TILE * (part + 1))
            keys = slice(0, TILE * (part + 1))
            score = nt(own_lanes(k[keys], head), q[rows])
            share = jnp.exp(score - logs[head : head + 1, rows])
            share = jnp.where(seen(score, TILE * part), share, 0.0)
            share_grad = nt(own_lanes(v[keys], head), dc[rows])
            inner = jnp.sum(share_grad * share, axis=0, keepdims=True)
            score_grad = (share * (share_grad - inner)).astype(BF16)
            value_sum.append(nn(share.astype(BF16), dc[rows]))
            key_sum.append(nn(score_grad, q[rows]))
            query_parts.append(tn(score_grad, k[keys]))
        key_terms.append(key_sum)
        value_terms.append(value_sum)
        query_terms.append(query_parts)
    lane = lax.broadcasted_iota(jnp.int32, (TILE, 2 * DH), 1)
    pick = lambda a, b: jnp.where(lane < DH, a, b)
    dq, dk, dv = [], [], []
    for part in range(last):
        rows = slice(TILE * part, TILE * (part + 1))
        dq.append((pick(query_terms[0][part], query_terms[1][part]) * SCALE).astype(BF16))
        for terms, out in ((key_terms, dk), (value_terms, dv)):
            total = None
            for later in range(part, last):
                term = pick(terms[0][later][rows], terms[1][later][rows])
                total = term if total is None else total + term
            out.append(total)
    return [jnp.concatenate(parts, axis=0) for parts in (dq, dk, dv)]


def rows_kernel(
    place_ref,
    x_ref,
    q_ref,
    k16_ref,
    v16_ref,
    tokens_c_ref,
    tokens_log_ref,
    mine_ref,
    other_ref,
    wo_ref,
    wf_ref,
    table_ref,
    keep_ref,
    send_ref,
    h_ref,
    g_ref,
    du_ref,
    df_ref,
    da_ref,
    dc_ref,
    c_ref,
    log_ref,
    sums_ref,
    slope_ref,
):
    row = lambda r: table_ref[r : r + 1, :]
    slot = pl.program_id(0)
    side = lax.axis_index("tensor")
    live = place_ref[LOCAL * side + slot] >= 0

    @pl.when(slot == 0)
    def _():
        sums_ref[...] = jnp.zeros_like(sums_ref)

    def add(r, value):
        sums_ref[r : r + 1, :] += value

    log_tokens = jnp.concatenate([tokens_log_ref[0, h] for h in range(HEADS // 2)], axis=0)
    context, log_total = with_memory(
        q_ref[0], k16_ref[0], v16_ref[0], tokens_c_ref[0], log_tokens
    )
    c_ref[0] = context
    for h in range(HEADS // 2):
        log_ref[0, h] = log_total[2 * h : 2 * h + 2]
    unit1, inverse1 = normalized(x_ref[0].astype(F32) + nt(context, wo_ref[0]) + row(OUT_BIAS))
    hidden = (unit1 * row(GAIN1) + row(SHIFT1)).astype(BF16)
    h_ref[0] = hidden
    second = hidden.astype(F32) + row(DOWN_BIAS)
    for i in range(FF // D):
        cols = slice(D * i, D * (i + 1))
        up = nt(hidden, wf_ref[0, cols]) + row(UP_BIAS + i)
        active, slope = gelu_parts(up)
        active = active.astype(BF16)
        g_ref[0, :, cols] = active
        slope_ref[:, cols] = slope.astype(BF16)
        second = second + nn(active, wf_ref[1, cols])
    unit2, inverse2 = normalized(second)
    output = jnp.where(live, unit2 * row(GAIN2) + row(SHIFT2), 0.0)
    keep, send = split_rows(side, output)
    keep_ref[0] = keep.astype(BF16)
    send_ref[0] = send.astype(BF16)

    grad = whole_rows(side, mine_ref[LOCAL * side + slot], other_ref[0])
    grad = jnp.where(live, grad, 0.0)
    add(GAIN2, row_sum(grad * unit2))
    add(SHIFT2, row_sum(grad))
    second_grad = normalized_back(grad * row(GAIN2), unit2, inverse2)
    down_grad = second_grad.astype(BF16)
    df_ref[0] = down_grad
    add(DOWN_BIAS, row_sum(down_grad.astype(F32)))
    hidden_grad = second_grad
    for i in range(FF // D):
        cols = slice(D * i, D * (i + 1))
        up_grad = (nt(down_grad, wf_ref[1, cols]) * slope_ref[:, cols].astype(F32)).astype(BF16)
        du_ref[0, :, cols] = up_grad
        add(UP_BIAS + i, row_sum(up_grad.astype(F32)))
        hidden_grad = hidden_grad + nn(up_grad, wf_ref[0, cols])
    add(GAIN1, row_sum(hidden_grad * unit1))
    add(SHIFT1, row_sum(hidden_grad))
    branch_grad = normalized_back(hidden_grad * row(GAIN1), unit1, inverse1).astype(BF16)
    da_ref[0] = branch_grad
    add(OUT_BIAS, row_sum(branch_grad.astype(F32)))
    dc_ref[0] = nn(branch_grad, wo_ref[0]).astype(BF16)


def rows_part(place, x, q, k, v, c, log_tokens, cot, other, attn, ffn, table):
    half = cot.shape[1]
    whole, whole_wide = sds((LOCAL, SEG, D), BF16), sds((LOCAL, SEG, FF), BF16)
    part, logs = sds((LOCAL, half, D), BF16), sds((LOCAL, HEADS // 2, 2, SEG), F32)
    rows, wide = slot_rows(), slot_rows(FF)
    thin = pl.BlockSpec((1, THIN, D), lambda s: (s, 0, 0))
    log_rows = pl.BlockSpec((1, HEADS // 2, 2, SEG), lambda s: (s, 0, 0, 0))
    return pl.pallas_call(
        rows_kernel,
        grid=(LOCAL,),
        in_specs=[SMEM, rows, rows, thin, thin, rows, log_rows]
        + [once(cot.shape, (0, 0, 0)), half_rows(half)]
        + [once((1, D, D), (3, 0, 0)), once((2, FF, D), (0, 0, 0)), once((NVEC, D), (0, 0))],
        out_specs=[half_rows(half)] * 2
        + [rows, wide, wide, rows, rows, rows, rows, log_rows, once((THIN, D), (0, 0))],
        out_shape=[part] * 2
        + [whole, whole_wide, whole_wide, whole, whole, whole, whole, logs, sds((THIN, D), F32)],
        scratch_shapes=[pltpu.VMEM((SEG, FF), BF16)],
        name="rows_part",
        compiler_params=params(),
    )(place, x, q, k, v, c, log_tokens, cot, other, attn, ffn, table)


CHUNK = 768


def memory_key_gradient(q, k16, v16, dc, context, logs, masks):
    score = nt(by_head(k16, masks), q).reshape(HEADS, THIN, SEG)
    key = lax.broadcasted_iota(jnp.int32, score.shape, 1)
    share = jnp.where(key < MEM, jnp.exp(score - logs[:, None]), 0.0)
    share_grad = nt(by_head(v16, masks), dc).reshape(HEADS, THIN, SEG)
    product = dc.astype(F32) * context.astype(F32)
    coarse = product.astype(BF16)
    fine = (product - coarse.astype(F32)).astype(BF16)
    head = lax.broadcasted_iota(jnp.int32, (THIN, D), 0)
    ones = jnp.where(head == lax.broadcasted_iota(jnp.int32, (THIN, D), 1) // DH, 1.0, 0.0)
    ones = ones.astype(BF16)
    inner = (nt(ones, coarse) + nt(ones, fine))[0:HEADS]
    score_grad = (share * (share_grad - inner[:, None])).reshape(HEADS * THIN, SEG)
    share = share.reshape(HEADS * THIN, SEG).astype(BF16)
    dk = own_columns(nn(score_grad.astype(BF16), q), masks)
    return dk, own_columns(nn(share, dc), masks)


def chain_back_kernel(
    place_ref,
    table_ref,
    attn_ref,
    ffn_ref,
    q_ref,
    k_ref,
    v_ref,
    saved_d_ref,
    saved_f_ref,
    saved_s_ref,
    g_ref,
    du_ref,
    df_ref,
    h_ref,
    keep_ref,
    send_ref,
    dc_ref,
    log_ref,
    da_in,
    c_in,
    da_ref,
    c_ref,
    dq_ref,
    dk_ref,
    dv_ref,
    sums_ref,
    terms_ref,
    rows_ref,
    wa,
    wf,
    qb,
    kb,
    vb,
    dcb,
    cb,
    logs,
    dqb,
    dkb,
    dvb,
    tiles,
    df,
    hid,
    gb,
    dub,
    staged,
    save_d,
    save_f,
    save_s,
    thin_d,
    thin_f,
    sums,
    left,
    given,
    sem_w,
    sem_in,
    sem_ff,
    sem_chunk,
    sem_out,
    sem_stage,
    sem_grad,
    sem_swap,
):
    del da_in, c_in
    place = z, x, c, y = my_place()
    loads = [
        pltpu.make_async_copy(attn_ref, wa, sem_w.at[0]),
        pltpu.make_async_copy(ffn_ref.at[0], wf.at[0], sem_w.at[1]),
        pltpu.make_async_copy(ffn_ref.at[1], wf.at[1], sem_w.at[2]),
    ]
    first_rows = lambda ref: ref.at[:, pl.ds(0, THIN)]
    saved = [
        pltpu.make_async_copy(saved_d_ref, save_d, sem_in.at[2]),
        pltpu.make_async_copy(saved_f_ref, save_f, sem_in.at[3]),
        pltpu.make_async_copy(saved_s_ref, save_s, sem_in.at[4]),
    ]
    reads = [
        pltpu.make_async_copy(src, dst, sem_in.at[5 + i])
        for i, (src, dst) in enumerate(
            ((q_ref, qb), (k_ref, kb), (v_ref, vb), (dc_ref, dcb), (c_ref, cb), (log_ref, logs))
        )
    ]
    merged = (da_ref, c_ref)
    tile_reads = [
        pltpu.make_async_copy(first_rows(ref), tiles.at[i], sem_in.at[i])
        for i, ref in enumerate(merged)
    ]
    rows_in = [
        pltpu.make_async_copy(df_ref, df, sem_ff.at[0]),
        pltpu.make_async_copy(h_ref, hid, sem_ff.at[1]),
    ]

    def chunk_reads(i):
        lanes = pl.ds(pl.multiple_of(CHUNK * i, CHUNK), CHUNK)
        slot = lax.rem(i, 2)
        return [
            pltpu.make_async_copy(src.at[:, :, lanes], dst.at[slot], sem_chunk.at[slot, j])
            for j, (src, dst) in enumerate(((g_ref, gb), (du_ref, dub)))
        ]

    @pl.when(y == 1)
    def _():
        for copy in reads + loads[:1] + saved + loads[:0:-1] + tile_reads:
            copy.start()
        for copy in rows_in + chunk_reads(0) + chunk_reads(1):
            copy.start()

    @pl.when(y == 0)
    def _():
        for copy in rows_in + chunk_reads(0) + chunk_reads(1):
            copy.start()
        for copy in reads + saved + loads[:0:-1] + loads[:1] + tile_reads:
            copy.start()

    pair_barrier(place)
    swap = place_rows(place, keep_ref, send_ref, rows_ref, sem_swap)
    for copy in swap:
        copy.start()
    handed = remote(left, given, sem_grad.at[0], sem_grad.at[1], device(z, x, c, 1 - y))

    sums[...] = jnp.zeros_like(sums)
    thin_d[...] = jnp.zeros_like(thin_d)
    thin_f[...] = jnp.zeros_like(thin_f)
    for buf in (dqb, dkb, dvb):
        buf[...] = jnp.zeros_like(buf)
    masks = head_masks()
    memory_row = lax.broadcasted_iota(jnp.int32, (THIN, 1), 0) < MEM
    row = lambda r: table_ref[r : r + 1, :]

    def add(r, value):
        sums[r : r + 1, :] += value

    def attend_at(i, carry):
        s, h = i // (HEADS // 2), lax.rem(i, HEADS // 2)
        lanes = pl.ds(pl.multiple_of(h * 2 * DH, 2 * DH), 2 * DH)
        pair = (buf[s, :, lanes] for buf in (qb, kb, vb, dcb))
        dq, dk, dv = attend_back_pair(*pair, logs[s, h])
        dqb[s, THIN:, lanes] = dq[THIN:]
        dqb[s, 0:THIN, lanes] = jnp.where(memory_row, dqb[s, 0:THIN, lanes], dq[0:THIN])
        dkb[s, :, lanes] = (dk + dkb[s, :, lanes].astype(F32)).astype(BF16)
        dvb[s, :, lanes] = (dv + dvb[s, :, lanes].astype(F32)).astype(BF16)
        return carry

    pairs = LOCAL * HEADS // 2

    def key_gradient(s):
        rows = jnp.concatenate([logs[s, h] for h in range(HEADS // 2)], axis=0)
        return memory_key_gradient(
            qb[s], kb[s, 0:THIN], vb[s, 0:THIN], dcb[s], cb[s], rows, masks
        )

    def slots(turn, grad):
        waited = set()

        def need(*copies):
            for copy in copies:
                if id(copy) not in waited:
                    waited.add(id(copy))
                    copy.wait()

        for s in reversed(range(LOCAL)):
            if turn == 1 and s == LOCAL - 1:
                grad = jnp.zeros((THIN, D), F32)
            else:
                after = place_ref[LOCAL * turn + s + 1]
                grad = jnp.where(memory_row, jnp.where(after > 0, grad, 0.0), 0.0)
                need(*saved)
                unit1, unit2 = save_d[s, 1].astype(F32), save_d[s, 2].astype(F32)
                base = HEADS * THIN
                log_total = save_s[s, 0:base, 0:1]
                inverse1 = save_s[s, base : base + THIN, 0:1]
                inverse2 = save_s[s, base + THIN :, 0:1]
                add(GAIN2, row_sum(grad * unit2))
                add(SHIFT2, row_sum(grad))
                second_grad = normalized_back(grad * row(GAIN2), unit2, inverse2)
                down_grad = second_grad.astype(BF16)
                add(DOWN_BIAS, row_sum(down_grad.astype(F32)))
                need(loads[2])
                up_grad = (nt(down_grad, wf[1]) * save_f[s, 1].astype(F32)).astype(BF16)
                up_sum = row_sum(up_grad.astype(F32))
                for i in range(FF // D):
                    add(UP_BIAS + i, up_sum[:, D * i : D * (i + 1)])
                need(loads[1])
                hidden_grad = second_grad + nn(up_grad, wf[0])
                add(GAIN1, row_sum(hidden_grad * unit1))
                add(SHIFT1, row_sum(hidden_grad))
                pre_grad = normalized_back(hidden_grad * row(GAIN1), unit1, inverse1)
                branch_grad = pre_grad.astype(BF16)
                add(OUT_BIAS, row_sum(branch_grad.astype(F32)))
                need(loads[0])
                context_grad = nn(branch_grad, wa[3]).astype(BF16)
                dc_heads = by_head(context_grad, masks)
                q_heads = by_head(qb[s, 0:THIN], masks)
                score = nt(q_heads, kb[s])
                share = jnp.exp(score - log_total) * copies_of(score.shape)
                share_grad = nt(dc_heads, vb[s])
                inner = jnp.sum(share_grad * share, axis=-1, keepdims=True)
                score_grad = (share * (share_grad - inner)).astype(BF16)
                query_grad = (own_columns(nn(score_grad, kb[s]), masks) * SCALE).astype(BF16)
                dkb[s] = (dkb[s].astype(F32) + tn(score_grad, q_heads)).astype(BF16)
                dvb[s] = (dvb[s].astype(F32) + tn(share.astype(BF16), dc_heads)).astype(BF16)
                dqb[s, 0:THIN] = jnp.where(memory_row, query_grad, dqb[s, 0:THIN])
                thin_d[s, 0] = down_grad
                thin_d[s, 1] = save_d[s, 0]
                thin_f[s, 0] = up_grad
                thin_f[s, 1] = save_f[s, 0]
                need(*tile_reads)
                for i, value in enumerate((branch_grad, save_d[s, 3])):
                    tiles[i, s] = jnp.where(memory_row, value, tiles[i, s])
                grad = pre_grad + nt(query_grad, wa[0])
            need(loads[0])
            dk, dv = dkb[s, 0:THIN], dvb[s, 0:THIN]
            if turn == 1:
                early_k, early_v = key_gradient(s)
                dk = (dk.astype(F32) + early_k).astype(BF16)
                dv = (dv.astype(F32) + early_v).astype(BF16)
            grad = grad + nt(dk, wa[1]) + nt(dv, wa[2])
            first = jnp.where(place_ref[LOCAL * turn + s] == 0, grad, 0.0)
            sums[FIRST_MEMORY : FIRST_MEMORY + THIN, :] += first
        return grad

    @pl.when(y == 1)
    def _():
        for copy in reads:
            copy.wait()
        left[...] = slots(1, None)
        handed.start()
        lax.fori_loop(0, pairs, attend_at, 0)

    @pl.when(y == 0)
    def _():
        for copy in reads:
            copy.wait()
        lax.fori_loop(0, pairs, attend_at, 0)
        handed.wait_recv()
        slots(0, given[...])

    writes = [
        pltpu.make_async_copy(dqb, dq_ref, sem_out.at[0]),
        pltpu.make_async_copy(dkb, dk_ref, sem_out.at[1]),
        pltpu.make_async_copy(dvb, dv_ref, sem_out.at[2]),
        pltpu.make_async_copy(sums, sums_ref, sem_out.at[3]),
        *[
            pltpu.make_async_copy(tiles.at[i], first_rows(ref), sem_out.at[5 + i])
            for i, ref in enumerate(merged)
        ],
    ]
    for copy in writes:
        copy.start()

    for copy in rows_in:
        copy.wait()
    for s in range(LOCAL):
        df[s, 0:THIN] = jnp.where(memory_row, thin_d[s, 0], df[s, 0:THIN])
        hid[s, 0:THIN] = jnp.where(memory_row, thin_d[s, 1], hid[s, 0:THIN])
    chunks = FF // CHUNK

    def store(i):
        lanes = pl.ds(pl.multiple_of(CHUNK * i, CHUNK), CHUNK)
        slot = lax.rem(i, 2)
        return pltpu.make_async_copy(
            staged.at[slot], terms_ref.at[:, lanes], sem_stage.at[slot]
        )

    def chunk(i, carry):
        slot = lax.rem(i, 2)
        for copy in chunk_reads(i):
            copy.wait()
        lanes = pl.ds(pl.multiple_of(CHUNK * i, CHUNK), CHUNK)
        for s in range(LOCAL):
            for j, buf in ((1, gb), (0, dub)):
                old = buf[slot, s, 0:THIN]
                buf[slot, s, 0:THIN] = jnp.where(memory_row, thin_f[s, j, :, lanes], old)

        @pl.when(i >= 2)
        def _():
            store(i - 2).wait()

        for j, (buf, rows) in enumerate(((dub, hid), (gb, df))):
            terms = tn(
                buf[slot].reshape(LOCAL * SEG, CHUNK), rows[...].reshape(LOCAL * SEG, D)
            )
            staged[slot, j] = terms.astype(BF16)
        store(i).start()

        @pl.when(i + 2 < chunks)
        def _():
            for copy in chunk_reads(i + 2):
                copy.start()

        return carry

    lax.fori_loop(0, chunks, chunk, 0)

    @pl.when(y == 1)
    def _():
        handed.wait_send()

    for copy in [*writes, store(chunks - 2), store(chunks - 1)]:
        copy.wait()
    for copy in swap:
        copy.wait()


THIN_SHAPES = (
    sds((LOCAL, 2, THIN, D), BF16),
    sds((LOCAL, 2, THIN, FF), BF16),
    sds((FIRST_MEMORY + THIN, D), F32),
)


def chain_back(place, table, attn, ffn, q, k, v, saved, g, du, df, h, halves, dc, logs, da, c):
    whole = sds((LOCAL, SEG, D), BF16)
    rows = pltpu.VMEM(whole.shape, BF16)
    dma = lambda *shape: pltpu.SemaphoreType.DMA(shape)
    outs = pl.pallas_call(
        chain_back_kernel,
        in_specs=[SMEM, VMEM] + [ANY] * 18,
        out_specs=[ANY] * 8,
        out_shape=[whole] * 5
        + [THIN_SHAPES[2]]
        + [sds((2, FF, D), BF16), sds((2 * LOCAL, *halves[0].shape[1:]), BF16)],
        input_output_aliases={18: 0, 19: 1},
        scratch_shapes=[
            pltpu.VMEM((4, D, D), BF16),
            pltpu.VMEM((2, FF, D), BF16),
            *[rows] * 5,
            pltpu.VMEM(logs.shape, F32),
            rows,
            rows,
            rows,
            pltpu.VMEM((2, LOCAL, THIN, D), BF16),
            rows,
            rows,
            pltpu.VMEM((2, LOCAL, SEG, CHUNK), BF16),
            pltpu.VMEM((2, LOCAL, SEG, CHUNK), BF16),
            pltpu.VMEM((2, 2, CHUNK, D), BF16),
            *[pltpu.VMEM(s.shape, s.dtype) for s in SAVED + THIN_SHAPES],
            pltpu.VMEM((THIN, D), F32),
            pltpu.VMEM((THIN, D), F32),
            dma(3),
            dma(11),
            dma(2),
            dma(2, 2),
            dma(8),
            dma(2),
            dma(2),
            dma(3),
        ],
        name="chain_back",
        compiler_params=params(collective_id=3, has_side_effects=True),
    )(place, table, attn, ffn, q, k, v, *saved, g, du, df, h, *halves, dc, logs, da, c)
    return outs


def table_row(ref, index, entries):
    blocks = []
    lane = lax.broadcasted_iota(jnp.int32, (1, 128), 1)
    for block in range(D // 128):
        at, end = index * D + 128 * block, index * D + 128 * (block + 1)
        target, value = 0, jnp.zeros((1, 128), F32)
        while at < end:
            shard, inner = at // entries, at % entries
            count = min(end - at, entries - inner, 128 - inner % 128)
            place = (shard // 8, shard // 4 % 2, shard // 2 % 2, shard % 2)
            source = ref[place][inner // 128 : inner // 128 + 1]
            shift = (target - inner) % 128
            if shift:
                source = pltpu.roll(source, shift, 1)
            value = jnp.where((lane >= target) & (lane < target + count), source, value)
            at, target = at + count, target + count
        blocks.append(value)
    return jnp.concatenate(blocks, axis=1)


def head_kernel(
    nz,
    entries,
    attn_src,
    ffn_src,
    vec_src,
    tokens,
    attn_ref,
    ffn_ref,
    vec_ref,
    x_ref,
    q_ref,
    k_ref,
    v_ref,
    c_ref,
    log_ref,
    wa,
    vec,
    mine,
    other,
    xb,
    qb,
    kb,
    vb,
    cb,
    logs,
    send_sem,
    recv_sem,
    own_sem,
    swap_sem,
    out_sem,
):
    place = my_place()
    side = place[3]
    halves = swap_halves(place, tokens, other, swap_sem)
    own = [
        pltpu.make_async_copy(attn_src, attn_view(wa, *place), own_sem.at[0]),
        pltpu.make_async_copy(vec_src, vec_view(vec, *place), own_sem.at[1]),
        pltpu.make_async_copy(ffn_src, ffn_view(ffn_ref, *place), own_sem.at[2]),
        pltpu.make_async_copy(tokens.at[pl.ds(LOCAL * side, LOCAL)], mine, own_sem.at[3]),
    ]
    for copy in own:
        copy.start()
    entry_barrier(nz)
    steps = functools.partial(gather_steps, nz, place, send_sem=send_sem, recv_sem=recv_sem)
    begin, step, end_arrive, end_send = steps(
        1, True, [(0, wa, attn_view), (1, vec, vec_view)]
    )
    late = [
        steps(place[2], bool(i), [(2 + i, ffn_ref.at[i], hidden_view)]) for i in range(2)
    ]
    own[0].wait()
    own[1].wait()
    begin()
    halves.start()

    def loop(t, carry):
        step(t)
        return carry

    lax.fori_loop(1, nz + 2, loop, 0)
    own[2].wait()
    for begin2, _, _, _ in late:
        begin2()
    own[3].wait()
    halves.wait()
    end_arrive()
    outs = [
        pltpu.make_async_copy(wa, attn_ref, out_sem.at[0]),
        pltpu.make_async_copy(vec, vec_ref, out_sem.at[1]),
    ]
    for copy in outs:
        copy.start()

    weight = lambda i: wa[i].reshape(D, D)

    def project_slot(s):
        x = whole_rows(side, mine[s], other[s]).astype(BF16)
        xb[s] = x
        qb[s] = ((nn(x, weight(0)) + table_row(vec, QUERY_BIAS, entries)) * SCALE).astype(BF16)
        kb[s] = nn(x, weight(1)).astype(BF16)
        vb[s] = (nn(x, weight(2)) + table_row(vec, VALUE_BIAS, entries)).astype(BF16)
        for i, (buf, out) in enumerate(((xb, x_ref), (qb, q_ref), (kb, k_ref), (vb, v_ref))):
            outs.append(pltpu.make_async_copy(buf.at[s], out.at[s], out_sem.at[2 + 4 * s + i]))
            outs[-1].start()

    def attend_at(i, carry):
        s, h = i // (HEADS // 2), i % (HEADS // 2)
        lanes = pl.ds(pl.multiple_of(h * 2 * DH, 2 * DH), 2 * DH)
        context, log_rows = attend_pair(qb[s, :, lanes], kb[s, :, lanes], vb[s, :, lanes])
        cb[s, :, lanes] = context
        for head in range(2):
            logs[s, h, head : head + 1] = log_rows[head]
        return carry

    project_slot(0)
    project_slot(1)
    pairs = LOCAL * HEADS // 2
    done = 0
    for t in range(1, nz + 2):
        for _, step2, _, _ in late:
            step2(t)
        upto = pairs * t // (nz + 1)
        lax.fori_loop(done, upto, attend_at, 0)
        done = upto
    outs.append(pltpu.make_async_copy(cb, c_ref, out_sem.at[2 + 4 * LOCAL]))
    outs.append(pltpu.make_async_copy(logs, log_ref, out_sem.at[3 + 4 * LOCAL]))
    outs[-1].start()
    outs[-2].start()
    end_send()
    for _, _, end_arrive2, end_send2 in late:
        end_send2()
        end_arrive2()
    for copy in outs:
        copy.wait()


def head(nz, attention, hidden_major, vec, tokens, entries):
    rows, hidden = attention.shape[1], hidden_major.shape[1]
    whole = sds((LOCAL, SEG, D), BF16)
    logs = (LOCAL, HEADS // 2, 2, SEG)
    attn_shape, vec_shape = (4, nz, 2, 2, rows, D), (nz, 2, 2, 2, *VEC_TILE)
    half = pltpu.VMEM((LOCAL, *tokens.shape[1:]), BF16)
    return pl.pallas_call(
        functools.partial(head_kernel, nz, entries),
        in_specs=[ANY] * 4,
        out_specs=[ANY] * 9,
        out_shape=[
            sds(attn_shape, BF16),
            sds((2, nz, 2, 2, 2, hidden, D), BF16),
            sds(vec_shape, F32),
            *[whole] * 5,
            sds(logs, F32),
        ],
        scratch_shapes=[
            pltpu.VMEM(attn_shape, BF16),
            pltpu.VMEM(vec_shape, F32),
            half,
            half,
            *[pltpu.VMEM(whole.shape, BF16)] * 5,
            pltpu.VMEM(logs, F32),
            pltpu.SemaphoreType.DMA((11, nz, 4)),
            pltpu.SemaphoreType.DMA((8, nz, 4)),
            pltpu.SemaphoreType.DMA((4,)),
            pltpu.SemaphoreType.DMA((2,)),
            pltpu.SemaphoreType.DMA((4 + 4 * LOCAL,)),
        ],
        name="head",
        compiler_params=params(collective_id=0, has_side_effects=True),
    )(attention, hidden_major, vec, tokens)


def token_grad_kernel(place_ref, da_ref, dq_ref, dk_ref, dv_ref, w_ref, keep_ref, send_ref):
    side = lax.axis_index("tensor")
    total = da_ref[0].astype(F32)
    for i, ref in enumerate((dq_ref, dk_ref, dv_ref)):
        total = total + nt(ref[0], w_ref[i])
    live = place_ref[LOCAL * side + pl.program_id(0)] >= 0
    keep, send = split_rows(side, jnp.where(live, total, 0.0))
    keep_ref[0] = keep.astype(BF16)
    send_ref[0] = send.astype(BF16)


def token_gradient(place, da, dq, dk, dv, attn):
    half = (SEG - MEM) // 2
    return pl.pallas_call(
        token_grad_kernel,
        grid=(LOCAL,),
        in_specs=[SMEM] + [slot_rows()] * 4 + [once((3, D, D), (0, 0, 0))],
        out_specs=[half_rows(half)] * 2,
        out_shape=[sds((LOCAL, half, D), BF16)] * 2,
        name="token_gradient",
        compiler_params=params(),
    )(place, da, dq, dk, dv, attn)


def flat(ref):
    return ref[...].reshape(LOCAL * ref.shape[1], ref.shape[2])


def attn_grad_kernel(
    x_ref, da_ref, dq_ref, dk_ref, dv_ref, c_ref, sums_ref, thin_sums_ref, out_ref, vec_ref
):
    x = flat(x_ref)
    dq, dv = flat(dq_ref), flat(dv_ref)
    out_ref[0] = tn(x, dq).astype(BF16)
    out_ref[1] = tn(x, flat(dk_ref)).astype(BF16)
    out_ref[2] = tn(x, dv).astype(BF16)
    out_ref[3] = tn(flat(da_ref), flat(c_ref)).astype(BF16)
    vec_ref[...] = thin_sums_ref[...]
    vec_ref[0:FIRST_MEMORY] = thin_sums_ref[0:FIRST_MEMORY] + sums_ref[0:FIRST_MEMORY]
    vec_ref[QUERY_BIAS : QUERY_BIAS + 1] = row_sum(dq.astype(F32))
    vec_ref[VALUE_BIAS : VALUE_BIAS + 1] = row_sum(dv.astype(F32))


def attn_gradient(x, da, dq, dk, dv, c, sums, thin_sums, chunk=256):
    part = pl.BlockSpec((LOCAL, SEG, chunk), lambda i: (0, 0, i))
    full = once((LOCAL, SEG, D), (0, 0, 0))
    lanes = lambda rows: pl.BlockSpec((rows, chunk), lambda i: (0, i))
    return pl.pallas_call(
        attn_grad_kernel,
        grid=(D // chunk,),
        in_specs=[full, full, part, part, part, part, lanes(THIN), lanes(FIRST_MEMORY + THIN)],
        out_specs=[
            pl.BlockSpec((4, D, chunk), lambda i: (0, 0, i)),
            lanes(FIRST_MEMORY + THIN),
        ],
        out_shape=[sds((4, D, D), BF16), sds((FIRST_MEMORY + THIN, D), F32)],
        name="attn_gradient",
        compiler_params=params(),
    )(x, da, dq, dk, dv, c, sums, thin_sums)


def scatter_steps(nz, place, lead, z_second, pieces, send_sem, recv_sem):
    z, x, c, y = place
    first, second, both = partners(place, lead)
    to_first = device(z, first[0], c, first[1])
    to_second = device(z, second[0], c, second[1])
    to_core = device(z, x, 1 - c, y)
    f_first, f_second = 2 - lead, 1 + lead

    def at(f):
        fx, fy = f // 2, f % 2
        return x + fx * (1 - 2 * x), y + fy * (1 - 2 * y)

    def term(piece, zz, core, f):
        xx, yy = at(f)
        return piece[2](piece[1], zz, xx, core, yy)

    def copies(kind, zz, target, src, dst):
        return [
            remote(src(p), dst(p), send_sem.at[kind, zz, p[0]], recv_sem.at[kind, zz, p[0]], target)
            for p in pieces
        ]

    def core_copies(zz, f):
        return copies(
            f, zz, to_core, lambda p: term(p, zz, 1 - c, f), lambda p: p[3].at[zz, f]
        )

    def second_copies(zz, across):
        f = 3 if across else f_second
        return copies(
            4 + across, zz, to_second, lambda p: p[3].at[zz, f], lambda p: p[4].at[zz, across]
        )

    def first_copies(zz):
        slot = 0 if z_second else zz
        return copies(6, zz, to_first, lambda p: p[4].at[zz, 1], lambda p: p[5].at[slot])

    def partial(p, zz, f):
        return p[4].at[zz, f] if z_second else p[5].at[zz]

    def beside(p, above, zz, f):
        return p[6 + above].at[zz, f] if z_second else p[6 + above].at[zz]

    def up_copies(zz, f):
        return copies(
            7 + 2 * f,
            zz,
            device(z + 1, x, c, y),
            lambda p: partial(p, zz, f),
            lambda p: beside(p, 0, zz, f),
        )

    def down_copies(zz, f):
        return copies(
            8 + 2 * f,
            zz,
            device(z - 1, x, c, y),
            lambda p: partial(p, zz, f),
            lambda p: beside(p, 1, zz, f),
        )

    def run(group, what):
        for copy in group:
            getattr(copy, what)()

    def add(into, other):
        for p in pieces:
            a, b = into(p), other(p)
            a[...] = (a[...].astype(F32) + b[...].astype(F32)).astype(a.dtype)

    def turn(k):
        upper = z // (nz // 2)
        return (1 - upper) * (nz - 1 - k) + upper * k

    def start(zz):
        for f in (3, 1, 2, 0):
            run(core_copies(zz, f), "start")

    def stage0(zz):
        for f in (3, 1, 2, 0):
            run(core_copies(zz, f), "wait_recv")
            add(lambda p: p[3].at[zz, f], lambda p: term(p, zz, c, f))
        run(second_copies(zz, 1), "start")
        run(second_copies(zz, 0), "start")

    def from_below(zz, f):
        run(up_copies(zz, f), "wait_recv")
        add(lambda p: partial(p, zz, f), lambda p: beside(p, 0, zz, f))

    def from_above(zz, f):
        run(down_copies(zz, f), "wait_recv")
        add(lambda p: partial(p, zz, f), lambda p: beside(p, 1, zz, f))

    def along(zz, f):
        @pl.when(zz > z)
        def _():
            @pl.when(z > 0)
            def _():
                from_below(zz, f)

            run(up_copies(zz, f), "start")

        @pl.when(zz < z)
        def _():
            @pl.when(z < nz - 1)
            def _():
                from_above(zz, f)

            run(down_copies(zz, f), "start")

    def stage1(zz):
        run(second_copies(zz, 1), "wait_recv")
        add(lambda p: p[4].at[zz, 1], lambda p: p[3].at[zz, f_first])
        if z_second:
            along(zz, 1)
        else:
            run(first_copies(zz), "start")

    def stage2(zz):
        run(second_copies(zz, 0), "wait_recv")
        add(lambda p: p[4].at[zz, 0], lambda p: p[3].at[zz, 0])
        if not z_second:
            run(first_copies(zz), "wait_recv")
            add(lambda p: p[5].at[zz], lambda p: p[4].at[zz, 0])
        along(zz, 0)

    def staged(stage):
        return lambda k: stage(turn(k))

    def at_owner(f):
        @pl.when(z > 0)
        def _():
            from_below(z, f)

        @pl.when(z < nz - 1)
        def _():
            from_above(z, f)

    def end(outs):
        if z_second:
            at_owner(1)
            run(first_copies(z), "start")
        at_owner(0)
        if z_second:
            run(first_copies(z), "wait_recv")
            add(lambda p: p[4].at[z, 0], lambda p: p[5].at[0])
        for p, out in zip(pieces, outs):
            out[...] = partial(p, z, 0)[...]

    def sent(zz, carry):
        for f in range(4):
            run(core_copies(zz, f), "wait_send")
        run(second_copies(zz, 1), "wait_send")
        run(second_copies(zz, 0), "wait_send")
        for f in range(2 if z_second else 1):

            @pl.when(zz > z)
            def _():
                run(up_copies(zz, f), "wait_send")

            @pl.when(zz < z)
            def _():
                run(down_copies(zz, f), "wait_send")

        if z_second:

            @pl.when(zz == z)
            def _():
                run(first_copies(zz), "wait_send")

        else:
            run(first_copies(zz), "wait_send")
        return carry

    stages = [staged(stage) for stage in (stage0, stage1, stage2)]
    return start, stages, turn, end, lambda: lax.fori_loop(0, nz, sent, 0)


def scatter_places(nz, shape, z_second):
    lead = (nz, 2) if z_second else (nz,)
    return [
        pltpu.VMEM((nz, 4, *shape), BF16),
        pltpu.VMEM((nz, 2, *shape), BF16),
        pltpu.VMEM((1 if z_second else nz, *shape), BF16),
        pltpu.VMEM((*lead, *shape), BF16),
        pltpu.VMEM((*lead, *shape), BF16),
    ]


VEC_ROWS = FIRST_MEMORY + THIN


def tail_kernel(nz, *refs):
    (
        place_ref,
        sums_ref,
        thin_sums_ref,
        ffn_terms,
        *rows_refs,
        w_ref,
        attn_out,
        ffn_out,
        vec_out,
        grad_ref,
        terms_f,
        terms_a,
        rows,
        wb,
        keep,
        send,
    ) = refs[:21]
    places = [refs[21 + 5 * i : 26 + 5 * i] for i in range(3)]
    vec_mine, vec_given, vec_z, send_sem, recv_sem, block_sem, in_sem, swap_sem, vec_sem = refs[36:]
    place = z, x, c, y = my_place()
    blocks = lambda zz: pltpu.make_async_copy(
        ffn_terms.at[:, zz], terms_f.at[:, zz], block_sem.at[zz]
    )
    rows_in = [
        pltpu.make_async_copy(src, rows.at[i], in_sem.at[2 + i]) for i, src in enumerate(rows_refs)
    ]
    rows_in.append(pltpu.make_async_copy(w_ref.at[pl.ds(0, 3)], wb, in_sem.at[8]))
    steps = functools.partial(scatter_steps, nz, place, send_sem=send_sem, recv_sem=recv_sem)
    up = steps(c, False, [(0, terms_f.at[0], hidden_view, *places[0])])
    down = steps(1 - c, True, [(1, terms_f.at[1], hidden_view, *places[1])])
    attn = steps(1 - c, True, [(2, terms_a, attn_view, *places[2])])
    turn = up[2]
    for k in range(nz):
        blocks(turn(k)).start()
    for copy in rows_in:
        copy.start()

    barrier = pltpu.get_barrier_semaphore()
    others = [device(lax.rem(z + dz, nz), x, c, y) for dz in range(1, nz)]
    for other in [device(z, 1 - x, c, y), device(z, x, 1 - c, y), device(z, x, c, 1 - y), *others]:
        pl.semaphore_signal(
            barrier, inc=1, device_id=other, device_id_type=pl.DeviceIdType.MESH
        )
    pl.semaphore_wait(barrier, 2 + nz)

    def begin(k, carry):
        zz = turn(k)
        blocks(zz).wait()
        up[0](zz)
        down[0](zz)
        return carry

    def attn_terms(i, carry):
        left, right = rows[i // 3], rows[i + 2]
        value = tn(left.reshape(LOCAL * SEG, D), right.reshape(LOCAL * SEG, D))
        terms_a[i] = value.astype(BF16).reshape(terms_a.shape[1:])
        return carry

    def token_rows(s):
        total = rows[1, s].astype(F32)
        for i in range(3):
            total = total + nt(rows[2 + i, s], wb[i])
        live = place_ref[LOCAL * y + s] >= 0
        stay, go = split_rows(y, jnp.where(live, total, 0.0))
        keep[s] = stay.astype(BF16)
        send[s] = go.astype(BF16)

    def vec_copies(phase):
        if phase < 3:
            target = (device(z, x, 1 - c, y), device(z, x, c, 1 - y), device(z, 1 - x, c, y))[phase]
            sems = vec_sem.at[0, phase], vec_sem.at[1, phase]
            return [remote(vec_mine.at[phase], vec_given.at[phase], *sems, target)]
        return [
            remote(
                vec_mine.at[3], vec_z.at[dz], vec_sem.at[0, 3 + dz], vec_sem.at[1, 3 + dz], target
            )
            for dz, target in enumerate(others)
        ]

    def vec_start(phase):
        if phase == 0:
            vec_mine[0] = thin_sums_ref[...]
            vec_mine[0, 0:FIRST_MEMORY] = (
                thin_sums_ref[0:FIRST_MEMORY] + sums_ref[0:FIRST_MEMORY]
            )
            for r, i in ((QUERY_BIAS, 2), (VALUE_BIAS, 4)):
                total = row_sum(rows[i].reshape(LOCAL * SEG, D).astype(F32))
                vec_mine[0, r : r + 1] = total
        else:
            for copy in vec_copies(phase - 1):
                copy.wait_recv()
            vec_mine[phase] = vec_mine[phase - 1] + vec_given[phase - 1]
        for copy in vec_copies(phase):
            copy.start()

    swap = place_rows(place, keep, send, grad_ref, swap_sem)

    def stage(i, *groups):
        for k in groups[-1]:
            for group in groups[:-1]:
                group[1][i](k)

    def step(k, *groups):
        for lag in range(3):
            if 0 <= k - lag < nz:
                stage(lag, *groups, (k - lag,))

    lax.fori_loop(0, 1, begin, 0)
    for k in range(nz):
        if k + 1 < nz:
            lax.fori_loop(k + 1, k + 2, begin, 0)
        step(k, up, down)
        if k == 0:
            for copy in rows_in:
                copy.wait()
        if k < 2:
            lax.fori_loop(2 * k, 2 * k + 2, attn_terms, 0)
        if k == 1:
            vec_start(0)
        if k == 2:
            token_rows(0)
            vec_start(1)
        if k == 3:
            token_rows(1)
        if k >= 1:
            attn[0](turn(k - 1))
        if k >= 2:
            step(k - 2, attn)
    for copy in swap:
        copy.start()
    attn[0](turn(nz - 1))
    step(nz, up, down)
    vec_start(2)
    step(2, attn)
    step(nz + 1, up, down)
    vec_start(3)
    step(3, attn)
    up[3]([ffn_out.at[0]])
    step(4, attn)
    down[3]([ffn_out.at[1]])
    step(5, attn)
    attn[3]([attn_out])
    total = vec_mine[3]
    for dz, copy in enumerate(vec_copies(3)):
        copy.wait_recv()
        total = total + vec_z[dz]
    vec_out[...] = total
    for phase in range(4):
        for copy in vec_copies(phase):
            copy.wait_send()
    for group in (up, down, attn):
        group[4]()
    for copy in swap:
        copy.wait()


def tail(place, sums, thin_sums, ffn_terms, x, da, dq, dk, dv, c, attn, shapes):
    nz = lax.axis_size("dp") // 4
    rows, hidden, half = shapes
    attn_shape, ffn_shape = (4, nz, 2, 2, rows, D), (2, nz, 2, 2, 2, hidden, D)
    part = pltpu.VMEM((LOCAL, half, D), BF16)
    dma = lambda *shape: pltpu.SemaphoreType.DMA(shape)
    return pl.pallas_call(
        functools.partial(tail_kernel, nz),
        in_specs=[SMEM, VMEM, VMEM] + [ANY] * 8,
        out_specs=[VMEM] * 3 + [ANY],
        out_shape=[
            sds((4, rows, HALF), BF16),
            sds((2, hidden, D), BF16),
            sds((VEC_ROWS, D), F32),
            sds((2 * LOCAL, half, D), BF16),
        ],
        scratch_shapes=[
            pltpu.VMEM(ffn_shape, BF16),
            pltpu.VMEM(attn_shape, BF16),
            pltpu.VMEM((6, LOCAL, SEG, D), BF16),
            pltpu.VMEM((3, D, D), BF16),
            part,
            part,
            *scatter_places(nz, (hidden, D), False),
            *scatter_places(nz, (hidden, D), True),
            *scatter_places(nz, (4, rows, HALF), True),
            pltpu.VMEM((4, VEC_ROWS, D), F32),
            pltpu.VMEM((3, VEC_ROWS, D), F32),
            pltpu.VMEM((nz - 1, VEC_ROWS, D), F32),
            dma(11, nz, 3),
            dma(11, nz, 3),
            dma(nz),
            dma(9),
            dma(3),
            dma(2, 2 + nz),
        ],
        name="tail",
        compiler_params=params(62, collective_id=1, has_side_effects=True),
    )(place, sums, thin_sums, ffn_terms.reshape(ffn_shape), x, da, dq, dk, dv, c, attn)


def update(gradient, momentum, weight, average, rate, grad_scale):
    scaled = gradient * grad_scale
    moment = MOMENTUM * momentum + scaled
    weight_new = weight - rate * (scaled + MOMENTUM * moment)
    return (moment, weight_new, AVERAGE_DECAY * average + (1.0 - AVERAGE_DECAY) * weight_new)


VEC_TILE = (8, 128)


def in_tiles(rows):
    size = VEC_TILE[0] * VEC_TILE[1]
    padded = jnp.pad(rows, [(0, 0)] * (rows.ndim - 1) + [(0, size - rows.shape[-1])])
    return padded.reshape(*rows.shape[:-1], *VEC_TILE)


def start(attention, feedforward, vectors, tokens):
    nz = lax.axis_size("dp") // 4
    rows, hidden, entries = attention.shape[1], feedforward.shape[2], vectors.shape[0]
    attention = attention.astype(BF16)
    hidden_major = jnp.swapaxes(feedforward.astype(BF16), 1, 2)
    vec = in_tiles(vectors.astype(BF16).astype(F32))
    aligned = rows % THIN == 0
    if aligned:
        attn, ffn, table, *work = head(nz, attention, hidden_major, vec, tokens, entries)
    else:
        attn, ffn, table, other = gather(
            nz,
            0,
            [
                (attention, (4, nz, 2, 2, rows, D), attn_view),
                (hidden_major, (2, nz, 2, 2, 2, hidden, D), ffn_view),
                (vec, (nz, 2, 2, 2, *VEC_TILE), vec_view),
            ],
            tokens,
        )
    attn, ffn = attn.reshape(4, D, D), ffn.reshape(2, FF, D)
    table = table.reshape(nz * 8, VEC_TILE[0] * VEC_TILE[1])[:, :entries].reshape(NVEC, D)
    if not aligned:
        work = project(tokens, other, attn, table)
        work = [*work, *attend(*work[1:])]
    return attn, ffn, table, work


def scatter_gradients(attn_terms, ffn_terms, vec_terms, shapes):
    nz = lax.axis_size("dp") // 4
    rows, hidden, entries = shapes
    attn, ffn, vec = scatter(
        nz,
        1,
        [
            (attn_terms.reshape(4, nz, 2, 2, rows, D), (4, rows, HALF), attn_view),
            (ffn_terms.reshape(2, nz, 2, 2, 2, hidden, D), (2, hidden, D), ffn_view),
            (in_tiles(vec_terms.reshape(nz, 2, 2, 2, entries)), VEC_TILE, vec_view),
        ],
    )
    return attn.astype(F32), jnp.swapaxes(ffn, 1, 2).astype(F32), vec.reshape(-1)[:entries]


def swap(value):
    return lax.ppermute(value, "tensor", [(0, 1), (1, 0)])


def joined_kernel(keep_ref, other_ref, out_ref, sem):
    side = lax.axis_index("tensor")
    copies = [
        pltpu.make_async_copy(keep_ref, out_ref.at[pl.ds(LOCAL * side, LOCAL)], sem.at[0]),
        pltpu.make_async_copy(other_ref, out_ref.at[pl.ds(LOCAL * (1 - side), LOCAL)], sem.at[1]),
    ]
    for c in copies:
        c.start()
    for c in copies:
        c.wait()


def joined(keep, other):
    return pl.pallas_call(
        joined_kernel,
        in_specs=[ANY] * 2,
        out_specs=ANY,
        out_shape=sds((2 * LOCAL, *keep.shape[1:]), keep.dtype),
        scratch_shapes=[pltpu.SemaphoreType.DMA((2,))],
        name="joined",
        compiler_params=params(16),
    )(keep, other)


def on_device(
    tokens,
    slot_position,
    cotangent,
    attention,
    feedforward,
    vectors,
    attn_momentum,
    ffn_momentum,
    vec_momentum,
    attn_average,
    ffn_average,
    vec_average,
):
    place = slot_position
    attn, ffn, table, work = start(attention, feedforward, vectors, tokens)
    x, q, k, v, c, log_tokens = work

    (x, q, k, v), saved, cot_other = chain(place, table, attn, ffn, x, q, k, v, cotangent)
    keep, send, h, g, du, df, da, dc, c, log_total, sums = rows_part(
        place, x, q, k, v, c, log_tokens, cotangent, cot_other, attn, ffn, table
    )
    da, c, dq, dk, dv, thin_sums, ffn_terms, activations = chain_back(
        place, table, attn, ffn, q, k, v, saved, g, du, df, h, (keep, send), dc, log_total, da, c
    )
    rows, hidden, entries = attention.shape[1], feedforward.shape[2], vectors.shape[0]
    if rows % THIN == 0:
        shapes = (rows, hidden, tokens.shape[1])
        attn_grad, ffn_grad, vec_sums, token_grad = tail(
            place, sums, thin_sums, ffn_terms, x, da, dq, dk, dv, c, attn, shapes
        )
        attn_grad = attn_grad.astype(F32)
        ffn_grad = jnp.swapaxes(ffn_grad, 1, 2).astype(F32)
        index = lax.axis_index("dp") * 2 + lax.axis_index("tensor")
        vec_grad = lax.dynamic_slice_in_dim(
            vec_sums[:NVEC].reshape(-1), index * entries, entries
        )
    else:
        keep, send = token_gradient(place, da, dq, dk, dv, attn)
        token_grad = joined(keep, swap(send))
        attn_terms, vec_terms = attn_gradient(x, da, dq, dk, dv, c, sums, thin_sums)
        attn_grad, ffn_grad, vec_grad = scatter_gradients(
            attn_terms, ffn_terms, vec_terms[:NVEC], (rows, hidden, entries)
        )
    grad_scale = 1.0 / math.sqrt(lax.axis_size("dp") * SLOTS * ROWS)
    attn_new = update(attn_grad, attn_momentum, attention, attn_average, ATTENTION_RATE, grad_scale)
    ffn_new = update(ffn_grad, ffn_momentum, feedforward, ffn_average, FEEDFORWARD_RATE, grad_scale)
    vec_new = update(vec_grad, vec_momentum, vectors, vec_average, VECTOR_RATE, grad_scale)
    return (
        activations,
        token_grad,
        attn_new[0],
        ffn_new[0],
        vec_new[0],
        attn_new[1],
        ffn_new[1],
        vec_new[1],
        attn_new[2],
        ffn_new[2],
        vec_new[2],
    )


def solution(mesh):
    attn_spec = P(None, "dp", "tensor")
    ffn_spec = P(None, None, ("dp", "tensor"))
    vec_spec = P(("dp", "tensor"))
    rows_spec = P("dp", "tensor", None)
    states = (attn_spec, ffn_spec, vec_spec)
    return jax.shard_map(
        on_device,
        mesh=mesh,
        in_specs=(rows_spec, P("dp"), rows_spec) + states * 3,
        out_specs=(rows_spec, rows_spec) + states * 3,
        check_vma=False,
    )
```

```python
import functools
import math

import jax
import jax.numpy as jnp
from jax import lax
from jax.experimental import pallas as pl
from jax.experimental.pallas import tpu as pltpu
from jax.sharding import PartitionSpec as P

D = 768
HEADS = 12
DH = 64
FF = 3072
MEM = 10
SLOTS = 4
ROWS = 522
NVEC = 22

HALF = D // 2
SEG = ROWS - MEM
THIN = 16
LOCAL = 2
TILE = 256

EPSILON = 1e-05
MOMENTUM = 0.9
AVERAGE_DECAY = 0.75
ATTENTION_RATE = 0.06
FEEDFORWARD_RATE = 0.02
VECTOR_RATE = 0.1
MASK_VALUE = -1e30
SCALE = 1.0 / math.sqrt(DH)

F32 = jnp.float32
BF16 = jnp.bfloat16
MIB = 1 << 20

QUERY_BIAS, VALUE_BIAS, OUT_BIAS, GAIN1, SHIFT1, DOWN_BIAS, GAIN2, SHIFT2, UP_BIAS = range(9)
FIRST_MEMORY = UP_BIAS + FF // D


def nn(a, b):
    return lax.dot_general(a, b, (((1,), (0,)), ((), ())), preferred_element_type=F32)


def nt(a, b):
    return lax.dot_general(a, b, (((1,), (1,)), ((), ())), preferred_element_type=F32)


def tn(a, b):
    return lax.dot_general(a, b, (((0,), (0,)), ((), ())), preferred_element_type=F32)


def normalized(rows):
    center = rows - jnp.mean(rows, axis=-1, keepdims=True)
    spread = jnp.mean(center * center, axis=-1, keepdims=True)
    inverse = lax.rsqrt(spread + EPSILON)
    return center * inverse, inverse


def normalized_back(grad, unit, inverse):
    mean_grad = jnp.mean(grad, axis=-1, keepdims=True)
    mean_along = jnp.mean(grad * unit, axis=-1, keepdims=True)
    return inverse * (grad - mean_grad - unit * mean_along)


def gelu_parts(u):
    size = jnp.abs(u)
    t = 1.0 / (1.0 + (0.3275911 / math.sqrt(2.0)) * size)
    bell = jnp.exp(-0.5 * u * u)
    poly = t * (
        0.5 * 0.254829592
        + t
        * (
            0.5 * -0.284496736
            + t * (0.5 * 1.421413741 + t * (0.5 * -1.453152027 + t * (0.5 * 1.061405429)))
        )
    )
    tail = poly * bell
    cdf = jnp.where(u < 0, tail, 1.0 - tail)
    return u * cdf, cdf + (u * (1.0 / math.sqrt(2.0 * math.pi))) * bell


def row_sum(block):
    return jnp.sum(block, axis=0, keepdims=True)


def params(limit=60, **more):
    return pltpu.CompilerParams(vmem_limit_bytes=limit * MIB, **more)


def once(shape, index):
    return pl.BlockSpec(shape, lambda *_: index, pipeline_mode=pl.Buffered(1))


ANY = pl.BlockSpec(memory_space=pltpu.HBM)
SMEM = pl.BlockSpec(memory_space=pltpu.SMEM)
VMEM = pl.BlockSpec(memory_space=pltpu.VMEM)


def sds(shape, dtype):
    return jax.ShapeDtypeStruct(shape, dtype)


def my_place():
    dp = lax.axis_index("dp")
    return dp // 4, (dp // 2) % 2, dp % 2, lax.axis_index("tensor")


def device(z, x, c, y):
    return {"dp": (z * 2 + x) * 2 + c, "tensor": y}


def entry_barrier(nz):
    z, x, c, y = my_place()
    barrier = pltpu.get_barrier_semaphore()
    signal = lambda d: pl.semaphore_signal(
        barrier, inc=1, device_id=d, device_id_type=pl.DeviceIdType.MESH
    )
    signal(device(z, 1 - x, c, y))
    signal(device(z, x, 1 - c, y))
    signal(device(z, x, c, 1 - y))

    @pl.when(z > 0)
    def _():
        signal(device(z - 1, x, c, y))

    @pl.when(z < nz - 1)
    def _():
        signal(device(z + 1, x, c, y))

    up = lax.convert_element_type(z < nz - 1, jnp.int32)
    down = lax.convert_element_type(z > 0, jnp.int32)
    pl.semaphore_wait(barrier, 3 + up + down)


def attn_view(ref, z, x, c, y):
    return ref.at[:, z, x, c, :, pl.ds(pl.multiple_of(y * HALF, HALF), HALF)]


def ffn_view(ref, z, x, c, y):
    return ref.at[:, z, x, c, y]


def vec_view(ref, z, x, c, y):
    return ref.at[z, x, c, y]


def hidden_view(ref, z, x, c, y):
    return ref.at[z, x, c, y]


def partners(place, lead):
    _, x, _, y = place
    first = (x + (1 - lead) * (1 - 2 * x), y + lead * (1 - 2 * y))
    second = (x + lead * (1 - 2 * x), y + (1 - lead) * (1 - 2 * y))
    return first, second, (1 - x, 1 - y)


COLUMN, FIRST, SECOND, BOTH, CORE = 0, 1, 2, 3, 4
UP, DOWN, UP_FIRST, DOWN_FIRST = 0, 8, 9, 10


def remote(src, dst, send_sem, recv_sem, target):
    return pltpu.make_async_remote_copy(
        src_ref=src,
        dst_ref=dst,
        send_sem=send_sem,
        recv_sem=recv_sem,
        device_id=target,
        device_id_type=pl.DeviceIdType.MESH,
    )


def gather_steps(nz, place, lead, z_second, pieces, send_sem, recv_sem):
    z, x, c, y = place
    first, second, both = partners(place, lead)
    to_first = device(z, first[0], c, first[1])
    to_second = device(z, second[0], c, second[1])
    to_core = device(z, x, 1 - c, y)

    def copies(send, recv, shard, target):
        return [
            remote(
                view(out, *shard),
                view(out, *shard),
                send_sem.at[send, shard[0], i],
                recv_sem.at[recv, shard[0], i],
                target,
            )
            for i, out, view in pieces
        ]

    def start(*args):
        for copy in copies(*args):
            copy.start()

    def arrived(*args):
        for copy in copies(*args):
            copy.wait_recv()

    def sent(*args):
        for copy in copies(*args):
            copy.wait_send()

    def column(zz):
        return (zz, x, c, y)

    def of_first(zz):
        return (zz, first[0], c, first[1])

    def of_second(zz):
        return (zz, second[0], c, second[1])

    def of_both(zz):
        return (zz, both[0], c, both[1])

    core_first, core_second = CORE + 2 - lead, CORE + 1 + lead

    def move_up(zz):
        return (UP, COLUMN, column(zz), device(z + 1, x, c, y))

    def move_down(zz):
        return (DOWN, COLUMN, column(zz), device(z - 1, x, c, y))

    def first_up(zz):
        return (UP_FIRST, FIRST, of_first(zz), device(z + 1, x, c, y))

    def first_down(zz):
        return (DOWN_FIRST, FIRST, of_first(zz), device(z - 1, x, c, y))

    def along(zz, rising, falling, up, down):
        if rising:

            @pl.when(z < nz - 1)
            def _():
                start(*up(zz))

        if falling:

            @pl.when(z > 0)
            def _():
                start(*down(zz))

    def stage0(zz, rising, falling, wait):
        if wait:
            arrived(UP, COLUMN, column(zz), to_core)
        if z_second and not wait:
            start(FIRST, FIRST, column(zz), to_first)
        along(zz, rising, falling, move_up, move_down)
        if not z_second:
            start(FIRST, FIRST, column(zz), to_first)
        start(SECOND, SECOND, column(zz), to_second)
        start(CORE, CORE, column(zz), to_core)

    def stage1(zz, rising, falling):
        arrived(FIRST, FIRST, of_first(zz), to_first)
        if z_second:
            along(zz, rising, falling, first_up, first_down)
        start(BOTH, BOTH, of_first(zz), to_second)
        start(core_first, core_first, of_first(zz), to_core)

    def stage2(zz, rising, falling):
        arrived(SECOND, SECOND, of_second(zz), to_second)
        start(core_second, core_second, of_second(zz), to_core)
        arrived(BOTH, BOTH, of_both(zz), to_second)
        start(CORE + 3, CORE + 3, of_both(zz), to_core)

    def begin():
        stage0(z, True, True, False)

    def step(t):
        @pl.when((t < nz) & (z - t >= 0))
        def _():
            stage0(z - t, True, False, True)

        @pl.when((t < nz) & (z + t < nz))
        def _():
            stage0(z + t, False, True, True)

        for lag, stage in ((1, stage1), (2, stage2)):
            late = t - lag

            @pl.when(late == 0)
            def _():
                stage(z, True, True)

            @pl.when((late > 0) & (late < nz) & (z - late >= 0))
            def _():
                stage(z - late, True, False)

            @pl.when((late > 0) & (late < nz) & (z + late < nz))
            def _():
                stage(z + late, False, True)

    def all_arrived(zz, carry):
        for fx in range(2):
            for fy in range(2):
                kind = CORE + 2 * fx + fy
                shard = (zz, x + fx * (1 - 2 * x), 1 - c, y + fy * (1 - 2 * y))
                arrived(kind, kind, shard, to_core)
        return carry

    def all_sent(zz, carry):
        @pl.when((zz <= z) & (z < nz - 1))
        def _():
            sent(*move_up(zz))

        @pl.when((zz >= z) & (z > 0))
        def _():
            sent(*move_down(zz))

        if z_second:

            @pl.when((zz <= z) & (z < nz - 1))
            def _():
                sent(*first_up(zz))

            @pl.when((zz >= z) & (z > 0))
            def _():
                sent(*first_down(zz))

            @pl.when(zz == z)
            def _():
                sent(FIRST, FIRST, column(zz), to_first)

        else:
            sent(FIRST, FIRST, column(zz), to_first)
        sent(SECOND, SECOND, column(zz), to_second)
        sent(BOTH, BOTH, of_first(zz), to_second)
        sent(CORE, CORE, column(zz), to_core)
        sent(core_first, core_first, of_first(zz), to_core)
        sent(core_second, core_second, of_second(zz), to_core)
        sent(CORE + 3, CORE + 3, of_both(zz), to_core)
        return carry

    def end_arrive():
        lax.fori_loop(0, nz, all_arrived, 0)

    def end_send():
        lax.fori_loop(0, nz, all_sent, 0)

    return begin, step, end_arrive, end_send


def swap_halves(place, rows, other, sem):
    z, x, c, y = place
    return remote(
        rows.at[pl.ds(LOCAL * (1 - y), LOCAL)],
        other,
        sem.at[0],
        sem.at[1],
        device(z, x, c, 1 - y),
    )


def place_rows(place, keep, send, out, sem):
    z, x, c, y = place
    own = out.at[pl.ds(LOCAL * y, LOCAL)]
    return [
        pltpu.make_async_copy(keep, own, sem.at[2]),
        remote(send, own, sem.at[0], sem.at[1], device(z, x, c, 1 - y)),
    ]


def gather_kernel(nz, views, *refs):
    n = len(views)
    srcs, tokens, outs, other = refs[:n], refs[n], refs[n + 1 : 2 * n + 1], refs[2 * n + 1]
    send_sem, recv_sem, own_sem, swap_sem = refs[2 * n + 2 :]
    place = my_place()
    halves = swap_halves(place, tokens, other, swap_sem)
    own = [
        pltpu.make_async_copy(src, view(out, *place), own_sem.at[i])
        for i, (src, out, view) in enumerate(zip(srcs, outs, views))
    ]
    for copy in own:
        copy.start()
    entry_barrier(nz)
    halves.start()
    for copy in own:
        copy.wait()
    pieces = [(i, out, view) for i, (out, view) in enumerate(zip(outs, views))]
    begin, step, end_arrive, end_send = gather_steps(
        nz, place, place[2], False, pieces, send_sem, recv_sem
    )
    begin()

    def loop(t, carry):
        step(t)
        return carry

    lax.fori_loop(1, nz + 2, loop, 0)
    end_send()
    end_arrive()
    halves.wait()


def gather(nz, collective_id, parts, tokens):
    shards, shapes, views = zip(*parts)
    n = len(parts)
    return pl.pallas_call(
        functools.partial(gather_kernel, nz, views),
        in_specs=[ANY] * (n + 1),
        out_specs=[ANY] * (n + 1),
        out_shape=[sds(shape, shard.dtype) for shard, shape in zip(shards, shapes)]
        + [sds((LOCAL, *tokens.shape[1:]), tokens.dtype)],
        scratch_shapes=[
            pltpu.SemaphoreType.DMA((11, nz, n)),
            pltpu.SemaphoreType.DMA((8, nz, n)),
            pltpu.SemaphoreType.DMA((n,)),
            pltpu.SemaphoreType.DMA((2,)),
        ],
        name="gather",
        compiler_params=params(collective_id=collective_id, has_side_effects=True),
    )(*shards, tokens)


def scatter_kernel(nz, views, *refs):
    n = len(views)
    terms, outs = refs[:n], refs[n : 2 * n]
    mine, from_core, from_second, from_first, from_below, from_above = (
        refs[2 * n + i * n : 3 * n + i * n] for i in range(6)
    )
    send_sem, recv_sem, own_sem = refs[8 * n :]
    place = z, x, c, y = my_place()
    first, second, both = partners(place, place[2])
    to_first = device(z, first[0], c, first[1])
    to_second = device(z, second[0], c, second[1])
    to_core = device(z, x, 1 - c, y)

    def copies(srcs, dsts, send, recv, zz, target):
        return [
            pltpu.make_async_remote_copy(
                src_ref=srcs[i],
                dst_ref=dsts[i],
                send_sem=send_sem.at[send, zz, i],
                recv_sem=recv_sem.at[recv, zz, i],
                device_id=target,
                device_id_type=pl.DeviceIdType.MESH,
            )
            for i in range(n)
        ]

    def slots(bufs, *index):
        return [b.at[index] for b in bufs]

    def pick(refs_, *index):
        return [b[index] for b in refs_]

    flips = [(fx, fy) for fx in range(2) for fy in range(2)]

    def at(fx, fy):
        return x + fx * (1 - 2 * x), y + fy * (1 - 2 * y)

    def core_copies(zz, f):
        fx, fy = flips[f]
        xx, yy = at(fx, fy)
        return copies(
            [view(t, zz, xx, 1 - c, yy) for t, view in zip(terms, views)],
            slots(from_core, zz, f),
            f,
            f,
            zz,
            to_core,
        )

    def own_copies(zz, f):
        fx, fy = flips[f]
        xx, yy = at(fx, fy)
        return [
            pltpu.make_async_copy(
                view(t, zz, xx, c, yy), mine[i].at[zz, f], own_sem.at[f, zz, i]
            )
            for i, (t, view) in enumerate(zip(terms, views))
        ]

    f_first, f_second = 2 - c, 1 + c

    def second_copies(zz, across):
        return copies(
            slots(from_core, zz, 3 if across else f_second),
            slots(from_second, zz, 1 if across else 0),
            4 + across,
            4 + across,
            zz,
            to_second,
        )

    def first_copies(zz):
        return copies(slots(from_second, zz, 1), slots(from_first, zz), 6, 6, zz, to_first)

    def up_copies(zz):
        return copies(slots(from_first, zz), slots(from_below, zz), 7, 7, zz, device(z + 1, x, c, y))

    def down_copies(zz):
        return copies(slots(from_first, zz), slots(from_above, zz), 8, 8, zz, device(z - 1, x, c, y))

    def run(group, what):
        for copy in group:
            getattr(copy, what)()

    def add(into, index, other, other_index):
        for i in range(n):
            a, b = into[i].at[index], other[i].at[other_index]
            a[...] = (a[...].astype(F32) + b[...].astype(F32)).astype(a.dtype)

    def by_distance(t, do):
        @pl.when((t >= 0) & (t < nz) & (z - t >= 0))
        def _():
            do(z - t)

        @pl.when((t > 0) & (t < nz) & (z + t < nz))
        def _():
            do(z + t)

    def start_own(zz):
        for f in range(4):
            run(own_copies(zz, f), "start")

    def start_core(zz):
        for f in (3, 1, 2, 0):
            run(core_copies(zz, f), "start")

    def stage0(zz):
        for f in (3, 1, 2, 0):
            run(core_copies(zz, f), "wait_recv")
            run(own_copies(zz, f), "wait")
            add(from_core, (zz, f), mine, (zz, f))
        run(second_copies(zz, 1), "start")
        run(second_copies(zz, 0), "start")

    def stage1(zz):
        run(second_copies(zz, 1), "wait_recv")
        add(from_second, (zz, 1), from_core, (zz, f_first))
        run(first_copies(zz), "start")

    def stage2(zz):
        run(second_copies(zz, 0), "wait_recv")
        add(from_second, (zz, 0), from_core, (zz, 0))
        run(first_copies(zz), "wait_recv")
        add(from_first, (zz,), from_second, (zz, 0))

        @pl.when(zz > z)
        def _():
            @pl.when(z > 0)
            def _():
                run(up_copies(zz), "wait_recv")
                add(from_first, (zz,), from_below, (zz,))

            run(up_copies(zz), "start")

        @pl.when(zz < z)
        def _():
            @pl.when(z < nz - 1)
            def _():
                run(down_copies(zz), "wait_recv")
                add(from_first, (zz,), from_above, (zz,))

            run(down_copies(zz), "start")

    entry_barrier(nz)

    def begin(k, carry):
        by_distance(nz - 1 - k, start_core)
        by_distance(nz - 1 - k, start_own)
        return carry

    lax.fori_loop(0, nz, begin, 0)

    def step(k, carry):
        t = nz - 1 - k
        by_distance(t, stage0)
        by_distance(t + 1, stage1)
        by_distance(t + 2, stage2)
        return carry

    lax.fori_loop(0, nz + 2, step, 0)

    @pl.when(z > 0)
    def _():
        run(up_copies(z), "wait_recv")
        add(from_first, (z,), from_below, (z,))

    @pl.when(z < nz - 1)
    def _():
        run(down_copies(z), "wait_recv")
        add(from_first, (z,), from_above, (z,))

    for i in range(n):
        outs[i][...] = from_first[i][z]

    def finish(zz, carry):
        for f in range(4):
            run(core_copies(zz, f), "wait_send")
        run(second_copies(zz, 1), "wait_send")
        run(second_copies(zz, 0), "wait_send")
        run(first_copies(zz), "wait_send")

        @pl.when(zz > z)
        def _():
            run(up_copies(zz), "wait_send")

        @pl.when(zz < z)
        def _():
            run(down_copies(zz), "wait_send")

        return carry

    lax.fori_loop(0, nz, finish, 0)


def scatter(nz, collective_id, parts):
    terms, shapes, views = zip(*parts)
    n = len(parts)
    dtypes = [t.dtype for t in terms]

    def bufs(*lead):
        return [pltpu.VMEM((*lead, *shape), d) for shape, d in zip(shapes, dtypes)]

    return pl.pallas_call(
        functools.partial(scatter_kernel, nz, views),
        in_specs=[ANY] * n,
        out_specs=[VMEM] * n,
        out_shape=[sds(shape, d) for shape, d in zip(shapes, dtypes)],
        scratch_shapes=[
            *bufs(nz, 4),
            *bufs(nz, 4),
            *bufs(nz, 2),
            *bufs(nz),
            *bufs(nz),
            *bufs(nz),
            pltpu.SemaphoreType.DMA((9, nz, n)),
            pltpu.SemaphoreType.DMA((9, nz, n)),
            pltpu.SemaphoreType.DMA((4, nz, n)),
        ],
        name="scatter",
        compiler_params=params(62, collective_id=collective_id, has_side_effects=True),
    )(*terms)


def whole_rows(side, mine, other):
    mine, other = mine.astype(F32), other.astype(F32)
    first = jnp.where(side == 0, mine, other)
    second = jnp.where(side == 0, other, mine)
    return jnp.concatenate([jnp.zeros((MEM, D), F32), first, second], axis=0)


def split_rows(side, rows):
    half = (SEG - MEM) // 2
    first, second = rows[MEM : MEM + half], rows[MEM + half :]
    keep = jnp.where(side == 0, first, second)
    send = jnp.where(side == 0, second, first)
    return keep, send


def project_kernel(mine_ref, other_ref, w_ref, table_ref, x_ref, q_ref, k_ref, v_ref):
    side = lax.axis_index("tensor")
    mine = mine_ref[LOCAL * side + pl.program_id(0)]
    x = whole_rows(side, mine, other_ref[0]).astype(BF16)
    x_ref[0] = x
    query = nn(x, w_ref[0]) + table_ref[QUERY_BIAS : QUERY_BIAS + 1, :]
    q_ref[0] = (query * SCALE).astype(BF16)
    k_ref[0] = nn(x, w_ref[1]).astype(BF16)
    v_ref[0] = (nn(x, w_ref[2]) + table_ref[VALUE_BIAS : VALUE_BIAS + 1, :]).astype(BF16)


def slot_rows(width=D):
    return pl.BlockSpec((1, SEG, width), lambda s: (s, 0, 0))


def half_rows(half):
    return pl.BlockSpec((1, half, D), lambda s: (s, 0, 0))


def project(tokens, other, attn, table):
    return pl.pallas_call(
        project_kernel,
        grid=(LOCAL,),
        in_specs=[
            once(tokens.shape, (0, 0, 0)),
            half_rows(tokens.shape[1]),
            once((3, D, D), (0, 0, 0)),
            once((NVEC, D), (0, 0)),
        ],
        out_specs=[slot_rows()] * 4,
        out_shape=[sds((LOCAL, SEG, D), BF16)] * 4,
        name="project",
        compiler_params=params(),
    )(tokens, other, attn, table)


def head_masks():
    feature_head = lax.broadcasted_iota(jnp.int32, (1, D), 1) // DH
    return [feature_head == h for h in range(HEADS)]


def by_head(rows16, masks):
    zero = jnp.zeros_like(rows16)
    return jnp.concatenate([jnp.where(m, rows16, zero) for m in masks], axis=0)


def own_columns(blocks, masks):
    total = jnp.zeros((THIN, D), blocks.dtype)
    for h, m in enumerate(masks):
        total = jnp.where(m, blocks[THIN * h : THIN * (h + 1)], total)
    return total


def copies_of(key_mask_shape):
    row = lax.rem(lax.broadcasted_iota(jnp.int32, key_mask_shape, 0), THIN)
    key = lax.broadcasted_iota(jnp.int32, key_mask_shape, 1)
    return jnp.where((key < MEM) & (key <= row), 2.0, 1.0)


def pair_barrier(place):
    z, x, c, y = place
    barrier = pltpu.get_barrier_semaphore()
    pl.semaphore_signal(
        barrier,
        inc=1,
        device_id=device(z, x, c, 1 - y),
        device_id_type=pl.DeviceIdType.MESH,
    )
    pl.semaphore_wait(barrier, 1)


def chain_kernel(
    place_ref,
    table_ref,
    attn_ref,
    ffn_ref,
    x_in,
    q_in,
    k_in,
    v_in,
    cot_ref,
    x_ref,
    q_ref,
    k_ref,
    v_ref,
    saved_d_ref,
    saved_f_ref,
    saved_s_ref,
    cot_other_ref,
    wa,
    wf,
    xb,
    qb,
    kb,
    vb,
    save_d,
    save_f,
    save_s,
    left,
    given,
    sem_w,
    sem_x,
    sem_kv,
    sem_out,
    sem_memory,
    sem_cot,
):
    del x_in, q_in, k_in, v_in
    place = z, x, c, y = my_place()
    loads = [
        pltpu.make_async_copy(attn_ref, wa, sem_w.at[0]),
        pltpu.make_async_copy(ffn_ref.at[0], wf.at[0], sem_w.at[1]),
        pltpu.make_async_copy(ffn_ref.at[1], wf.at[1], sem_w.at[2]),
    ]
    tiles = [
        pltpu.make_async_copy(x_ref.at[s, pl.ds(0, THIN)], xb.at[s], sem_x.at[s])
        for s in range(LOCAL)
    ]
    keys = [
        pltpu.make_async_copy(src.at[s], dst.at[s], sem_kv.at[2 * s + i])
        for s in range(LOCAL)
        for i, (src, dst) in enumerate(((k_ref, kb), (v_ref, vb)))
    ]
    for copy in tiles + loads[:1] + keys + loads[1:]:
        copy.start()
    pair_barrier(place)
    cot_swap = swap_halves(place, cot_ref, cot_other_ref, sem_cot)
    cot_swap.start()
    handed = remote(left, given, sem_memory.at[0], sem_memory.at[1], device(z, x, c, 1 - y))

    masks = head_masks()
    memory_row = lax.broadcasted_iota(jnp.int32, (THIN, 1), 0) < MEM
    first = table_ref[FIRST_MEMORY:NVEC, :]
    first = jnp.concatenate([first, jnp.zeros((THIN - MEM, D), F32)], axis=0)
    row = lambda r: table_ref[r : r + 1, :]

    def slots(turn, memory):
        for s in range(LOCAL):
            tiles[s].wait()
            if s == 0:
                loads[0].wait()
            keys[2 * s].wait()
            keys[2 * s + 1].wait()
            if memory is None:
                memory = first
            else:
                memory = jnp.where(place_ref[LOCAL * turn + s] == 0, first, memory)
            x16 = jnp.where(memory_row, memory, xb[s].astype(F32)).astype(BF16)
            xb[s] = x16
            qb[s] = ((nn(x16, wa[0]) + row(QUERY_BIAS)) * SCALE).astype(BF16)
            kb[s, 0:THIN] = nn(x16, wa[1]).astype(BF16)
            vb[s, 0:THIN] = (nn(x16, wa[2]) + row(VALUE_BIAS)).astype(BF16)
            outs = [
                pltpu.make_async_copy(
                    src.at[s, pl.ds(0, THIN)], dst.at[s, pl.ds(0, THIN)], sem_out.at[4 * s + i]
                )
                for i, (src, dst) in enumerate(
                    ((xb, x_ref), (qb, q_ref), (kb, k_ref), (vb, v_ref))
                )
            ]
            for copy in outs:
                copy.start()
            if turn == 1 and s == LOCAL - 1:
                save_d[s] = jnp.zeros_like(save_d[s])
                save_f[s] = jnp.zeros_like(save_f[s])
                save_s[s] = jnp.zeros_like(save_s[s])
            else:
                q_heads = by_head(qb[s], masks)
                score = nt(q_heads, kb[s])
                top = jnp.max(score, axis=-1, keepdims=True)
                weight = jnp.exp(score - top) * copies_of(score.shape)
                total = jnp.sum(weight, axis=-1, keepdims=True)
                share = (weight / total).astype(BF16)
                log_total = top + jnp.log(total)
                context = own_columns(nn(share, vb[s]), masks).astype(BF16)
                unit1, inverse1 = normalized(
                    x16.astype(F32) + nt(context, wa[3]) + row(OUT_BIAS)
                )
                hidden = (unit1 * row(GAIN1) + row(SHIFT1)).astype(BF16)
                if s == 0:
                    loads[1].wait()
                up = nt(hidden, wf[0])
                up_bias = jnp.concatenate([row(UP_BIAS + i) for i in range(FF // D)], axis=1)
                active16, slope = gelu_parts(up + up_bias)
                active16 = active16.astype(BF16)
                if s == 0:
                    loads[2].wait()
                second = hidden.astype(F32) + nn(active16, wf[1]) + row(DOWN_BIAS)
                unit2, inverse2 = normalized(second)
                output = (unit2 * row(GAIN2) + row(SHIFT2)).astype(BF16)
                memory = output.astype(F32)
                if turn == 0 and s == LOCAL - 1:
                    left[...] = output
                    handed.start()
                save_d[s, 0] = hidden
                save_d[s, 1] = unit1.astype(BF16)
                save_d[s, 2] = unit2.astype(BF16)
                save_d[s, 3] = context
                save_f[s, 0] = active16
                save_f[s, 1] = slope.astype(BF16)
                wide = lambda v: jnp.broadcast_to(v, (v.shape[0], 128))
                save_s[s, 0 : HEADS * THIN] = wide(log_total)
                save_s[s, HEADS * THIN : HEADS * THIN + THIN] = wide(inverse1)
                save_s[s, HEADS * THIN + THIN :] = wide(inverse2)
            for copy in outs:
                copy.wait()

    @pl.when(y == 0)
    def _():
        slots(0, None)
        handed.wait_send()

    @pl.when(y == 1)
    def _():
        handed.wait_recv()
        slots(1, given[...].astype(F32))

    saves = [
        pltpu.make_async_copy(save_d, saved_d_ref, sem_out.at[0]),
        pltpu.make_async_copy(save_f, saved_f_ref, sem_out.at[1]),
        pltpu.make_async_copy(save_s, saved_s_ref, sem_out.at[2]),
    ]
    for copy in saves:
        copy.start()
    for copy in saves:
        copy.wait()
    cot_swap.wait()


SAVED = (
    sds((LOCAL, 4, THIN, D), BF16),
    sds((LOCAL, 2, THIN, FF), BF16),
    sds((LOCAL, HEADS * THIN + 2 * THIN, 128), F32),
)


def chain(place, table, attn, ffn, x, q, k, v, cot):
    whole = sds((LOCAL, SEG, D), BF16)
    outs = pl.pallas_call(
        chain_kernel,
        in_specs=[SMEM, VMEM] + [ANY] * 7,
        out_specs=[ANY] * 8,
        out_shape=[whole] * 4 + list(SAVED) + [sds((LOCAL, *cot.shape[1:]), BF16)],
        input_output_aliases={4 + i: i for i in range(4)},
        scratch_shapes=[
            pltpu.VMEM((4, D, D), BF16),
            pltpu.VMEM((2, FF, D), BF16),
            pltpu.VMEM((LOCAL, THIN, D), BF16),
            pltpu.VMEM((LOCAL, THIN, D), BF16),
            pltpu.VMEM((LOCAL, SEG, D), BF16),
            pltpu.VMEM((LOCAL, SEG, D), BF16),
            *[pltpu.VMEM(s.shape, s.dtype) for s in SAVED],
            pltpu.VMEM((THIN, D), BF16),
            pltpu.VMEM((THIN, D), BF16),
            pltpu.SemaphoreType.DMA((3,)),
            pltpu.SemaphoreType.DMA((LOCAL,)),
            pltpu.SemaphoreType.DMA((2 * LOCAL,)),
            pltpu.SemaphoreType.DMA((4 * LOCAL,)),
            pltpu.SemaphoreType.DMA((2,)),
            pltpu.SemaphoreType.DMA((2,)),
        ],
        name="chain",
        compiler_params=params(collective_id=2, has_side_effects=True),
    )(place, table, attn, ffn, x, q, k, v, cot)
    return outs[:4], outs[4:7], outs[7]


def own_lanes(block, head):
    lane = lax.broadcasted_iota(jnp.int32, block.shape, 1)
    return jnp.where((lane < DH) == (head == 0), block, jnp.zeros_like(block))


def seen(score, first_query):
    key = lax.broadcasted_iota(jnp.int32, score.shape, 0)
    query = lax.broadcasted_iota(jnp.int32, score.shape, 1) + first_query
    return key <= query


def attend_pair(q, k, v):
    contexts_of, logs_of = [], [[], []]
    for part in range(SEG // TILE):
        rows = slice(TILE * part, TILE * (part + 1))
        keys = slice(0, TILE * (part + 1))
        contexts = []
        for head in range(2):
            score = nt(own_lanes(k[keys], head), q[rows])
            key = lax.broadcasted_iota(jnp.int32, score.shape, 0)
            allowed = seen(score, TILE * part) & (key >= MEM)
            score = jnp.where(allowed, score, MASK_VALUE)
            top = jnp.max(score, axis=0, keepdims=True)
            weight = jnp.exp(score - top)
            total = jnp.sum(weight, axis=0, keepdims=True)
            share = (weight * (1.0 / total)).astype(BF16)
            logs_of[head].append(top + jnp.log(total))
            contexts.append(tn(share, v[keys]))
        lane = lax.broadcasted_iota(jnp.int32, contexts[0].shape, 1)
        contexts_of.append(jnp.where(lane < DH, contexts[0], contexts[1]).astype(BF16))
    return jnp.concatenate(contexts_of, axis=0), [jnp.concatenate(l, axis=1) for l in logs_of]


def attend_kernel(q_ref, k_ref, v_ref, c_ref, log_ref):
    context, logs = attend_pair(q_ref[0], k_ref[0], v_ref[0])
    c_ref[0] = context
    for head in range(2):
        log_ref[0, 0, head : head + 1] = logs[head]


def with_memory(q, k16, v16, context, log_tokens):
    masks = head_masks()
    score = nt(by_head(k16, masks), q).reshape(HEADS, THIN, SEG)
    key = lax.broadcasted_iota(jnp.int32, score.shape, 1)
    score = jnp.where(key < MEM, score, MASK_VALUE)
    top = jnp.maximum(jnp.max(score, axis=1), log_tokens)
    weight = jnp.exp(score - top[:, None])
    old = jnp.exp(log_tokens - top)
    total = jnp.sum(weight, axis=1) + old
    share = (weight * (1.0 / total)[:, None]).reshape(HEADS * THIN, SEG).astype(BF16)
    kept = old / total
    coarse = kept.astype(BF16)
    fine = (kept - coarse.astype(F32)).astype(BF16)
    pad = jnp.zeros((4, SEG), BF16)
    head = lax.rem(lax.broadcasted_iota(jnp.int32, (2 * THIN, D), 0), THIN)
    spread = jnp.where(head == lax.broadcasted_iota(jnp.int32, (2 * THIN, D), 1) // DH, 1.0, 0.0)
    factor = tn(jnp.concatenate([coarse, pad, fine, pad], axis=0), spread.astype(BF16))
    context = factor * context.astype(F32) + tn(share, by_head(v16, masks))
    return context.astype(BF16), top + jnp.log(total)


PAIR = pl.BlockSpec((1, SEG, 2 * DH), lambda s, h: (s, 0, h))
PAIR_LOG = pl.BlockSpec((1, 1, 2, SEG), lambda s, h: (s, h, 0, 0))


def attend(q, k, v):
    return pl.pallas_call(
        attend_kernel,
        grid=(LOCAL, HEADS // 2),
        in_specs=[PAIR] * 3,
        out_specs=[PAIR, PAIR_LOG],
        out_shape=[sds((LOCAL, SEG, D), BF16), sds((LOCAL, HEADS // 2, 2, SEG), F32)],
        name="attend",
        compiler_params=params(),
    )(q, k, v)


def attend_back_pair(q, k, v, dc, logs):
    last = SEG // TILE
    key_terms, value_terms, query_terms = [], [], []
    for head in range(2):
        key_sum, value_sum, query_parts = [], [], []
        for part in range(last):
            rows = slice(TILE * part, TILE * (part + 1))
            keys = slice(0, TILE * (part + 1))
            score = nt(own_lanes(k[keys], head), q[rows])
            share = jnp.exp(score - logs[head : head + 1, rows])
            share = jnp.where(seen(score, TILE * part), share, 0.0)
            share_grad = nt(own_lanes(v[keys], head), dc[rows])
            inner = jnp.sum(share_grad * share, axis=0, keepdims=True)
            score_grad = (share * (share_grad - inner)).astype(BF16)
            value_sum.append(nn(share.astype(BF16), dc[rows]))
            key_sum.append(nn(score_grad, q[rows]))
            query_parts.append(tn(score_grad, k[keys]))
        key_terms.append(key_sum)
        value_terms.append(value_sum)
        query_terms.append(query_parts)
    lane = lax.broadcasted_iota(jnp.int32, (TILE, 2 * DH), 1)
    pick = lambda a, b: jnp.where(lane < DH, a, b)
    dq, dk, dv = [], [], []
    for part in range(last):
        rows = slice(TILE * part, TILE * (part + 1))
        dq.append((pick(query_terms[0][part], query_terms[1][part]) * SCALE).astype(BF16))
        for terms, out in ((key_terms, dk), (value_terms, dv)):
            total = None
            for later in range(part, last):
                term = pick(terms[0][later][rows], terms[1][later][rows])
                total = term if total is None else total + term
            out.append(total)
    return [jnp.concatenate(parts, axis=0) for parts in (dq, dk, dv)]


def rows_kernel(
    place_ref,
    x_ref,
    q_ref,
    k16_ref,
    v16_ref,
    tokens_c_ref,
    tokens_log_ref,
    mine_ref,
    other_ref,
    wo_ref,
    wf_ref,
    table_ref,
    keep_ref,
    send_ref,
    h_ref,
    g_ref,
    du_ref,
    df_ref,
    da_ref,
    dc_ref,
    c_ref,
    log_ref,
    sums_ref,
    slope_ref,
):
    row = lambda r: table_ref[r : r + 1, :]
    slot = pl.program_id(0)
    side = lax.axis_index("tensor")
    live = place_ref[LOCAL * side + slot] >= 0

    @pl.when(slot == 0)
    def _():
        sums_ref[...] = jnp.zeros_like(sums_ref)

    def add(r, value):
        sums_ref[r : r + 1, :] += value

    log_tokens = jnp.concatenate([tokens_log_ref[0, h] for h in range(HEADS // 2)], axis=0)
    context, log_total = with_memory(
        q_ref[0], k16_ref[0], v16_ref[0], tokens_c_ref[0], log_tokens
    )
    c_ref[0] = context
    for h in range(HEADS // 2):
        log_ref[0, h] = log_total[2 * h : 2 * h + 2]
    unit1, inverse1 = normalized(x_ref[0].astype(F32) + nt(context, wo_ref[0]) + row(OUT_BIAS))
    hidden = (unit1 * row(GAIN1) + row(SHIFT1)).astype(BF16)
    h_ref[0] = hidden
    second = hidden.astype(F32) + row(DOWN_BIAS)
    for i in range(FF // D):
        cols = slice(D * i, D * (i + 1))
        up = nt(hidden, wf_ref[0, cols]) + row(UP_BIAS + i)
        active, slope = gelu_parts(up)
        active = active.astype(BF16)
        g_ref[0, :, cols] = active
        slope_ref[:, cols] = slope.astype(BF16)
        second = second + nn(active, wf_ref[1, cols])
    unit2, inverse2 = normalized(second)
    output = jnp.where(live, unit2 * row(GAIN2) + row(SHIFT2), 0.0)
    keep, send = split_rows(side, output)
    keep_ref[0] = keep.astype(BF16)
    send_ref[0] = send.astype(BF16)

    grad = whole_rows(side, mine_ref[LOCAL * side + slot], other_ref[0])
    grad = jnp.where(live, grad, 0.0)
    add(GAIN2, row_sum(grad * unit2))
    add(SHIFT2, row_sum(grad))
    second_grad = normalized_back(grad * row(GAIN2), unit2, inverse2)
    down_grad = second_grad.astype(BF16)
    df_ref[0] = down_grad
    add(DOWN_BIAS, row_sum(down_grad.astype(F32)))
    hidden_grad = second_grad
    for i in range(FF // D):
        cols = slice(D * i, D * (i + 1))
        up_grad = (nt(down_grad, wf_ref[1, cols]) * slope_ref[:, cols].astype(F32)).astype(BF16)
        du_ref[0, :, cols] = up_grad
        add(UP_BIAS + i, row_sum(up_grad.astype(F32)))
        hidden_grad = hidden_grad + nn(up_grad, wf_ref[0, cols])
    add(GAIN1, row_sum(hidden_grad * unit1))
    add(SHIFT1, row_sum(hidden_grad))
    branch_grad = normalized_back(hidden_grad * row(GAIN1), unit1, inverse1).astype(BF16)
    da_ref[0] = branch_grad
    add(OUT_BIAS, row_sum(branch_grad.astype(F32)))
    dc_ref[0] = nn(branch_grad, wo_ref[0]).astype(BF16)


def rows_part(place, x, q, k, v, c, log_tokens, cot, other, attn, ffn, table):
    half = cot.shape[1]
    whole, whole_wide = sds((LOCAL, SEG, D), BF16), sds((LOCAL, SEG, FF), BF16)
    part, logs = sds((LOCAL, half, D), BF16), sds((LOCAL, HEADS // 2, 2, SEG), F32)
    rows, wide = slot_rows(), slot_rows(FF)
    thin = pl.BlockSpec((1, THIN, D), lambda s: (s, 0, 0))
    log_rows = pl.BlockSpec((1, HEADS // 2, 2, SEG), lambda s: (s, 0, 0, 0))
    return pl.pallas_call(
        rows_kernel,
        grid=(LOCAL,),
        in_specs=[SMEM, rows, rows, thin, thin, rows, log_rows]
        + [once(cot.shape, (0, 0, 0)), half_rows(half)]
        + [once((1, D, D), (3, 0, 0)), once((2, FF, D), (0, 0, 0)), once((NVEC, D), (0, 0))],
        out_specs=[half_rows(half)] * 2
        + [rows, wide, wide, rows, rows, rows, rows, log_rows, once((THIN, D), (0, 0))],
        out_shape=[part] * 2
        + [whole, whole_wide, whole_wide, whole, whole, whole, whole, logs, sds((THIN, D), F32)],
        scratch_shapes=[pltpu.VMEM((SEG, FF), BF16)],
        name="rows_part",
        compiler_params=params(),
    )(place, x, q, k, v, c, log_tokens, cot, other, attn, ffn, table)


CHUNK = 768


def memory_key_gradient(q, k16, v16, dc, context, logs, masks):
    score = nt(by_head(k16, masks), q).reshape(HEADS, THIN, SEG)
    key = lax.broadcasted_iota(jnp.int32, score.shape, 1)
    share = jnp.where(key < MEM, jnp.exp(score - logs[:, None]), 0.0)
    share_grad = nt(by_head(v16, masks), dc).reshape(HEADS, THIN, SEG)
    product = dc.astype(F32) * context.astype(F32)
    coarse = product.astype(BF16)
    fine = (product - coarse.astype(F32)).astype(BF16)
    head = lax.broadcasted_iota(jnp.int32, (THIN, D), 0)
    ones = jnp.where(head == lax.broadcasted_iota(jnp.int32, (THIN, D), 1) // DH, 1.0, 0.0)
    ones = ones.astype(BF16)
    inner = (nt(ones, coarse) + nt(ones, fine))[0:HEADS]
    score_grad = (share * (share_grad - inner[:, None])).reshape(HEADS * THIN, SEG)
    share = share.reshape(HEADS * THIN, SEG).astype(BF16)
    dk = own_columns(nn(score_grad.astype(BF16), q), masks)
    return dk, own_columns(nn(share, dc), masks)


def chain_back_kernel(
    place_ref,
    table_ref,
    attn_ref,
    ffn_ref,
    q_ref,
    k_ref,
    v_ref,
    saved_d_ref,
    saved_f_ref,
    saved_s_ref,
    g_ref,
    du_ref,
    df_ref,
    h_ref,
    keep_ref,
    send_ref,
    dc_ref,
    log_ref,
    da_in,
    c_in,
    da_ref,
    c_ref,
    dq_ref,
    dk_ref,
    dv_ref,
    sums_ref,
    terms_ref,
    rows_ref,
    wa,
    wf,
    qb,
    kb,
    vb,
    dcb,
    cb,
    logs,
    dqb,
    dkb,
    dvb,
    tiles,
    df,
    hid,
    gb,
    dub,
    staged,
    save_d,
    save_f,
    save_s,
    thin_d,
    thin_f,
    sums,
    left,
    given,
    sem_w,
    sem_in,
    sem_ff,
    sem_chunk,
    sem_out,
    sem_stage,
    sem_grad,
    sem_swap,
):
    del da_in, c_in
    place = z, x, c, y = my_place()
    loads = [
        pltpu.make_async_copy(attn_ref, wa, sem_w.at[0]),
        pltpu.make_async_copy(ffn_ref.at[0], wf.at[0], sem_w.at[1]),
        pltpu.make_async_copy(ffn_ref.at[1], wf.at[1], sem_w.at[2]),
    ]
    first_rows = lambda ref: ref.at[:, pl.ds(0, THIN)]
    saved = [
        pltpu.make_async_copy(saved_d_ref, save_d, sem_in.at[2]),
        pltpu.make_async_copy(saved_f_ref, save_f, sem_in.at[3]),
        pltpu.make_async_copy(saved_s_ref, save_s, sem_in.at[4]),
    ]
    reads = [
        pltpu.make_async_copy(src, dst, sem_in.at[5 + i])
        for i, (src, dst) in enumerate(
            ((q_ref, qb), (k_ref, kb), (v_ref, vb), (dc_ref, dcb), (c_ref, cb), (log_ref, logs))
        )
    ]
    merged = (da_ref, c_ref)
    tile_reads = [
        pltpu.make_async_copy(first_rows(ref), tiles.at[i], sem_in.at[i])
        for i, ref in enumerate(merged)
    ]
    rows_in = [
        pltpu.make_async_copy(df_ref, df, sem_ff.at[0]),
        pltpu.make_async_copy(h_ref, hid, sem_ff.at[1]),
    ]

    def chunk_reads(i):
        lanes = pl.ds(pl.multiple_of(CHUNK * i, CHUNK), CHUNK)
        slot = lax.rem(i, 2)
        return [
            pltpu.make_async_copy(src.at[:, :, lanes], dst.at[slot], sem_chunk.at[slot, j])
            for j, (src, dst) in enumerate(((g_ref, gb), (du_ref, dub)))
        ]

    @pl.when(y == 1)
    def _():
        for copy in reads + loads[:1] + saved + loads[:0:-1] + tile_reads:
            copy.start()
        for copy in rows_in + chunk_reads(0) + chunk_reads(1):
            copy.start()

    @pl.when(y == 0)
    def _():
        for copy in rows_in + chunk_reads(0) + chunk_reads(1):
            copy.start()
        for copy in reads + saved + loads[:0:-1] + loads[:1] + tile_reads:
            copy.start()

    pair_barrier(place)
    swap = place_rows(place, keep_ref, send_ref, rows_ref, sem_swap)
    for copy in swap:
        copy.start()
    handed = remote(left, given, sem_grad.at[0], sem_grad.at[1], device(z, x, c, 1 - y))

    sums[...] = jnp.zeros_like(sums)
    thin_d[...] = jnp.zeros_like(thin_d)
    thin_f[...] = jnp.zeros_like(thin_f)
    for buf in (dqb, dkb, dvb):
        buf[...] = jnp.zeros_like(buf)
    masks = head_masks()
    memory_row = lax.broadcasted_iota(jnp.int32, (THIN, 1), 0) < MEM
    row = lambda r: table_ref[r : r + 1, :]

    def add(r, value):
        sums[r : r + 1, :] += value

    def attend_at(i, carry):
        s, h = i // (HEADS // 2), lax.rem(i, HEADS // 2)
        lanes = pl.ds(pl.multiple_of(h * 2 * DH, 2 * DH), 2 * DH)
        pair = (buf[s, :, lanes] for buf in (qb, kb, vb, dcb))
        dq, dk, dv = attend_back_pair(*pair, logs[s, h])
        dqb[s, THIN:, lanes] = dq[THIN:]
        dqb[s, 0:THIN, lanes] = jnp.where(memory_row, dqb[s, 0:THIN, lanes], dq[0:THIN])
        dkb[s, :, lanes] = (dk + dkb[s, :, lanes].astype(F32)).astype(BF16)
        dvb[s, :, lanes] = (dv + dvb[s, :, lanes].astype(F32)).astype(BF16)
        return carry

    pairs = LOCAL * HEADS // 2

    def key_gradient(s):
        rows = jnp.concatenate([logs[s, h] for h in range(HEADS // 2)], axis=0)
        return memory_key_gradient(
            qb[s], kb[s, 0:THIN], vb[s, 0:THIN], dcb[s], cb[s], rows, masks
        )

    def slots(turn, grad):
        waited = set()

        def need(*copies):
            for copy in copies:
                if id(copy) not in waited:
                    waited.add(id(copy))
                    copy.wait()

        for s in reversed(range(LOCAL)):
            if turn == 1 and s == LOCAL - 1:
                grad = jnp.zeros((THIN, D), F32)
            else:
                after = place_ref[LOCAL * turn + s + 1]
                grad = jnp.where(memory_row, jnp.where(after > 0, grad, 0.0), 0.0)
                need(*saved)
                unit1, unit2 = save_d[s, 1].astype(F32), save_d[s, 2].astype(F32)
                base = HEADS * THIN
                log_total = save_s[s, 0:base, 0:1]
                inverse1 = save_s[s, base : base + THIN, 0:1]
                inverse2 = save_s[s, base + THIN :, 0:1]
                add(GAIN2, row_sum(grad * unit2))
                add(SHIFT2, row_sum(grad))
                second_grad = normalized_back(grad * row(GAIN2), unit2, inverse2)
                down_grad = second_grad.astype(BF16)
                add(DOWN_BIAS, row_sum(down_grad.astype(F32)))
                need(loads[2])
                up_grad = (nt(down_grad, wf[1]) * save_f[s, 1].astype(F32)).astype(BF16)
                up_sum = row_sum(up_grad.astype(F32))
                for i in range(FF // D):
                    add(UP_BIAS + i, up_sum[:, D * i : D * (i + 1)])
                need(loads[1])
                hidden_grad = second_grad + nn(up_grad, wf[0])
                add(GAIN1, row_sum(hidden_grad * unit1))
                add(SHIFT1, row_sum(hidden_grad))
                pre_grad = normalized_back(hidden_grad * row(GAIN1), unit1, inverse1)
                branch_grad = pre_grad.astype(BF16)
                add(OUT_BIAS, row_sum(branch_grad.astype(F32)))
                need(loads[0])
                context_grad = nn(branch_grad, wa[3]).astype(BF16)
                dc_heads = by_head(context_grad, masks)
                q_heads = by_head(qb[s, 0:THIN], masks)
                score = nt(q_heads, kb[s])
                share = jnp.exp(score - log_total) * copies_of(score.shape)
                share_grad = nt(dc_heads, vb[s])
                inner = jnp.sum(share_grad * share, axis=-1, keepdims=True)
                score_grad = (share * (share_grad - inner)).astype(BF16)
                query_grad = (own_columns(nn(score_grad, kb[s]), masks) * SCALE).astype(BF16)
                dkb[s] = (dkb[s].astype(F32) + tn(score_grad, q_heads)).astype(BF16)
                dvb[s] = (dvb[s].astype(F32) + tn(share.astype(BF16), dc_heads)).astype(BF16)
                dqb[s, 0:THIN] = jnp.where(memory_row, query_grad, dqb[s, 0:THIN])
                thin_d[s, 0] = down_grad
                thin_d[s, 1] = save_d[s, 0]
                thin_f[s, 0] = up_grad
                thin_f[s, 1] = save_f[s, 0]
                need(*tile_reads)
                for i, value in enumerate((branch_grad, save_d[s, 3])):
                    tiles[i, s] = jnp.where(memory_row, value, tiles[i, s])
                grad = pre_grad + nt(query_grad, wa[0])
            need(loads[0])
            dk, dv = dkb[s, 0:THIN], dvb[s, 0:THIN]
            if turn == 1:
                early_k, early_v = key_gradient(s)
                dk = (dk.astype(F32) + early_k).astype(BF16)
                dv = (dv.astype(F32) + early_v).astype(BF16)
            grad = grad + nt(dk, wa[1]) + nt(dv, wa[2])
            first = jnp.where(place_ref[LOCAL * turn + s] == 0, grad, 0.0)
            sums[FIRST_MEMORY : FIRST_MEMORY + THIN, :] += first
        return grad

    @pl.when(y == 1)
    def _():
        for copy in reads:
            copy.wait()
        left[...] = slots(1, None)
        handed.start()
        lax.fori_loop(0, pairs, attend_at, 0)

    @pl.when(y == 0)
    def _():
        for copy in reads:
            copy.wait()
        lax.fori_loop(0, pairs, attend_at, 0)
        handed.wait_recv()
        slots(0, given[...])

    writes = [
        pltpu.make_async_copy(dqb, dq_ref, sem_out.at[0]),
        pltpu.make_async_copy(dkb, dk_ref, sem_out.at[1]),
        pltpu.make_async_copy(dvb, dv_ref, sem_out.at[2]),
        pltpu.make_async_copy(sums, sums_ref, sem_out.at[3]),
        *[
            pltpu.make_async_copy(tiles.at[i], first_rows(ref), sem_out.at[5 + i])
            for i, ref in enumerate(merged)
        ],
    ]
    for copy in writes:
        copy.start()

    for copy in rows_in:
        copy.wait()
    for s in range(LOCAL):
        df[s, 0:THIN] = jnp.where(memory_row, thin_d[s, 0], df[s, 0:THIN])
        hid[s, 0:THIN] = jnp.where(memory_row, thin_d[s, 1], hid[s, 0:THIN])
    chunks = FF // CHUNK

    def store(i):
        lanes = pl.ds(pl.multiple_of(CHUNK * i, CHUNK), CHUNK)
        slot = lax.rem(i, 2)
        return pltpu.make_async_copy(
            staged.at[slot], terms_ref.at[:, lanes], sem_stage.at[slot]
        )

    def chunk(i, carry):
        slot = lax.rem(i, 2)
        for copy in chunk_reads(i):
            copy.wait()
        lanes = pl.ds(pl.multiple_of(CHUNK * i, CHUNK), CHUNK)
        for s in range(LOCAL):
            for j, buf in ((1, gb), (0, dub)):
                old = buf[slot, s, 0:THIN]
                buf[slot, s, 0:THIN] = jnp.where(memory_row, thin_f[s, j, :, lanes], old)

        @pl.when(i >= 2)
        def _():
            store(i - 2).wait()

        for j, (buf, rows) in enumerate(((dub, hid), (gb, df))):
            terms = tn(
                buf[slot].reshape(LOCAL * SEG, CHUNK), rows[...].reshape(LOCAL * SEG, D)
            )
            staged[slot, j] = terms.astype(BF16)
        store(i).start()

        @pl.when(i + 2 < chunks)
        def _():
            for copy in chunk_reads(i + 2):
                copy.start()

        return carry

    lax.fori_loop(0, chunks, chunk, 0)

    @pl.when(y == 1)
    def _():
        handed.wait_send()

    for copy in [*writes, store(chunks - 2), store(chunks - 1)]:
        copy.wait()
    for copy in swap:
        copy.wait()


THIN_SHAPES = (
    sds((LOCAL, 2, THIN, D), BF16),
    sds((LOCAL, 2, THIN, FF), BF16),
    sds((FIRST_MEMORY + THIN, D), F32),
)


def chain_back(place, table, attn, ffn, q, k, v, saved, g, du, df, h, halves, dc, logs, da, c):
    whole = sds((LOCAL, SEG, D), BF16)
    rows = pltpu.VMEM(whole.shape, BF16)
    dma = lambda *shape: pltpu.SemaphoreType.DMA(shape)
    outs = pl.pallas_call(
        chain_back_kernel,
        in_specs=[SMEM, VMEM] + [ANY] * 18,
        out_specs=[ANY] * 8,
        out_shape=[whole] * 5
        + [THIN_SHAPES[2]]
        + [sds((2, FF, D), BF16), sds((2 * LOCAL, *halves[0].shape[1:]), BF16)],
        input_output_aliases={18: 0, 19: 1},
        scratch_shapes=[
            pltpu.VMEM((4, D, D), BF16),
            pltpu.VMEM((2, FF, D), BF16),
            *[rows] * 5,
            pltpu.VMEM(logs.shape, F32),
            rows,
            rows,
            rows,
            pltpu.VMEM((2, LOCAL, THIN, D), BF16),
            rows,
            rows,
            pltpu.VMEM((2, LOCAL, SEG, CHUNK), BF16),
            pltpu.VMEM((2, LOCAL, SEG, CHUNK), BF16),
            pltpu.VMEM((2, 2, CHUNK, D), BF16),
            *[pltpu.VMEM(s.shape, s.dtype) for s in SAVED + THIN_SHAPES],
            pltpu.VMEM((THIN, D), F32),
            pltpu.VMEM((THIN, D), F32),
            dma(3),
            dma(11),
            dma(2),
            dma(2, 2),
            dma(8),
            dma(2),
            dma(2),
            dma(3),
        ],
        name="chain_back",
        compiler_params=params(collective_id=3, has_side_effects=True),
    )(place, table, attn, ffn, q, k, v, *saved, g, du, df, h, *halves, dc, logs, da, c)
    return outs


def table_row(ref, index, entries):
    blocks = []
    lane = lax.broadcasted_iota(jnp.int32, (1, 128), 1)
    for block in range(D // 128):
        at, end = index * D + 128 * block, index * D + 128 * (block + 1)
        target, value = 0, jnp.zeros((1, 128), F32)
        while at < end:
            shard, inner = at // entries, at % entries
            count = min(end - at, entries - inner, 128 - inner % 128)
            place = (shard // 8, shard // 4 % 2, shard // 2 % 2, shard % 2)
            source = ref[place][inner // 128 : inner // 128 + 1]
            shift = (target - inner) % 128
            if shift:
                source = pltpu.roll(source, shift, 1)
            value = jnp.where((lane >= target) & (lane < target + count), source, value)
            at, target = at + count, target + count
        blocks.append(value)
    return jnp.concatenate(blocks, axis=1)


def head_kernel(
    nz,
    entries,
    attn_src,
    ffn_src,
    vec_src,
    tokens,
    attn_ref,
    ffn_ref,
    vec_ref,
    x_ref,
    q_ref,
    k_ref,
    v_ref,
    c_ref,
    log_ref,
    wa,
    vec,
    mine,
    other,
    xb,
    qb,
    kb,
    vb,
    cb,
    logs,
    send_sem,
    recv_sem,
    own_sem,
    swap_sem,
    out_sem,
):
    place = my_place()
    side = place[3]
    halves = swap_halves(place, tokens, other, swap_sem)
    own = [
        pltpu.make_async_copy(attn_src, attn_view(wa, *place), own_sem.at[0]),
        pltpu.make_async_copy(vec_src, vec_view(vec, *place), own_sem.at[1]),
        pltpu.make_async_copy(ffn_src, ffn_view(ffn_ref, *place), own_sem.at[2]),
        pltpu.make_async_copy(tokens.at[pl.ds(LOCAL * side, LOCAL)], mine, own_sem.at[3]),
    ]
    for copy in own:
        copy.start()
    entry_barrier(nz)
    steps = functools.partial(gather_steps, nz, place, send_sem=send_sem, recv_sem=recv_sem)
    begin, step, end_arrive, end_send = steps(
        1, True, [(0, wa, attn_view), (1, vec, vec_view)]
    )
    late = [
        steps(place[2], bool(i), [(2 + i, ffn_ref.at[i], hidden_view)]) for i in range(2)
    ]
    own[0].wait()
    own[1].wait()
    begin()
    halves.start()

    def loop(t, carry):
        step(t)
        return carry

    lax.fori_loop(1, nz + 2, loop, 0)
    own[2].wait()
    for begin2, _, _, _ in late:
        begin2()
    own[3].wait()
    halves.wait()
    end_arrive()
    outs = [
        pltpu.make_async_copy(wa, attn_ref, out_sem.at[0]),
        pltpu.make_async_copy(vec, vec_ref, out_sem.at[1]),
    ]
    for copy in outs:
        copy.start()

    weight = lambda i: wa[i].reshape(D, D)

    def project_slot(s):
        x = whole_rows(side, mine[s], other[s]).astype(BF16)
        xb[s] = x
        qb[s] = ((nn(x, weight(0)) + table_row(vec, QUERY_BIAS, entries)) * SCALE).astype(BF16)
        kb[s] = nn(x, weight(1)).astype(BF16)
        vb[s] = (nn(x, weight(2)) + table_row(vec, VALUE_BIAS, entries)).astype(BF16)
        for i, (buf, out) in enumerate(((xb, x_ref), (qb, q_ref), (kb, k_ref), (vb, v_ref))):
            outs.append(pltpu.make_async_copy(buf.at[s], out.at[s], out_sem.at[2 + 4 * s + i]))
            outs[-1].start()

    def attend_at(i, carry):
        s, h = i // (HEADS // 2), i % (HEADS // 2)
        lanes = pl.ds(pl.multiple_of(h * 2 * DH, 2 * DH), 2 * DH)
        context, log_rows = attend_pair(qb[s, :, lanes], kb[s, :, lanes], vb[s, :, lanes])
        cb[s, :, lanes] = context
        for head in range(2):
            logs[s, h, head : head + 1] = log_rows[head]
        return carry

    project_slot(0)
    project_slot(1)
    pairs = LOCAL * HEADS // 2
    done = 0
    for t in range(1, nz + 2):
        for _, step2, _, _ in late:
            step2(t)
        upto = pairs * t // (nz + 1)
        lax.fori_loop(done, upto, attend_at, 0)
        done = upto
    outs.append(pltpu.make_async_copy(cb, c_ref, out_sem.at[2 + 4 * LOCAL]))
    outs.append(pltpu.make_async_copy(logs, log_ref, out_sem.at[3 + 4 * LOCAL]))
    outs[-1].start()
    outs[-2].start()
    end_send()
    for _, _, end_arrive2, end_send2 in late:
        end_send2()
        end_arrive2()
    for copy in outs:
        copy.wait()


def head(nz, attention, hidden_major, vec, tokens, entries):
    rows, hidden = attention.shape[1], hidden_major.shape[1]
    whole = sds((LOCAL, SEG, D), BF16)
    logs = (LOCAL, HEADS // 2, 2, SEG)
    attn_shape, vec_shape = (4, nz, 2, 2, rows, D), (nz, 2, 2, 2, *VEC_TILE)
    half = pltpu.VMEM((LOCAL, *tokens.shape[1:]), BF16)
    return pl.pallas_call(
        functools.partial(head_kernel, nz, entries),
        in_specs=[ANY] * 4,
        out_specs=[ANY] * 9,
        out_shape=[
            sds(attn_shape, BF16),
            sds((2, nz, 2, 2, 2, hidden, D), BF16),
            sds(vec_shape, F32),
            *[whole] * 5,
            sds(logs, F32),
        ],
        scratch_shapes=[
            pltpu.VMEM(attn_shape, BF16),
            pltpu.VMEM(vec_shape, F32),
            half,
            half,
            *[pltpu.VMEM(whole.shape, BF16)] * 5,
            pltpu.VMEM(logs, F32),
            pltpu.SemaphoreType.DMA((11, nz, 4)),
            pltpu.SemaphoreType.DMA((8, nz, 4)),
            pltpu.SemaphoreType.DMA((4,)),
            pltpu.SemaphoreType.DMA((2,)),
            pltpu.SemaphoreType.DMA((4 + 4 * LOCAL,)),
        ],
        name="head",
        compiler_params=params(collective_id=0, has_side_effects=True),
    )(attention, hidden_major, vec, tokens)


def token_grad_kernel(place_ref, da_ref, dq_ref, dk_ref, dv_ref, w_ref, keep_ref, send_ref):
    side = lax.axis_index("tensor")
    total = da_ref[0].astype(F32)
    for i, ref in enumerate((dq_ref, dk_ref, dv_ref)):
        total = total + nt(ref[0], w_ref[i])
    live = place_ref[LOCAL * side + pl.program_id(0)] >= 0
    keep, send = split_rows(side, jnp.where(live, total, 0.0))
    keep_ref[0] = keep.astype(BF16)
    send_ref[0] = send.astype(BF16)


def token_gradient(place, da, dq, dk, dv, attn):
    half = (SEG - MEM) // 2
    return pl.pallas_call(
        token_grad_kernel,
        grid=(LOCAL,),
        in_specs=[SMEM] + [slot_rows()] * 4 + [once((3, D, D), (0, 0, 0))],
        out_specs=[half_rows(half)] * 2,
        out_shape=[sds((LOCAL, half, D), BF16)] * 2,
        name="token_gradient",
        compiler_params=params(),
    )(place, da, dq, dk, dv, attn)


def flat(ref):
    return ref[...].reshape(LOCAL * ref.shape[1], ref.shape[2])


def attn_grad_kernel(
    x_ref, da_ref, dq_ref, dk_ref, dv_ref, c_ref, sums_ref, thin_sums_ref, out_ref, vec_ref
):
    x = flat(x_ref)
    dq, dv = flat(dq_ref), flat(dv_ref)
    out_ref[0] = tn(x, dq).astype(BF16)
    out_ref[1] = tn(x, flat(dk_ref)).astype(BF16)
    out_ref[2] = tn(x, dv).astype(BF16)
    out_ref[3] = tn(flat(da_ref), flat(c_ref)).astype(BF16)
    vec_ref[...] = thin_sums_ref[...]
    vec_ref[0:FIRST_MEMORY] = thin_sums_ref[0:FIRST_MEMORY] + sums_ref[0:FIRST_MEMORY]
    vec_ref[QUERY_BIAS : QUERY_BIAS + 1] = row_sum(dq.astype(F32))
    vec_ref[VALUE_BIAS : VALUE_BIAS + 1] = row_sum(dv.astype(F32))


def attn_gradient(x, da, dq, dk, dv, c, sums, thin_sums, chunk=256):
    part = pl.BlockSpec((LOCAL, SEG, chunk), lambda i: (0, 0, i))
    full = once((LOCAL, SEG, D), (0, 0, 0))
    lanes = lambda rows: pl.BlockSpec((rows, chunk), lambda i: (0, i))
    return pl.pallas_call(
        attn_grad_kernel,
        grid=(D // chunk,),
        in_specs=[full, full, part, part, part, part, lanes(THIN), lanes(FIRST_MEMORY + THIN)],
        out_specs=[
            pl.BlockSpec((4, D, chunk), lambda i: (0, 0, i)),
            lanes(FIRST_MEMORY + THIN),
        ],
        out_shape=[sds((4, D, D), BF16), sds((FIRST_MEMORY + THIN, D), F32)],
        name="attn_gradient",
        compiler_params=params(),
    )(x, da, dq, dk, dv, c, sums, thin_sums)


def scatter_steps(nz, place, lead, z_second, pieces, send_sem, recv_sem):
    z, x, c, y = place
    first, second, both = partners(place, lead)
    to_first = device(z, first[0], c, first[1])
    to_second = device(z, second[0], c, second[1])
    to_core = device(z, x, 1 - c, y)
    f_first, f_second = 2 - lead, 1 + lead

    def at(f):
        fx, fy = f // 2, f % 2
        return x + fx * (1 - 2 * x), y + fy * (1 - 2 * y)

    def term(piece, zz, core, f):
        xx, yy = at(f)
        return piece[2](piece[1], zz, xx, core, yy)

    def copies(kind, zz, target, src, dst):
        return [
            remote(src(p), dst(p), send_sem.at[kind, zz, p[0]], recv_sem.at[kind, zz, p[0]], target)
            for p in pieces
        ]

    def core_copies(zz, f):
        return copies(
            f, zz, to_core, lambda p: term(p, zz, 1 - c, f), lambda p: p[3].at[zz, f]
        )

    def second_copies(zz, across):
        f = 3 if across else f_second
        return copies(
            4 + across, zz, to_second, lambda p: p[3].at[zz, f], lambda p: p[4].at[zz, across]
        )

    def first_copies(zz):
        slot = 0 if z_second else zz
        return copies(6, zz, to_first, lambda p: p[4].at[zz, 1], lambda p: p[5].at[slot])

    def partial(p, zz, f):
        return p[4].at[zz, f] if z_second else p[5].at[zz]

    def beside(p, above, zz, f):
        return p[6 + above].at[zz, f] if z_second else p[6 + above].at[zz]

    def up_copies(zz, f):
        return copies(
            7 + 2 * f,
            zz,
            device(z + 1, x, c, y),
            lambda p: partial(p, zz, f),
            lambda p: beside(p, 0, zz, f),
        )

    def down_copies(zz, f):
        return copies(
            8 + 2 * f,
            zz,
            device(z - 1, x, c, y),
            lambda p: partial(p, zz, f),
            lambda p: beside(p, 1, zz, f),
        )

    def run(group, what):
        for copy in group:
            getattr(copy, what)()

    def add(into, other):
        for p in pieces:
            a, b = into(p), other(p)
            a[...] = (a[...].astype(F32) + b[...].astype(F32)).astype(a.dtype)

    def turn(k):
        upper = z // (nz // 2)
        return (1 - upper) * (nz - 1 - k) + upper * k

    def start(zz):
        for f in (3, 1, 2, 0):
            run(core_copies(zz, f), "start")

    def stage0(zz):
        for f in (3, 1, 2, 0):
            run(core_copies(zz, f), "wait_recv")
            add(lambda p: p[3].at[zz, f], lambda p: term(p, zz, c, f))
        run(second_copies(zz, 1), "start")
        run(second_copies(zz, 0), "start")

    def from_below(zz, f):
        run(up_copies(zz, f), "wait_recv")
        add(lambda p: partial(p, zz, f), lambda p: beside(p, 0, zz, f))

    def from_above(zz, f):
        run(down_copies(zz, f), "wait_recv")
        add(lambda p: partial(p, zz, f), lambda p: beside(p, 1, zz, f))

    def from_end(zz, f):
        @pl.when((zz > z) & (z == 0))
        def _():
            run(up_copies(zz, f), "start")

        @pl.when((zz < z) & (z == nz - 1))
        def _():
            run(down_copies(zz, f), "start")

    def along(zz, f):
        @pl.when((zz > z) & (z > 0))
        def _():
            from_below(zz, f)
            run(up_copies(zz, f), "start")

        @pl.when((zz < z) & (z < nz - 1))
        def _():
            from_above(zz, f)
            run(down_copies(zz, f), "start")

    def stage1(zz):
        run(second_copies(zz, 1), "wait_recv")
        add(lambda p: p[4].at[zz, 1], lambda p: p[3].at[zz, f_first])
        if z_second:
            from_end(zz, 1)
        else:
            run(first_copies(zz), "start")

    def stage2(zz):
        run(second_copies(zz, 0), "wait_recv")
        add(lambda p: p[4].at[zz, 0], lambda p: p[3].at[zz, 0])
        if not z_second:
            run(first_copies(zz), "wait_recv")
            add(lambda p: p[5].at[zz], lambda p: p[4].at[zz, 0])
        from_end(zz, 0)
        if z_second:
            along(zz, 1)

    def stage3(zz):
        along(zz, 0)

    def staged(stage):
        return lambda k: stage(turn(k))

    def at_owner(f):
        @pl.when(z > 0)
        def _():
            from_below(z, f)

        @pl.when(z < nz - 1)
        def _():
            from_above(z, f)

    def end(outs):
        if z_second:
            at_owner(1)
            run(first_copies(z), "start")
        at_owner(0)
        if z_second:
            run(first_copies(z), "wait_recv")
            add(lambda p: p[4].at[z, 0], lambda p: p[5].at[0])
        for p, out in zip(pieces, outs):
            out[...] = partial(p, z, 0)[...]

    def sent(zz, carry):
        for f in range(4):
            run(core_copies(zz, f), "wait_send")
        run(second_copies(zz, 1), "wait_send")
        run(second_copies(zz, 0), "wait_send")
        for f in range(2 if z_second else 1):

            @pl.when(zz > z)
            def _():
                run(up_copies(zz, f), "wait_send")

            @pl.when(zz < z)
            def _():
                run(down_copies(zz, f), "wait_send")

        if z_second:

            @pl.when(zz == z)
            def _():
                run(first_copies(zz), "wait_send")

        else:
            run(first_copies(zz), "wait_send")
        return carry

    stages = [staged(stage) for stage in (stage0, stage1, stage2, stage3)]
    return start, stages, turn, end, lambda: lax.fori_loop(0, nz, sent, 0)


def scatter_places(nz, shape, z_second):
    lead = (nz, 2) if z_second else (nz,)
    return [
        pltpu.VMEM((nz, 4, *shape), BF16),
        pltpu.VMEM((nz, 2, *shape), BF16),
        pltpu.VMEM((1 if z_second else nz, *shape), BF16),
        pltpu.VMEM((*lead, *shape), BF16),
        pltpu.VMEM((*lead, *shape), BF16),
    ]


VEC_ROWS = FIRST_MEMORY + THIN


def tail_kernel(nz, *refs):
    (
        place_ref,
        sums_ref,
        thin_sums_ref,
        ffn_terms,
        *rows_refs,
        w_ref,
        attn_out,
        ffn_out,
        vec_out,
        grad_ref,
        terms_f,
        terms_a,
        rows,
        wb,
        keep,
        send,
    ) = refs[:21]
    places = [refs[21 + 5 * i : 26 + 5 * i] for i in range(3)]
    vec_mine, vec_given, vec_z, send_sem, recv_sem, block_sem, in_sem, swap_sem, vec_sem = refs[36:]
    place = z, x, c, y = my_place()
    blocks = lambda zz: pltpu.make_async_copy(
        ffn_terms.at[:, zz], terms_f.at[:, zz], block_sem.at[zz]
    )
    rows_in = [
        pltpu.make_async_copy(src, rows.at[i], in_sem.at[2 + i]) for i, src in enumerate(rows_refs)
    ]
    rows_in.append(pltpu.make_async_copy(w_ref.at[pl.ds(0, 3)], wb, in_sem.at[8]))
    steps = functools.partial(scatter_steps, nz, place, send_sem=send_sem, recv_sem=recv_sem)
    up = steps(c, False, [(0, terms_f.at[0], hidden_view, *places[0])])
    down = steps(1 - c, True, [(1, terms_f.at[1], hidden_view, *places[1])])
    attn = steps(1 - c, True, [(2, terms_a, attn_view, *places[2])])
    turn = up[2]
    for k in range(nz):
        blocks(turn(k)).start()
    for copy in rows_in:
        copy.start()

    barrier = pltpu.get_barrier_semaphore()
    others = [device(lax.rem(z + dz, nz), x, c, y) for dz in range(1, nz)]
    for other in [device(z, 1 - x, c, y), device(z, x, 1 - c, y), device(z, x, c, 1 - y), *others]:
        pl.semaphore_signal(
            barrier, inc=1, device_id=other, device_id_type=pl.DeviceIdType.MESH
        )
    pl.semaphore_wait(barrier, 2 + nz)

    def begin(k, carry):
        zz = turn(k)
        blocks(zz).wait()
        up[0](zz)
        down[0](zz)
        return carry

    def attn_terms(i, carry):
        left, right = rows[i // 3], rows[i + 2]
        value = tn(left.reshape(LOCAL * SEG, D), right.reshape(LOCAL * SEG, D))
        terms_a[i] = value.astype(BF16).reshape(terms_a.shape[1:])
        return carry

    def token_rows(s):
        total = rows[1, s].astype(F32)
        for i in range(3):
            total = total + nt(rows[2 + i, s], wb[i])
        live = place_ref[LOCAL * y + s] >= 0
        stay, go = split_rows(y, jnp.where(live, total, 0.0))
        keep[s] = stay.astype(BF16)
        send[s] = go.astype(BF16)

    def vec_copies(phase):
        if phase < 3:
            target = (device(z, x, 1 - c, y), device(z, x, c, 1 - y), device(z, 1 - x, c, y))[phase]
            sems = vec_sem.at[0, phase], vec_sem.at[1, phase]
            return [remote(vec_mine.at[phase], vec_given.at[phase], *sems, target)]
        return [
            remote(
                vec_mine.at[3], vec_z.at[dz], vec_sem.at[0, 3 + dz], vec_sem.at[1, 3 + dz], target
            )
            for dz, target in enumerate(others)
        ]

    def vec_start(phase):
        if phase == 0:
            vec_mine[0] = thin_sums_ref[...]
            vec_mine[0, 0:FIRST_MEMORY] = (
                thin_sums_ref[0:FIRST_MEMORY] + sums_ref[0:FIRST_MEMORY]
            )
            for r, i in ((QUERY_BIAS, 2), (VALUE_BIAS, 4)):
                total = row_sum(rows[i].reshape(LOCAL * SEG, D).astype(F32))
                vec_mine[0, r : r + 1] = total
        else:
            for copy in vec_copies(phase - 1):
                copy.wait_recv()
            vec_mine[phase] = vec_mine[phase - 1] + vec_given[phase - 1]
        for copy in vec_copies(phase):
            copy.start()

    swap = place_rows(place, keep, send, grad_ref, swap_sem)

    def stage(i, *groups):
        for k in groups[-1]:
            for group in groups[:-1]:
                group[1][i](k)

    def step(k, *groups):
        for lag in range(4):
            if 0 <= k - lag < nz:
                stage(lag, *groups, (k - lag,))

    lax.fori_loop(0, 2, begin, 0)
    step(0, up, down)
    for copy in rows_in:
        copy.wait()
    lax.fori_loop(0, 2, attn_terms, 0)
    lax.fori_loop(2, 3, begin, 0)
    step(1, up, down)
    lax.fori_loop(2, 4, attn_terms, 0)
    vec_start(0)
    lax.fori_loop(3, 4, begin, 0)
    attn[0](turn(0))
    step(2, up, down)
    step(0, attn)
    attn[0](turn(1))
    token_rows(0)
    vec_start(1)
    step(3, up, down)
    step(1, attn)
    attn[0](turn(2))
    token_rows(1)
    for copy in swap:
        copy.start()
    step(4, up, down)
    step(2, attn)
    attn[0](turn(3))
    vec_start(2)
    step(5, up, down)
    step(3, attn)
    vec_start(3)
    step(6, up, down)
    step(4, attn)
    up[3]([ffn_out.at[0]])
    step(5, attn)
    down[3]([ffn_out.at[1]])
    step(6, attn)
    attn[3]([attn_out])
    total = vec_mine[3]
    for dz, copy in enumerate(vec_copies(3)):
        copy.wait_recv()
        total = total + vec_z[dz]
    vec_out[...] = total
    for phase in range(4):
        for copy in vec_copies(phase):
            copy.wait_send()
    for group in (up, down, attn):
        group[4]()
    for copy in swap:
        copy.wait()


def tail(place, sums, thin_sums, ffn_terms, x, da, dq, dk, dv, c, attn, shapes):
    nz = lax.axis_size("dp") // 4
    rows, hidden, half = shapes
    attn_shape, ffn_shape = (4, nz, 2, 2, rows, D), (2, nz, 2, 2, 2, hidden, D)
    part = pltpu.VMEM((LOCAL, half, D), BF16)
    dma = lambda *shape: pltpu.SemaphoreType.DMA(shape)
    return pl.pallas_call(
        functools.partial(tail_kernel, nz),
        in_specs=[SMEM, VMEM, VMEM] + [ANY] * 8,
        out_specs=[VMEM] * 3 + [ANY],
        out_shape=[
            sds((4, rows, HALF), BF16),
            sds((2, hidden, D), BF16),
            sds((VEC_ROWS, D), F32),
            sds((2 * LOCAL, half, D), BF16),
        ],
        scratch_shapes=[
            pltpu.VMEM(ffn_shape, BF16),
            pltpu.VMEM(attn_shape, BF16),
            pltpu.VMEM((6, LOCAL, SEG, D), BF16),
            pltpu.VMEM((3, D, D), BF16),
            part,
            part,
            *scatter_places(nz, (hidden, D), False),
            *scatter_places(nz, (hidden, D), True),
            *scatter_places(nz, (4, rows, HALF), True),
            pltpu.VMEM((4, VEC_ROWS, D), F32),
            pltpu.VMEM((3, VEC_ROWS, D), F32),
            pltpu.VMEM((nz - 1, VEC_ROWS, D), F32),
            dma(11, nz, 3),
            dma(11, nz, 3),
            dma(nz),
            dma(9),
            dma(3),
            dma(2, 2 + nz),
        ],
        name="tail",
        compiler_params=params(62, collective_id=1, has_side_effects=True),
    )(place, sums, thin_sums, ffn_terms.reshape(ffn_shape), x, da, dq, dk, dv, c, attn)


def update(gradient, momentum, weight, average, rate, grad_scale):
    scaled = gradient * grad_scale
    moment = MOMENTUM * momentum + scaled
    weight_new = weight - rate * (scaled + MOMENTUM * moment)
    return (moment, weight_new, AVERAGE_DECAY * average + (1.0 - AVERAGE_DECAY) * weight_new)


VEC_TILE = (8, 128)


def in_tiles(rows):
    size = VEC_TILE[0] * VEC_TILE[1]
    padded = jnp.pad(rows, [(0, 0)] * (rows.ndim - 1) + [(0, size - rows.shape[-1])])
    return padded.reshape(*rows.shape[:-1], *VEC_TILE)


def start(attention, feedforward, vectors, tokens):
    nz = lax.axis_size("dp") // 4
    rows, hidden, entries = attention.shape[1], feedforward.shape[2], vectors.shape[0]
    attention = attention.astype(BF16)
    hidden_major = jnp.swapaxes(feedforward.astype(BF16), 1, 2)
    vec = in_tiles(vectors.astype(BF16).astype(F32))
    aligned = rows % THIN == 0
    if aligned:
        attn, ffn, table, *work = head(nz, attention, hidden_major, vec, tokens, entries)
    else:
        attn, ffn, table, other = gather(
            nz,
            0,
            [
                (attention, (4, nz, 2, 2, rows, D), attn_view),
                (hidden_major, (2, nz, 2, 2, 2, hidden, D), ffn_view),
                (vec, (nz, 2, 2, 2, *VEC_TILE), vec_view),
            ],
            tokens,
        )
    attn, ffn = attn.reshape(4, D, D), ffn.reshape(2, FF, D)
    table = table.reshape(nz * 8, VEC_TILE[0] * VEC_TILE[1])[:, :entries].reshape(NVEC, D)
    if not aligned:
        work = project(tokens, other, attn, table)
        work = [*work, *attend(*work[1:])]
    return attn, ffn, table, work


def scatter_gradients(attn_terms, ffn_terms, vec_terms, shapes):
    nz = lax.axis_size("dp") // 4
    rows, hidden, entries = shapes
    attn, ffn, vec = scatter(
        nz,
        1,
        [
            (attn_terms.reshape(4, nz, 2, 2, rows, D), (4, rows, HALF), attn_view),
            (ffn_terms.reshape(2, nz, 2, 2, 2, hidden, D), (2, hidden, D), ffn_view),
            (in_tiles(vec_terms.reshape(nz, 2, 2, 2, entries)), VEC_TILE, vec_view),
        ],
    )
    return attn.astype(F32), jnp.swapaxes(ffn, 1, 2).astype(F32), vec.reshape(-1)[:entries]


def swap(value):
    return lax.ppermute(value, "tensor", [(0, 1), (1, 0)])


def joined_kernel(keep_ref, other_ref, out_ref, sem):
    side = lax.axis_index("tensor")
    copies = [
        pltpu.make_async_copy(keep_ref, out_ref.at[pl.ds(LOCAL * side, LOCAL)], sem.at[0]),
        pltpu.make_async_copy(other_ref, out_ref.at[pl.ds(LOCAL * (1 - side), LOCAL)], sem.at[1]),
    ]
    for c in copies:
        c.start()
    for c in copies:
        c.wait()


def joined(keep, other):
    return pl.pallas_call(
        joined_kernel,
        in_specs=[ANY] * 2,
        out_specs=ANY,
        out_shape=sds((2 * LOCAL, *keep.shape[1:]), keep.dtype),
        scratch_shapes=[pltpu.SemaphoreType.DMA((2,))],
        name="joined",
        compiler_params=params(16),
    )(keep, other)


def on_device(
    tokens,
    slot_position,
    cotangent,
    attention,
    feedforward,
    vectors,
    attn_momentum,
    ffn_momentum,
    vec_momentum,
    attn_average,
    ffn_average,
    vec_average,
):
    place = slot_position
    attn, ffn, table, work = start(attention, feedforward, vectors, tokens)
    x, q, k, v, c, log_tokens = work

    (x, q, k, v), saved, cot_other = chain(place, table, attn, ffn, x, q, k, v, cotangent)
    keep, send, h, g, du, df, da, dc, c, log_total, sums = rows_part(
        place, x, q, k, v, c, log_tokens, cotangent, cot_other, attn, ffn, table
    )
    da, c, dq, dk, dv, thin_sums, ffn_terms, activations = chain_back(
        place, table, attn, ffn, q, k, v, saved, g, du, df, h, (keep, send), dc, log_total, da, c
    )
    rows, hidden, entries = attention.shape[1], feedforward.shape[2], vectors.shape[0]
    if rows % THIN == 0:
        shapes = (rows, hidden, tokens.shape[1])
        attn_grad, ffn_grad, vec_sums, token_grad = tail(
            place, sums, thin_sums, ffn_terms, x, da, dq, dk, dv, c, attn, shapes
        )
        attn_grad = attn_grad.astype(F32)
        ffn_grad = jnp.swapaxes(ffn_grad, 1, 2).astype(F32)
        index = lax.axis_index("dp") * 2 + lax.axis_index("tensor")
        vec_grad = lax.dynamic_slice_in_dim(
            vec_sums[:NVEC].reshape(-1), index * entries, entries
        )
    else:
        keep, send = token_gradient(place, da, dq, dk, dv, attn)
        token_grad = joined(keep, swap(send))
        attn_terms, vec_terms = attn_gradient(x, da, dq, dk, dv, c, sums, thin_sums)
        attn_grad, ffn_grad, vec_grad = scatter_gradients(
            attn_terms, ffn_terms, vec_terms[:NVEC], (rows, hidden, entries)
        )
    grad_scale = 1.0 / math.sqrt(lax.axis_size("dp") * SLOTS * ROWS)
    attn_new = update(attn_grad, attn_momentum, attention, attn_average, ATTENTION_RATE, grad_scale)
    ffn_new = update(ffn_grad, ffn_momentum, feedforward, ffn_average, FEEDFORWARD_RATE, grad_scale)
    vec_new = update(vec_grad, vec_momentum, vectors, vec_average, VECTOR_RATE, grad_scale)
    return (
        activations,
        token_grad,
        attn_new[0],
        ffn_new[0],
        vec_new[0],
        attn_new[1],
        ffn_new[1],
        vec_new[1],
        attn_new[2],
        ffn_new[2],
        vec_new[2],
    )


def solution(mesh):
    attn_spec = P(None, "dp", "tensor")
    ffn_spec = P(None, None, ("dp", "tensor"))
    vec_spec = P(("dp", "tensor"))
    rows_spec = P("dp", "tensor", None)
    states = (attn_spec, ffn_spec, vec_spec)
    return jax.shard_map(
        on_device,
        mesh=mesh,
        in_specs=(rows_spec, P("dp"), rows_spec) + states * 3,
        out_specs=(rows_spec, rows_spec) + states * 3,
        check_vma=False,
    )
```

```python
import functools
import math

import jax
import jax.numpy as jnp
from jax import lax
from jax.experimental import pallas as pl
from jax.experimental.pallas import tpu as pltpu
from jax.sharding import PartitionSpec as P

D = 768
HEADS = 12
DH = 64
FF = 3072
MEM = 10
SLOTS = 4
ROWS = 522
NVEC = 22

HALF = D // 2
SEG = ROWS - MEM
THIN = 16
LOCAL = 2
TILE = 256

EPSILON = 1e-05
MOMENTUM = 0.9
AVERAGE_DECAY = 0.75
ATTENTION_RATE = 0.06
FEEDFORWARD_RATE = 0.02
VECTOR_RATE = 0.1
MASK_VALUE = -1e30
SCALE = 1.0 / math.sqrt(DH)

F32 = jnp.float32
BF16 = jnp.bfloat16
MIB = 1 << 20

QUERY_BIAS, VALUE_BIAS, OUT_BIAS, GAIN1, SHIFT1, DOWN_BIAS, GAIN2, SHIFT2, UP_BIAS = range(9)
FIRST_MEMORY = UP_BIAS + FF // D


def nn(a, b):
    return lax.dot_general(a, b, (((1,), (0,)), ((), ())), preferred_element_type=F32)


def nt(a, b):
    return lax.dot_general(a, b, (((1,), (1,)), ((), ())), preferred_element_type=F32)


def tn(a, b):
    return lax.dot_general(a, b, (((0,), (0,)), ((), ())), preferred_element_type=F32)


def normalized(rows):
    center = rows - jnp.mean(rows, axis=-1, keepdims=True)
    spread = jnp.mean(center * center, axis=-1, keepdims=True)
    inverse = lax.rsqrt(spread + EPSILON)
    return center * inverse, inverse


def normalized_back(grad, unit, inverse):
    mean_grad = jnp.mean(grad, axis=-1, keepdims=True)
    mean_along = jnp.mean(grad * unit, axis=-1, keepdims=True)
    return inverse * (grad - mean_grad - unit * mean_along)


def gelu_parts(u):
    size = jnp.abs(u)
    t = 1.0 / (1.0 + (0.3275911 / math.sqrt(2.0)) * size)
    bell = jnp.exp(-0.5 * u * u)
    poly = t * (
        0.5 * 0.254829592
        + t
        * (
            0.5 * -0.284496736
            + t * (0.5 * 1.421413741 + t * (0.5 * -1.453152027 + t * (0.5 * 1.061405429)))
        )
    )
    tail = poly * bell
    cdf = jnp.where(u < 0, tail, 1.0 - tail)
    return u * cdf, cdf + (u * (1.0 / math.sqrt(2.0 * math.pi))) * bell


def row_sum(block):
    return jnp.sum(block, axis=0, keepdims=True)


def params(limit=60, **more):
    return pltpu.CompilerParams(vmem_limit_bytes=limit * MIB, **more)


def once(shape, index):
    return pl.BlockSpec(shape, lambda *_: index, pipeline_mode=pl.Buffered(1))


ANY = pl.BlockSpec(memory_space=pltpu.HBM)
SMEM = pl.BlockSpec(memory_space=pltpu.SMEM)
VMEM = pl.BlockSpec(memory_space=pltpu.VMEM)


def sds(shape, dtype):
    return jax.ShapeDtypeStruct(shape, dtype)


def my_place():
    dp = lax.axis_index("dp")
    return dp // 4, (dp // 2) % 2, dp % 2, lax.axis_index("tensor")


def device(z, x, c, y):
    return {"dp": (z * 2 + x) * 2 + c, "tensor": y}


def entry_barrier(nz):
    z, x, c, y = my_place()
    barrier = pltpu.get_barrier_semaphore()
    signal = lambda d: pl.semaphore_signal(
        barrier, inc=1, device_id=d, device_id_type=pl.DeviceIdType.MESH
    )
    signal(device(z, 1 - x, c, y))
    signal(device(z, x, 1 - c, y))
    signal(device(z, x, c, 1 - y))

    @pl.when(z > 0)
    def _():
        signal(device(z - 1, x, c, y))

    @pl.when(z < nz - 1)
    def _():
        signal(device(z + 1, x, c, y))

    up = lax.convert_element_type(z < nz - 1, jnp.int32)
    down = lax.convert_element_type(z > 0, jnp.int32)
    pl.semaphore_wait(barrier, 3 + up + down)


def attn_view(ref, z, x, c, y):
    return ref.at[:, z, x, c, :, pl.ds(pl.multiple_of(y * HALF, HALF), HALF)]


def ffn_view(ref, z, x, c, y):
    return ref.at[:, z, x, c, y]


def vec_view(ref, z, x, c, y):
    return ref.at[z, x, c, y]


def hidden_view(ref, z, x, c, y):
    return ref.at[z, x, c, y]


def partners(place, lead):
    _, x, _, y = place
    first = (x + (1 - lead) * (1 - 2 * x), y + lead * (1 - 2 * y))
    second = (x + lead * (1 - 2 * x), y + (1 - lead) * (1 - 2 * y))
    return first, second, (1 - x, 1 - y)


COLUMN, FIRST, SECOND, BOTH, CORE = 0, 1, 2, 3, 4
UP, DOWN, UP_FIRST, DOWN_FIRST = 0, 8, 9, 10


def remote(src, dst, send_sem, recv_sem, target):
    return pltpu.make_async_remote_copy(
        src_ref=src,
        dst_ref=dst,
        send_sem=send_sem,
        recv_sem=recv_sem,
        device_id=target,
        device_id_type=pl.DeviceIdType.MESH,
    )


def gather_steps(nz, place, lead, z_second, pieces, send_sem, recv_sem):
    z, x, c, y = place
    first, second, both = partners(place, lead)
    to_first = device(z, first[0], c, first[1])
    to_second = device(z, second[0], c, second[1])
    to_core = device(z, x, 1 - c, y)

    def copies(send, recv, shard, target):
        return [
            remote(
                view(out, *shard),
                view(out, *shard),
                send_sem.at[send, shard[0], i],
                recv_sem.at[recv, shard[0], i],
                target,
            )
            for i, out, view in pieces
        ]

    def start(*args):
        for copy in copies(*args):
            copy.start()

    def arrived(*args):
        for copy in copies(*args):
            copy.wait_recv()

    def sent(*args):
        for copy in copies(*args):
            copy.wait_send()

    def column(zz):
        return (zz, x, c, y)

    def of_first(zz):
        return (zz, first[0], c, first[1])

    def of_second(zz):
        return (zz, second[0], c, second[1])

    def of_both(zz):
        return (zz, both[0], c, both[1])

    core_first, core_second = CORE + 2 - lead, CORE + 1 + lead

    def move_up(zz):
        return (UP, COLUMN, column(zz), device(z + 1, x, c, y))

    def move_down(zz):
        return (DOWN, COLUMN, column(zz), device(z - 1, x, c, y))

    def first_up(zz):
        return (UP_FIRST, FIRST, of_first(zz), device(z + 1, x, c, y))

    def first_down(zz):
        return (DOWN_FIRST, FIRST, of_first(zz), device(z - 1, x, c, y))

    def along(zz, rising, falling, up, down):
        if rising:

            @pl.when(z < nz - 1)
            def _():
                start(*up(zz))

        if falling:

            @pl.when(z > 0)
            def _():
                start(*down(zz))

    def stage0(zz, rising, falling, wait):
        if wait:
            arrived(UP, COLUMN, column(zz), to_core)
        if z_second and not wait:
            start(FIRST, FIRST, column(zz), to_first)
        along(zz, rising, falling, move_up, move_down)
        if not z_second:
            start(FIRST, FIRST, column(zz), to_first)
        start(SECOND, SECOND, column(zz), to_second)
        start(CORE, CORE, column(zz), to_core)

    def stage1(zz, rising, falling):
        arrived(FIRST, FIRST, of_first(zz), to_first)
        if z_second:
            along(zz, rising, falling, first_up, first_down)
        start(BOTH, BOTH, of_first(zz), to_second)
        start(core_first, core_first, of_first(zz), to_core)

    def stage2(zz, rising, falling):
        arrived(SECOND, SECOND, of_second(zz), to_second)
        start(core_second, core_second, of_second(zz), to_core)
        arrived(BOTH, BOTH, of_both(zz), to_second)
        start(CORE + 3, CORE + 3, of_both(zz), to_core)

    def begin():
        stage0(z, True, True, False)

    def step(t):
        @pl.when((t < nz) & (z - t >= 0))
        def _():
            stage0(z - t, True, False, True)

        @pl.when((t < nz) & (z + t < nz))
        def _():
            stage0(z + t, False, True, True)

        for lag, stage in ((1, stage1), (2, stage2)):
            late = t - lag

            @pl.when(late == 0)
            def _():
                stage(z, True, True)

            @pl.when((late > 0) & (late < nz) & (z - late >= 0))
            def _():
                stage(z - late, True, False)

            @pl.when((late > 0) & (late < nz) & (z + late < nz))
            def _():
                stage(z + late, False, True)

    def all_arrived(zz, carry):
        for fx in range(2):
            for fy in range(2):
                kind = CORE + 2 * fx + fy
                shard = (zz, x + fx * (1 - 2 * x), 1 - c, y + fy * (1 - 2 * y))
                arrived(kind, kind, shard, to_core)
        return carry

    def all_sent(zz, carry):
        @pl.when((zz <= z) & (z < nz - 1))
        def _():
            sent(*move_up(zz))

        @pl.when((zz >= z) & (z > 0))
        def _():
            sent(*move_down(zz))

        if z_second:

            @pl.when((zz <= z) & (z < nz - 1))
            def _():
                sent(*first_up(zz))

            @pl.when((zz >= z) & (z > 0))
            def _():
                sent(*first_down(zz))

            @pl.when(zz == z)
            def _():
                sent(FIRST, FIRST, column(zz), to_first)

        else:
            sent(FIRST, FIRST, column(zz), to_first)
        sent(SECOND, SECOND, column(zz), to_second)
        sent(BOTH, BOTH, of_first(zz), to_second)
        sent(CORE, CORE, column(zz), to_core)
        sent(core_first, core_first, of_first(zz), to_core)
        sent(core_second, core_second, of_second(zz), to_core)
        sent(CORE + 3, CORE + 3, of_both(zz), to_core)
        return carry

    def end_arrive():
        lax.fori_loop(0, nz, all_arrived, 0)

    def end_send():
        lax.fori_loop(0, nz, all_sent, 0)

    return begin, step, end_arrive, end_send


def swap_halves(place, rows, other, sem):
    z, x, c, y = place
    return remote(
        rows.at[pl.ds(LOCAL * (1 - y), LOCAL)],
        other,
        sem.at[0],
        sem.at[1],
        device(z, x, c, 1 - y),
    )


def place_rows(place, keep, send, out, sem):
    z, x, c, y = place
    own = out.at[pl.ds(LOCAL * y, LOCAL)]
    return [
        pltpu.make_async_copy(keep, own, sem.at[2]),
        remote(send, own, sem.at[0], sem.at[1], device(z, x, c, 1 - y)),
    ]


def gather_kernel(nz, views, *refs):
    n = len(views)
    srcs, tokens, outs, other = refs[:n], refs[n], refs[n + 1 : 2 * n + 1], refs[2 * n + 1]
    send_sem, recv_sem, own_sem, swap_sem = refs[2 * n + 2 :]
    place = my_place()
    halves = swap_halves(place, tokens, other, swap_sem)
    own = [
        pltpu.make_async_copy(src, view(out, *place), own_sem.at[i])
        for i, (src, out, view) in enumerate(zip(srcs, outs, views))
    ]
    for copy in own:
        copy.start()
    entry_barrier(nz)
    halves.start()
    for copy in own:
        copy.wait()
    pieces = [(i, out, view) for i, (out, view) in enumerate(zip(outs, views))]
    begin, step, end_arrive, end_send = gather_steps(
        nz, place, place[2], False, pieces, send_sem, recv_sem
    )
    begin()

    def loop(t, carry):
        step(t)
        return carry

    lax.fori_loop(1, nz + 2, loop, 0)
    end_send()
    end_arrive()
    halves.wait()


def gather(nz, collective_id, parts, tokens):
    shards, shapes, views = zip(*parts)
    n = len(parts)
    return pl.pallas_call(
        functools.partial(gather_kernel, nz, views),
        in_specs=[ANY] * (n + 1),
        out_specs=[ANY] * (n + 1),
        out_shape=[sds(shape, shard.dtype) for shard, shape in zip(shards, shapes)]
        + [sds((LOCAL, *tokens.shape[1:]), tokens.dtype)],
        scratch_shapes=[
            pltpu.SemaphoreType.DMA((11, nz, n)),
            pltpu.SemaphoreType.DMA((8, nz, n)),
            pltpu.SemaphoreType.DMA((n,)),
            pltpu.SemaphoreType.DMA((2,)),
        ],
        name="gather",
        compiler_params=params(collective_id=collective_id, has_side_effects=True),
    )(*shards, tokens)


def scatter_kernel(nz, views, *refs):
    n = len(views)
    terms, outs = refs[:n], refs[n : 2 * n]
    mine, from_core, from_second, from_first, from_below, from_above = (
        refs[2 * n + i * n : 3 * n + i * n] for i in range(6)
    )
    send_sem, recv_sem, own_sem = refs[8 * n :]
    place = z, x, c, y = my_place()
    first, second, both = partners(place, place[2])
    to_first = device(z, first[0], c, first[1])
    to_second = device(z, second[0], c, second[1])
    to_core = device(z, x, 1 - c, y)

    def copies(srcs, dsts, send, recv, zz, target):
        return [
            pltpu.make_async_remote_copy(
                src_ref=srcs[i],
                dst_ref=dsts[i],
                send_sem=send_sem.at[send, zz, i],
                recv_sem=recv_sem.at[recv, zz, i],
                device_id=target,
                device_id_type=pl.DeviceIdType.MESH,
            )
            for i in range(n)
        ]

    def slots(bufs, *index):
        return [b.at[index] for b in bufs]

    def pick(refs_, *index):
        return [b[index] for b in refs_]

    flips = [(fx, fy) for fx in range(2) for fy in range(2)]

    def at(fx, fy):
        return x + fx * (1 - 2 * x), y + fy * (1 - 2 * y)

    def core_copies(zz, f):
        fx, fy = flips[f]
        xx, yy = at(fx, fy)
        return copies(
            [view(t, zz, xx, 1 - c, yy) for t, view in zip(terms, views)],
            slots(from_core, zz, f),
            f,
            f,
            zz,
            to_core,
        )

    def own_copies(zz, f):
        fx, fy = flips[f]
        xx, yy = at(fx, fy)
        return [
            pltpu.make_async_copy(
                view(t, zz, xx, c, yy), mine[i].at[zz, f], own_sem.at[f, zz, i]
            )
            for i, (t, view) in enumerate(zip(terms, views))
        ]

    f_first, f_second = 2 - c, 1 + c

    def second_copies(zz, across):
        return copies(
            slots(from_core, zz, 3 if across else f_second),
            slots(from_second, zz, 1 if across else 0),
            4 + across,
            4 + across,
            zz,
            to_second,
        )

    def first_copies(zz):
        return copies(slots(from_second, zz, 1), slots(from_first, zz), 6, 6, zz, to_first)

    def up_copies(zz):
        return copies(slots(from_first, zz), slots(from_below, zz), 7, 7, zz, device(z + 1, x, c, y))

    def down_copies(zz):
        return copies(slots(from_first, zz), slots(from_above, zz), 8, 8, zz, device(z - 1, x, c, y))

    def run(group, what):
        for copy in group:
            getattr(copy, what)()

    def add(into, index, other, other_index):
        for i in range(n):
            a, b = into[i].at[index], other[i].at[other_index]
            a[...] = (a[...].astype(F32) + b[...].astype(F32)).astype(a.dtype)

    def by_distance(t, do):
        @pl.when((t >= 0) & (t < nz) & (z - t >= 0))
        def _():
            do(z - t)

        @pl.when((t > 0) & (t < nz) & (z + t < nz))
        def _():
            do(z + t)

    def start_own(zz):
        for f in range(4):
            run(own_copies(zz, f), "start")

    def start_core(zz):
        for f in (3, 1, 2, 0):
            run(core_copies(zz, f), "start")

    def stage0(zz):
        for f in (3, 1, 2, 0):
            run(core_copies(zz, f), "wait_recv")
            run(own_copies(zz, f), "wait")
            add(from_core, (zz, f), mine, (zz, f))
        run(second_copies(zz, 1), "start")
        run(second_copies(zz, 0), "start")

    def stage1(zz):
        run(second_copies(zz, 1), "wait_recv")
        add(from_second, (zz, 1), from_core, (zz, f_first))
        run(first_copies(zz), "start")

    def stage2(zz):
        run(second_copies(zz, 0), "wait_recv")
        add(from_second, (zz, 0), from_core, (zz, 0))
        run(first_copies(zz), "wait_recv")
        add(from_first, (zz,), from_second, (zz, 0))

        @pl.when(zz > z)
        def _():
            @pl.when(z > 0)
            def _():
                run(up_copies(zz), "wait_recv")
                add(from_first, (zz,), from_below, (zz,))

            run(up_copies(zz), "start")

        @pl.when(zz < z)
        def _():
            @pl.when(z < nz - 1)
            def _():
                run(down_copies(zz), "wait_recv")
                add(from_first, (zz,), from_above, (zz,))

            run(down_copies(zz), "start")

    entry_barrier(nz)

    def begin(k, carry):
        by_distance(nz - 1 - k, start_core)
        by_distance(nz - 1 - k, start_own)
        return carry

    lax.fori_loop(0, nz, begin, 0)

    def step(k, carry):
        t = nz - 1 - k
        by_distance(t, stage0)
        by_distance(t + 1, stage1)
        by_distance(t + 2, stage2)
        return carry

    lax.fori_loop(0, nz + 2, step, 0)

    @pl.when(z > 0)
    def _():
        run(up_copies(z), "wait_recv")
        add(from_first, (z,), from_below, (z,))

    @pl.when(z < nz - 1)
    def _():
        run(down_copies(z), "wait_recv")
        add(from_first, (z,), from_above, (z,))

    for i in range(n):
        outs[i][...] = from_first[i][z]

    def finish(zz, carry):
        for f in range(4):
            run(core_copies(zz, f), "wait_send")
        run(second_copies(zz, 1), "wait_send")
        run(second_copies(zz, 0), "wait_send")
        run(first_copies(zz), "wait_send")

        @pl.when(zz > z)
        def _():
            run(up_copies(zz), "wait_send")

        @pl.when(zz < z)
        def _():
            run(down_copies(zz), "wait_send")

        return carry

    lax.fori_loop(0, nz, finish, 0)


def scatter(nz, collective_id, parts):
    terms, shapes, views = zip(*parts)
    n = len(parts)
    dtypes = [t.dtype for t in terms]

    def bufs(*lead):
        return [pltpu.VMEM((*lead, *shape), d) for shape, d in zip(shapes, dtypes)]

    return pl.pallas_call(
        functools.partial(scatter_kernel, nz, views),
        in_specs=[ANY] * n,
        out_specs=[VMEM] * n,
        out_shape=[sds(shape, d) for shape, d in zip(shapes, dtypes)],
        scratch_shapes=[
            *bufs(nz, 4),
            *bufs(nz, 4),
            *bufs(nz, 2),
            *bufs(nz),
            *bufs(nz),
            *bufs(nz),
            pltpu.SemaphoreType.DMA((9, nz, n)),
            pltpu.SemaphoreType.DMA((9, nz, n)),
            pltpu.SemaphoreType.DMA((4, nz, n)),
        ],
        name="scatter",
        compiler_params=params(62, collective_id=collective_id, has_side_effects=True),
    )(*terms)


def whole_rows(side, mine, other):
    mine, other = mine.astype(F32), other.astype(F32)
    first = jnp.where(side == 0, mine, other)
    second = jnp.where(side == 0, other, mine)
    return jnp.concatenate([jnp.zeros((MEM, D), F32), first, second], axis=0)


def split_rows(side, rows):
    half = (SEG - MEM) // 2
    first, second = rows[MEM : MEM + half], rows[MEM + half :]
    keep = jnp.where(side == 0, first, second)
    send = jnp.where(side == 0, second, first)
    return keep, send


def project_kernel(mine_ref, other_ref, w_ref, table_ref, x_ref, q_ref, k_ref, v_ref):
    side = lax.axis_index("tensor")
    mine = mine_ref[LOCAL * side + pl.program_id(0)]
    x = whole_rows(side, mine, other_ref[0]).astype(BF16)
    x_ref[0] = x
    query = nn(x, w_ref[0]) + table_ref[QUERY_BIAS : QUERY_BIAS + 1, :]
    q_ref[0] = (query * SCALE).astype(BF16)
    k_ref[0] = nn(x, w_ref[1]).astype(BF16)
    v_ref[0] = (nn(x, w_ref[2]) + table_ref[VALUE_BIAS : VALUE_BIAS + 1, :]).astype(BF16)


def slot_rows(width=D):
    return pl.BlockSpec((1, SEG, width), lambda s: (s, 0, 0))


def half_rows(half):
    return pl.BlockSpec((1, half, D), lambda s: (s, 0, 0))


def project(tokens, other, attn, table):
    return pl.pallas_call(
        project_kernel,
        grid=(LOCAL,),
        in_specs=[
            once(tokens.shape, (0, 0, 0)),
            half_rows(tokens.shape[1]),
            once((3, D, D), (0, 0, 0)),
            once((NVEC, D), (0, 0)),
        ],
        out_specs=[slot_rows()] * 4,
        out_shape=[sds((LOCAL, SEG, D), BF16)] * 4,
        name="project",
        compiler_params=params(),
    )(tokens, other, attn, table)


def head_masks():
    feature_head = lax.broadcasted_iota(jnp.int32, (1, D), 1) // DH
    return [feature_head == h for h in range(HEADS)]


def by_head(rows16, masks):
    zero = jnp.zeros_like(rows16)
    return jnp.concatenate([jnp.where(m, rows16, zero) for m in masks], axis=0)


def own_columns(blocks, masks):
    total = jnp.zeros((THIN, D), blocks.dtype)
    for h, m in enumerate(masks):
        total = jnp.where(m, blocks[THIN * h : THIN * (h + 1)], total)
    return total


def copies_of(key_mask_shape):
    row = lax.rem(lax.broadcasted_iota(jnp.int32, key_mask_shape, 0), THIN)
    key = lax.broadcasted_iota(jnp.int32, key_mask_shape, 1)
    return jnp.where((key < MEM) & (key <= row), 2.0, 1.0)


def pair_barrier(place):
    z, x, c, y = place
    barrier = pltpu.get_barrier_semaphore()
    pl.semaphore_signal(
        barrier,
        inc=1,
        device_id=device(z, x, c, 1 - y),
        device_id_type=pl.DeviceIdType.MESH,
    )
    pl.semaphore_wait(barrier, 1)


def chain_kernel(
    place_ref,
    table_ref,
    attn_ref,
    ffn_ref,
    x_in,
    q_in,
    k_in,
    v_in,
    cot_ref,
    x_ref,
    q_ref,
    k_ref,
    v_ref,
    saved_d_ref,
    saved_f_ref,
    saved_s_ref,
    cot_other_ref,
    wa,
    wf,
    xb,
    qb,
    kb,
    vb,
    save_d,
    save_f,
    save_s,
    left,
    given,
    sem_w,
    sem_x,
    sem_kv,
    sem_out,
    sem_memory,
    sem_cot,
):
    del x_in, q_in, k_in, v_in
    place = z, x, c, y = my_place()
    loads = [
        pltpu.make_async_copy(attn_ref, wa, sem_w.at[0]),
        pltpu.make_async_copy(ffn_ref.at[0], wf.at[0], sem_w.at[1]),
        pltpu.make_async_copy(ffn_ref.at[1], wf.at[1], sem_w.at[2]),
    ]
    tiles = [
        pltpu.make_async_copy(x_ref.at[s, pl.ds(0, THIN)], xb.at[s], sem_x.at[s])
        for s in range(LOCAL)
    ]
    keys = [
        pltpu.make_async_copy(src.at[s], dst.at[s], sem_kv.at[2 * s + i])
        for s in range(LOCAL)
        for i, (src, dst) in enumerate(((k_ref, kb), (v_ref, vb)))
    ]
    for copy in tiles + loads[:1] + keys + loads[1:]:
        copy.start()
    pair_barrier(place)
    cot_swap = swap_halves(place, cot_ref, cot_other_ref, sem_cot)
    cot_swap.start()
    handed = remote(left, given, sem_memory.at[0], sem_memory.at[1], device(z, x, c, 1 - y))

    masks = head_masks()
    memory_row = lax.broadcasted_iota(jnp.int32, (THIN, 1), 0) < MEM
    first = table_ref[FIRST_MEMORY:NVEC, :]
    first = jnp.concatenate([first, jnp.zeros((THIN - MEM, D), F32)], axis=0)
    row = lambda r: table_ref[r : r + 1, :]

    def slots(turn, memory):
        for s in range(LOCAL):
            tiles[s].wait()
            if s == 0:
                loads[0].wait()
            keys[2 * s].wait()
            keys[2 * s + 1].wait()
            if memory is None:
                memory = first
            else:
                memory = jnp.where(place_ref[LOCAL * turn + s] == 0, first, memory)
            x16 = jnp.where(memory_row, memory, xb[s].astype(F32)).astype(BF16)
            xb[s] = x16
            qb[s] = ((nn(x16, wa[0]) + row(QUERY_BIAS)) * SCALE).astype(BF16)
            kb[s, 0:THIN] = nn(x16, wa[1]).astype(BF16)
            vb[s, 0:THIN] = (nn(x16, wa[2]) + row(VALUE_BIAS)).astype(BF16)
            outs = [
                pltpu.make_async_copy(
                    src.at[s, pl.ds(0, THIN)], dst.at[s, pl.ds(0, THIN)], sem_out.at[4 * s + i]
                )
                for i, (src, dst) in enumerate(
                    ((xb, x_ref), (qb, q_ref), (kb, k_ref), (vb, v_ref))
                )
            ]
            for copy in outs:
                copy.start()
            if turn == 1 and s == LOCAL - 1:
                save_d[s] = jnp.zeros_like(save_d[s])
                save_f[s] = jnp.zeros_like(save_f[s])
                save_s[s] = jnp.zeros_like(save_s[s])
            else:
                q_heads = by_head(qb[s], masks)
                score = nt(q_heads, kb[s])
                top = jnp.max(score, axis=-1, keepdims=True)
                weight = jnp.exp(score - top) * copies_of(score.shape)
                total = jnp.sum(weight, axis=-1, keepdims=True)
                share = (weight / total).astype(BF16)
                log_total = top + jnp.log(total)
                context = own_columns(nn(share, vb[s]), masks).astype(BF16)
                unit1, inverse1 = normalized(
                    x16.astype(F32) + nt(context, wa[3]) + row(OUT_BIAS)
                )
                hidden = (unit1 * row(GAIN1) + row(SHIFT1)).astype(BF16)
                if s == 0:
                    loads[1].wait()
                up = nt(hidden, wf[0])
                up_bias = jnp.concatenate([row(UP_BIAS + i) for i in range(FF // D)], axis=1)
                active16, slope = gelu_parts(up + up_bias)
                active16 = active16.astype(BF16)
                if s == 0:
                    loads[2].wait()
                second = hidden.astype(F32) + nn(active16, wf[1]) + row(DOWN_BIAS)
                unit2, inverse2 = normalized(second)
                output = (unit2 * row(GAIN2) + row(SHIFT2)).astype(BF16)
                memory = output.astype(F32)
                if turn == 0 and s == LOCAL - 1:
                    left[...] = output
                    handed.start()
                save_d[s, 0] = hidden
                save_d[s, 1] = unit1.astype(BF16)
                save_d[s, 2] = unit2.astype(BF16)
                save_d[s, 3] = context
                save_f[s, 0] = active16
                save_f[s, 1] = slope.astype(BF16)
                wide = lambda v: jnp.broadcast_to(v, (v.shape[0], 128))
                save_s[s, 0 : HEADS * THIN] = wide(log_total)
                save_s[s, HEADS * THIN : HEADS * THIN + THIN] = wide(inverse1)
                save_s[s, HEADS * THIN + THIN :] = wide(inverse2)
            for copy in outs:
                copy.wait()

    @pl.when(y == 0)
    def _():
        slots(0, None)
        handed.wait_send()

    @pl.when(y == 1)
    def _():
        handed.wait_recv()
        slots(1, given[...].astype(F32))

    saves = [
        pltpu.make_async_copy(save_d, saved_d_ref, sem_out.at[0]),
        pltpu.make_async_copy(save_f, saved_f_ref, sem_out.at[1]),
        pltpu.make_async_copy(save_s, saved_s_ref, sem_out.at[2]),
    ]
    for copy in saves:
        copy.start()
    for copy in saves:
        copy.wait()
    cot_swap.wait()


SAVED = (
    sds((LOCAL, 4, THIN, D), BF16),
    sds((LOCAL, 2, THIN, FF), BF16),
    sds((LOCAL, HEADS * THIN + 2 * THIN, 128), F32),
)


def chain(place, table, attn, ffn, x, q, k, v, cot):
    whole = sds((LOCAL, SEG, D), BF16)
    outs = pl.pallas_call(
        chain_kernel,
        in_specs=[SMEM, VMEM] + [ANY] * 7,
        out_specs=[ANY] * 8,
        out_shape=[whole] * 4 + list(SAVED) + [sds((LOCAL, *cot.shape[1:]), BF16)],
        input_output_aliases={4 + i: i for i in range(4)},
        scratch_shapes=[
            pltpu.VMEM((4, D, D), BF16),
            pltpu.VMEM((2, FF, D), BF16),
            pltpu.VMEM((LOCAL, THIN, D), BF16),
            pltpu.VMEM((LOCAL, THIN, D), BF16),
            pltpu.VMEM((LOCAL, SEG, D), BF16),
            pltpu.VMEM((LOCAL, SEG, D), BF16),
            *[pltpu.VMEM(s.shape, s.dtype) for s in SAVED],
            pltpu.VMEM((THIN, D), BF16),
            pltpu.VMEM((THIN, D), BF16),
            pltpu.SemaphoreType.DMA((3,)),
            pltpu.SemaphoreType.DMA((LOCAL,)),
            pltpu.SemaphoreType.DMA((2 * LOCAL,)),
            pltpu.SemaphoreType.DMA((4 * LOCAL,)),
            pltpu.SemaphoreType.DMA((2,)),
            pltpu.SemaphoreType.DMA((2,)),
        ],
        name="chain",
        compiler_params=params(collective_id=2, has_side_effects=True),
    )(place, table, attn, ffn, x, q, k, v, cot)
    return outs[:4], outs[4:7], outs[7]


def own_lanes(block, head):
    lane = lax.broadcasted_iota(jnp.int32, block.shape, 1)
    return jnp.where((lane < DH) == (head == 0), block, jnp.zeros_like(block))


def seen(score, first_query):
    key = lax.broadcasted_iota(jnp.int32, score.shape, 0)
    query = lax.broadcasted_iota(jnp.int32, score.shape, 1) + first_query
    return key <= query


def attend_pair(q, k, v):
    contexts_of, logs_of = [], [[], []]
    for part in range(SEG // TILE):
        rows = slice(TILE * part, TILE * (part + 1))
        keys = slice(0, TILE * (part + 1))
        contexts = []
        for head in range(2):
            score = nt(own_lanes(k[keys], head), q[rows])
            key = lax.broadcasted_iota(jnp.int32, score.shape, 0)
            allowed = seen(score, TILE * part) & (key >= MEM)
            score = jnp.where(allowed, score, MASK_VALUE)
            top = jnp.max(score, axis=0, keepdims=True)
            weight = jnp.exp(score - top)
            total = jnp.sum(weight, axis=0, keepdims=True)
            share = (weight * (1.0 / total)).astype(BF16)
            logs_of[head].append(top + jnp.log(total))
            contexts.append(tn(share, v[keys]))
        lane = lax.broadcasted_iota(jnp.int32, contexts[0].shape, 1)
        contexts_of.append(jnp.where(lane < DH, contexts[0], contexts[1]).astype(BF16))
    return jnp.concatenate(contexts_of, axis=0), [jnp.concatenate(l, axis=1) for l in logs_of]


def attend_kernel(q_ref, k_ref, v_ref, c_ref, log_ref):
    context, logs = attend_pair(q_ref[0], k_ref[0], v_ref[0])
    c_ref[0] = context
    for head in range(2):
        log_ref[0, 0, head : head + 1] = logs[head]


def with_memory(q, k16, v16, context, log_tokens):
    masks = head_masks()
    score = nt(by_head(k16, masks), q).reshape(HEADS, THIN, SEG)
    key = lax.broadcasted_iota(jnp.int32, score.shape, 1)
    score = jnp.where(key < MEM, score, MASK_VALUE)
    top = jnp.maximum(jnp.max(score, axis=1), log_tokens)
    weight = jnp.exp(score - top[:, None])
    old = jnp.exp(log_tokens - top)
    total = jnp.sum(weight, axis=1) + old
    share = (weight * (1.0 / total)[:, None]).reshape(HEADS * THIN, SEG).astype(BF16)
    kept = old / total
    coarse = kept.astype(BF16)
    fine = (kept - coarse.astype(F32)).astype(BF16)
    pad = jnp.zeros((4, SEG), BF16)
    head = lax.rem(lax.broadcasted_iota(jnp.int32, (2 * THIN, D), 0), THIN)
    spread = jnp.where(head == lax.broadcasted_iota(jnp.int32, (2 * THIN, D), 1) // DH, 1.0, 0.0)
    factor = tn(jnp.concatenate([coarse, pad, fine, pad], axis=0), spread.astype(BF16))
    context = factor * context.astype(F32) + tn(share, by_head(v16, masks))
    return context.astype(BF16), top + jnp.log(total)


PAIR = pl.BlockSpec((1, SEG, 2 * DH), lambda s, h: (s, 0, h))
PAIR_LOG = pl.BlockSpec((1, 1, 2, SEG), lambda s, h: (s, h, 0, 0))


def attend(q, k, v):
    return pl.pallas_call(
        attend_kernel,
        grid=(LOCAL, HEADS // 2),
        in_specs=[PAIR] * 3,
        out_specs=[PAIR, PAIR_LOG],
        out_shape=[sds((LOCAL, SEG, D), BF16), sds((LOCAL, HEADS // 2, 2, SEG), F32)],
        name="attend",
        compiler_params=params(),
    )(q, k, v)


def attend_back_pair(q, k, v, dc, logs):
    last = SEG // TILE
    key_terms, value_terms, query_terms = [], [], []
    for head in range(2):
        key_sum, value_sum, query_parts = [], [], []
        for part in range(last):
            rows = slice(TILE * part, TILE * (part + 1))
            keys = slice(0, TILE * (part + 1))
            score = nt(own_lanes(k[keys], head), q[rows])
            share = jnp.exp(score - logs[head : head + 1, rows])
            diagonal = jnp.where(seen(share[rows], 0), share[rows], 0.0)
            share = jnp.concatenate([share[: TILE * part], diagonal], axis=0) if part else diagonal
            share_grad = nt(own_lanes(v[keys], head), dc[rows])
            inner = jnp.sum(share_grad * share, axis=0, keepdims=True)
            score_grad = (share * (share_grad - inner)).astype(BF16)
            value_sum.append(nn(share.astype(BF16), dc[rows]))
            key_sum.append(nn(score_grad, q[rows]))
            query_parts.append(tn(score_grad, k[keys]))
        key_terms.append(key_sum)
        value_terms.append(value_sum)
        query_terms.append(query_parts)
    lane = lax.broadcasted_iota(jnp.int32, (TILE, 2 * DH), 1)
    pick = lambda a, b: jnp.where(lane < DH, a, b)
    dq, dk, dv = [], [], []
    for part in range(last):
        rows = slice(TILE * part, TILE * (part + 1))
        dq.append((pick(query_terms[0][part], query_terms[1][part]) * SCALE).astype(BF16))
        for terms, out in ((key_terms, dk), (value_terms, dv)):
            total = None
            for later in range(part, last):
                term = pick(terms[0][later][rows], terms[1][later][rows])
                total = term if total is None else total + term
            out.append(total)
    return [jnp.concatenate(parts, axis=0) for parts in (dq, dk, dv)]


def rows_kernel(
    place_ref,
    x_ref,
    q_ref,
    k16_ref,
    v16_ref,
    tokens_c_ref,
    tokens_log_ref,
    mine_ref,
    other_ref,
    wo_ref,
    wf_ref,
    table_ref,
    keep_ref,
    send_ref,
    h_ref,
    g_ref,
    du_ref,
    df_ref,
    da_ref,
    dc_ref,
    c_ref,
    log_ref,
    sums_ref,
    slope_ref,
):
    row = lambda r: table_ref[r : r + 1, :]
    slot = pl.program_id(0)
    side = lax.axis_index("tensor")
    live = place_ref[LOCAL * side + slot] >= 0

    @pl.when(slot == 0)
    def _():
        sums_ref[...] = jnp.zeros_like(sums_ref)

    def add(r, value):
        sums_ref[r : r + 1, :] += value

    log_tokens = jnp.concatenate([tokens_log_ref[0, h] for h in range(HEADS // 2)], axis=0)
    context, log_total = with_memory(
        q_ref[0], k16_ref[0], v16_ref[0], tokens_c_ref[0], log_tokens
    )
    c_ref[0] = context
    for h in range(HEADS // 2):
        log_ref[0, h] = log_total[2 * h : 2 * h + 2]
    unit1, inverse1 = normalized(x_ref[0].astype(F32) + nt(context, wo_ref[0]) + row(OUT_BIAS))
    hidden = (unit1 * row(GAIN1) + row(SHIFT1)).astype(BF16)
    h_ref[0] = hidden
    second = hidden.astype(F32) + row(DOWN_BIAS)
    for i in range(FF // D):
        cols = slice(D * i, D * (i + 1))
        up = nt(hidden, wf_ref[0, cols]) + row(UP_BIAS + i)
        active, slope = gelu_parts(up)
        active = active.astype(BF16)
        g_ref[0, :, cols] = active
        slope_ref[:, cols] = slope.astype(BF16)
        second = second + nn(active, wf_ref[1, cols])
    unit2, inverse2 = normalized(second)
    output = jnp.where(live, unit2 * row(GAIN2) + row(SHIFT2), 0.0)
    keep, send = split_rows(side, output)
    keep_ref[0] = keep.astype(BF16)
    send_ref[0] = send.astype(BF16)

    grad = whole_rows(side, mine_ref[LOCAL * side + slot], other_ref[0])
    grad = jnp.where(live, grad, 0.0)
    add(GAIN2, row_sum(grad * unit2))
    add(SHIFT2, row_sum(grad))
    second_grad = normalized_back(grad * row(GAIN2), unit2, inverse2)
    down_grad = second_grad.astype(BF16)
    df_ref[0] = down_grad
    add(DOWN_BIAS, row_sum(down_grad.astype(F32)))
    hidden_grad = second_grad
    for i in range(FF // D):
        cols = slice(D * i, D * (i + 1))
        up_grad = (nt(down_grad, wf_ref[1, cols]) * slope_ref[:, cols].astype(F32)).astype(BF16)
        du_ref[0, :, cols] = up_grad
        add(UP_BIAS + i, row_sum(up_grad.astype(F32)))
        hidden_grad = hidden_grad + nn(up_grad, wf_ref[0, cols])
    add(GAIN1, row_sum(hidden_grad * unit1))
    add(SHIFT1, row_sum(hidden_grad))
    branch_grad = normalized_back(hidden_grad * row(GAIN1), unit1, inverse1).astype(BF16)
    da_ref[0] = branch_grad
    add(OUT_BIAS, row_sum(branch_grad.astype(F32)))
    dc_ref[0] = nn(branch_grad, wo_ref[0]).astype(BF16)


def rows_part(place, x, q, k, v, c, log_tokens, cot, other, attn, ffn, table):
    half = cot.shape[1]
    whole, whole_wide = sds((LOCAL, SEG, D), BF16), sds((LOCAL, SEG, FF), BF16)
    part, logs = sds((LOCAL, half, D), BF16), sds((LOCAL, HEADS // 2, 2, SEG), F32)
    rows, wide = slot_rows(), slot_rows(FF)
    thin = pl.BlockSpec((1, THIN, D), lambda s: (s, 0, 0))
    log_rows = pl.BlockSpec((1, HEADS // 2, 2, SEG), lambda s: (s, 0, 0, 0))
    return pl.pallas_call(
        rows_kernel,
        grid=(LOCAL,),
        in_specs=[SMEM, rows, rows, thin, thin, rows, log_rows]
        + [once(cot.shape, (0, 0, 0)), half_rows(half)]
        + [once((1, D, D), (3, 0, 0)), once((2, FF, D), (0, 0, 0)), once((NVEC, D), (0, 0))],
        out_specs=[half_rows(half)] * 2
        + [rows, wide, wide, rows, rows, rows, rows, log_rows, once((THIN, D), (0, 0))],
        out_shape=[part] * 2
        + [whole, whole_wide, whole_wide, whole, whole, whole, whole, logs, sds((THIN, D), F32)],
        scratch_shapes=[pltpu.VMEM((SEG, FF), BF16)],
        name="rows_part",
        compiler_params=params(),
    )(place, x, q, k, v, c, log_tokens, cot, other, attn, ffn, table)


CHUNK = 768


def memory_key_gradient(q, k16, v16, dc, context, logs, masks):
    score = nt(by_head(k16, masks), q).reshape(HEADS, THIN, SEG)
    key = lax.broadcasted_iota(jnp.int32, score.shape, 1)
    share = jnp.where(key < MEM, jnp.exp(score - logs[:, None]), 0.0)
    share_grad = nt(by_head(v16, masks), dc).reshape(HEADS, THIN, SEG)
    product = dc.astype(F32) * context.astype(F32)
    coarse = product.astype(BF16)
    fine = (product - coarse.astype(F32)).astype(BF16)
    head = lax.broadcasted_iota(jnp.int32, (THIN, D), 0)
    ones = jnp.where(head == lax.broadcasted_iota(jnp.int32, (THIN, D), 1) // DH, 1.0, 0.0)
    ones = ones.astype(BF16)
    inner = (nt(ones, coarse) + nt(ones, fine))[0:HEADS]
    score_grad = (share * (share_grad - inner[:, None])).reshape(HEADS * THIN, SEG)
    share = share.reshape(HEADS * THIN, SEG).astype(BF16)
    dk = own_columns(nn(score_grad.astype(BF16), q), masks)
    return dk, own_columns(nn(share, dc), masks)


def chain_back_kernel(
    place_ref,
    table_ref,
    attn_ref,
    ffn_ref,
    q_ref,
    k_ref,
    v_ref,
    saved_d_ref,
    saved_f_ref,
    saved_s_ref,
    g_ref,
    du_ref,
    df_ref,
    h_ref,
    keep_ref,
    send_ref,
    dc_ref,
    log_ref,
    da_in,
    c_in,
    da_ref,
    c_ref,
    dq_ref,
    dk_ref,
    dv_ref,
    sums_ref,
    terms_ref,
    rows_ref,
    wa,
    wf,
    qb,
    kb,
    vb,
    dcb,
    cb,
    logs,
    dqb,
    dkb,
    dvb,
    tiles,
    df,
    hid,
    gb,
    dub,
    staged,
    save_d,
    save_f,
    save_s,
    thin_d,
    thin_f,
    sums,
    left,
    given,
    sem_w,
    sem_in,
    sem_ff,
    sem_chunk,
    sem_out,
    sem_stage,
    sem_grad,
    sem_swap,
):
    del da_in, c_in
    place = z, x, c, y = my_place()
    loads = [
        pltpu.make_async_copy(attn_ref, wa, sem_w.at[0]),
        pltpu.make_async_copy(ffn_ref.at[0], wf.at[0], sem_w.at[1]),
        pltpu.make_async_copy(ffn_ref.at[1], wf.at[1], sem_w.at[2]),
    ]
    first_rows = lambda ref: ref.at[:, pl.ds(0, THIN)]
    saved = [
        pltpu.make_async_copy(saved_d_ref, save_d, sem_in.at[2]),
        pltpu.make_async_copy(saved_f_ref, save_f, sem_in.at[3]),
        pltpu.make_async_copy(saved_s_ref, save_s, sem_in.at[4]),
    ]
    reads = [
        pltpu.make_async_copy(src, dst, sem_in.at[5 + i])
        for i, (src, dst) in enumerate(
            ((q_ref, qb), (k_ref, kb), (v_ref, vb), (dc_ref, dcb), (c_ref, cb), (log_ref, logs))
        )
    ]
    merged = (da_ref, c_ref)
    tile_reads = [
        pltpu.make_async_copy(first_rows(ref), tiles.at[i], sem_in.at[i])
        for i, ref in enumerate(merged)
    ]
    rows_in = [
        pltpu.make_async_copy(df_ref, df, sem_ff.at[0]),
        pltpu.make_async_copy(h_ref, hid, sem_ff.at[1]),
    ]

    def chunk_reads(i):
        lanes = pl.ds(pl.multiple_of(CHUNK * i, CHUNK), CHUNK)
        slot = lax.rem(i, 2)
        return [
            pltpu.make_async_copy(src.at[:, :, lanes], dst.at[slot], sem_chunk.at[slot, j])
            for j, (src, dst) in enumerate(((g_ref, gb), (du_ref, dub)))
        ]

    @pl.when(y == 1)
    def _():
        for copy in reads + loads[:1] + saved + loads[:0:-1] + tile_reads:
            copy.start()
        for copy in rows_in + chunk_reads(0) + chunk_reads(1):
            copy.start()

    @pl.when(y == 0)
    def _():
        for copy in rows_in + chunk_reads(0) + chunk_reads(1):
            copy.start()
        for copy in reads + saved + loads[:0:-1] + loads[:1] + tile_reads:
            copy.start()

    pair_barrier(place)
    swap = place_rows(place, keep_ref, send_ref, rows_ref, sem_swap)
    for copy in swap:
        copy.start()
    handed = remote(left, given, sem_grad.at[0], sem_grad.at[1], device(z, x, c, 1 - y))

    sums[...] = jnp.zeros_like(sums)
    thin_d[...] = jnp.zeros_like(thin_d)
    thin_f[...] = jnp.zeros_like(thin_f)
    for buf in (dqb, dkb, dvb):
        buf[...] = jnp.zeros_like(buf)
    masks = head_masks()
    memory_row = lax.broadcasted_iota(jnp.int32, (THIN, 1), 0) < MEM
    row = lambda r: table_ref[r : r + 1, :]

    def add(r, value):
        sums[r : r + 1, :] += value

    def attend_at(i, carry):
        s, h = i // (HEADS // 2), lax.rem(i, HEADS // 2)
        lanes = pl.ds(pl.multiple_of(h * 2 * DH, 2 * DH), 2 * DH)
        pair = (buf[s, :, lanes] for buf in (qb, kb, vb, dcb))
        dq, dk, dv = attend_back_pair(*pair, logs[s, h])
        dqb[s, THIN:, lanes] = dq[THIN:]
        dqb[s, 0:THIN, lanes] = jnp.where(memory_row, dqb[s, 0:THIN, lanes], dq[0:THIN])
        dkb[s, :, lanes] = (dk + dkb[s, :, lanes].astype(F32)).astype(BF16)
        dvb[s, :, lanes] = (dv + dvb[s, :, lanes].astype(F32)).astype(BF16)
        return carry

    pairs = LOCAL * HEADS // 2

    def key_gradient(s):
        rows = jnp.concatenate([logs[s, h] for h in range(HEADS // 2)], axis=0)
        return memory_key_gradient(
            qb[s], kb[s, 0:THIN], vb[s, 0:THIN], dcb[s], cb[s], rows, masks
        )

    def slots(turn, grad):
        waited = set()

        def need(*copies):
            for copy in copies:
                if id(copy) not in waited:
                    waited.add(id(copy))
                    copy.wait()

        for s in reversed(range(LOCAL)):
            if turn == 1 and s == LOCAL - 1:
                grad = jnp.zeros((THIN, D), F32)
            else:
                after = place_ref[LOCAL * turn + s + 1]
                grad = jnp.where(memory_row, jnp.where(after > 0, grad, 0.0), 0.0)
                need(*saved)
                unit1, unit2 = save_d[s, 1].astype(F32), save_d[s, 2].astype(F32)
                base = HEADS * THIN
                log_total = save_s[s, 0:base, 0:1]
                inverse1 = save_s[s, base : base + THIN, 0:1]
                inverse2 = save_s[s, base + THIN :, 0:1]
                add(GAIN2, row_sum(grad * unit2))
                add(SHIFT2, row_sum(grad))
                second_grad = normalized_back(grad * row(GAIN2), unit2, inverse2)
                down_grad = second_grad.astype(BF16)
                add(DOWN_BIAS, row_sum(down_grad.astype(F32)))
                need(loads[2])
                up_grad = (nt(down_grad, wf[1]) * save_f[s, 1].astype(F32)).astype(BF16)
                up_sum = row_sum(up_grad.astype(F32))
                for i in range(FF // D):
                    add(UP_BIAS + i, up_sum[:, D * i : D * (i + 1)])
                need(loads[1])
                hidden_grad = second_grad + nn(up_grad, wf[0])
                add(GAIN1, row_sum(hidden_grad * unit1))
                add(SHIFT1, row_sum(hidden_grad))
                pre_grad = normalized_back(hidden_grad * row(GAIN1), unit1, inverse1)
                branch_grad = pre_grad.astype(BF16)
                add(OUT_BIAS, row_sum(branch_grad.astype(F32)))
                need(loads[0])
                context_grad = nn(branch_grad, wa[3]).astype(BF16)
                dc_heads = by_head(context_grad, masks)
                q_heads = by_head(qb[s, 0:THIN], masks)
                score = nt(q_heads, kb[s])
                share = jnp.exp(score - log_total) * copies_of(score.shape)
                share_grad = nt(dc_heads, vb[s])
                inner = jnp.sum(share_grad * share, axis=-1, keepdims=True)
                score_grad = (share * (share_grad - inner)).astype(BF16)
                query_grad = (own_columns(nn(score_grad, kb[s]), masks) * SCALE).astype(BF16)
                dkb[s] = (dkb[s].astype(F32) + tn(score_grad, q_heads)).astype(BF16)
                dvb[s] = (dvb[s].astype(F32) + tn(share.astype(BF16), dc_heads)).astype(BF16)
                dqb[s, 0:THIN] = jnp.where(memory_row, query_grad, dqb[s, 0:THIN])
                thin_d[s, 0] = down_grad
                thin_d[s, 1] = save_d[s, 0]
                thin_f[s, 0] = up_grad
                thin_f[s, 1] = save_f[s, 0]
                need(*tile_reads)
                for i, value in enumerate((branch_grad, save_d[s, 3])):
                    tiles[i, s] = jnp.where(memory_row, value, tiles[i, s])
                grad = pre_grad + nt(query_grad, wa[0])
            need(loads[0])
            dk, dv = dkb[s, 0:THIN], dvb[s, 0:THIN]
            if turn == 1:
                early_k, early_v = key_gradient(s)
                dk = (dk.astype(F32) + early_k).astype(BF16)
                dv = (dv.astype(F32) + early_v).astype(BF16)
            grad = grad + nt(dk, wa[1]) + nt(dv, wa[2])
            first = jnp.where(place_ref[LOCAL * turn + s] == 0, grad, 0.0)
            sums[FIRST_MEMORY : FIRST_MEMORY + THIN, :] += first
        return grad

    @pl.when(y == 1)
    def _():
        for copy in reads:
            copy.wait()
        left[...] = slots(1, None)
        handed.start()
        lax.fori_loop(0, pairs, attend_at, 0)

    @pl.when(y == 0)
    def _():
        for copy in reads:
            copy.wait()
        lax.fori_loop(0, pairs, attend_at, 0)
        handed.wait_recv()
        slots(0, given[...])

    writes = [
        pltpu.make_async_copy(dqb, dq_ref, sem_out.at[0]),
        pltpu.make_async_copy(dkb, dk_ref, sem_out.at[1]),
        pltpu.make_async_copy(dvb, dv_ref, sem_out.at[2]),
        pltpu.make_async_copy(sums, sums_ref, sem_out.at[3]),
        *[
            pltpu.make_async_copy(tiles.at[i], first_rows(ref), sem_out.at[5 + i])
            for i, ref in enumerate(merged)
        ],
    ]
    for copy in writes:
        copy.start()

    for copy in rows_in:
        copy.wait()
    for s in range(LOCAL):
        df[s, 0:THIN] = jnp.where(memory_row, thin_d[s, 0], df[s, 0:THIN])
        hid[s, 0:THIN] = jnp.where(memory_row, thin_d[s, 1], hid[s, 0:THIN])
    chunks = FF // CHUNK

    def store(i):
        lanes = pl.ds(pl.multiple_of(CHUNK * i, CHUNK), CHUNK)
        slot = lax.rem(i, 2)
        return pltpu.make_async_copy(
            staged.at[slot], terms_ref.at[:, lanes], sem_stage.at[slot]
        )

    def chunk(i, carry):
        slot = lax.rem(i, 2)
        for copy in chunk_reads(i):
            copy.wait()
        lanes = pl.ds(pl.multiple_of(CHUNK * i, CHUNK), CHUNK)
        for s in range(LOCAL):
            for j, buf in ((1, gb), (0, dub)):
                old = buf[slot, s, 0:THIN]
                buf[slot, s, 0:THIN] = jnp.where(memory_row, thin_f[s, j, :, lanes], old)

        @pl.when(i >= 2)
        def _():
            store(i - 2).wait()

        for j, (buf, rows) in enumerate(((dub, hid), (gb, df))):
            terms = tn(
                buf[slot].reshape(LOCAL * SEG, CHUNK), rows[...].reshape(LOCAL * SEG, D)
            )
            staged[slot, j] = terms.astype(BF16)
        store(i).start()

        @pl.when(i + 2 < chunks)
        def _():
            for copy in chunk_reads(i + 2):
                copy.start()

        return carry

    lax.fori_loop(0, chunks, chunk, 0)

    @pl.when(y == 1)
    def _():
        handed.wait_send()

    for copy in [*writes, store(chunks - 2), store(chunks - 1)]:
        copy.wait()
    for copy in swap:
        copy.wait()


THIN_SHAPES = (
    sds((LOCAL, 2, THIN, D), BF16),
    sds((LOCAL, 2, THIN, FF), BF16),
    sds((FIRST_MEMORY + THIN, D), F32),
)


def chain_back(place, table, attn, ffn, q, k, v, saved, g, du, df, h, halves, dc, logs, da, c):
    whole = sds((LOCAL, SEG, D), BF16)
    rows = pltpu.VMEM(whole.shape, BF16)
    dma = lambda *shape: pltpu.SemaphoreType.DMA(shape)
    outs = pl.pallas_call(
        chain_back_kernel,
        in_specs=[SMEM, VMEM] + [ANY] * 18,
        out_specs=[ANY] * 8,
        out_shape=[whole] * 5
        + [THIN_SHAPES[2]]
        + [sds((2, FF, D), BF16), sds((2 * LOCAL, *halves[0].shape[1:]), BF16)],
        input_output_aliases={18: 0, 19: 1},
        scratch_shapes=[
            pltpu.VMEM((4, D, D), BF16),
            pltpu.VMEM((2, FF, D), BF16),
            *[rows] * 5,
            pltpu.VMEM(logs.shape, F32),
            rows,
            rows,
            rows,
            pltpu.VMEM((2, LOCAL, THIN, D), BF16),
            rows,
            rows,
            pltpu.VMEM((2, LOCAL, SEG, CHUNK), BF16),
            pltpu.VMEM((2, LOCAL, SEG, CHUNK), BF16),
            pltpu.VMEM((2, 2, CHUNK, D), BF16),
            *[pltpu.VMEM(s.shape, s.dtype) for s in SAVED + THIN_SHAPES],
            pltpu.VMEM((THIN, D), F32),
            pltpu.VMEM((THIN, D), F32),
            dma(3),
            dma(11),
            dma(2),
            dma(2, 2),
            dma(8),
            dma(2),
            dma(2),
            dma(3),
        ],
        name="chain_back",
        compiler_params=params(collective_id=3, has_side_effects=True),
    )(place, table, attn, ffn, q, k, v, *saved, g, du, df, h, *halves, dc, logs, da, c)
    return outs


def table_row(ref, index, entries):
    blocks = []
    lane = lax.broadcasted_iota(jnp.int32, (1, 128), 1)
    for block in range(D // 128):
        at, end = index * D + 128 * block, index * D + 128 * (block + 1)
        target, value = 0, jnp.zeros((1, 128), F32)
        while at < end:
            shard, inner = at // entries, at % entries
            count = min(end - at, entries - inner, 128 - inner % 128)
            place = (shard // 8, shard // 4 % 2, shard // 2 % 2, shard % 2)
            source = ref[place][inner // 128 : inner // 128 + 1]
            shift = (target - inner) % 128
            if shift:
                source = pltpu.roll(source, shift, 1)
            value = jnp.where((lane >= target) & (lane < target + count), source, value)
            at, target = at + count, target + count
        blocks.append(value)
    return jnp.concatenate(blocks, axis=1)


def head_kernel(
    nz,
    entries,
    attn_src,
    ffn_src,
    vec_src,
    tokens,
    attn_ref,
    ffn_ref,
    vec_ref,
    x_ref,
    q_ref,
    k_ref,
    v_ref,
    c_ref,
    log_ref,
    wa,
    vec,
    mine,
    other,
    xb,
    qb,
    kb,
    vb,
    cb,
    logs,
    send_sem,
    recv_sem,
    own_sem,
    swap_sem,
    out_sem,
):
    place = my_place()
    side = place[3]
    halves = swap_halves(place, tokens, other, swap_sem)
    own = [
        pltpu.make_async_copy(attn_src, attn_view(wa, *place), own_sem.at[0]),
        pltpu.make_async_copy(vec_src, vec_view(vec, *place), own_sem.at[1]),
        pltpu.make_async_copy(ffn_src, ffn_view(ffn_ref, *place), own_sem.at[2]),
        pltpu.make_async_copy(tokens.at[pl.ds(LOCAL * side, LOCAL)], mine, own_sem.at[3]),
    ]
    for copy in own:
        copy.start()
    entry_barrier(nz)
    steps = functools.partial(gather_steps, nz, place, send_sem=send_sem, recv_sem=recv_sem)
    begin, step, end_arrive, end_send = steps(
        1, True, [(0, wa, attn_view), (1, vec, vec_view)]
    )
    late = [
        steps(place[2], bool(i), [(2 + i, ffn_ref.at[i], hidden_view)]) for i in range(2)
    ]
    own[0].wait()
    own[1].wait()
    begin()
    step(1)
    halves.start()

    def loop(t, carry):
        step(t)
        return carry

    lax.fori_loop(2, nz + 2, loop, 0)
    own[2].wait()
    for begin2, _, _, _ in late:
        begin2()
    own[3].wait()
    halves.wait()
    end_arrive()
    outs = [
        pltpu.make_async_copy(wa, attn_ref, out_sem.at[0]),
        pltpu.make_async_copy(vec, vec_ref, out_sem.at[1]),
    ]
    for copy in outs:
        copy.start()

    weight = lambda i: wa[i].reshape(D, D)

    def project_slot(s):
        x = whole_rows(side, mine[s], other[s]).astype(BF16)
        xb[s] = x
        qb[s] = ((nn(x, weight(0)) + table_row(vec, QUERY_BIAS, entries)) * SCALE).astype(BF16)
        kb[s] = nn(x, weight(1)).astype(BF16)
        vb[s] = (nn(x, weight(2)) + table_row(vec, VALUE_BIAS, entries)).astype(BF16)
        for i, (buf, out) in enumerate(((xb, x_ref), (qb, q_ref), (kb, k_ref), (vb, v_ref))):
            outs.append(pltpu.make_async_copy(buf.at[s], out.at[s], out_sem.at[2 + 4 * s + i]))
            outs[-1].start()

    def attend_at(i, carry):
        s, h = i // (HEADS // 2), i % (HEADS // 2)
        lanes = pl.ds(pl.multiple_of(h * 2 * DH, 2 * DH), 2 * DH)
        context, log_rows = attend_pair(qb[s, :, lanes], kb[s, :, lanes], vb[s, :, lanes])
        cb[s, :, lanes] = context
        for head in range(2):
            logs[s, h, head : head + 1] = log_rows[head]
        return carry

    project_slot(0)
    project_slot(1)
    pairs = LOCAL * HEADS // 2
    done = 0
    for t in range(1, nz + 2):
        for _, step2, _, _ in late:
            step2(t)
        upto = pairs * t // (nz + 1)
        lax.fori_loop(done, upto, attend_at, 0)
        done = upto
    outs.append(pltpu.make_async_copy(cb, c_ref, out_sem.at[2 + 4 * LOCAL]))
    outs.append(pltpu.make_async_copy(logs, log_ref, out_sem.at[3 + 4 * LOCAL]))
    outs[-1].start()
    outs[-2].start()
    end_send()
    for _, _, end_arrive2, end_send2 in late:
        end_send2()
        end_arrive2()
    for copy in outs:
        copy.wait()


def head(nz, attention, hidden_major, vec, tokens, entries):
    rows, hidden = attention.shape[1], hidden_major.shape[1]
    whole = sds((LOCAL, SEG, D), BF16)
    logs = (LOCAL, HEADS // 2, 2, SEG)
    attn_shape, vec_shape = (4, nz, 2, 2, rows, D), (nz, 2, 2, 2, *VEC_TILE)
    half = pltpu.VMEM((LOCAL, *tokens.shape[1:]), BF16)
    return pl.pallas_call(
        functools.partial(head_kernel, nz, entries),
        in_specs=[ANY] * 4,
        out_specs=[ANY] * 9,
        out_shape=[
            sds(attn_shape, BF16),
            sds((2, nz, 2, 2, 2, hidden, D), BF16),
            sds(vec_shape, F32),
            *[whole] * 5,
            sds(logs, F32),
        ],
        scratch_shapes=[
            pltpu.VMEM(attn_shape, BF16),
            pltpu.VMEM(vec_shape, F32),
            half,
            half,
            *[pltpu.VMEM(whole.shape, BF16)] * 5,
            pltpu.VMEM(logs, F32),
            pltpu.SemaphoreType.DMA((11, nz, 4)),
            pltpu.SemaphoreType.DMA((8, nz, 4)),
            pltpu.SemaphoreType.DMA((4,)),
            pltpu.SemaphoreType.DMA((2,)),
            pltpu.SemaphoreType.DMA((4 + 4 * LOCAL,)),
        ],
        name="head",
        compiler_params=params(collective_id=0, has_side_effects=True),
    )(attention, hidden_major, vec, tokens)


def token_grad_kernel(place_ref, da_ref, dq_ref, dk_ref, dv_ref, w_ref, keep_ref, send_ref):
    side = lax.axis_index("tensor")
    total = da_ref[0].astype(F32)
    for i, ref in enumerate((dq_ref, dk_ref, dv_ref)):
        total = total + nt(ref[0], w_ref[i])
    live = place_ref[LOCAL * side + pl.program_id(0)] >= 0
    keep, send = split_rows(side, jnp.where(live, total, 0.0))
    keep_ref[0] = keep.astype(BF16)
    send_ref[0] = send.astype(BF16)


def token_gradient(place, da, dq, dk, dv, attn):
    half = (SEG - MEM) // 2
    return pl.pallas_call(
        token_grad_kernel,
        grid=(LOCAL,),
        in_specs=[SMEM] + [slot_rows()] * 4 + [once((3, D, D), (0, 0, 0))],
        out_specs=[half_rows(half)] * 2,
        out_shape=[sds((LOCAL, half, D), BF16)] * 2,
        name="token_gradient",
        compiler_params=params(),
    )(place, da, dq, dk, dv, attn)


def flat(ref):
    return ref[...].reshape(LOCAL * ref.shape[1], ref.shape[2])


def attn_grad_kernel(
    x_ref, da_ref, dq_ref, dk_ref, dv_ref, c_ref, sums_ref, thin_sums_ref, out_ref, vec_ref
):
    x = flat(x_ref)
    dq, dv = flat(dq_ref), flat(dv_ref)
    out_ref[0] = tn(x, dq).astype(BF16)
    out_ref[1] = tn(x, flat(dk_ref)).astype(BF16)
    out_ref[2] = tn(x, dv).astype(BF16)
    out_ref[3] = tn(flat(da_ref), flat(c_ref)).astype(BF16)
    vec_ref[...] = thin_sums_ref[...]
    vec_ref[0:FIRST_MEMORY] = thin_sums_ref[0:FIRST_MEMORY] + sums_ref[0:FIRST_MEMORY]
    vec_ref[QUERY_BIAS : QUERY_BIAS + 1] = row_sum(dq.astype(F32))
    vec_ref[VALUE_BIAS : VALUE_BIAS + 1] = row_sum(dv.astype(F32))


def attn_gradient(x, da, dq, dk, dv, c, sums, thin_sums, chunk=256):
    part = pl.BlockSpec((LOCAL, SEG, chunk), lambda i: (0, 0, i))
    full = once((LOCAL, SEG, D), (0, 0, 0))
    lanes = lambda rows: pl.BlockSpec((rows, chunk), lambda i: (0, i))
    return pl.pallas_call(
        attn_grad_kernel,
        grid=(D // chunk,),
        in_specs=[full, full, part, part, part, part, lanes(THIN), lanes(FIRST_MEMORY + THIN)],
        out_specs=[
            pl.BlockSpec((4, D, chunk), lambda i: (0, 0, i)),
            lanes(FIRST_MEMORY + THIN),
        ],
        out_shape=[sds((4, D, D), BF16), sds((FIRST_MEMORY + THIN, D), F32)],
        name="attn_gradient",
        compiler_params=params(),
    )(x, da, dq, dk, dv, c, sums, thin_sums)


def scatter_steps(nz, place, lead, z_second, pieces, send_sem, recv_sem):
    z, x, c, y = place
    first, second, both = partners(place, lead)
    to_first = device(z, first[0], c, first[1])
    to_second = device(z, second[0], c, second[1])
    to_core = device(z, x, 1 - c, y)
    f_first, f_second = 2 - lead, 1 + lead

    def at(f):
        fx, fy = f // 2, f % 2
        return x + fx * (1 - 2 * x), y + fy * (1 - 2 * y)

    def term(piece, zz, core, f):
        xx, yy = at(f)
        return piece[2](piece[1], zz, xx, core, yy)

    def copies(kind, zz, target, src, dst):
        return [
            remote(src(p), dst(p), send_sem.at[kind, zz, p[0]], recv_sem.at[kind, zz, p[0]], target)
            for p in pieces
        ]

    def core_copies(zz, f):
        return copies(
            f, zz, to_core, lambda p: term(p, zz, 1 - c, f), lambda p: p[3].at[zz, f]
        )

    def second_copies(zz, across):
        f = 3 if across else f_second
        return copies(
            4 + across, zz, to_second, lambda p: p[3].at[zz, f], lambda p: p[4].at[zz, across]
        )

    def first_copies(zz):
        slot = 0 if z_second else zz
        return copies(6, zz, to_first, lambda p: p[4].at[zz, 1], lambda p: p[5].at[slot])

    def partial(p, zz, f):
        return p[4].at[zz, f] if z_second else p[5].at[zz]

    def beside(p, above, zz, f):
        return p[6 + above].at[zz, f] if z_second else p[6 + above].at[zz]

    def up_copies(zz, f):
        return copies(
            7 + 2 * f,
            zz,
            device(z + 1, x, c, y),
            lambda p: partial(p, zz, f),
            lambda p: beside(p, 0, zz, f),
        )

    def down_copies(zz, f):
        return copies(
            8 + 2 * f,
            zz,
            device(z - 1, x, c, y),
            lambda p: partial(p, zz, f),
            lambda p: beside(p, 1, zz, f),
        )

    def run(group, what):
        for copy in group:
            getattr(copy, what)()

    def add(into, other):
        for p in pieces:
            a, b = into(p), other(p)
            a[...] = (a[...].astype(F32) + b[...].astype(F32)).astype(a.dtype)

    def turn(k):
        upper = z // (nz // 2)
        return (1 - upper) * (nz - 1 - k) + upper * k

    def start(zz):
        for f in (3, 1, 2, 0):
            run(core_copies(zz, f), "start")

    def stage0(zz):
        for f in (3, 1, 2, 0):
            run(core_copies(zz, f), "wait_recv")
            add(lambda p: p[3].at[zz, f], lambda p: term(p, zz, c, f))
        run(second_copies(zz, 1), "start")
        run(second_copies(zz, 0), "start")

    def from_below(zz, f):
        run(up_copies(zz, f), "wait_recv")
        add(lambda p: partial(p, zz, f), lambda p: beside(p, 0, zz, f))

    def from_above(zz, f):
        run(down_copies(zz, f), "wait_recv")
        add(lambda p: partial(p, zz, f), lambda p: beside(p, 1, zz, f))

    def from_end(zz, f):
        @pl.when((zz > z) & (z == 0))
        def _():
            run(up_copies(zz, f), "start")

        @pl.when((zz < z) & (z == nz - 1))
        def _():
            run(down_copies(zz, f), "start")

    def along(zz, f):
        @pl.when((zz > z) & (z > 0))
        def _():
            from_below(zz, f)
            run(up_copies(zz, f), "start")

        @pl.when((zz < z) & (z < nz - 1))
        def _():
            from_above(zz, f)
            run(down_copies(zz, f), "start")

    def stage1(zz):
        run(second_copies(zz, 1), "wait_recv")
        add(lambda p: p[4].at[zz, 1], lambda p: p[3].at[zz, f_first])
        if z_second:
            from_end(zz, 1)
        else:
            run(first_copies(zz), "start")

    def stage2(zz):
        run(second_copies(zz, 0), "wait_recv")
        add(lambda p: p[4].at[zz, 0], lambda p: p[3].at[zz, 0])
        if not z_second:
            run(first_copies(zz), "wait_recv")
            add(lambda p: p[5].at[zz], lambda p: p[4].at[zz, 0])
        from_end(zz, 0)
        if z_second:
            along(zz, 1)

    def stage3(zz):
        along(zz, 0)

    def staged(stage):
        return lambda k: stage(turn(k))

    def at_owner(f):
        @pl.when(z > 0)
        def _():
            from_below(z, f)

        @pl.when(z < nz - 1)
        def _():
            from_above(z, f)

    def end(outs):
        if z_second:
            at_owner(1)
            run(first_copies(z), "start")
        at_owner(0)
        if z_second:
            run(first_copies(z), "wait_recv")
            add(lambda p: p[4].at[z, 0], lambda p: p[5].at[0])
        for p, out in zip(pieces, outs):
            out[...] = partial(p, z, 0)[...]

    def sent(zz, carry):
        for f in range(4):
            run(core_copies(zz, f), "wait_send")
        run(second_copies(zz, 1), "wait_send")
        run(second_copies(zz, 0), "wait_send")
        for f in range(2 if z_second else 1):

            @pl.when(zz > z)
            def _():
                run(up_copies(zz, f), "wait_send")

            @pl.when(zz < z)
            def _():
                run(down_copies(zz, f), "wait_send")

        if z_second:

            @pl.when(zz == z)
            def _():
                run(first_copies(zz), "wait_send")

        else:
            run(first_copies(zz), "wait_send")
        return carry

    stages = [staged(stage) for stage in (stage0, stage1, stage2, stage3)]
    return start, stages, turn, end, lambda: lax.fori_loop(0, nz, sent, 0)


def scatter_places(nz, shape, z_second):
    lead = (nz, 2) if z_second else (nz,)
    return [
        pltpu.VMEM((nz, 4, *shape), BF16),
        pltpu.VMEM((nz, 2, *shape), BF16),
        pltpu.VMEM((1 if z_second else nz, *shape), BF16),
        pltpu.VMEM((*lead, *shape), BF16),
        pltpu.VMEM((*lead, *shape), BF16),
    ]


VEC_ROWS = FIRST_MEMORY + THIN


def tail_kernel(nz, *refs):
    (
        place_ref,
        sums_ref,
        thin_sums_ref,
        ffn_terms,
        *rows_refs,
        w_ref,
        attn_out,
        ffn_out,
        vec_out,
        grad_ref,
        terms_f,
        terms_a,
        rows,
        wb,
        keep,
        send,
    ) = refs[:21]
    places = [refs[21 + 5 * i : 26 + 5 * i] for i in range(3)]
    vec_mine, vec_given, vec_z, send_sem, recv_sem, block_sem, in_sem, swap_sem, vec_sem = refs[36:]
    place = z, x, c, y = my_place()
    blocks = lambda zz: pltpu.make_async_copy(
        ffn_terms.at[:, zz], terms_f.at[:, zz], block_sem.at[zz]
    )
    rows_in = [
        pltpu.make_async_copy(src, rows.at[i], in_sem.at[2 + i]) for i, src in enumerate(rows_refs)
    ]
    rows_in.append(pltpu.make_async_copy(w_ref.at[pl.ds(0, 3)], wb, in_sem.at[8]))
    steps = functools.partial(scatter_steps, nz, place, send_sem=send_sem, recv_sem=recv_sem)
    up = steps(c, True, [(0, terms_f.at[0], hidden_view, *places[0])])
    down = steps(1 - c, True, [(1, terms_f.at[1], hidden_view, *places[1])])
    attn = steps(1, False, [(2, terms_a, attn_view, *places[2])])
    turn = up[2]
    for k in range(nz):
        blocks(turn(k)).start()
    for copy in rows_in:
        copy.start()

    barrier = pltpu.get_barrier_semaphore()
    others = [device(lax.rem(z + dz, nz), x, c, y) for dz in range(1, nz)]
    for other in [device(z, 1 - x, c, y), device(z, x, 1 - c, y), device(z, x, c, 1 - y), *others]:
        pl.semaphore_signal(
            barrier, inc=1, device_id=other, device_id_type=pl.DeviceIdType.MESH
        )
    pl.semaphore_wait(barrier, 2 + nz)

    def begin(k, carry):
        zz = turn(k)
        blocks(zz).wait()
        up[0](zz)
        down[0](zz)
        return carry

    def attn_terms(i, carry):
        left, right = rows[i // 3], rows[i + 2]
        value = tn(left.reshape(LOCAL * SEG, D), right.reshape(LOCAL * SEG, D))
        terms_a[i] = value.astype(BF16).reshape(terms_a.shape[1:])
        return carry

    def token_rows(s):
        total = rows[1, s].astype(F32)
        for i in range(3):
            total = total + nt(rows[2 + i, s], wb[i])
        live = place_ref[LOCAL * y + s] >= 0
        stay, go = split_rows(y, jnp.where(live, total, 0.0))
        keep[s] = stay.astype(BF16)
        send[s] = go.astype(BF16)

    def vec_copies(phase):
        if phase < 3:
            target = (device(z, x, 1 - c, y), device(z, x, c, 1 - y), device(z, 1 - x, c, y))[phase]
            sems = vec_sem.at[0, phase], vec_sem.at[1, phase]
            return [remote(vec_mine.at[phase], vec_given.at[phase], *sems, target)]
        return [
            remote(
                vec_mine.at[3], vec_z.at[dz], vec_sem.at[0, 3 + dz], vec_sem.at[1, 3 + dz], target
            )
            for dz, target in enumerate(others)
        ]

    def vec_start(phase):
        if phase == 0:
            vec_mine[0] = thin_sums_ref[...]
            vec_mine[0, 0:FIRST_MEMORY] = (
                thin_sums_ref[0:FIRST_MEMORY] + sums_ref[0:FIRST_MEMORY]
            )
            for r, i in ((QUERY_BIAS, 2), (VALUE_BIAS, 4)):
                total = row_sum(rows[i].reshape(LOCAL * SEG, D).astype(F32))
                vec_mine[0, r : r + 1] = total
        else:
            for copy in vec_copies(phase - 1):
                copy.wait_recv()
            vec_mine[phase] = vec_mine[phase - 1] + vec_given[phase - 1]
        for copy in vec_copies(phase):
            copy.start()

    swap = place_rows(place, keep, send, grad_ref, swap_sem)

    def stage(i, *groups):
        for k in groups[-1]:
            for group in groups[:-1]:
                group[1][i](k)

    def step(k, *groups):
        for lag in range(4):
            if 0 <= k - lag < nz:
                stage(lag, *groups, (k - lag,))

    lax.fori_loop(0, 2, begin, 0)
    step(0, up, down)
    for copy in rows_in:
        copy.wait()
    lax.fori_loop(0, 2, attn_terms, 0)
    lax.fori_loop(2, 3, begin, 0)
    step(1, up, down)
    lax.fori_loop(2, 4, attn_terms, 0)
    vec_start(0)
    lax.fori_loop(3, 4, begin, 0)
    attn[0](turn(0))
    step(2, up, down)
    step(0, attn)
    attn[0](turn(1))
    token_rows(0)
    vec_start(1)
    step(3, up, down)
    step(1, attn)
    attn[0](turn(2))
    token_rows(1)
    for copy in swap:
        copy.start()
    step(4, up, down)
    step(2, attn)
    attn[0](turn(3))
    vec_start(2)
    step(5, up, down)
    step(3, attn)
    vec_start(3)
    step(6, up, down)
    step(4, attn)
    up[3]([ffn_out.at[0]])
    step(5, attn)
    down[3]([ffn_out.at[1]])
    step(6, attn)
    attn[3]([attn_out])
    total = vec_mine[3]
    for dz, copy in enumerate(vec_copies(3)):
        copy.wait_recv()
        total = total + vec_z[dz]
    vec_out[...] = total
    for phase in range(4):
        for copy in vec_copies(phase):
            copy.wait_send()
    for group in (up, down, attn):
        group[4]()
    for copy in swap:
        copy.wait()


def tail(place, sums, thin_sums, ffn_terms, x, da, dq, dk, dv, c, attn, shapes):
    nz = lax.axis_size("dp") // 4
    rows, hidden, half = shapes
    attn_shape, ffn_shape = (4, nz, 2, 2, rows, D), (2, nz, 2, 2, 2, hidden, D)
    part = pltpu.VMEM((LOCAL, half, D), BF16)
    dma = lambda *shape: pltpu.SemaphoreType.DMA(shape)
    return pl.pallas_call(
        functools.partial(tail_kernel, nz),
        in_specs=[SMEM, VMEM, VMEM] + [ANY] * 8,
        out_specs=[VMEM] * 3 + [ANY],
        out_shape=[
            sds((4, rows, HALF), BF16),
            sds((2, hidden, D), BF16),
            sds((VEC_ROWS, D), F32),
            sds((2 * LOCAL, half, D), BF16),
        ],
        scratch_shapes=[
            pltpu.VMEM(ffn_shape, BF16),
            pltpu.VMEM(attn_shape, BF16),
            pltpu.VMEM((6, LOCAL, SEG, D), BF16),
            pltpu.VMEM((3, D, D), BF16),
            part,
            part,
            *scatter_places(nz, (hidden, D), True),
            *scatter_places(nz, (hidden, D), True),
            *scatter_places(nz, (4, rows, HALF), False),
            pltpu.VMEM((4, VEC_ROWS, D), F32),
            pltpu.VMEM((3, VEC_ROWS, D), F32),
            pltpu.VMEM((nz - 1, VEC_ROWS, D), F32),
            dma(11, nz, 3),
            dma(11, nz, 3),
            dma(nz),
            dma(9),
            dma(3),
            dma(2, 2 + nz),
        ],
        name="tail",
        compiler_params=params(62, collective_id=1, has_side_effects=True),
    )(place, sums, thin_sums, ffn_terms.reshape(ffn_shape), x, da, dq, dk, dv, c, attn)


def update(gradient, momentum, weight, average, rate, grad_scale):
    scaled = gradient * grad_scale
    moment = MOMENTUM * momentum + scaled
    weight_new = weight - rate * (scaled + MOMENTUM * moment)
    return (moment, weight_new, AVERAGE_DECAY * average + (1.0 - AVERAGE_DECAY) * weight_new)


VEC_TILE = (8, 128)


def in_tiles(rows):
    size = VEC_TILE[0] * VEC_TILE[1]
    padded = jnp.pad(rows, [(0, 0)] * (rows.ndim - 1) + [(0, size - rows.shape[-1])])
    return padded.reshape(*rows.shape[:-1], *VEC_TILE)


def start(attention, feedforward, vectors, tokens):
    nz = lax.axis_size("dp") // 4
    rows, hidden, entries = attention.shape[1], feedforward.shape[2], vectors.shape[0]
    attention = attention.astype(BF16)
    hidden_major = jnp.swapaxes(feedforward.astype(BF16), 1, 2)
    vec = in_tiles(vectors.astype(BF16).astype(F32))
    aligned = rows % THIN == 0
    if aligned:
        attn, ffn, table, *work = head(nz, attention, hidden_major, vec, tokens, entries)
    else:
        attn, ffn, table, other = gather(
            nz,
            0,
            [
                (attention, (4, nz, 2, 2, rows, D), attn_view),
                (hidden_major, (2, nz, 2, 2, 2, hidden, D), ffn_view),
                (vec, (nz, 2, 2, 2, *VEC_TILE), vec_view),
            ],
            tokens,
        )
    attn, ffn = attn.reshape(4, D, D), ffn.reshape(2, FF, D)
    table = table.reshape(nz * 8, VEC_TILE[0] * VEC_TILE[1])[:, :entries].reshape(NVEC, D)
    if not aligned:
        work = project(tokens, other, attn, table)
        work = [*work, *attend(*work[1:])]
    return attn, ffn, table, work


def scatter_gradients(attn_terms, ffn_terms, vec_terms, shapes):
    nz = lax.axis_size("dp") // 4
    rows, hidden, entries = shapes
    attn, ffn, vec = scatter(
        nz,
        1,
        [
            (attn_terms.reshape(4, nz, 2, 2, rows, D), (4, rows, HALF), attn_view),
            (ffn_terms.reshape(2, nz, 2, 2, 2, hidden, D), (2, hidden, D), ffn_view),
            (in_tiles(vec_terms.reshape(nz, 2, 2, 2, entries)), VEC_TILE, vec_view),
        ],
    )
    return attn.astype(F32), jnp.swapaxes(ffn, 1, 2).astype(F32), vec.reshape(-1)[:entries]


def swap(value):
    return lax.ppermute(value, "tensor", [(0, 1), (1, 0)])


def joined_kernel(keep_ref, other_ref, out_ref, sem):
    side = lax.axis_index("tensor")
    copies = [
        pltpu.make_async_copy(keep_ref, out_ref.at[pl.ds(LOCAL * side, LOCAL)], sem.at[0]),
        pltpu.make_async_copy(other_ref, out_ref.at[pl.ds(LOCAL * (1 - side), LOCAL)], sem.at[1]),
    ]
    for c in copies:
        c.start()
    for c in copies:
        c.wait()


def joined(keep, other):
    return pl.pallas_call(
        joined_kernel,
        in_specs=[ANY] * 2,
        out_specs=ANY,
        out_shape=sds((2 * LOCAL, *keep.shape[1:]), keep.dtype),
        scratch_shapes=[pltpu.SemaphoreType.DMA((2,))],
        name="joined",
        compiler_params=params(16),
    )(keep, other)


def on_device(
    tokens,
    slot_position,
    cotangent,
    attention,
    feedforward,
    vectors,
    attn_momentum,
    ffn_momentum,
    vec_momentum,
    attn_average,
    ffn_average,
    vec_average,
):
    place = slot_position
    attn, ffn, table, work = start(attention, feedforward, vectors, tokens)
    x, q, k, v, c, log_tokens = work

    (x, q, k, v), saved, cot_other = chain(place, table, attn, ffn, x, q, k, v, cotangent)
    keep, send, h, g, du, df, da, dc, c, log_total, sums = rows_part(
        place, x, q, k, v, c, log_tokens, cotangent, cot_other, attn, ffn, table
    )
    da, c, dq, dk, dv, thin_sums, ffn_terms, activations = chain_back(
        place, table, attn, ffn, q, k, v, saved, g, du, df, h, (keep, send), dc, log_total, da, c
    )
    rows, hidden, entries = attention.shape[1], feedforward.shape[2], vectors.shape[0]
    if rows % THIN == 0:
        shapes = (rows, hidden, tokens.shape[1])
        attn_grad, ffn_grad, vec_sums, token_grad = tail(
            place, sums, thin_sums, ffn_terms, x, da, dq, dk, dv, c, attn, shapes
        )
        attn_grad = attn_grad.astype(F32)
        ffn_grad = jnp.swapaxes(ffn_grad, 1, 2).astype(F32)
        index = lax.axis_index("dp") * 2 + lax.axis_index("tensor")
        vec_grad = lax.dynamic_slice_in_dim(
            vec_sums[:NVEC].reshape(-1), index * entries, entries
        )
    else:
        keep, send = token_gradient(place, da, dq, dk, dv, attn)
        token_grad = joined(keep, swap(send))
        attn_terms, vec_terms = attn_gradient(x, da, dq, dk, dv, c, sums, thin_sums)
        attn_grad, ffn_grad, vec_grad = scatter_gradients(
            attn_terms, ffn_terms, vec_terms[:NVEC], (rows, hidden, entries)
        )
    grad_scale = 1.0 / math.sqrt(lax.axis_size("dp") * SLOTS * ROWS)
    attn_new = update(attn_grad, attn_momentum, attention, attn_average, ATTENTION_RATE, grad_scale)
    ffn_new = update(ffn_grad, ffn_momentum, feedforward, ffn_average, FEEDFORWARD_RATE, grad_scale)
    vec_new = update(vec_grad, vec_momentum, vectors, vec_average, VECTOR_RATE, grad_scale)
    return (
        activations,
        token_grad,
        attn_new[0],
        ffn_new[0],
        vec_new[0],
        attn_new[1],
        ffn_new[1],
        vec_new[1],
        attn_new[2],
        ffn_new[2],
        vec_new[2],
    )


def solution(mesh):
    attn_spec = P(None, "dp", "tensor")
    ffn_spec = P(None, None, ("dp", "tensor"))
    vec_spec = P(("dp", "tensor"))
    rows_spec = P("dp", "tensor", None)
    states = (attn_spec, ffn_spec, vec_spec)
    return jax.shard_map(
        on_device,
        mesh=mesh,
        in_specs=(rows_spec, P("dp"), rows_spec) + states * 3,
        out_specs=(rows_spec, rows_spec) + states * 3,
        check_vma=False,
    )
```

```python
import functools
import math

import jax
import jax.numpy as jnp
from jax import lax
from jax.experimental import pallas as pl
from jax.experimental.pallas import tpu as pltpu
from jax.sharding import PartitionSpec as P

D = 768
HEADS = 12
DH = 64
FF = 3072
MEM = 10
SLOTS = 4
ROWS = 522
NVEC = 22

HALF = D // 2
SEG = ROWS - MEM
THIN = 16
LOCAL = 2
TILE = 256

EPSILON = 1e-05
MOMENTUM = 0.9
AVERAGE_DECAY = 0.75
ATTENTION_RATE = 0.06
FEEDFORWARD_RATE = 0.02
VECTOR_RATE = 0.1
MASK_VALUE = -1e30
SCALE = 1.0 / math.sqrt(DH)

F32 = jnp.float32
BF16 = jnp.bfloat16
MIB = 1 << 20

QUERY_BIAS, VALUE_BIAS, OUT_BIAS, GAIN1, SHIFT1, DOWN_BIAS, GAIN2, SHIFT2, UP_BIAS = range(9)
FIRST_MEMORY = UP_BIAS + FF // D


def nn(a, b):
    return lax.dot_general(a, b, (((1,), (0,)), ((), ())), preferred_element_type=F32)


def nt(a, b):
    return lax.dot_general(a, b, (((1,), (1,)), ((), ())), preferred_element_type=F32)


def tn(a, b):
    return lax.dot_general(a, b, (((0,), (0,)), ((), ())), preferred_element_type=F32)


def normalized(rows):
    center = rows - jnp.mean(rows, axis=-1, keepdims=True)
    spread = jnp.mean(center * center, axis=-1, keepdims=True)
    inverse = lax.rsqrt(spread + EPSILON)
    return center * inverse, inverse


def normalized_back(grad, unit, inverse):
    mean_grad = jnp.mean(grad, axis=-1, keepdims=True)
    mean_along = jnp.mean(grad * unit, axis=-1, keepdims=True)
    return inverse * (grad - mean_grad - unit * mean_along)


def gelu_parts(u):
    size = jnp.abs(u)
    t = 1.0 / (1.0 + (0.3275911 / math.sqrt(2.0)) * size)
    bell = jnp.exp(-0.5 * u * u)
    poly = t * (
        0.5 * 0.254829592
        + t
        * (
            0.5 * -0.284496736
            + t * (0.5 * 1.421413741 + t * (0.5 * -1.453152027 + t * (0.5 * 1.061405429)))
        )
    )
    tail = poly * bell
    cdf = jnp.where(u < 0, tail, 1.0 - tail)
    return u * cdf, cdf + (u * (1.0 / math.sqrt(2.0 * math.pi))) * bell


def row_sum(block):
    return jnp.sum(block, axis=0, keepdims=True)


def params(limit=60, **more):
    return pltpu.CompilerParams(vmem_limit_bytes=limit * MIB, **more)


def once(shape, index):
    return pl.BlockSpec(shape, lambda *_: index, pipeline_mode=pl.Buffered(1))


ANY = pl.BlockSpec(memory_space=pltpu.HBM)
SMEM = pl.BlockSpec(memory_space=pltpu.SMEM)
VMEM = pl.BlockSpec(memory_space=pltpu.VMEM)


def sds(shape, dtype):
    return jax.ShapeDtypeStruct(shape, dtype)


def my_place():
    dp = lax.axis_index("dp")
    return dp // 4, (dp // 2) % 2, dp % 2, lax.axis_index("tensor")


def device(z, x, c, y):
    return {"dp": (z * 2 + x) * 2 + c, "tensor": y}


def entry_barrier(nz):
    z, x, c, y = my_place()
    barrier = pltpu.get_barrier_semaphore()
    signal = lambda d: pl.semaphore_signal(
        barrier, inc=1, device_id=d, device_id_type=pl.DeviceIdType.MESH
    )
    signal(device(z, 1 - x, c, y))
    signal(device(z, x, 1 - c, y))
    signal(device(z, x, c, 1 - y))

    @pl.when(z > 0)
    def _():
        signal(device(z - 1, x, c, y))

    @pl.when(z < nz - 1)
    def _():
        signal(device(z + 1, x, c, y))

    up = lax.convert_element_type(z < nz - 1, jnp.int32)
    down = lax.convert_element_type(z > 0, jnp.int32)
    pl.semaphore_wait(barrier, 3 + up + down)


def attn_view(ref, z, x, c, y):
    return ref.at[:, z, x, c, :, pl.ds(pl.multiple_of(y * HALF, HALF), HALF)]


def ffn_view(ref, z, x, c, y):
    return ref.at[:, z, x, c, y]


def vec_view(ref, z, x, c, y):
    return ref.at[z, x, c, y]


def hidden_view(ref, z, x, c, y):
    return ref.at[z, x, c, y]


def partners(place, lead):
    _, x, _, y = place
    first = (x + (1 - lead) * (1 - 2 * x), y + lead * (1 - 2 * y))
    second = (x + lead * (1 - 2 * x), y + (1 - lead) * (1 - 2 * y))
    return first, second, (1 - x, 1 - y)


COLUMN, FIRST, SECOND, BOTH, CORE = 0, 1, 2, 3, 4
UP, DOWN, UP_FIRST, DOWN_FIRST = 0, 8, 9, 10


def remote(src, dst, send_sem, recv_sem, target):
    return pltpu.make_async_remote_copy(
        src_ref=src,
        dst_ref=dst,
        send_sem=send_sem,
        recv_sem=recv_sem,
        device_id=target,
        device_id_type=pl.DeviceIdType.MESH,
    )


def gather_steps(nz, place, lead, z_second, pieces, send_sem, recv_sem):
    z, x, c, y = place
    first, second, both = partners(place, lead)
    to_first = device(z, first[0], c, first[1])
    to_second = device(z, second[0], c, second[1])
    to_core = device(z, x, 1 - c, y)

    def copies(send, recv, shard, target):
        return [
            remote(
                view(out, *shard),
                view(out, *shard),
                send_sem.at[send, shard[0], i],
                recv_sem.at[recv, shard[0], i],
                target,
            )
            for i, out, view in pieces
        ]

    def start(*args):
        for copy in copies(*args):
            copy.start()

    def arrived(*args):
        for copy in copies(*args):
            copy.wait_recv()

    def sent(*args):
        for copy in copies(*args):
            copy.wait_send()

    def column(zz):
        return (zz, x, c, y)

    def of_first(zz):
        return (zz, first[0], c, first[1])

    def of_second(zz):
        return (zz, second[0], c, second[1])

    def of_both(zz):
        return (zz, both[0], c, both[1])

    core_first, core_second = CORE + 2 - lead, CORE + 1 + lead

    def move_up(zz):
        return (UP, COLUMN, column(zz), device(z + 1, x, c, y))

    def move_down(zz):
        return (DOWN, COLUMN, column(zz), device(z - 1, x, c, y))

    def first_up(zz):
        return (UP_FIRST, FIRST, of_first(zz), device(z + 1, x, c, y))

    def first_down(zz):
        return (DOWN_FIRST, FIRST, of_first(zz), device(z - 1, x, c, y))

    def along(zz, rising, falling, up, down):
        if rising:

            @pl.when(z < nz - 1)
            def _():
                start(*up(zz))

        if falling:

            @pl.when(z > 0)
            def _():
                start(*down(zz))

    def stage0(zz, rising, falling, wait):
        if wait:
            arrived(UP, COLUMN, column(zz), to_core)
        if z_second and not wait:
            start(FIRST, FIRST, column(zz), to_first)
        along(zz, rising, falling, move_up, move_down)
        if not z_second:
            start(FIRST, FIRST, column(zz), to_first)
        start(SECOND, SECOND, column(zz), to_second)
        start(CORE, CORE, column(zz), to_core)

    def stage1(zz, rising, falling):
        arrived(FIRST, FIRST, of_first(zz), to_first)
        if z_second:
            along(zz, rising, falling, first_up, first_down)
        start(BOTH, BOTH, of_first(zz), to_second)
        start(core_first, core_first, of_first(zz), to_core)

    def stage2(zz, rising, falling):
        arrived(SECOND, SECOND, of_second(zz), to_second)
        start(core_second, core_second, of_second(zz), to_core)
        arrived(BOTH, BOTH, of_both(zz), to_second)
        start(CORE + 3, CORE + 3, of_both(zz), to_core)

    def begin():
        stage0(z, True, True, False)

    def step(t):
        @pl.when((t < nz) & (z - t >= 0))
        def _():
            stage0(z - t, True, False, True)

        @pl.when((t < nz) & (z + t < nz))
        def _():
            stage0(z + t, False, True, True)

        for lag, stage in ((1, stage1), (2, stage2)):
            late = t - lag

            @pl.when(late == 0)
            def _():
                stage(z, True, True)

            @pl.when((late > 0) & (late < nz) & (z - late >= 0))
            def _():
                stage(z - late, True, False)

            @pl.when((late > 0) & (late < nz) & (z + late < nz))
            def _():
                stage(z + late, False, True)

    def all_arrived(zz, carry):
        for fx in range(2):
            for fy in range(2):
                kind = CORE + 2 * fx + fy
                shard = (zz, x + fx * (1 - 2 * x), 1 - c, y + fy * (1 - 2 * y))
                arrived(kind, kind, shard, to_core)
        return carry

    def all_sent(zz, carry):
        @pl.when((zz <= z) & (z < nz - 1))
        def _():
            sent(*move_up(zz))

        @pl.when((zz >= z) & (z > 0))
        def _():
            sent(*move_down(zz))

        if z_second:

            @pl.when((zz <= z) & (z < nz - 1))
            def _():
                sent(*first_up(zz))

            @pl.when((zz >= z) & (z > 0))
            def _():
                sent(*first_down(zz))

            @pl.when(zz == z)
            def _():
                sent(FIRST, FIRST, column(zz), to_first)

        else:
            sent(FIRST, FIRST, column(zz), to_first)
        sent(SECOND, SECOND, column(zz), to_second)
        sent(BOTH, BOTH, of_first(zz), to_second)
        sent(CORE, CORE, column(zz), to_core)
        sent(core_first, core_first, of_first(zz), to_core)
        sent(core_second, core_second, of_second(zz), to_core)
        sent(CORE + 3, CORE + 3, of_both(zz), to_core)
        return carry

    def end_arrive():
        lax.fori_loop(0, nz, all_arrived, 0)

    def end_send():
        lax.fori_loop(0, nz, all_sent, 0)

    return begin, step, end_arrive, end_send


def swap_halves(place, rows, other, sem):
    z, x, c, y = place
    return remote(
        rows.at[pl.ds(LOCAL * (1 - y), LOCAL)],
        other,
        sem.at[0],
        sem.at[1],
        device(z, x, c, 1 - y),
    )


def place_rows(place, keep, send, out, sem):
    z, x, c, y = place
    own = out.at[pl.ds(LOCAL * y, LOCAL)]
    return [
        pltpu.make_async_copy(keep, own, sem.at[2]),
        remote(send, own, sem.at[0], sem.at[1], device(z, x, c, 1 - y)),
    ]


def gather_kernel(nz, views, *refs):
    n = len(views)
    srcs, tokens, outs, other = refs[:n], refs[n], refs[n + 1 : 2 * n + 1], refs[2 * n + 1]
    send_sem, recv_sem, own_sem, swap_sem = refs[2 * n + 2 :]
    place = my_place()
    halves = swap_halves(place, tokens, other, swap_sem)
    own = [
        pltpu.make_async_copy(src, view(out, *place), own_sem.at[i])
        for i, (src, out, view) in enumerate(zip(srcs, outs, views))
    ]
    for copy in own:
        copy.start()
    entry_barrier(nz)
    halves.start()
    for copy in own:
        copy.wait()
    pieces = [(i, out, view) for i, (out, view) in enumerate(zip(outs, views))]
    begin, step, end_arrive, end_send = gather_steps(
        nz, place, place[2], False, pieces, send_sem, recv_sem
    )
    begin()

    def loop(t, carry):
        step(t)
        return carry

    lax.fori_loop(1, nz + 2, loop, 0)
    end_send()
    end_arrive()
    halves.wait()


def gather(nz, collective_id, parts, tokens):
    shards, shapes, views = zip(*parts)
    n = len(parts)
    return pl.pallas_call(
        functools.partial(gather_kernel, nz, views),
        in_specs=[ANY] * (n + 1),
        out_specs=[ANY] * (n + 1),
        out_shape=[sds(shape, shard.dtype) for shard, shape in zip(shards, shapes)]
        + [sds((LOCAL, *tokens.shape[1:]), tokens.dtype)],
        scratch_shapes=[
            pltpu.SemaphoreType.DMA((11, nz, n)),
            pltpu.SemaphoreType.DMA((8, nz, n)),
            pltpu.SemaphoreType.DMA((n,)),
            pltpu.SemaphoreType.DMA((2,)),
        ],
        name="gather",
        compiler_params=params(collective_id=collective_id, has_side_effects=True),
    )(*shards, tokens)


def scatter_kernel(nz, views, *refs):
    n = len(views)
    terms, outs = refs[:n], refs[n : 2 * n]
    mine, from_core, from_second, from_first, from_below, from_above = (
        refs[2 * n + i * n : 3 * n + i * n] for i in range(6)
    )
    send_sem, recv_sem, own_sem = refs[8 * n :]
    place = z, x, c, y = my_place()
    first, second, both = partners(place, place[2])
    to_first = device(z, first[0], c, first[1])
    to_second = device(z, second[0], c, second[1])
    to_core = device(z, x, 1 - c, y)

    def copies(srcs, dsts, send, recv, zz, target):
        return [
            pltpu.make_async_remote_copy(
                src_ref=srcs[i],
                dst_ref=dsts[i],
                send_sem=send_sem.at[send, zz, i],
                recv_sem=recv_sem.at[recv, zz, i],
                device_id=target,
                device_id_type=pl.DeviceIdType.MESH,
            )
            for i in range(n)
        ]

    def slots(bufs, *index):
        return [b.at[index] for b in bufs]

    def pick(refs_, *index):
        return [b[index] for b in refs_]

    flips = [(fx, fy) for fx in range(2) for fy in range(2)]

    def at(fx, fy):
        return x + fx * (1 - 2 * x), y + fy * (1 - 2 * y)

    def core_copies(zz, f):
        fx, fy = flips[f]
        xx, yy = at(fx, fy)
        return copies(
            [view(t, zz, xx, 1 - c, yy) for t, view in zip(terms, views)],
            slots(from_core, zz, f),
            f,
            f,
            zz,
            to_core,
        )

    def own_copies(zz, f):
        fx, fy = flips[f]
        xx, yy = at(fx, fy)
        return [
            pltpu.make_async_copy(
                view(t, zz, xx, c, yy), mine[i].at[zz, f], own_sem.at[f, zz, i]
            )
            for i, (t, view) in enumerate(zip(terms, views))
        ]

    f_first, f_second = 2 - c, 1 + c

    def second_copies(zz, across):
        return copies(
            slots(from_core, zz, 3 if across else f_second),
            slots(from_second, zz, 1 if across else 0),
            4 + across,
            4 + across,
            zz,
            to_second,
        )

    def first_copies(zz):
        return copies(slots(from_second, zz, 1), slots(from_first, zz), 6, 6, zz, to_first)

    def up_copies(zz):
        return copies(slots(from_first, zz), slots(from_below, zz), 7, 7, zz, device(z + 1, x, c, y))

    def down_copies(zz):
        return copies(slots(from_first, zz), slots(from_above, zz), 8, 8, zz, device(z - 1, x, c, y))

    def run(group, what):
        for copy in group:
            getattr(copy, what)()

    def add(into, index, other, other_index):
        for i in range(n):
            a, b = into[i].at[index], other[i].at[other_index]
            a[...] = (a[...].astype(F32) + b[...].astype(F32)).astype(a.dtype)

    def by_distance(t, do):
        @pl.when((t >= 0) & (t < nz) & (z - t >= 0))
        def _():
            do(z - t)

        @pl.when((t > 0) & (t < nz) & (z + t < nz))
        def _():
            do(z + t)

    def start_own(zz):
        for f in range(4):
            run(own_copies(zz, f), "start")

    def start_core(zz):
        for f in (3, 1, 2, 0):
            run(core_copies(zz, f), "start")

    def stage0(zz):
        for f in (3, 1, 2, 0):
            run(core_copies(zz, f), "wait_recv")
            run(own_copies(zz, f), "wait")
            add(from_core, (zz, f), mine, (zz, f))
        run(second_copies(zz, 1), "start")
        run(second_copies(zz, 0), "start")

    def stage1(zz):
        run(second_copies(zz, 1), "wait_recv")
        add(from_second, (zz, 1), from_core, (zz, f_first))
        run(first_copies(zz), "start")

    def stage2(zz):
        run(second_copies(zz, 0), "wait_recv")
        add(from_second, (zz, 0), from_core, (zz, 0))
        run(first_copies(zz), "wait_recv")
        add(from_first, (zz,), from_second, (zz, 0))

        @pl.when(zz > z)
        def _():
            @pl.when(z > 0)
            def _():
                run(up_copies(zz), "wait_recv")
                add(from_first, (zz,), from_below, (zz,))

            run(up_copies(zz), "start")

        @pl.when(zz < z)
        def _():
            @pl.when(z < nz - 1)
            def _():
                run(down_copies(zz), "wait_recv")
                add(from_first, (zz,), from_above, (zz,))

            run(down_copies(zz), "start")

    entry_barrier(nz)

    def begin(k, carry):
        by_distance(nz - 1 - k, start_core)
        by_distance(nz - 1 - k, start_own)
        return carry

    lax.fori_loop(0, nz, begin, 0)

    def step(k, carry):
        t = nz - 1 - k
        by_distance(t, stage0)
        by_distance(t + 1, stage1)
        by_distance(t + 2, stage2)
        return carry

    lax.fori_loop(0, nz + 2, step, 0)

    @pl.when(z > 0)
    def _():
        run(up_copies(z), "wait_recv")
        add(from_first, (z,), from_below, (z,))

    @pl.when(z < nz - 1)
    def _():
        run(down_copies(z), "wait_recv")
        add(from_first, (z,), from_above, (z,))

    for i in range(n):
        outs[i][...] = from_first[i][z]

    def finish(zz, carry):
        for f in range(4):
            run(core_copies(zz, f), "wait_send")
        run(second_copies(zz, 1), "wait_send")
        run(second_copies(zz, 0), "wait_send")
        run(first_copies(zz), "wait_send")

        @pl.when(zz > z)
        def _():
            run(up_copies(zz), "wait_send")

        @pl.when(zz < z)
        def _():
            run(down_copies(zz), "wait_send")

        return carry

    lax.fori_loop(0, nz, finish, 0)


def scatter(nz, collective_id, parts):
    terms, shapes, views = zip(*parts)
    n = len(parts)
    dtypes = [t.dtype for t in terms]

    def bufs(*lead):
        return [pltpu.VMEM((*lead, *shape), d) for shape, d in zip(shapes, dtypes)]

    return pl.pallas_call(
        functools.partial(scatter_kernel, nz, views),
        in_specs=[ANY] * n,
        out_specs=[VMEM] * n,
        out_shape=[sds(shape, d) for shape, d in zip(shapes, dtypes)],
        scratch_shapes=[
            *bufs(nz, 4),
            *bufs(nz, 4),
            *bufs(nz, 2),
            *bufs(nz),
            *bufs(nz),
            *bufs(nz),
            pltpu.SemaphoreType.DMA((9, nz, n)),
            pltpu.SemaphoreType.DMA((9, nz, n)),
            pltpu.SemaphoreType.DMA((4, nz, n)),
        ],
        name="scatter",
        compiler_params=params(62, collective_id=collective_id, has_side_effects=True),
    )(*terms)


def whole_rows(side, mine, other):
    mine, other = mine.astype(F32), other.astype(F32)
    first = jnp.where(side == 0, mine, other)
    second = jnp.where(side == 0, other, mine)
    return jnp.concatenate([jnp.zeros((MEM, D), F32), first, second], axis=0)


def split_rows(side, rows):
    half = (SEG - MEM) // 2
    first, second = rows[MEM : MEM + half], rows[MEM + half :]
    keep = jnp.where(side == 0, first, second)
    send = jnp.where(side == 0, second, first)
    return keep, send


def project_kernel(mine_ref, other_ref, w_ref, table_ref, x_ref, q_ref, k_ref, v_ref):
    side = lax.axis_index("tensor")
    mine = mine_ref[LOCAL * side + pl.program_id(0)]
    x = whole_rows(side, mine, other_ref[0]).astype(BF16)
    x_ref[0] = x
    query = nn(x, w_ref[0]) + table_ref[QUERY_BIAS : QUERY_BIAS + 1, :]
    q_ref[0] = (query * SCALE).astype(BF16)
    k_ref[0] = nn(x, w_ref[1]).astype(BF16)
    v_ref[0] = (nn(x, w_ref[2]) + table_ref[VALUE_BIAS : VALUE_BIAS + 1, :]).astype(BF16)


def slot_rows(width=D):
    return pl.BlockSpec((1, SEG, width), lambda s: (s, 0, 0))


def half_rows(half):
    return pl.BlockSpec((1, half, D), lambda s: (s, 0, 0))


def project(tokens, other, attn, table):
    return pl.pallas_call(
        project_kernel,
        grid=(LOCAL,),
        in_specs=[
            once(tokens.shape, (0, 0, 0)),
            half_rows(tokens.shape[1]),
            once((3, D, D), (0, 0, 0)),
            once((NVEC, D), (0, 0)),
        ],
        out_specs=[slot_rows()] * 4,
        out_shape=[sds((LOCAL, SEG, D), BF16)] * 4,
        name="project",
        compiler_params=params(),
    )(tokens, other, attn, table)


def head_masks():
    feature_head = lax.broadcasted_iota(jnp.int32, (1, D), 1) // DH
    return [feature_head == h for h in range(HEADS)]


def by_head(rows16, masks):
    zero = jnp.zeros_like(rows16)
    return jnp.concatenate([jnp.where(m, rows16, zero) for m in masks], axis=0)


def own_columns(blocks, masks):
    total = jnp.zeros((THIN, D), blocks.dtype)
    for h, m in enumerate(masks):
        total = jnp.where(m, blocks[THIN * h : THIN * (h + 1)], total)
    return total


def copies_of(key_mask_shape):
    row = lax.rem(lax.broadcasted_iota(jnp.int32, key_mask_shape, 0), THIN)
    key = lax.broadcasted_iota(jnp.int32, key_mask_shape, 1)
    return jnp.where((key < MEM) & (key <= row), 2.0, 1.0)


def pair_barrier(place):
    z, x, c, y = place
    barrier = pltpu.get_barrier_semaphore()
    pl.semaphore_signal(
        barrier,
        inc=1,
        device_id=device(z, x, c, 1 - y),
        device_id_type=pl.DeviceIdType.MESH,
    )
    pl.semaphore_wait(barrier, 1)


def chain_kernel(
    place_ref,
    table_ref,
    attn_ref,
    ffn_ref,
    x_in,
    q_in,
    k_in,
    v_in,
    cot_ref,
    x_ref,
    q_ref,
    k_ref,
    v_ref,
    saved_d_ref,
    saved_f_ref,
    saved_s_ref,
    cot_other_ref,
    wa,
    wf,
    xb,
    qb,
    kb,
    vb,
    save_d,
    save_f,
    save_s,
    left,
    given,
    sem_w,
    sem_x,
    sem_kv,
    sem_out,
    sem_memory,
    sem_cot,
):
    del x_in, q_in, k_in, v_in
    place = z, x, c, y = my_place()
    loads = [
        pltpu.make_async_copy(attn_ref, wa, sem_w.at[0]),
        pltpu.make_async_copy(ffn_ref.at[0], wf.at[0], sem_w.at[1]),
        pltpu.make_async_copy(ffn_ref.at[1], wf.at[1], sem_w.at[2]),
    ]
    tiles = [
        pltpu.make_async_copy(x_ref.at[s, pl.ds(0, THIN)], xb.at[s], sem_x.at[s])
        for s in range(LOCAL)
    ]
    keys = [
        pltpu.make_async_copy(src.at[s], dst.at[s], sem_kv.at[2 * s + i])
        for s in range(LOCAL)
        for i, (src, dst) in enumerate(((k_ref, kb), (v_ref, vb)))
    ]
    for copy in tiles + loads[:1] + keys + loads[1:]:
        copy.start()
    pair_barrier(place)
    cot_swap = swap_halves(place, cot_ref, cot_other_ref, sem_cot)
    cot_swap.start()
    handed = remote(left, given, sem_memory.at[0], sem_memory.at[1], device(z, x, c, 1 - y))

    masks = head_masks()
    memory_row = lax.broadcasted_iota(jnp.int32, (THIN, 1), 0) < MEM
    first = table_ref[FIRST_MEMORY:NVEC, :]
    first = jnp.concatenate([first, jnp.zeros((THIN - MEM, D), F32)], axis=0)
    row = lambda r: table_ref[r : r + 1, :]

    def slots(turn, memory):
        for s in range(LOCAL):
            tiles[s].wait()
            if s == 0:
                loads[0].wait()
            keys[2 * s].wait()
            keys[2 * s + 1].wait()
            if memory is None:
                memory = first
            else:
                memory = jnp.where(place_ref[LOCAL * turn + s] == 0, first, memory)
            x16 = jnp.where(memory_row, memory, xb[s].astype(F32)).astype(BF16)
            xb[s] = x16
            qb[s] = ((nn(x16, wa[0]) + row(QUERY_BIAS)) * SCALE).astype(BF16)
            kb[s, 0:THIN] = nn(x16, wa[1]).astype(BF16)
            vb[s, 0:THIN] = (nn(x16, wa[2]) + row(VALUE_BIAS)).astype(BF16)
            outs = [
                pltpu.make_async_copy(
                    src.at[s, pl.ds(0, THIN)], dst.at[s, pl.ds(0, THIN)], sem_out.at[4 * s + i]
                )
                for i, (src, dst) in enumerate(
                    ((xb, x_ref), (qb, q_ref), (kb, k_ref), (vb, v_ref))
                )
            ]
            for copy in outs:
                copy.start()
            if turn == 1 and s == LOCAL - 1:
                save_d[s] = jnp.zeros_like(save_d[s])
                save_f[s] = jnp.zeros_like(save_f[s])
                save_s[s] = jnp.zeros_like(save_s[s])
            else:
                q_heads = by_head(qb[s], masks)
                score = nt(q_heads, kb[s])
                top = jnp.max(score, axis=-1, keepdims=True)
                weight = jnp.exp(score - top) * copies_of(score.shape)
                total = jnp.sum(weight, axis=-1, keepdims=True)
                share = (weight / total).astype(BF16)
                log_total = top + jnp.log(total)
                context = own_columns(nn(share, vb[s]), masks).astype(BF16)
                unit1, inverse1 = normalized(
                    x16.astype(F32) + nt(context, wa[3]) + row(OUT_BIAS)
                )
                hidden = (unit1 * row(GAIN1) + row(SHIFT1)).astype(BF16)
                if s == 0:
                    loads[1].wait()
                up = nt(hidden, wf[0])
                up_bias = jnp.concatenate([row(UP_BIAS + i) for i in range(FF // D)], axis=1)
                active16, slope = gelu_parts(up + up_bias)
                active16 = active16.astype(BF16)
                if s == 0:
                    loads[2].wait()
                second = hidden.astype(F32) + nn(active16, wf[1]) + row(DOWN_BIAS)
                unit2, inverse2 = normalized(second)
                output = (unit2 * row(GAIN2) + row(SHIFT2)).astype(BF16)
                memory = output.astype(F32)
                if turn == 0 and s == LOCAL - 1:
                    left[...] = output
                    handed.start()
                save_d[s, 0] = hidden
                save_d[s, 1] = unit1.astype(BF16)
                save_d[s, 2] = unit2.astype(BF16)
                save_d[s, 3] = context
                save_f[s, 0] = active16
                save_f[s, 1] = slope.astype(BF16)
                wide = lambda v: jnp.broadcast_to(v, (v.shape[0], 128))
                save_s[s, 0 : HEADS * THIN] = wide(log_total)
                save_s[s, HEADS * THIN : HEADS * THIN + THIN] = wide(inverse1)
                save_s[s, HEADS * THIN + THIN :] = wide(inverse2)
            for copy in outs:
                copy.wait()

    @pl.when(y == 0)
    def _():
        slots(0, None)
        handed.wait_send()

    @pl.when(y == 1)
    def _():
        handed.wait_recv()
        slots(1, given[...].astype(F32))

    saves = [
        pltpu.make_async_copy(save_d, saved_d_ref, sem_out.at[0]),
        pltpu.make_async_copy(save_f, saved_f_ref, sem_out.at[1]),
        pltpu.make_async_copy(save_s, saved_s_ref, sem_out.at[2]),
    ]
    for copy in saves:
        copy.start()
    for copy in saves:
        copy.wait()
    cot_swap.wait()


SAVED = (
    sds((LOCAL, 4, THIN, D), BF16),
    sds((LOCAL, 2, THIN, FF), BF16),
    sds((LOCAL, HEADS * THIN + 2 * THIN, 128), F32),
)


def chain(place, table, attn, ffn, x, q, k, v, cot):
    whole = sds((LOCAL, SEG, D), BF16)
    outs = pl.pallas_call(
        chain_kernel,
        in_specs=[SMEM, VMEM] + [ANY] * 7,
        out_specs=[ANY] * 8,
        out_shape=[whole] * 4 + list(SAVED) + [sds((LOCAL, *cot.shape[1:]), BF16)],
        input_output_aliases={4 + i: i for i in range(4)},
        scratch_shapes=[
            pltpu.VMEM((4, D, D), BF16),
            pltpu.VMEM((2, FF, D), BF16),
            pltpu.VMEM((LOCAL, THIN, D), BF16),
            pltpu.VMEM((LOCAL, THIN, D), BF16),
            pltpu.VMEM((LOCAL, SEG, D), BF16),
            pltpu.VMEM((LOCAL, SEG, D), BF16),
            *[pltpu.VMEM(s.shape, s.dtype) for s in SAVED],
            pltpu.VMEM((THIN, D), BF16),
            pltpu.VMEM((THIN, D), BF16),
            pltpu.SemaphoreType.DMA((3,)),
            pltpu.SemaphoreType.DMA((LOCAL,)),
            pltpu.SemaphoreType.DMA((2 * LOCAL,)),
            pltpu.SemaphoreType.DMA((4 * LOCAL,)),
            pltpu.SemaphoreType.DMA((2,)),
            pltpu.SemaphoreType.DMA((2,)),
        ],
        name="chain",
        compiler_params=params(collective_id=2, has_side_effects=True),
    )(place, table, attn, ffn, x, q, k, v, cot)
    return outs[:4], outs[4:7], outs[7]


def own_lanes(block, head):
    lane = lax.broadcasted_iota(jnp.int32, block.shape, 1)
    return jnp.where((lane < DH) == (head == 0), block, jnp.zeros_like(block))


def seen(score, first_query):
    key = lax.broadcasted_iota(jnp.int32, score.shape, 0)
    query = lax.broadcasted_iota(jnp.int32, score.shape, 1) + first_query
    return key <= query


def attend_pair(q, k, v):
    contexts_of, logs_of = [], [[], []]
    for part in range(SEG // TILE):
        rows = slice(TILE * part, TILE * (part + 1))
        keys = slice(0, TILE * (part + 1))
        contexts = []
        for head in range(2):
            score = nt(own_lanes(k[keys], head), q[rows])
            key = lax.broadcasted_iota(jnp.int32, score.shape, 0)
            allowed = seen(score, TILE * part) & (key >= MEM)
            score = jnp.where(allowed, score, MASK_VALUE)
            top = jnp.max(score, axis=0, keepdims=True)
            weight = jnp.exp(score - top)
            total = jnp.sum(weight, axis=0, keepdims=True)
            share = (weight * (1.0 / total)).astype(BF16)
            logs_of[head].append(top + jnp.log(total))
            contexts.append(tn(share, v[keys]))
        lane = lax.broadcasted_iota(jnp.int32, contexts[0].shape, 1)
        contexts_of.append(jnp.where(lane < DH, contexts[0], contexts[1]).astype(BF16))
    return jnp.concatenate(contexts_of, axis=0), [jnp.concatenate(l, axis=1) for l in logs_of]


def attend_kernel(q_ref, k_ref, v_ref, c_ref, log_ref):
    context, logs = attend_pair(q_ref[0], k_ref[0], v_ref[0])
    c_ref[0] = context
    for head in range(2):
        log_ref[0, 0, head : head + 1] = logs[head]


def with_memory(q, k16, v16, context, log_tokens):
    masks = head_masks()
    score = nt(by_head(k16, masks), q).reshape(HEADS, THIN, SEG)
    key = lax.broadcasted_iota(jnp.int32, score.shape, 1)
    score = jnp.where(key < MEM, score, MASK_VALUE)
    top = jnp.maximum(jnp.max(score, axis=1), log_tokens)
    weight = jnp.exp(score - top[:, None])
    old = jnp.exp(log_tokens - top)
    total = jnp.sum(weight, axis=1) + old
    share = (weight * (1.0 / total)[:, None]).reshape(HEADS * THIN, SEG).astype(BF16)
    kept = old / total
    coarse = kept.astype(BF16)
    fine = (kept - coarse.astype(F32)).astype(BF16)
    pad = jnp.zeros((4, SEG), BF16)
    head = lax.rem(lax.broadcasted_iota(jnp.int32, (2 * THIN, D), 0), THIN)
    spread = jnp.where(head == lax.broadcasted_iota(jnp.int32, (2 * THIN, D), 1) // DH, 1.0, 0.0)
    factor = tn(jnp.concatenate([coarse, pad, fine, pad], axis=0), spread.astype(BF16))
    context = factor * context.astype(F32) + tn(share, by_head(v16, masks))
    return context.astype(BF16), top + jnp.log(total)


PAIR = pl.BlockSpec((1, SEG, 2 * DH), lambda s, h: (s, 0, h))
PAIR_LOG = pl.BlockSpec((1, 1, 2, SEG), lambda s, h: (s, h, 0, 0))


def attend(q, k, v):
    return pl.pallas_call(
        attend_kernel,
        grid=(LOCAL, HEADS // 2),
        in_specs=[PAIR] * 3,
        out_specs=[PAIR, PAIR_LOG],
        out_shape=[sds((LOCAL, SEG, D), BF16), sds((LOCAL, HEADS // 2, 2, SEG), F32)],
        name="attend",
        compiler_params=params(),
    )(q, k, v)


def attend_back_pair(q, k, v, dc, logs):
    last = SEG // TILE
    key_terms, value_terms, query_terms = [], [], []
    for head in range(2):
        key_sum, value_sum, query_parts = [], [], []
        for part in range(last):
            rows = slice(TILE * part, TILE * (part + 1))
            keys = slice(0, TILE * (part + 1))
            score = nt(own_lanes(k[keys], head), q[rows])
            share = jnp.exp(score - logs[head : head + 1, rows])
            diagonal = jnp.where(seen(share[rows], 0), share[rows], 0.0)
            share = jnp.concatenate([share[: TILE * part], diagonal], axis=0) if part else diagonal
            share_grad = nt(own_lanes(v[keys], head), dc[rows])
            inner = jnp.sum(share_grad * share, axis=0, keepdims=True)
            score_grad = (share * (share_grad - inner)).astype(BF16)
            value_sum.append(nn(share.astype(BF16), dc[rows]))
            key_sum.append(nn(score_grad, q[rows]))
            query_parts.append(tn(score_grad, k[keys]))
        key_terms.append(key_sum)
        value_terms.append(value_sum)
        query_terms.append(query_parts)
    lane = lax.broadcasted_iota(jnp.int32, (TILE, 2 * DH), 1)
    pick = lambda a, b: jnp.where(lane < DH, a, b)
    dq, dk, dv = [], [], []
    for part in range(last):
        rows = slice(TILE * part, TILE * (part + 1))
        dq.append((pick(query_terms[0][part], query_terms[1][part]) * SCALE).astype(BF16))
        for terms, out in ((key_terms, dk), (value_terms, dv)):
            total = None
            for later in range(part, last):
                term = pick(terms[0][later][rows], terms[1][later][rows])
                total = term if total is None else total + term
            out.append(total)
    return [jnp.concatenate(parts, axis=0) for parts in (dq, dk, dv)]


def rows_kernel(
    place_ref,
    x_ref,
    q_ref,
    k16_ref,
    v16_ref,
    tokens_c_ref,
    tokens_log_ref,
    mine_ref,
    other_ref,
    wo_ref,
    wf_ref,
    table_ref,
    keep_ref,
    send_ref,
    h_ref,
    g_ref,
    du_ref,
    df_ref,
    da_ref,
    dc_ref,
    c_ref,
    log_ref,
    sums_ref,
    slope_ref,
):
    row = lambda r: table_ref[r : r + 1, :]
    slot = pl.program_id(0)
    side = lax.axis_index("tensor")
    live = place_ref[LOCAL * side + slot] >= 0

    @pl.when(slot == 0)
    def _():
        sums_ref[...] = jnp.zeros_like(sums_ref)

    def add(r, value):
        sums_ref[r : r + 1, :] += value

    log_tokens = jnp.concatenate([tokens_log_ref[0, h] for h in range(HEADS // 2)], axis=0)
    context, log_total = with_memory(
        q_ref[0], k16_ref[0], v16_ref[0], tokens_c_ref[0], log_tokens
    )
    c_ref[0] = context
    for h in range(HEADS // 2):
        log_ref[0, h] = log_total[2 * h : 2 * h + 2]
    unit1, inverse1 = normalized(x_ref[0].astype(F32) + nt(context, wo_ref[0]) + row(OUT_BIAS))
    hidden = (unit1 * row(GAIN1) + row(SHIFT1)).astype(BF16)
    h_ref[0] = hidden
    second = hidden.astype(F32) + row(DOWN_BIAS)
    for i in range(FF // D):
        cols = slice(D * i, D * (i + 1))
        up = nt(hidden, wf_ref[0, cols]) + row(UP_BIAS + i)
        active, slope = gelu_parts(up)
        active = active.astype(BF16)
        g_ref[0, :, cols] = active
        slope_ref[:, cols] = slope.astype(BF16)
        second = second + nn(active, wf_ref[1, cols])
    unit2, inverse2 = normalized(second)
    output = jnp.where(live, unit2 * row(GAIN2) + row(SHIFT2), 0.0)
    keep, send = split_rows(side, output)
    keep_ref[0] = keep.astype(BF16)
    send_ref[0] = send.astype(BF16)

    grad = whole_rows(side, mine_ref[LOCAL * side + slot], other_ref[0])
    grad = jnp.where(live, grad, 0.0)
    add(GAIN2, row_sum(grad * unit2))
    add(SHIFT2, row_sum(grad))
    second_grad = normalized_back(grad * row(GAIN2), unit2, inverse2)
    down_grad = second_grad.astype(BF16)
    df_ref[0] = down_grad
    add(DOWN_BIAS, row_sum(down_grad.astype(F32)))
    hidden_grad = second_grad
    for i in range(FF // D):
        cols = slice(D * i, D * (i + 1))
        up_grad = (nt(down_grad, wf_ref[1, cols]) * slope_ref[:, cols].astype(F32)).astype(BF16)
        du_ref[0, :, cols] = up_grad
        add(UP_BIAS + i, row_sum(up_grad.astype(F32)))
        hidden_grad = hidden_grad + nn(up_grad, wf_ref[0, cols])
    add(GAIN1, row_sum(hidden_grad * unit1))
    add(SHIFT1, row_sum(hidden_grad))
    branch_grad = normalized_back(hidden_grad * row(GAIN1), unit1, inverse1).astype(BF16)
    da_ref[0] = branch_grad
    add(OUT_BIAS, row_sum(branch_grad.astype(F32)))
    dc_ref[0] = nn(branch_grad, wo_ref[0]).astype(BF16)


def rows_part(place, x, q, k, v, c, log_tokens, cot, other, attn, ffn, table):
    half = cot.shape[1]
    whole, whole_wide = sds((LOCAL, SEG, D), BF16), sds((LOCAL, SEG, FF), BF16)
    part, logs = sds((LOCAL, half, D), BF16), sds((LOCAL, HEADS // 2, 2, SEG), F32)
    rows, wide = slot_rows(), slot_rows(FF)
    thin = pl.BlockSpec((1, THIN, D), lambda s: (s, 0, 0))
    log_rows = pl.BlockSpec((1, HEADS // 2, 2, SEG), lambda s: (s, 0, 0, 0))
    return pl.pallas_call(
        rows_kernel,
        grid=(LOCAL,),
        in_specs=[SMEM, rows, rows, thin, thin, rows, log_rows]
        + [once(cot.shape, (0, 0, 0)), half_rows(half)]
        + [once((1, D, D), (3, 0, 0)), once((2, FF, D), (0, 0, 0)), once((NVEC, D), (0, 0))],
        out_specs=[half_rows(half)] * 2
        + [rows, wide, wide, rows, rows, rows, rows, log_rows, once((THIN, D), (0, 0))],
        out_shape=[part] * 2
        + [whole, whole_wide, whole_wide, whole, whole, whole, whole, logs, sds((THIN, D), F32)],
        scratch_shapes=[pltpu.VMEM((SEG, FF), BF16)],
        name="rows_part",
        compiler_params=params(),
    )(place, x, q, k, v, c, log_tokens, cot, other, attn, ffn, table)


CHUNK = 768


def memory_key_gradient(q, k16, v16, dc, context, logs, masks):
    score = nt(by_head(k16, masks), q).reshape(HEADS, THIN, SEG)
    key = lax.broadcasted_iota(jnp.int32, score.shape, 1)
    share = jnp.where(key < MEM, jnp.exp(score - logs[:, None]), 0.0)
    share_grad = nt(by_head(v16, masks), dc).reshape(HEADS, THIN, SEG)
    product = dc.astype(F32) * context.astype(F32)
    coarse = product.astype(BF16)
    fine = (product - coarse.astype(F32)).astype(BF16)
    head = lax.broadcasted_iota(jnp.int32, (THIN, D), 0)
    ones = jnp.where(head == lax.broadcasted_iota(jnp.int32, (THIN, D), 1) // DH, 1.0, 0.0)
    ones = ones.astype(BF16)
    inner = (nt(ones, coarse) + nt(ones, fine))[0:HEADS]
    score_grad = (share * (share_grad - inner[:, None])).reshape(HEADS * THIN, SEG)
    share = share.reshape(HEADS * THIN, SEG).astype(BF16)
    dk = own_columns(nn(score_grad.astype(BF16), q), masks)
    return dk, own_columns(nn(share, dc), masks)


def chain_back_kernel(
    place_ref,
    table_ref,
    attn_ref,
    ffn_ref,
    q_ref,
    k_ref,
    v_ref,
    saved_d_ref,
    saved_f_ref,
    saved_s_ref,
    g_ref,
    du_ref,
    df_ref,
    h_ref,
    keep_ref,
    send_ref,
    dc_ref,
    log_ref,
    da_in,
    c_in,
    da_ref,
    c_ref,
    dq_ref,
    dk_ref,
    dv_ref,
    sums_ref,
    terms_ref,
    rows_ref,
    wa,
    wf,
    qb,
    kb,
    vb,
    dcb,
    cb,
    logs,
    dqb,
    dkb,
    dvb,
    tiles,
    df,
    hid,
    gb,
    dub,
    staged,
    save_d,
    save_f,
    save_s,
    thin_d,
    thin_f,
    sums,
    left,
    given,
    sem_w,
    sem_in,
    sem_ff,
    sem_chunk,
    sem_out,
    sem_stage,
    sem_grad,
    sem_swap,
):
    del da_in, c_in
    place = z, x, c, y = my_place()
    loads = [
        pltpu.make_async_copy(attn_ref, wa, sem_w.at[0]),
        pltpu.make_async_copy(ffn_ref.at[0], wf.at[0], sem_w.at[1]),
        pltpu.make_async_copy(ffn_ref.at[1], wf.at[1], sem_w.at[2]),
    ]
    first_rows = lambda ref: ref.at[:, pl.ds(0, THIN)]
    saved = [
        pltpu.make_async_copy(saved_d_ref, save_d, sem_in.at[2]),
        pltpu.make_async_copy(saved_f_ref, save_f, sem_in.at[3]),
        pltpu.make_async_copy(saved_s_ref, save_s, sem_in.at[4]),
    ]
    reads = [
        pltpu.make_async_copy(src, dst, sem_in.at[5 + i])
        for i, (src, dst) in enumerate(
            ((q_ref, qb), (k_ref, kb), (v_ref, vb), (dc_ref, dcb), (c_ref, cb), (log_ref, logs))
        )
    ]
    merged = (da_ref, c_ref)
    tile_reads = [
        pltpu.make_async_copy(first_rows(ref), tiles.at[i], sem_in.at[i])
        for i, ref in enumerate(merged)
    ]
    rows_in = [
        pltpu.make_async_copy(df_ref, df, sem_ff.at[0]),
        pltpu.make_async_copy(h_ref, hid, sem_ff.at[1]),
    ]

    def chunk_reads(i):
        lanes = pl.ds(pl.multiple_of(CHUNK * i, CHUNK), CHUNK)
        slot = lax.rem(i, 2)
        return [
            pltpu.make_async_copy(src.at[:, :, lanes], dst.at[slot], sem_chunk.at[slot, j])
            for j, (src, dst) in enumerate(((g_ref, gb), (du_ref, dub)))
        ]

    @pl.when(y == 1)
    def _():
        for copy in reads + loads[:1] + saved + loads[:0:-1] + tile_reads:
            copy.start()
        for copy in rows_in + chunk_reads(0) + chunk_reads(1):
            copy.start()

    @pl.when(y == 0)
    def _():
        for copy in rows_in + chunk_reads(0) + chunk_reads(1):
            copy.start()
        for copy in reads + saved + loads[:0:-1] + loads[:1] + tile_reads:
            copy.start()

    pair_barrier(place)
    swap = place_rows(place, keep_ref, send_ref, rows_ref, sem_swap)
    for copy in swap:
        copy.start()
    handed = remote(left, given, sem_grad.at[0], sem_grad.at[1], device(z, x, c, 1 - y))

    sums[...] = jnp.zeros_like(sums)
    thin_d[...] = jnp.zeros_like(thin_d)
    thin_f[...] = jnp.zeros_like(thin_f)
    for buf in (dqb, dkb, dvb):
        buf[...] = jnp.zeros_like(buf)
    masks = head_masks()
    memory_row = lax.broadcasted_iota(jnp.int32, (THIN, 1), 0) < MEM
    row = lambda r: table_ref[r : r + 1, :]

    def add(r, value):
        sums[r : r + 1, :] += value

    def attend_at(i, carry):
        s, h = i // (HEADS // 2), lax.rem(i, HEADS // 2)
        lanes = pl.ds(pl.multiple_of(h * 2 * DH, 2 * DH), 2 * DH)
        pair = (buf[s, :, lanes] for buf in (qb, kb, vb, dcb))
        dq, dk, dv = attend_back_pair(*pair, logs[s, h])
        dqb[s, THIN:, lanes] = dq[THIN:]
        dqb[s, 0:THIN, lanes] = jnp.where(memory_row, dqb[s, 0:THIN, lanes], dq[0:THIN])
        dkb[s, :, lanes] = (dk + dkb[s, :, lanes].astype(F32)).astype(BF16)
        dvb[s, :, lanes] = (dv + dvb[s, :, lanes].astype(F32)).astype(BF16)
        return carry

    pairs = LOCAL * HEADS // 2

    def key_gradient(s):
        rows = jnp.concatenate([logs[s, h] for h in range(HEADS // 2)], axis=0)
        return memory_key_gradient(
            qb[s], kb[s, 0:THIN], vb[s, 0:THIN], dcb[s], cb[s], rows, masks
        )

    def slots(turn, grad):
        waited = set()

        def need(*copies):
            for copy in copies:
                if id(copy) not in waited:
                    waited.add(id(copy))
                    copy.wait()

        for s in reversed(range(LOCAL)):
            if turn == 1 and s == LOCAL - 1:
                grad = jnp.zeros((THIN, D), F32)
            else:
                after = place_ref[LOCAL * turn + s + 1]
                grad = jnp.where(memory_row, jnp.where(after > 0, grad, 0.0), 0.0)
                need(*saved)
                unit1, unit2 = save_d[s, 1].astype(F32), save_d[s, 2].astype(F32)
                base = HEADS * THIN
                log_total = save_s[s, 0:base, 0:1]
                inverse1 = save_s[s, base : base + THIN, 0:1]
                inverse2 = save_s[s, base + THIN :, 0:1]
                add(GAIN2, row_sum(grad * unit2))
                add(SHIFT2, row_sum(grad))
                second_grad = normalized_back(grad * row(GAIN2), unit2, inverse2)
                down_grad = second_grad.astype(BF16)
                add(DOWN_BIAS, row_sum(down_grad.astype(F32)))
                need(loads[2])
                up_grad = (nt(down_grad, wf[1]) * save_f[s, 1].astype(F32)).astype(BF16)
                up_sum = row_sum(up_grad.astype(F32))
                for i in range(FF // D):
                    add(UP_BIAS + i, up_sum[:, D * i : D * (i + 1)])
                need(loads[1])
                hidden_grad = second_grad + nn(up_grad, wf[0])
                add(GAIN1, row_sum(hidden_grad * unit1))
                add(SHIFT1, row_sum(hidden_grad))
                pre_grad = normalized_back(hidden_grad * row(GAIN1), unit1, inverse1)
                branch_grad = pre_grad.astype(BF16)
                add(OUT_BIAS, row_sum(branch_grad.astype(F32)))
                need(loads[0])
                context_grad = nn(branch_grad, wa[3]).astype(BF16)
                dc_heads = by_head(context_grad, masks)
                q_heads = by_head(qb[s, 0:THIN], masks)
                score = nt(q_heads, kb[s])
                share = jnp.exp(score - log_total) * copies_of(score.shape)
                share_grad = nt(dc_heads, vb[s])
                inner = jnp.sum(share_grad * share, axis=-1, keepdims=True)
                score_grad = (share * (share_grad - inner)).astype(BF16)
                query_grad = (own_columns(nn(score_grad, kb[s]), masks) * SCALE).astype(BF16)
                dkb[s] = (dkb[s].astype(F32) + tn(score_grad, q_heads)).astype(BF16)
                dvb[s] = (dvb[s].astype(F32) + tn(share.astype(BF16), dc_heads)).astype(BF16)
                dqb[s, 0:THIN] = jnp.where(memory_row, query_grad, dqb[s, 0:THIN])
                thin_d[s, 0] = down_grad
                thin_d[s, 1] = save_d[s, 0]
                thin_f[s, 0] = up_grad
                thin_f[s, 1] = save_f[s, 0]
                need(*tile_reads)
                for i, value in enumerate((branch_grad, save_d[s, 3])):
                    tiles[i, s] = jnp.where(memory_row, value, tiles[i, s])
                grad = pre_grad + nt(query_grad, wa[0])
            need(loads[0])
            dk, dv = dkb[s, 0:THIN], dvb[s, 0:THIN]
            if turn == 1:
                early_k, early_v = key_gradient(s)
                dk = (dk.astype(F32) + early_k).astype(BF16)
                dv = (dv.astype(F32) + early_v).astype(BF16)
            grad = grad + nt(dk, wa[1]) + nt(dv, wa[2])
            first = jnp.where(place_ref[LOCAL * turn + s] == 0, grad, 0.0)
            sums[FIRST_MEMORY : FIRST_MEMORY + THIN, :] += first
        return grad

    @pl.when(y == 1)
    def _():
        for copy in reads:
            copy.wait()
        left[...] = slots(1, None)
        handed.start()
        lax.fori_loop(0, pairs, attend_at, 0)

    @pl.when(y == 0)
    def _():
        for copy in reads:
            copy.wait()
        lax.fori_loop(0, pairs, attend_at, 0)
        handed.wait_recv()
        slots(0, given[...])

    writes = [
        pltpu.make_async_copy(dqb, dq_ref, sem_out.at[0]),
        pltpu.make_async_copy(dkb, dk_ref, sem_out.at[1]),
        pltpu.make_async_copy(dvb, dv_ref, sem_out.at[2]),
        pltpu.make_async_copy(sums, sums_ref, sem_out.at[3]),
        *[
            pltpu.make_async_copy(tiles.at[i], first_rows(ref), sem_out.at[5 + i])
            for i, ref in enumerate(merged)
        ],
    ]
    for copy in writes:
        copy.start()

    for copy in rows_in:
        copy.wait()
    for s in range(LOCAL):
        df[s, 0:THIN] = jnp.where(memory_row, thin_d[s, 0], df[s, 0:THIN])
        hid[s, 0:THIN] = jnp.where(memory_row, thin_d[s, 1], hid[s, 0:THIN])
    chunks = FF // CHUNK

    def store(i):
        lanes = pl.ds(pl.multiple_of(CHUNK * i, CHUNK), CHUNK)
        slot = lax.rem(i, 2)
        return pltpu.make_async_copy(
            staged.at[slot], terms_ref.at[:, lanes], sem_stage.at[slot]
        )

    def chunk(i, carry):
        slot = lax.rem(i, 2)
        for copy in chunk_reads(i):
            copy.wait()
        lanes = pl.ds(pl.multiple_of(CHUNK * i, CHUNK), CHUNK)
        for s in range(LOCAL):
            for j, buf in ((1, gb), (0, dub)):
                old = buf[slot, s, 0:THIN]
                buf[slot, s, 0:THIN] = jnp.where(memory_row, thin_f[s, j, :, lanes], old)

        @pl.when(i >= 2)
        def _():
            store(i - 2).wait()

        for j, (buf, rows) in enumerate(((dub, hid), (gb, df))):
            terms = tn(
                buf[slot].reshape(LOCAL * SEG, CHUNK), rows[...].reshape(LOCAL * SEG, D)
            )
            staged[slot, j] = terms.astype(BF16)
        store(i).start()

        @pl.when(i + 2 < chunks)
        def _():
            for copy in chunk_reads(i + 2):
                copy.start()

        return carry

    lax.fori_loop(0, chunks, chunk, 0)

    @pl.when(y == 1)
    def _():
        handed.wait_send()

    for copy in [*writes, store(chunks - 2), store(chunks - 1)]:
        copy.wait()
    for copy in swap:
        copy.wait()


THIN_SHAPES = (
    sds((LOCAL, 2, THIN, D), BF16),
    sds((LOCAL, 2, THIN, FF), BF16),
    sds((FIRST_MEMORY + THIN, D), F32),
)


def chain_back(place, table, attn, ffn, q, k, v, saved, g, du, df, h, halves, dc, logs, da, c):
    whole = sds((LOCAL, SEG, D), BF16)
    rows = pltpu.VMEM(whole.shape, BF16)
    dma = lambda *shape: pltpu.SemaphoreType.DMA(shape)
    outs = pl.pallas_call(
        chain_back_kernel,
        in_specs=[SMEM, VMEM] + [ANY] * 18,
        out_specs=[ANY] * 8,
        out_shape=[whole] * 5
        + [THIN_SHAPES[2]]
        + [sds((2, FF, D), BF16), sds((2 * LOCAL, *halves[0].shape[1:]), BF16)],
        input_output_aliases={18: 0, 19: 1},
        scratch_shapes=[
            pltpu.VMEM((4, D, D), BF16),
            pltpu.VMEM((2, FF, D), BF16),
            *[rows] * 5,
            pltpu.VMEM(logs.shape, F32),
            rows,
            rows,
            rows,
            pltpu.VMEM((2, LOCAL, THIN, D), BF16),
            rows,
            rows,
            pltpu.VMEM((2, LOCAL, SEG, CHUNK), BF16),
            pltpu.VMEM((2, LOCAL, SEG, CHUNK), BF16),
            pltpu.VMEM((2, 2, CHUNK, D), BF16),
            *[pltpu.VMEM(s.shape, s.dtype) for s in SAVED + THIN_SHAPES],
            pltpu.VMEM((THIN, D), F32),
            pltpu.VMEM((THIN, D), F32),
            dma(3),
            dma(11),
            dma(2),
            dma(2, 2),
            dma(8),
            dma(2),
            dma(2),
            dma(3),
        ],
        name="chain_back",
        compiler_params=params(collective_id=3, has_side_effects=True),
    )(place, table, attn, ffn, q, k, v, *saved, g, du, df, h, *halves, dc, logs, da, c)
    return outs


def table_row(ref, index, entries):
    blocks = []
    lane = lax.broadcasted_iota(jnp.int32, (1, 128), 1)
    for block in range(D // 128):
        at, end = index * D + 128 * block, index * D + 128 * (block + 1)
        target, value = 0, jnp.zeros((1, 128), F32)
        while at < end:
            shard, inner = at // entries, at % entries
            count = min(end - at, entries - inner, 128 - inner % 128)
            place = (shard // 8, shard // 4 % 2, shard // 2 % 2, shard % 2)
            source = ref[place][inner // 128 : inner // 128 + 1]
            shift = (target - inner) % 128
            if shift:
                source = pltpu.roll(source, shift, 1)
            value = jnp.where((lane >= target) & (lane < target + count), source, value)
            at, target = at + count, target + count
        blocks.append(value)
    return jnp.concatenate(blocks, axis=1)


def head_kernel(
    nz,
    entries,
    attn_src,
    ffn_src,
    vec_src,
    tokens,
    attn_ref,
    ffn_ref,
    table_ref,
    x_ref,
    q_ref,
    k_ref,
    v_ref,
    c_ref,
    log_ref,
    wa,
    vec,
    table,
    mine,
    other,
    xb,
    qb,
    kb,
    vb,
    cb,
    logs,
    send_sem,
    recv_sem,
    own_sem,
    swap_sem,
    out_sem,
):
    place = my_place()
    side = place[3]
    halves = swap_halves(place, tokens, other, swap_sem)
    own = [
        pltpu.make_async_copy(attn_src, attn_view(wa, *place), own_sem.at[0]),
        pltpu.make_async_copy(vec_src, vec_view(vec, *place), own_sem.at[1]),
        pltpu.make_async_copy(ffn_src, ffn_view(ffn_ref, *place), own_sem.at[2]),
        pltpu.make_async_copy(tokens.at[pl.ds(LOCAL * side, LOCAL)], mine, own_sem.at[3]),
    ]
    for copy in own:
        copy.start()
    entry_barrier(nz)
    steps = functools.partial(gather_steps, nz, place, send_sem=send_sem, recv_sem=recv_sem)
    begin, step, end_arrive, end_send = steps(
        1, True, [(0, wa, attn_view), (1, vec, vec_view)]
    )
    late = [
        steps(place[2], bool(i), [(2 + i, ffn_ref.at[i], hidden_view)]) for i in range(2)
    ]
    own[0].wait()
    own[1].wait()
    begin()
    step(1)
    halves.start()

    def loop(t, carry):
        step(t)
        return carry

    lax.fori_loop(2, nz + 2, loop, 0)
    own[2].wait()
    for begin2, _, _, _ in late:
        begin2()
    own[3].wait()
    halves.wait()
    end_arrive()
    for index in range(NVEC):
        table[index : index + 1] = table_row(vec, index, entries)
    outs = [
        pltpu.make_async_copy(wa, attn_ref, out_sem.at[0]),
        pltpu.make_async_copy(table, table_ref, out_sem.at[1]),
    ]
    for copy in outs:
        copy.start()

    weight = lambda i: wa[i].reshape(D, D)

    def project_slot(s):
        x = whole_rows(side, mine[s], other[s]).astype(BF16)
        xb[s] = x
        qb[s] = ((nn(x, weight(0)) + table[QUERY_BIAS : QUERY_BIAS + 1]) * SCALE).astype(BF16)
        kb[s] = nn(x, weight(1)).astype(BF16)
        vb[s] = (nn(x, weight(2)) + table[VALUE_BIAS : VALUE_BIAS + 1]).astype(BF16)
        for i, (buf, out) in enumerate(((xb, x_ref), (qb, q_ref), (kb, k_ref), (vb, v_ref))):
            outs.append(pltpu.make_async_copy(buf.at[s], out.at[s], out_sem.at[2 + 4 * s + i]))
            outs[-1].start()

    def attend_at(i, carry):
        s, h = i // (HEADS // 2), i % (HEADS // 2)
        lanes = pl.ds(pl.multiple_of(h * 2 * DH, 2 * DH), 2 * DH)
        context, log_rows = attend_pair(qb[s, :, lanes], kb[s, :, lanes], vb[s, :, lanes])
        cb[s, :, lanes] = context
        for head in range(2):
            logs[s, h, head : head + 1] = log_rows[head]
        return carry

    project_slot(0)
    project_slot(1)
    pairs = LOCAL * HEADS // 2
    done = 0
    for t in range(1, nz + 2):
        for _, step2, _, _ in late:
            step2(t)
        upto = pairs * t // (nz + 1)
        lax.fori_loop(done, upto, attend_at, 0)
        done = upto
    outs.append(pltpu.make_async_copy(cb, c_ref, out_sem.at[2 + 4 * LOCAL]))
    outs.append(pltpu.make_async_copy(logs, log_ref, out_sem.at[3 + 4 * LOCAL]))
    outs[-1].start()
    outs[-2].start()
    end_send()
    for _, _, end_arrive2, end_send2 in late:
        end_send2()
        end_arrive2()
    for copy in outs:
        copy.wait()


def head(nz, attention, hidden_major, vec, tokens, entries):
    rows, hidden = attention.shape[1], hidden_major.shape[1]
    whole = sds((LOCAL, SEG, D), BF16)
    logs = (LOCAL, HEADS // 2, 2, SEG)
    attn_shape, vec_shape = (4, nz, 2, 2, rows, D), (nz, 2, 2, 2, *VEC_TILE)
    half = pltpu.VMEM((LOCAL, *tokens.shape[1:]), BF16)
    return pl.pallas_call(
        functools.partial(head_kernel, nz, entries),
        in_specs=[ANY] * 4,
        out_specs=[ANY] * 9,
        out_shape=[
            sds(attn_shape, BF16),
            sds((2, nz, 2, 2, 2, hidden, D), BF16),
            sds((NVEC, D), F32),
            *[whole] * 5,
            sds(logs, F32),
        ],
        scratch_shapes=[
            pltpu.VMEM(attn_shape, BF16),
            pltpu.VMEM(vec_shape, F32),
            pltpu.VMEM((NVEC, D), F32),
            half,
            half,
            *[pltpu.VMEM(whole.shape, BF16)] * 5,
            pltpu.VMEM(logs, F32),
            pltpu.SemaphoreType.DMA((11, nz, 4)),
            pltpu.SemaphoreType.DMA((8, nz, 4)),
            pltpu.SemaphoreType.DMA((4,)),
            pltpu.SemaphoreType.DMA((2,)),
            pltpu.SemaphoreType.DMA((4 + 4 * LOCAL,)),
        ],
        name="head",
        compiler_params=params(collective_id=0, has_side_effects=True),
    )(attention, hidden_major, vec, tokens)


def token_grad_kernel(place_ref, da_ref, dq_ref, dk_ref, dv_ref, w_ref, keep_ref, send_ref):
    side = lax.axis_index("tensor")
    total = da_ref[0].astype(F32)
    for i, ref in enumerate((dq_ref, dk_ref, dv_ref)):
        total = total + nt(ref[0], w_ref[i])
    live = place_ref[LOCAL * side + pl.program_id(0)] >= 0
    keep, send = split_rows(side, jnp.where(live, total, 0.0))
    keep_ref[0] = keep.astype(BF16)
    send_ref[0] = send.astype(BF16)


def token_gradient(place, da, dq, dk, dv, attn):
    half = (SEG - MEM) // 2
    return pl.pallas_call(
        token_grad_kernel,
        grid=(LOCAL,),
        in_specs=[SMEM] + [slot_rows()] * 4 + [once((3, D, D), (0, 0, 0))],
        out_specs=[half_rows(half)] * 2,
        out_shape=[sds((LOCAL, half, D), BF16)] * 2,
        name="token_gradient",
        compiler_params=params(),
    )(place, da, dq, dk, dv, attn)


def flat(ref):
    return ref[...].reshape(LOCAL * ref.shape[1], ref.shape[2])


def attn_grad_kernel(
    x_ref, da_ref, dq_ref, dk_ref, dv_ref, c_ref, sums_ref, thin_sums_ref, out_ref, vec_ref
):
    x = flat(x_ref)
    dq, dv = flat(dq_ref), flat(dv_ref)
    out_ref[0] = tn(x, dq).astype(BF16)
    out_ref[1] = tn(x, flat(dk_ref)).astype(BF16)
    out_ref[2] = tn(x, dv).astype(BF16)
    out_ref[3] = tn(flat(da_ref), flat(c_ref)).astype(BF16)
    vec_ref[...] = thin_sums_ref[...]
    vec_ref[0:FIRST_MEMORY] = thin_sums_ref[0:FIRST_MEMORY] + sums_ref[0:FIRST_MEMORY]
    vec_ref[QUERY_BIAS : QUERY_BIAS + 1] = row_sum(dq.astype(F32))
    vec_ref[VALUE_BIAS : VALUE_BIAS + 1] = row_sum(dv.astype(F32))


def attn_gradient(x, da, dq, dk, dv, c, sums, thin_sums, chunk=256):
    part = pl.BlockSpec((LOCAL, SEG, chunk), lambda i: (0, 0, i))
    full = once((LOCAL, SEG, D), (0, 0, 0))
    lanes = lambda rows: pl.BlockSpec((rows, chunk), lambda i: (0, i))
    return pl.pallas_call(
        attn_grad_kernel,
        grid=(D // chunk,),
        in_specs=[full, full, part, part, part, part, lanes(THIN), lanes(FIRST_MEMORY + THIN)],
        out_specs=[
            pl.BlockSpec((4, D, chunk), lambda i: (0, 0, i)),
            lanes(FIRST_MEMORY + THIN),
        ],
        out_shape=[sds((4, D, D), BF16), sds((FIRST_MEMORY + THIN, D), F32)],
        name="attn_gradient",
        compiler_params=params(),
    )(x, da, dq, dk, dv, c, sums, thin_sums)


def scatter_steps(nz, place, lead, z_second, pieces, send_sem, recv_sem):
    z, x, c, y = place
    first, second, both = partners(place, lead)
    to_first = device(z, first[0], c, first[1])
    to_second = device(z, second[0], c, second[1])
    to_core = device(z, x, 1 - c, y)
    f_first, f_second = 2 - lead, 1 + lead

    def at(f):
        fx, fy = f // 2, f % 2
        return x + fx * (1 - 2 * x), y + fy * (1 - 2 * y)

    def term(piece, zz, core, f):
        xx, yy = at(f)
        return piece[2](piece[1], zz, xx, core, yy)

    def copies(kind, zz, target, src, dst):
        return [
            remote(src(p), dst(p), send_sem.at[kind, zz, p[0]], recv_sem.at[kind, zz, p[0]], target)
            for p in pieces
        ]

    def core_copies(zz, f):
        return copies(
            f, zz, to_core, lambda p: term(p, zz, 1 - c, f), lambda p: p[3].at[zz, f]
        )

    def second_copies(zz, across):
        f = 3 if across else f_second
        return copies(
            4 + across, zz, to_second, lambda p: p[3].at[zz, f], lambda p: p[4].at[zz, across]
        )

    def first_copies(zz):
        slot = 0 if z_second else zz
        return copies(6, zz, to_first, lambda p: p[4].at[zz, 1], lambda p: p[5].at[slot])

    def partial(p, zz, f):
        return p[4].at[zz, f] if z_second else p[5].at[zz]

    def beside(p, above, zz, f):
        return p[6 + above].at[zz, f] if z_second else p[6 + above].at[zz]

    def up_copies(zz, f):
        return copies(
            7 + 2 * f,
            zz,
            device(z + 1, x, c, y),
            lambda p: partial(p, zz, f),
            lambda p: beside(p, 0, zz, f),
        )

    def down_copies(zz, f):
        return copies(
            8 + 2 * f,
            zz,
            device(z - 1, x, c, y),
            lambda p: partial(p, zz, f),
            lambda p: beside(p, 1, zz, f),
        )

    def run(group, what):
        for copy in group:
            getattr(copy, what)()

    def add(into, other):
        for p in pieces:
            a, b = into(p), other(p)
            a[...] = (a[...].astype(F32) + b[...].astype(F32)).astype(a.dtype)

    def turn(k):
        upper = z // (nz // 2)
        return (1 - upper) * (nz - 1 - k) + upper * k

    def start(zz):
        for f in (3, 1, 2, 0):
            run(core_copies(zz, f), "start")

    def stage0(zz):
        for f in (3, 1, 2, 0):
            run(core_copies(zz, f), "wait_recv")
            add(lambda p: p[3].at[zz, f], lambda p: term(p, zz, c, f))
        run(second_copies(zz, 1), "start")
        run(second_copies(zz, 0), "start")

    def from_below(zz, f):
        run(up_copies(zz, f), "wait_recv")
        add(lambda p: partial(p, zz, f), lambda p: beside(p, 0, zz, f))

    def from_above(zz, f):
        run(down_copies(zz, f), "wait_recv")
        add(lambda p: partial(p, zz, f), lambda p: beside(p, 1, zz, f))

    def from_end(zz, f):
        @pl.when((zz > z) & (z == 0))
        def _():
            run(up_copies(zz, f), "start")

        @pl.when((zz < z) & (z == nz - 1))
        def _():
            run(down_copies(zz, f), "start")

    def along(zz, f):
        @pl.when((zz > z) & (z > 0))
        def _():
            from_below(zz, f)
            run(up_copies(zz, f), "start")

        @pl.when((zz < z) & (z < nz - 1))
        def _():
            from_above(zz, f)
            run(down_copies(zz, f), "start")

    def stage1(zz):
        run(second_copies(zz, 1), "wait_recv")
        add(lambda p: p[4].at[zz, 1], lambda p: p[3].at[zz, f_first])
        if z_second:
            from_end(zz, 1)
        else:
            run(first_copies(zz), "start")

    def stage2(zz):
        run(second_copies(zz, 0), "wait_recv")
        add(lambda p: p[4].at[zz, 0], lambda p: p[3].at[zz, 0])
        if not z_second:
            run(first_copies(zz), "wait_recv")
            add(lambda p: p[5].at[zz], lambda p: p[4].at[zz, 0])
        from_end(zz, 0)
        if z_second:
            along(zz, 1)

    def stage3(zz):
        along(zz, 0)

    def staged(stage):
        return lambda k: stage(turn(k))

    def at_owner(f):
        @pl.when(z > 0)
        def _():
            from_below(z, f)

        @pl.when(z < nz - 1)
        def _():
            from_above(z, f)

    def end(outs):
        if z_second:
            at_owner(1)
            run(first_copies(z), "start")
        at_owner(0)
        if z_second:
            run(first_copies(z), "wait_recv")
            add(lambda p: p[4].at[z, 0], lambda p: p[5].at[0])
        for p, out in zip(pieces, outs):
            out[...] = partial(p, z, 0)[...]

    def sent(zz, carry):
        for f in range(4):
            run(core_copies(zz, f), "wait_send")
        run(second_copies(zz, 1), "wait_send")
        run(second_copies(zz, 0), "wait_send")
        for f in range(2 if z_second else 1):

            @pl.when(zz > z)
            def _():
                run(up_copies(zz, f), "wait_send")

            @pl.when(zz < z)
            def _():
                run(down_copies(zz, f), "wait_send")

        if z_second:

            @pl.when(zz == z)
            def _():
                run(first_copies(zz), "wait_send")

        else:
            run(first_copies(zz), "wait_send")
        return carry

    stages = [staged(stage) for stage in (stage0, stage1, stage2, stage3)]
    return start, stages, turn, end, lambda: lax.fori_loop(0, nz, sent, 0)


def scatter_places(nz, shape, z_second):
    lead = (nz, 2) if z_second else (nz,)
    return [
        pltpu.VMEM((nz, 4, *shape), BF16),
        pltpu.VMEM((nz, 2, *shape), BF16),
        pltpu.VMEM((1 if z_second else nz, *shape), BF16),
        pltpu.VMEM((*lead, *shape), BF16),
        pltpu.VMEM((*lead, *shape), BF16),
    ]


VEC_ROWS = FIRST_MEMORY + THIN


def tail_kernel(nz, *refs):
    (
        place_ref,
        sums_ref,
        thin_sums_ref,
        ffn_terms,
        *rows_refs,
        w_ref,
        attn_out,
        ffn_out,
        vec_out,
        grad_ref,
        terms_f,
        terms_a,
        rows,
        wb,
        keep,
        send,
    ) = refs[:21]
    places = [refs[21 + 5 * i : 26 + 5 * i] for i in range(3)]
    vec_mine, vec_given, vec_z, send_sem, recv_sem, block_sem, in_sem, swap_sem, vec_sem = refs[36:]
    place = z, x, c, y = my_place()
    blocks = lambda zz: pltpu.make_async_copy(
        ffn_terms.at[:, zz], terms_f.at[:, zz], block_sem.at[zz]
    )
    rows_in = [
        pltpu.make_async_copy(src, rows.at[i], in_sem.at[2 + i]) for i, src in enumerate(rows_refs)
    ]
    rows_in.append(pltpu.make_async_copy(w_ref.at[pl.ds(0, 3)], wb, in_sem.at[8]))
    steps = functools.partial(scatter_steps, nz, place, send_sem=send_sem, recv_sem=recv_sem)
    up = steps(c, True, [(0, terms_f.at[0], hidden_view, *places[0])])
    down = steps(1 - c, True, [(1, terms_f.at[1], hidden_view, *places[1])])
    attn = steps(1, False, [(2, terms_a, attn_view, *places[2])])
    turn = up[2]
    for k in range(nz):
        blocks(turn(k)).start()
    for copy in rows_in:
        copy.start()

    barrier = pltpu.get_barrier_semaphore()
    others = [device(lax.rem(z + dz, nz), x, c, y) for dz in range(1, nz)]
    for other in [device(z, 1 - x, c, y), device(z, x, 1 - c, y), device(z, x, c, 1 - y), *others]:
        pl.semaphore_signal(
            barrier, inc=1, device_id=other, device_id_type=pl.DeviceIdType.MESH
        )
    pl.semaphore_wait(barrier, 2 + nz)

    def begin(k, carry):
        zz = turn(k)
        blocks(zz).wait()
        up[0](zz)
        down[0](zz)
        return carry

    def attn_terms(i, carry):
        left, right = rows[i // 3], rows[i + 2]
        value = tn(left.reshape(LOCAL * SEG, D), right.reshape(LOCAL * SEG, D))
        terms_a[i] = value.astype(BF16).reshape(terms_a.shape[1:])
        return carry

    def token_rows(s):
        total = rows[1, s].astype(F32)
        for i in range(3):
            total = total + nt(rows[2 + i, s], wb[i])
        live = place_ref[LOCAL * y + s] >= 0
        stay, go = split_rows(y, jnp.where(live, total, 0.0))
        keep[s] = stay.astype(BF16)
        send[s] = go.astype(BF16)

    def vec_copies(phase):
        if phase < 3:
            target = (device(z, x, 1 - c, y), device(z, x, c, 1 - y), device(z, 1 - x, c, y))[phase]
            sems = vec_sem.at[0, phase], vec_sem.at[1, phase]
            return [remote(vec_mine.at[phase], vec_given.at[phase], *sems, target)]
        return [
            remote(
                vec_mine.at[3], vec_z.at[dz], vec_sem.at[0, 3 + dz], vec_sem.at[1, 3 + dz], target
            )
            for dz, target in enumerate(others)
        ]

    def vec_start(phase):
        if phase == 0:
            vec_mine[0] = thin_sums_ref[...]
            vec_mine[0, 0:FIRST_MEMORY] = (
                thin_sums_ref[0:FIRST_MEMORY] + sums_ref[0:FIRST_MEMORY]
            )
            for r, i in ((QUERY_BIAS, 2), (VALUE_BIAS, 4)):
                total = row_sum(rows[i].reshape(LOCAL * SEG, D).astype(F32))
                vec_mine[0, r : r + 1] = total
        else:
            for copy in vec_copies(phase - 1):
                copy.wait_recv()
            vec_mine[phase] = vec_mine[phase - 1] + vec_given[phase - 1]
        for copy in vec_copies(phase):
            copy.start()

    swap = place_rows(place, keep, send, grad_ref, swap_sem)

    def stage(i, *groups):
        for k in groups[-1]:
            for group in groups[:-1]:
                group[1][i](k)

    def step(k, *groups):
        for lag in range(4):
            if 0 <= k - lag < nz:
                stage(lag, *groups, (k - lag,))

    lax.fori_loop(0, 2, begin, 0)
    step(0, up, down)
    for copy in rows_in:
        copy.wait()
    lax.fori_loop(0, 2, attn_terms, 0)
    lax.fori_loop(2, 3, begin, 0)
    step(1, up, down)
    lax.fori_loop(2, 4, attn_terms, 0)
    vec_start(0)
    lax.fori_loop(3, 4, begin, 0)
    attn[0](turn(0))
    step(2, up, down)
    step(0, attn)
    attn[0](turn(1))
    token_rows(0)
    vec_start(1)
    step(3, up, down)
    step(1, attn)
    attn[0](turn(2))
    token_rows(1)
    for copy in swap:
        copy.start()
    step(4, up, down)
    step(2, attn)
    attn[0](turn(3))
    vec_start(2)
    step(5, up, down)
    step(3, attn)
    vec_start(3)
    step(6, up, down)
    step(4, attn)
    up[3]([ffn_out.at[0]])
    step(5, attn)
    down[3]([ffn_out.at[1]])
    step(6, attn)
    attn[3]([attn_out])
    total = vec_mine[3]
    for dz, copy in enumerate(vec_copies(3)):
        copy.wait_recv()
        total = total + vec_z[dz]
    vec_out[...] = total
    for phase in range(4):
        for copy in vec_copies(phase):
            copy.wait_send()
    for group in (up, down, attn):
        group[4]()
    for copy in swap:
        copy.wait()


def tail(place, sums, thin_sums, ffn_terms, x, da, dq, dk, dv, c, attn, shapes):
    nz = lax.axis_size("dp") // 4
    rows, hidden, half = shapes
    attn_shape, ffn_shape = (4, nz, 2, 2, rows, D), (2, nz, 2, 2, 2, hidden, D)
    part = pltpu.VMEM((LOCAL, half, D), BF16)
    dma = lambda *shape: pltpu.SemaphoreType.DMA(shape)
    return pl.pallas_call(
        functools.partial(tail_kernel, nz),
        in_specs=[SMEM, VMEM, VMEM] + [ANY] * 8,
        out_specs=[VMEM] * 3 + [ANY],
        out_shape=[
            sds((4, rows, HALF), BF16),
            sds((2, hidden, D), BF16),
            sds((VEC_ROWS, D), F32),
            sds((2 * LOCAL, half, D), BF16),
        ],
        scratch_shapes=[
            pltpu.VMEM(ffn_shape, BF16),
            pltpu.VMEM(attn_shape, BF16),
            pltpu.VMEM((6, LOCAL, SEG, D), BF16),
            pltpu.VMEM((3, D, D), BF16),
            part,
            part,
            *scatter_places(nz, (hidden, D), True),
            *scatter_places(nz, (hidden, D), True),
            *scatter_places(nz, (4, rows, HALF), False),
            pltpu.VMEM((4, VEC_ROWS, D), F32),
            pltpu.VMEM((3, VEC_ROWS, D), F32),
            pltpu.VMEM((nz - 1, VEC_ROWS, D), F32),
            dma(11, nz, 3),
            dma(11, nz, 3),
            dma(nz),
            dma(9),
            dma(3),
            dma(2, 2 + nz),
        ],
        name="tail",
        compiler_params=params(62, collective_id=1, has_side_effects=True),
    )(place, sums, thin_sums, ffn_terms.reshape(ffn_shape), x, da, dq, dk, dv, c, attn)


def update(gradient, momentum, weight, average, rate, grad_scale):
    scaled = gradient * grad_scale
    moment = MOMENTUM * momentum + scaled
    weight_new = weight - rate * (scaled + MOMENTUM * moment)
    return (moment, weight_new, AVERAGE_DECAY * average + (1.0 - AVERAGE_DECAY) * weight_new)


VEC_TILE = (8, 128)


def in_tiles(rows):
    size = VEC_TILE[0] * VEC_TILE[1]
    padded = jnp.pad(rows, [(0, 0)] * (rows.ndim - 1) + [(0, size - rows.shape[-1])])
    return padded.reshape(*rows.shape[:-1], *VEC_TILE)


def start(attention, feedforward, vectors, tokens):
    nz = lax.axis_size("dp") // 4
    rows, hidden, entries = attention.shape[1], feedforward.shape[2], vectors.shape[0]
    attention = attention.astype(BF16)
    hidden_major = jnp.swapaxes(feedforward.astype(BF16), 1, 2)
    vec = in_tiles(vectors.astype(BF16).astype(F32))
    aligned = rows % THIN == 0
    if aligned:
        attn, ffn, table, *work = head(nz, attention, hidden_major, vec, tokens, entries)
    else:
        attn, ffn, table, other = gather(
            nz,
            0,
            [
                (attention, (4, nz, 2, 2, rows, D), attn_view),
                (hidden_major, (2, nz, 2, 2, 2, hidden, D), ffn_view),
                (vec, (nz, 2, 2, 2, *VEC_TILE), vec_view),
            ],
            tokens,
        )
    attn, ffn = attn.reshape(4, D, D), ffn.reshape(2, FF, D)
    if not aligned:
        table = table.reshape(nz * 8, VEC_TILE[0] * VEC_TILE[1])[:, :entries].reshape(NVEC, D)
        work = project(tokens, other, attn, table)
        work = [*work, *attend(*work[1:])]
    return attn, ffn, table, work


def scatter_gradients(attn_terms, ffn_terms, vec_terms, shapes):
    nz = lax.axis_size("dp") // 4
    rows, hidden, entries = shapes
    attn, ffn, vec = scatter(
        nz,
        1,
        [
            (attn_terms.reshape(4, nz, 2, 2, rows, D), (4, rows, HALF), attn_view),
            (ffn_terms.reshape(2, nz, 2, 2, 2, hidden, D), (2, hidden, D), ffn_view),
            (in_tiles(vec_terms.reshape(nz, 2, 2, 2, entries)), VEC_TILE, vec_view),
        ],
    )
    return attn.astype(F32), jnp.swapaxes(ffn, 1, 2).astype(F32), vec.reshape(-1)[:entries]


def swap(value):
    return lax.ppermute(value, "tensor", [(0, 1), (1, 0)])


def joined_kernel(keep_ref, other_ref, out_ref, sem):
    side = lax.axis_index("tensor")
    copies = [
        pltpu.make_async_copy(keep_ref, out_ref.at[pl.ds(LOCAL * side, LOCAL)], sem.at[0]),
        pltpu.make_async_copy(other_ref, out_ref.at[pl.ds(LOCAL * (1 - side), LOCAL)], sem.at[1]),
    ]
    for c in copies:
        c.start()
    for c in copies:
        c.wait()


def joined(keep, other):
    return pl.pallas_call(
        joined_kernel,
        in_specs=[ANY] * 2,
        out_specs=ANY,
        out_shape=sds((2 * LOCAL, *keep.shape[1:]), keep.dtype),
        scratch_shapes=[pltpu.SemaphoreType.DMA((2,))],
        name="joined",
        compiler_params=params(16),
    )(keep, other)


def on_device(
    tokens,
    slot_position,
    cotangent,
    attention,
    feedforward,
    vectors,
    attn_momentum,
    ffn_momentum,
    vec_momentum,
    attn_average,
    ffn_average,
    vec_average,
):
    place = slot_position
    attn, ffn, table, work = start(attention, feedforward, vectors, tokens)
    x, q, k, v, c, log_tokens = work

    (x, q, k, v), saved, cot_other = chain(place, table, attn, ffn, x, q, k, v, cotangent)
    keep, send, h, g, du, df, da, dc, c, log_total, sums = rows_part(
        place, x, q, k, v, c, log_tokens, cotangent, cot_other, attn, ffn, table
    )
    da, c, dq, dk, dv, thin_sums, ffn_terms, activations = chain_back(
        place, table, attn, ffn, q, k, v, saved, g, du, df, h, (keep, send), dc, log_total, da, c
    )
    rows, hidden, entries = attention.shape[1], feedforward.shape[2], vectors.shape[0]
    if rows % THIN == 0:
        shapes = (rows, hidden, tokens.shape[1])
        attn_grad, ffn_grad, vec_sums, token_grad = tail(
            place, sums, thin_sums, ffn_terms, x, da, dq, dk, dv, c, attn, shapes
        )
        attn_grad = attn_grad.astype(F32)
        ffn_grad = jnp.swapaxes(ffn_grad, 1, 2).astype(F32)
        index = lax.axis_index("dp") * 2 + lax.axis_index("tensor")
        vec_grad = lax.dynamic_slice_in_dim(
            vec_sums[:NVEC].reshape(-1), index * entries, entries
        )
    else:
        keep, send = token_gradient(place, da, dq, dk, dv, attn)
        token_grad = joined(keep, swap(send))
        attn_terms, vec_terms = attn_gradient(x, da, dq, dk, dv, c, sums, thin_sums)
        attn_grad, ffn_grad, vec_grad = scatter_gradients(
            attn_terms, ffn_terms, vec_terms[:NVEC], (rows, hidden, entries)
        )
    grad_scale = 1.0 / math.sqrt(lax.axis_size("dp") * SLOTS * ROWS)
    attn_new = update(attn_grad, attn_momentum, attention, attn_average, ATTENTION_RATE, grad_scale)
    ffn_new = update(ffn_grad, ffn_momentum, feedforward, ffn_average, FEEDFORWARD_RATE, grad_scale)
    vec_new = update(vec_grad, vec_momentum, vectors, vec_average, VECTOR_RATE, grad_scale)
    return (
        activations,
        token_grad,
        attn_new[0],
        ffn_new[0],
        vec_new[0],
        attn_new[1],
        ffn_new[1],
        vec_new[1],
        attn_new[2],
        ffn_new[2],
        vec_new[2],
    )


def solution(mesh):
    attn_spec = P(None, "dp", "tensor")
    ffn_spec = P(None, None, ("dp", "tensor"))
    vec_spec = P(("dp", "tensor"))
    rows_spec = P("dp", "tensor", None)
    states = (attn_spec, ffn_spec, vec_spec)
    return jax.shard_map(
        on_device,
        mesh=mesh,
        in_specs=(rows_spec, P("dp"), rows_spec) + states * 3,
        out_specs=(rows_spec, rows_spec) + states * 3,
        check_vma=False,
    )
```

```python
import functools
import math

import jax
import jax.numpy as jnp
from jax import lax
from jax.experimental import pallas as pl
from jax.experimental.pallas import tpu as pltpu
from jax.sharding import PartitionSpec as P

D = 768
HEADS = 12
DH = 64
FF = 3072
MEM = 10
SLOTS = 4
ROWS = 522
NVEC = 22

HALF = D // 2
SEG = ROWS - MEM
THIN = 16
LOCAL = 2
TILE = 256

EPSILON = 1e-05
MOMENTUM = 0.9
AVERAGE_DECAY = 0.75
ATTENTION_RATE = 0.06
FEEDFORWARD_RATE = 0.02
VECTOR_RATE = 0.1
MASK_VALUE = -1e30
SCALE = 1.0 / math.sqrt(DH)

F32 = jnp.float32
BF16 = jnp.bfloat16
MIB = 1 << 20

QUERY_BIAS, VALUE_BIAS, OUT_BIAS, GAIN1, SHIFT1, DOWN_BIAS, GAIN2, SHIFT2, UP_BIAS = range(9)
FIRST_MEMORY = UP_BIAS + FF // D


def nn(a, b):
    return lax.dot_general(a, b, (((1,), (0,)), ((), ())), preferred_element_type=F32)


def nt(a, b):
    return lax.dot_general(a, b, (((1,), (1,)), ((), ())), preferred_element_type=F32)


def tn(a, b):
    return lax.dot_general(a, b, (((0,), (0,)), ((), ())), preferred_element_type=F32)


def normalized(rows):
    center = rows - jnp.mean(rows, axis=-1, keepdims=True)
    spread = jnp.mean(center * center, axis=-1, keepdims=True)
    inverse = lax.rsqrt(spread + EPSILON)
    return center * inverse, inverse


def normalized_back(grad, unit, inverse):
    mean_grad = jnp.mean(grad, axis=-1, keepdims=True)
    mean_along = jnp.mean(grad * unit, axis=-1, keepdims=True)
    return inverse * (grad - mean_grad - unit * mean_along)


def gelu_parts(u):
    size = jnp.abs(u)
    t = 1.0 / (1.0 + (0.3275911 / math.sqrt(2.0)) * size)
    bell = jnp.exp(-0.5 * u * u)
    poly = t * (
        0.5 * 0.254829592
        + t
        * (
            0.5 * -0.284496736
            + t * (0.5 * 1.421413741 + t * (0.5 * -1.453152027 + t * (0.5 * 1.061405429)))
        )
    )
    tail = poly * bell
    cdf = jnp.where(u < 0, tail, 1.0 - tail)
    return u * cdf, cdf + (u * (1.0 / math.sqrt(2.0 * math.pi))) * bell


def row_sum(block):
    return jnp.sum(block, axis=0, keepdims=True)


def params(limit=60, **more):
    return pltpu.CompilerParams(vmem_limit_bytes=limit * MIB, **more)


def once(shape, index):
    return pl.BlockSpec(shape, lambda *_: index, pipeline_mode=pl.Buffered(1))


ANY = pl.BlockSpec(memory_space=pltpu.HBM)
SMEM = pl.BlockSpec(memory_space=pltpu.SMEM)
VMEM = pl.BlockSpec(memory_space=pltpu.VMEM)


def sds(shape, dtype):
    return jax.ShapeDtypeStruct(shape, dtype)


def my_place():
    dp = lax.axis_index("dp")
    return dp // 4, (dp // 2) % 2, dp % 2, lax.axis_index("tensor")


def device(z, x, c, y):
    return {"dp": (z * 2 + x) * 2 + c, "tensor": y}


def entry_barrier(nz):
    z, x, c, y = my_place()
    barrier = pltpu.get_barrier_semaphore()
    signal = lambda d: pl.semaphore_signal(
        barrier, inc=1, device_id=d, device_id_type=pl.DeviceIdType.MESH
    )
    signal(device(z, 1 - x, c, y))
    signal(device(z, x, 1 - c, y))
    signal(device(z, x, c, 1 - y))

    @pl.when(z > 0)
    def _():
        signal(device(z - 1, x, c, y))

    @pl.when(z < nz - 1)
    def _():
        signal(device(z + 1, x, c, y))

    up = lax.convert_element_type(z < nz - 1, jnp.int32)
    down = lax.convert_element_type(z > 0, jnp.int32)
    pl.semaphore_wait(barrier, 3 + up + down)


def attn_view(ref, z, x, c, y):
    return ref.at[:, z, x, c, :, pl.ds(pl.multiple_of(y * HALF, HALF), HALF)]


def ffn_view(ref, z, x, c, y):
    return ref.at[:, z, x, c, y]


def vec_view(ref, z, x, c, y):
    return ref.at[z, x, c, y]


def hidden_view(ref, z, x, c, y):
    return ref.at[z, x, c, y]


def partners(place, lead):
    _, x, _, y = place
    first = (x + (1 - lead) * (1 - 2 * x), y + lead * (1 - 2 * y))
    second = (x + lead * (1 - 2 * x), y + (1 - lead) * (1 - 2 * y))
    return first, second, (1 - x, 1 - y)


COLUMN, FIRST, SECOND, BOTH, CORE = 0, 1, 2, 3, 4
UP, DOWN, UP_FIRST, DOWN_FIRST = 0, 8, 9, 10


def remote(src, dst, send_sem, recv_sem, target):
    return pltpu.make_async_remote_copy(
        src_ref=src,
        dst_ref=dst,
        send_sem=send_sem,
        recv_sem=recv_sem,
        device_id=target,
        device_id_type=pl.DeviceIdType.MESH,
    )


def gather_steps(nz, place, lead, z_second, pieces, send_sem, recv_sem):
    z, x, c, y = place
    first, second, both = partners(place, lead)
    to_first = device(z, first[0], c, first[1])
    to_second = device(z, second[0], c, second[1])
    to_core = device(z, x, 1 - c, y)

    def copies(send, recv, shard, target):
        return [
            remote(
                view(out, *shard),
                view(out, *shard),
                send_sem.at[send, shard[0], i],
                recv_sem.at[recv, shard[0], i],
                target,
            )
            for i, out, view in pieces
        ]

    def start(*args):
        for copy in copies(*args):
            copy.start()

    def arrived(*args):
        for copy in copies(*args):
            copy.wait_recv()

    def sent(*args):
        for copy in copies(*args):
            copy.wait_send()

    def column(zz):
        return (zz, x, c, y)

    def of_first(zz):
        return (zz, first[0], c, first[1])

    def of_second(zz):
        return (zz, second[0], c, second[1])

    def of_both(zz):
        return (zz, both[0], c, both[1])

    core_first, core_second = CORE + 2 - lead, CORE + 1 + lead

    def move_up(zz):
        return (UP, COLUMN, column(zz), device(z + 1, x, c, y))

    def move_down(zz):
        return (DOWN, COLUMN, column(zz), device(z - 1, x, c, y))

    def first_up(zz):
        return (UP_FIRST, FIRST, of_first(zz), device(z + 1, x, c, y))

    def first_down(zz):
        return (DOWN_FIRST, FIRST, of_first(zz), device(z - 1, x, c, y))

    def along(zz, rising, falling, up, down):
        if rising:

            @pl.when(z < nz - 1)
            def _():
                start(*up(zz))

        if falling:

            @pl.when(z > 0)
            def _():
                start(*down(zz))

    def stage0(zz, rising, falling, wait):
        if wait:
            arrived(UP, COLUMN, column(zz), to_core)
        if z_second and not wait:
            start(FIRST, FIRST, column(zz), to_first)
        along(zz, rising, falling, move_up, move_down)
        if not z_second:
            start(FIRST, FIRST, column(zz), to_first)
        start(SECOND, SECOND, column(zz), to_second)
        start(CORE, CORE, column(zz), to_core)

    def stage1(zz, rising, falling):
        arrived(FIRST, FIRST, of_first(zz), to_first)
        if z_second:
            along(zz, rising, falling, first_up, first_down)
        start(BOTH, BOTH, of_first(zz), to_second)
        start(core_first, core_first, of_first(zz), to_core)

    def stage2(zz, rising, falling):
        arrived(SECOND, SECOND, of_second(zz), to_second)
        start(core_second, core_second, of_second(zz), to_core)
        arrived(BOTH, BOTH, of_both(zz), to_second)
        start(CORE + 3, CORE + 3, of_both(zz), to_core)

    def begin():
        stage0(z, True, True, False)

    def step(t):
        @pl.when((t < nz) & (z - t >= 0))
        def _():
            stage0(z - t, True, False, True)

        @pl.when((t < nz) & (z + t < nz))
        def _():
            stage0(z + t, False, True, True)

        for lag, stage in ((1, stage1), (2, stage2)):
            late = t - lag

            @pl.when(late == 0)
            def _():
                stage(z, True, True)

            @pl.when((late > 0) & (late < nz) & (z - late >= 0))
            def _():
                stage(z - late, True, False)

            @pl.when((late > 0) & (late < nz) & (z + late < nz))
            def _():
                stage(z + late, False, True)

    def all_arrived(zz, carry):
        for fx in range(2):
            for fy in range(2):
                kind = CORE + 2 * fx + fy
                shard = (zz, x + fx * (1 - 2 * x), 1 - c, y + fy * (1 - 2 * y))
                arrived(kind, kind, shard, to_core)
        return carry

    def all_sent(zz, carry):
        @pl.when((zz <= z) & (z < nz - 1))
        def _():
            sent(*move_up(zz))

        @pl.when((zz >= z) & (z > 0))
        def _():
            sent(*move_down(zz))

        if z_second:

            @pl.when((zz <= z) & (z < nz - 1))
            def _():
                sent(*first_up(zz))

            @pl.when((zz >= z) & (z > 0))
            def _():
                sent(*first_down(zz))

            @pl.when(zz == z)
            def _():
                sent(FIRST, FIRST, column(zz), to_first)

        else:
            sent(FIRST, FIRST, column(zz), to_first)
        sent(SECOND, SECOND, column(zz), to_second)
        sent(BOTH, BOTH, of_first(zz), to_second)
        sent(CORE, CORE, column(zz), to_core)
        sent(core_first, core_first, of_first(zz), to_core)
        sent(core_second, core_second, of_second(zz), to_core)
        sent(CORE + 3, CORE + 3, of_both(zz), to_core)
        return carry

    def end_arrive():
        lax.fori_loop(0, nz, all_arrived, 0)

    def end_send():
        lax.fori_loop(0, nz, all_sent, 0)

    return begin, step, end_arrive, end_send


def swap_halves(place, rows, other, sem):
    z, x, c, y = place
    return remote(
        rows.at[pl.ds(LOCAL * (1 - y), LOCAL)],
        other,
        sem.at[0],
        sem.at[1],
        device(z, x, c, 1 - y),
    )


def place_rows(place, keep, send, out, sem):
    z, x, c, y = place
    own = out.at[pl.ds(LOCAL * y, LOCAL)]
    return [
        pltpu.make_async_copy(keep, own, sem.at[2]),
        remote(send, own, sem.at[0], sem.at[1], device(z, x, c, 1 - y)),
    ]


def gather_kernel(nz, views, *refs):
    n = len(views)
    srcs, tokens, outs, other = refs[:n], refs[n], refs[n + 1 : 2 * n + 1], refs[2 * n + 1]
    send_sem, recv_sem, own_sem, swap_sem = refs[2 * n + 2 :]
    place = my_place()
    halves = swap_halves(place, tokens, other, swap_sem)
    own = [
        pltpu.make_async_copy(src, view(out, *place), own_sem.at[i])
        for i, (src, out, view) in enumerate(zip(srcs, outs, views))
    ]
    for copy in own:
        copy.start()
    entry_barrier(nz)
    halves.start()
    for copy in own:
        copy.wait()
    pieces = [(i, out, view) for i, (out, view) in enumerate(zip(outs, views))]
    begin, step, end_arrive, end_send = gather_steps(
        nz, place, place[2], False, pieces, send_sem, recv_sem
    )
    begin()

    def loop(t, carry):
        step(t)
        return carry

    lax.fori_loop(1, nz + 2, loop, 0)
    end_send()
    end_arrive()
    halves.wait()


def gather(nz, collective_id, parts, tokens):
    shards, shapes, views = zip(*parts)
    n = len(parts)
    return pl.pallas_call(
        functools.partial(gather_kernel, nz, views),
        in_specs=[ANY] * (n + 1),
        out_specs=[ANY] * (n + 1),
        out_shape=[sds(shape, shard.dtype) for shard, shape in zip(shards, shapes)]
        + [sds((LOCAL, *tokens.shape[1:]), tokens.dtype)],
        scratch_shapes=[
            pltpu.SemaphoreType.DMA((11, nz, n)),
            pltpu.SemaphoreType.DMA((8, nz, n)),
            pltpu.SemaphoreType.DMA((n,)),
            pltpu.SemaphoreType.DMA((2,)),
        ],
        name="gather",
        compiler_params=params(collective_id=collective_id, has_side_effects=True),
    )(*shards, tokens)


def scatter_kernel(nz, views, *refs):
    n = len(views)
    terms, outs = refs[:n], refs[n : 2 * n]
    mine, from_core, from_second, from_first, from_below, from_above = (
        refs[2 * n + i * n : 3 * n + i * n] for i in range(6)
    )
    send_sem, recv_sem, own_sem = refs[8 * n :]
    place = z, x, c, y = my_place()
    first, second, both = partners(place, place[2])
    to_first = device(z, first[0], c, first[1])
    to_second = device(z, second[0], c, second[1])
    to_core = device(z, x, 1 - c, y)

    def copies(srcs, dsts, send, recv, zz, target):
        return [
            pltpu.make_async_remote_copy(
                src_ref=srcs[i],
                dst_ref=dsts[i],
                send_sem=send_sem.at[send, zz, i],
                recv_sem=recv_sem.at[recv, zz, i],
                device_id=target,
                device_id_type=pl.DeviceIdType.MESH,
            )
            for i in range(n)
        ]

    def slots(bufs, *index):
        return [b.at[index] for b in bufs]

    def pick(refs_, *index):
        return [b[index] for b in refs_]

    flips = [(fx, fy) for fx in range(2) for fy in range(2)]

    def at(fx, fy):
        return x + fx * (1 - 2 * x), y + fy * (1 - 2 * y)

    def core_copies(zz, f):
        fx, fy = flips[f]
        xx, yy = at(fx, fy)
        return copies(
            [view(t, zz, xx, 1 - c, yy) for t, view in zip(terms, views)],
            slots(from_core, zz, f),
            f,
            f,
            zz,
            to_core,
        )

    def own_copies(zz, f):
        fx, fy = flips[f]
        xx, yy = at(fx, fy)
        return [
            pltpu.make_async_copy(
                view(t, zz, xx, c, yy), mine[i].at[zz, f], own_sem.at[f, zz, i]
            )
            for i, (t, view) in enumerate(zip(terms, views))
        ]

    f_first, f_second = 2 - c, 1 + c

    def second_copies(zz, across):
        return copies(
            slots(from_core, zz, 3 if across else f_second),
            slots(from_second, zz, 1 if across else 0),
            4 + across,
            4 + across,
            zz,
            to_second,
        )

    def first_copies(zz):
        return copies(slots(from_second, zz, 1), slots(from_first, zz), 6, 6, zz, to_first)

    def up_copies(zz):
        return copies(slots(from_first, zz), slots(from_below, zz), 7, 7, zz, device(z + 1, x, c, y))

    def down_copies(zz):
        return copies(slots(from_first, zz), slots(from_above, zz), 8, 8, zz, device(z - 1, x, c, y))

    def run(group, what):
        for copy in group:
            getattr(copy, what)()

    def add(into, index, other, other_index):
        for i in range(n):
            a, b = into[i].at[index], other[i].at[other_index]
            a[...] = (a[...].astype(F32) + b[...].astype(F32)).astype(a.dtype)

    def by_distance(t, do):
        @pl.when((t >= 0) & (t < nz) & (z - t >= 0))
        def _():
            do(z - t)

        @pl.when((t > 0) & (t < nz) & (z + t < nz))
        def _():
            do(z + t)

    def start_own(zz):
        for f in range(4):
            run(own_copies(zz, f), "start")

    def start_core(zz):
        for f in (3, 1, 2, 0):
            run(core_copies(zz, f), "start")

    def stage0(zz):
        for f in (3, 1, 2, 0):
            run(core_copies(zz, f), "wait_recv")
            run(own_copies(zz, f), "wait")
            add(from_core, (zz, f), mine, (zz, f))
        run(second_copies(zz, 1), "start")
        run(second_copies(zz, 0), "start")

    def stage1(zz):
        run(second_copies(zz, 1), "wait_recv")
        add(from_second, (zz, 1), from_core, (zz, f_first))
        run(first_copies(zz), "start")

    def stage2(zz):
        run(second_copies(zz, 0), "wait_recv")
        add(from_second, (zz, 0), from_core, (zz, 0))
        run(first_copies(zz), "wait_recv")
        add(from_first, (zz,), from_second, (zz, 0))

        @pl.when(zz > z)
        def _():
            @pl.when(z > 0)
            def _():
                run(up_copies(zz), "wait_recv")
                add(from_first, (zz,), from_below, (zz,))

            run(up_copies(zz), "start")

        @pl.when(zz < z)
        def _():
            @pl.when(z < nz - 1)
            def _():
                run(down_copies(zz), "wait_recv")
                add(from_first, (zz,), from_above, (zz,))

            run(down_copies(zz), "start")

    entry_barrier(nz)

    def begin(k, carry):
        by_distance(nz - 1 - k, start_core)
        by_distance(nz - 1 - k, start_own)
        return carry

    lax.fori_loop(0, nz, begin, 0)

    def step(k, carry):
        t = nz - 1 - k
        by_distance(t, stage0)
        by_distance(t + 1, stage1)
        by_distance(t + 2, stage2)
        return carry

    lax.fori_loop(0, nz + 2, step, 0)

    @pl.when(z > 0)
    def _():
        run(up_copies(z), "wait_recv")
        add(from_first, (z,), from_below, (z,))

    @pl.when(z < nz - 1)
    def _():
        run(down_copies(z), "wait_recv")
        add(from_first, (z,), from_above, (z,))

    for i in range(n):
        outs[i][...] = from_first[i][z]

    def finish(zz, carry):
        for f in range(4):
            run(core_copies(zz, f), "wait_send")
        run(second_copies(zz, 1), "wait_send")
        run(second_copies(zz, 0), "wait_send")
        run(first_copies(zz), "wait_send")

        @pl.when(zz > z)
        def _():
            run(up_copies(zz), "wait_send")

        @pl.when(zz < z)
        def _():
            run(down_copies(zz), "wait_send")

        return carry

    lax.fori_loop(0, nz, finish, 0)


def scatter(nz, collective_id, parts):
    terms, shapes, views = zip(*parts)
    n = len(parts)
    dtypes = [t.dtype for t in terms]

    def bufs(*lead):
        return [pltpu.VMEM((*lead, *shape), d) for shape, d in zip(shapes, dtypes)]

    return pl.pallas_call(
        functools.partial(scatter_kernel, nz, views),
        in_specs=[ANY] * n,
        out_specs=[VMEM] * n,
        out_shape=[sds(shape, d) for shape, d in zip(shapes, dtypes)],
        scratch_shapes=[
            *bufs(nz, 4),
            *bufs(nz, 4),
            *bufs(nz, 2),
            *bufs(nz),
            *bufs(nz),
            *bufs(nz),
            pltpu.SemaphoreType.DMA((9, nz, n)),
            pltpu.SemaphoreType.DMA((9, nz, n)),
            pltpu.SemaphoreType.DMA((4, nz, n)),
        ],
        name="scatter",
        compiler_params=params(62, collective_id=collective_id, has_side_effects=True),
    )(*terms)


def whole_rows(side, mine, other):
    mine, other = mine.astype(F32), other.astype(F32)
    first = jnp.where(side == 0, mine, other)
    second = jnp.where(side == 0, other, mine)
    return jnp.concatenate([jnp.zeros((MEM, D), F32), first, second], axis=0)


def split_rows(side, rows):
    half = (SEG - MEM) // 2
    first, second = rows[MEM : MEM + half], rows[MEM + half :]
    keep = jnp.where(side == 0, first, second)
    send = jnp.where(side == 0, second, first)
    return keep, send


def project_kernel(mine_ref, other_ref, w_ref, table_ref, x_ref, q_ref, k_ref, v_ref):
    side = lax.axis_index("tensor")
    mine = mine_ref[LOCAL * side + pl.program_id(0)]
    x = whole_rows(side, mine, other_ref[0]).astype(BF16)
    x_ref[0] = x
    query = nn(x, w_ref[0]) + table_ref[QUERY_BIAS : QUERY_BIAS + 1, :]
    q_ref[0] = (query * SCALE).astype(BF16)
    k_ref[0] = nn(x, w_ref[1]).astype(BF16)
    v_ref[0] = (nn(x, w_ref[2]) + table_ref[VALUE_BIAS : VALUE_BIAS + 1, :]).astype(BF16)


def slot_rows(width=D):
    return pl.BlockSpec((1, SEG, width), lambda s: (s, 0, 0))


def half_rows(half):
    return pl.BlockSpec((1, half, D), lambda s: (s, 0, 0))


def project(tokens, other, attn, table):
    return pl.pallas_call(
        project_kernel,
        grid=(LOCAL,),
        in_specs=[
            once(tokens.shape, (0, 0, 0)),
            half_rows(tokens.shape[1]),
            once((3, D, D), (0, 0, 0)),
            once((NVEC, D), (0, 0)),
        ],
        out_specs=[slot_rows()] * 4,
        out_shape=[sds((LOCAL, SEG, D), BF16)] * 4,
        name="project",
        compiler_params=params(),
    )(tokens, other, attn, table)


def head_masks():
    feature_head = lax.broadcasted_iota(jnp.int32, (1, D), 1) // DH
    return [feature_head == h for h in range(HEADS)]


def by_head(rows16, masks):
    zero = jnp.zeros_like(rows16)
    return jnp.concatenate([jnp.where(m, rows16, zero) for m in masks], axis=0)


def own_columns(blocks, masks):
    total = jnp.zeros((THIN, D), blocks.dtype)
    for h, m in enumerate(masks):
        total = jnp.where(m, blocks[THIN * h : THIN * (h + 1)], total)
    return total


def copies_of(key_mask_shape):
    row = lax.rem(lax.broadcasted_iota(jnp.int32, key_mask_shape, 0), THIN)
    key = lax.broadcasted_iota(jnp.int32, key_mask_shape, 1)
    return jnp.where((key < MEM) & (key <= row), 2.0, 1.0)


def pair_barrier(place):
    z, x, c, y = place
    barrier = pltpu.get_barrier_semaphore()
    pl.semaphore_signal(
        barrier,
        inc=1,
        device_id=device(z, x, c, 1 - y),
        device_id_type=pl.DeviceIdType.MESH,
    )
    pl.semaphore_wait(barrier, 1)


def chain_kernel(
    place_ref,
    table_ref,
    attn_ref,
    ffn_ref,
    x_in,
    q_in,
    k_in,
    v_in,
    cot_ref,
    x_ref,
    q_ref,
    k_ref,
    v_ref,
    saved_d_ref,
    saved_f_ref,
    saved_s_ref,
    cot_other_ref,
    wa,
    wf,
    xb,
    qb,
    kb,
    vb,
    save_d,
    save_f,
    save_s,
    left,
    given,
    sem_w,
    sem_x,
    sem_kv,
    sem_out,
    sem_memory,
    sem_cot,
):
    del x_in, q_in, k_in, v_in
    place = z, x, c, y = my_place()
    loads = [
        pltpu.make_async_copy(attn_ref, wa, sem_w.at[0]),
        pltpu.make_async_copy(ffn_ref.at[0], wf.at[0], sem_w.at[1]),
        pltpu.make_async_copy(ffn_ref.at[1], wf.at[1], sem_w.at[2]),
    ]
    tiles = [
        pltpu.make_async_copy(x_ref.at[s, pl.ds(0, THIN)], xb.at[s], sem_x.at[s])
        for s in range(LOCAL)
    ]
    keys = [
        pltpu.make_async_copy(src.at[s], dst.at[s], sem_kv.at[2 * s + i])
        for s in range(LOCAL)
        for i, (src, dst) in enumerate(((k_ref, kb), (v_ref, vb)))
    ]
    for copy in tiles + loads[:1] + keys + loads[1:]:
        copy.start()
    pair_barrier(place)
    cot_swap = swap_halves(place, cot_ref, cot_other_ref, sem_cot)
    cot_swap.start()
    handed = remote(left, given, sem_memory.at[0], sem_memory.at[1], device(z, x, c, 1 - y))

    masks = head_masks()
    memory_row = lax.broadcasted_iota(jnp.int32, (THIN, 1), 0) < MEM
    first = table_ref[FIRST_MEMORY:NVEC, :]
    first = jnp.concatenate([first, jnp.zeros((THIN - MEM, D), F32)], axis=0)
    row = lambda r: table_ref[r : r + 1, :]

    def slots(turn, memory):
        for s in range(LOCAL):
            tiles[s].wait()
            if s == 0:
                loads[0].wait()
            keys[2 * s].wait()
            keys[2 * s + 1].wait()
            if memory is None:
                memory = first
            else:
                memory = jnp.where(place_ref[LOCAL * turn + s] == 0, first, memory)
            x16 = jnp.where(memory_row, memory, xb[s].astype(F32)).astype(BF16)
            xb[s] = x16
            qb[s] = ((nn(x16, wa[0]) + row(QUERY_BIAS)) * SCALE).astype(BF16)
            kb[s, 0:THIN] = nn(x16, wa[1]).astype(BF16)
            vb[s, 0:THIN] = (nn(x16, wa[2]) + row(VALUE_BIAS)).astype(BF16)
            outs = [
                pltpu.make_async_copy(
                    src.at[s, pl.ds(0, THIN)], dst.at[s, pl.ds(0, THIN)], sem_out.at[4 * s + i]
                )
                for i, (src, dst) in enumerate(
                    ((xb, x_ref), (qb, q_ref), (kb, k_ref), (vb, v_ref))
                )
            ]
            for copy in outs:
                copy.start()
            if turn == 1 and s == LOCAL - 1:
                save_d[s] = jnp.zeros_like(save_d[s])
                save_f[s] = jnp.zeros_like(save_f[s])
                save_s[s] = jnp.zeros_like(save_s[s])
            else:
                q_heads = by_head(qb[s], masks)
                score = nt(q_heads, kb[s])
                top = jnp.max(score, axis=-1, keepdims=True)
                weight = jnp.exp(score - top) * copies_of(score.shape)
                total = jnp.sum(weight, axis=-1, keepdims=True)
                share = (weight / total).astype(BF16)
                log_total = top + jnp.log(total)
                context = own_columns(nn(share, vb[s]), masks).astype(BF16)
                unit1, inverse1 = normalized(
                    x16.astype(F32) + nt(context, wa[3]) + row(OUT_BIAS)
                )
                hidden = (unit1 * row(GAIN1) + row(SHIFT1)).astype(BF16)
                if s == 0:
                    loads[1].wait()
                up = nt(hidden, wf[0])
                up_bias = jnp.concatenate([row(UP_BIAS + i) for i in range(FF // D)], axis=1)
                active16, slope = gelu_parts(up + up_bias)
                active16 = active16.astype(BF16)
                if s == 0:
                    loads[2].wait()
                second = hidden.astype(F32) + nn(active16, wf[1]) + row(DOWN_BIAS)
                unit2, inverse2 = normalized(second)
                output = (unit2 * row(GAIN2) + row(SHIFT2)).astype(BF16)
                memory = output.astype(F32)
                if turn == 0 and s == LOCAL - 1:
                    left[...] = output
                    handed.start()
                save_d[s, 0] = hidden
                save_d[s, 1] = unit1.astype(BF16)
                save_d[s, 2] = unit2.astype(BF16)
                save_d[s, 3] = context
                save_f[s, 0] = active16
                save_f[s, 1] = slope.astype(BF16)
                wide = lambda v: jnp.broadcast_to(v, (v.shape[0], 128))
                save_s[s, 0 : HEADS * THIN] = wide(log_total)
                save_s[s, HEADS * THIN : HEADS * THIN + THIN] = wide(inverse1)
                save_s[s, HEADS * THIN + THIN :] = wide(inverse2)
            for copy in outs:
                copy.wait()

    @pl.when(y == 0)
    def _():
        slots(0, None)
        handed.wait_send()

    @pl.when(y == 1)
    def _():
        handed.wait_recv()
        slots(1, given[...].astype(F32))

    saves = [
        pltpu.make_async_copy(save_d, saved_d_ref, sem_out.at[0]),
        pltpu.make_async_copy(save_f, saved_f_ref, sem_out.at[1]),
        pltpu.make_async_copy(save_s, saved_s_ref, sem_out.at[2]),
    ]
    for copy in saves:
        copy.start()
    for copy in saves:
        copy.wait()
    cot_swap.wait()


SAVED = (
    sds((LOCAL, 4, THIN, D), BF16),
    sds((LOCAL, 2, THIN, FF), BF16),
    sds((LOCAL, HEADS * THIN + 2 * THIN, 128), F32),
)


def chain(place, table, attn, ffn, x, q, k, v, cot):
    whole = sds((LOCAL, SEG, D), BF16)
    outs = pl.pallas_call(
        chain_kernel,
        in_specs=[SMEM, VMEM] + [ANY] * 7,
        out_specs=[ANY] * 8,
        out_shape=[whole] * 4 + list(SAVED) + [sds((LOCAL, *cot.shape[1:]), BF16)],
        input_output_aliases={4 + i: i for i in range(4)},
        scratch_shapes=[
            pltpu.VMEM((4, D, D), BF16),
            pltpu.VMEM((2, FF, D), BF16),
            pltpu.VMEM((LOCAL, THIN, D), BF16),
            pltpu.VMEM((LOCAL, THIN, D), BF16),
            pltpu.VMEM((LOCAL, SEG, D), BF16),
            pltpu.VMEM((LOCAL, SEG, D), BF16),
            *[pltpu.VMEM(s.shape, s.dtype) for s in SAVED],
            pltpu.VMEM((THIN, D), BF16),
            pltpu.VMEM((THIN, D), BF16),
            pltpu.SemaphoreType.DMA((3,)),
            pltpu.SemaphoreType.DMA((LOCAL,)),
            pltpu.SemaphoreType.DMA((2 * LOCAL,)),
            pltpu.SemaphoreType.DMA((4 * LOCAL,)),
            pltpu.SemaphoreType.DMA((2,)),
            pltpu.SemaphoreType.DMA((2,)),
        ],
        name="chain",
        compiler_params=params(collective_id=2, has_side_effects=True),
    )(place, table, attn, ffn, x, q, k, v, cot)
    return outs[:4], outs[4:7], outs[7]


def own_lanes(block, head):
    lane = lax.broadcasted_iota(jnp.int32, block.shape, 1)
    return jnp.where((lane < DH) == (head == 0), block, jnp.zeros_like(block))


def seen(score, first_query):
    key = lax.broadcasted_iota(jnp.int32, score.shape, 0)
    query = lax.broadcasted_iota(jnp.int32, score.shape, 1) + first_query
    return key <= query


def attend_pair(q, k, v):
    contexts_of, logs_of = [], [[], []]
    for part in range(SEG // TILE):
        rows = slice(TILE * part, TILE * (part + 1))
        keys = slice(0, TILE * (part + 1))
        contexts = []
        for head in range(2):
            score = nt(own_lanes(k[keys], head), q[rows])
            key = lax.broadcasted_iota(jnp.int32, score.shape, 0)
            allowed = seen(score, TILE * part) & (key >= MEM)
            score = jnp.where(allowed, score, MASK_VALUE)
            top = jnp.max(score, axis=0, keepdims=True)
            weight = jnp.exp(score - top)
            total = jnp.sum(weight, axis=0, keepdims=True)
            share = (weight * (1.0 / total)).astype(BF16)
            logs_of[head].append(top + jnp.log(total))
            contexts.append(tn(share, v[keys]))
        lane = lax.broadcasted_iota(jnp.int32, contexts[0].shape, 1)
        contexts_of.append(jnp.where(lane < DH, contexts[0], contexts[1]).astype(BF16))
    return jnp.concatenate(contexts_of, axis=0), [jnp.concatenate(l, axis=1) for l in logs_of]


def attend_kernel(q_ref, k_ref, v_ref, c_ref, log_ref):
    context, logs = attend_pair(q_ref[0], k_ref[0], v_ref[0])
    c_ref[0] = context
    for head in range(2):
        log_ref[0, 0, head : head + 1] = logs[head]


def with_memory(q, k16, v16, context, log_tokens):
    masks = head_masks()
    score = nt(by_head(k16, masks), q).reshape(HEADS, THIN, SEG)
    key = lax.broadcasted_iota(jnp.int32, score.shape, 1)
    score = jnp.where(key < MEM, score, MASK_VALUE)
    top = jnp.maximum(jnp.max(score, axis=1), log_tokens)
    weight = jnp.exp(score - top[:, None])
    old = jnp.exp(log_tokens - top)
    total = jnp.sum(weight, axis=1) + old
    share = (weight * (1.0 / total)[:, None]).reshape(HEADS * THIN, SEG).astype(BF16)
    kept = old / total
    coarse = kept.astype(BF16)
    fine = (kept - coarse.astype(F32)).astype(BF16)
    pad = jnp.zeros((4, SEG), BF16)
    head = lax.rem(lax.broadcasted_iota(jnp.int32, (2 * THIN, D), 0), THIN)
    spread = jnp.where(head == lax.broadcasted_iota(jnp.int32, (2 * THIN, D), 1) // DH, 1.0, 0.0)
    factor = tn(jnp.concatenate([coarse, pad, fine, pad], axis=0), spread.astype(BF16))
    context = factor * context.astype(F32) + tn(share, by_head(v16, masks))
    return context.astype(BF16), top + jnp.log(total)


PAIR = pl.BlockSpec((1, SEG, 2 * DH), lambda s, h: (s, 0, h))
PAIR_LOG = pl.BlockSpec((1, 1, 2, SEG), lambda s, h: (s, h, 0, 0))


def attend(q, k, v):
    return pl.pallas_call(
        attend_kernel,
        grid=(LOCAL, HEADS // 2),
        in_specs=[PAIR] * 3,
        out_specs=[PAIR, PAIR_LOG],
        out_shape=[sds((LOCAL, SEG, D), BF16), sds((LOCAL, HEADS // 2, 2, SEG), F32)],
        name="attend",
        compiler_params=params(),
    )(q, k, v)


def attend_back_pair(q, k, v, dc, logs):
    last = SEG // TILE
    key_terms, value_terms, query_terms = [], [], []
    for head in range(2):
        key_sum, value_sum, query_parts = [], [], []
        for part in range(last):
            rows = slice(TILE * part, TILE * (part + 1))
            keys = slice(0, TILE * (part + 1))
            score = nt(own_lanes(k[keys], head), q[rows])
            share = jnp.exp(score - logs[head : head + 1, rows])
            diagonal = jnp.where(seen(share[rows], 0), share[rows], 0.0)
            share = jnp.concatenate([share[: TILE * part], diagonal], axis=0) if part else diagonal
            share_grad = nt(own_lanes(v[keys], head), dc[rows])
            inner = jnp.sum(share_grad * share, axis=0, keepdims=True)
            score_grad = (share * (share_grad - inner)).astype(BF16)
            value_sum.append(nn(share.astype(BF16), dc[rows]))
            key_sum.append(nn(score_grad, q[rows]))
            query_parts.append(tn(score_grad, k[keys]))
        key_terms.append(key_sum)
        value_terms.append(value_sum)
        query_terms.append(query_parts)
    lane = lax.broadcasted_iota(jnp.int32, (TILE, 2 * DH), 1)
    pick = lambda a, b: jnp.where(lane < DH, a, b)
    dq, dk, dv = [], [], []
    for part in range(last):
        rows = slice(TILE * part, TILE * (part + 1))
        dq.append((pick(query_terms[0][part], query_terms[1][part]) * SCALE).astype(BF16))
        for terms, out in ((key_terms, dk), (value_terms, dv)):
            total = None
            for later in range(part, last):
                term = pick(terms[0][later][rows], terms[1][later][rows])
                total = term if total is None else total + term
            out.append(total)
    return [jnp.concatenate(parts, axis=0) for parts in (dq, dk, dv)]


def rows_kernel(
    place_ref,
    x_ref,
    q_ref,
    k16_ref,
    v16_ref,
    tokens_c_ref,
    tokens_log_ref,
    mine_ref,
    other_ref,
    wo_ref,
    wf_ref,
    table_ref,
    keep_ref,
    send_ref,
    h_ref,
    g_ref,
    du_ref,
    df_ref,
    da_ref,
    dc_ref,
    c_ref,
    log_ref,
    sums_ref,
    slope_ref,
):
    row = lambda r: table_ref[r : r + 1, :]
    slot = pl.program_id(0)
    side = lax.axis_index("tensor")
    live = place_ref[LOCAL * side + slot] >= 0

    @pl.when(slot == 0)
    def _():
        sums_ref[...] = jnp.zeros_like(sums_ref)

    def add(r, value):
        sums_ref[r : r + 1, :] += value

    log_tokens = jnp.concatenate([tokens_log_ref[0, h] for h in range(HEADS // 2)], axis=0)
    context, log_total = with_memory(
        q_ref[0], k16_ref[0], v16_ref[0], tokens_c_ref[0], log_tokens
    )
    c_ref[0] = context
    for h in range(HEADS // 2):
        log_ref[0, h] = log_total[2 * h : 2 * h + 2]
    unit1, inverse1 = normalized(x_ref[0].astype(F32) + nt(context, wo_ref[0]) + row(OUT_BIAS))
    hidden = (unit1 * row(GAIN1) + row(SHIFT1)).astype(BF16)
    h_ref[0] = hidden
    second = hidden.astype(F32) + row(DOWN_BIAS)
    for i in range(FF // D):
        cols = slice(D * i, D * (i + 1))
        up = nt(hidden, wf_ref[0, cols]) + row(UP_BIAS + i)
        active, slope = gelu_parts(up)
        active = active.astype(BF16)
        g_ref[0, :, cols] = active
        slope_ref[:, cols] = slope.astype(BF16)
        second = second + nn(active, wf_ref[1, cols])
    unit2, inverse2 = normalized(second)
    output = jnp.where(live, unit2 * row(GAIN2) + row(SHIFT2), 0.0)
    keep, send = split_rows(side, output)
    keep_ref[0] = keep.astype(BF16)
    send_ref[0] = send.astype(BF16)

    grad = whole_rows(side, mine_ref[LOCAL * side + slot], other_ref[0])
    grad = jnp.where(live, grad, 0.0)
    add(GAIN2, row_sum(grad * unit2))
    add(SHIFT2, row_sum(grad))
    second_grad = normalized_back(grad * row(GAIN2), unit2, inverse2)
    down_grad = second_grad.astype(BF16)
    df_ref[0] = down_grad
    add(DOWN_BIAS, row_sum(down_grad.astype(F32)))
    hidden_grad = second_grad
    for i in range(FF // D):
        cols = slice(D * i, D * (i + 1))
        up_grad = (nt(down_grad, wf_ref[1, cols]) * slope_ref[:, cols].astype(F32)).astype(BF16)
        du_ref[0, :, cols] = up_grad
        add(UP_BIAS + i, row_sum(up_grad.astype(F32)))
        hidden_grad = hidden_grad + nn(up_grad, wf_ref[0, cols])
    add(GAIN1, row_sum(hidden_grad * unit1))
    add(SHIFT1, row_sum(hidden_grad))
    branch_grad = normalized_back(hidden_grad * row(GAIN1), unit1, inverse1).astype(BF16)
    da_ref[0] = branch_grad
    add(OUT_BIAS, row_sum(branch_grad.astype(F32)))
    dc_ref[0] = nn(branch_grad, wo_ref[0]).astype(BF16)


def rows_part(place, x, q, k, v, c, log_tokens, cot, other, attn, ffn, table):
    half = cot.shape[1]
    whole, whole_wide = sds((LOCAL, SEG, D), BF16), sds((LOCAL, SEG, FF), BF16)
    part, logs = sds((LOCAL, half, D), BF16), sds((LOCAL, HEADS // 2, 2, SEG), F32)
    rows, wide = slot_rows(), slot_rows(FF)
    thin = pl.BlockSpec((1, THIN, D), lambda s: (s, 0, 0))
    log_rows = pl.BlockSpec((1, HEADS // 2, 2, SEG), lambda s: (s, 0, 0, 0))
    return pl.pallas_call(
        rows_kernel,
        grid=(LOCAL,),
        in_specs=[SMEM, rows, rows, thin, thin, rows, log_rows]
        + [once(cot.shape, (0, 0, 0)), half_rows(half)]
        + [once((1, D, D), (3, 0, 0)), once((2, FF, D), (0, 0, 0)), once((NVEC, D), (0, 0))],
        out_specs=[half_rows(half)] * 2
        + [rows, wide, wide, rows, rows, rows, rows, log_rows, once((THIN, D), (0, 0))],
        out_shape=[part] * 2
        + [whole, whole_wide, whole_wide, whole, whole, whole, whole, logs, sds((THIN, D), F32)],
        scratch_shapes=[pltpu.VMEM((SEG, FF), BF16)],
        name="rows_part",
        compiler_params=params(),
    )(place, x, q, k, v, c, log_tokens, cot, other, attn, ffn, table)


CHUNK = 768


def memory_key_gradient(q, k16, v16, dc, context, logs, masks):
    score = nt(by_head(k16, masks), q).reshape(HEADS, THIN, SEG)
    key = lax.broadcasted_iota(jnp.int32, score.shape, 1)
    share = jnp.where(key < MEM, jnp.exp(score - logs[:, None]), 0.0)
    share_grad = nt(by_head(v16, masks), dc).reshape(HEADS, THIN, SEG)
    product = dc.astype(F32) * context.astype(F32)
    coarse = product.astype(BF16)
    fine = (product - coarse.astype(F32)).astype(BF16)
    head = lax.broadcasted_iota(jnp.int32, (THIN, D), 0)
    ones = jnp.where(head == lax.broadcasted_iota(jnp.int32, (THIN, D), 1) // DH, 1.0, 0.0)
    ones = ones.astype(BF16)
    inner = (nt(ones, coarse) + nt(ones, fine))[0:HEADS]
    score_grad = (share * (share_grad - inner[:, None])).reshape(HEADS * THIN, SEG)
    share = share.reshape(HEADS * THIN, SEG).astype(BF16)
    dk = own_columns(nn(score_grad.astype(BF16), q), masks)
    return dk, own_columns(nn(share, dc), masks)


def chain_back_kernel(
    place_ref,
    table_ref,
    attn_ref,
    ffn_ref,
    q_ref,
    k_ref,
    v_ref,
    saved_d_ref,
    saved_f_ref,
    saved_s_ref,
    g_ref,
    du_ref,
    df_ref,
    h_ref,
    keep_ref,
    send_ref,
    dc_ref,
    log_ref,
    da_in,
    c_in,
    da_ref,
    c_ref,
    dq_ref,
    dk_ref,
    dv_ref,
    sums_ref,
    terms_ref,
    rows_ref,
    wa,
    wf,
    qb,
    kb,
    vb,
    dcb,
    cb,
    logs,
    dqb,
    dkb,
    dvb,
    tiles,
    df,
    hid,
    gb,
    dub,
    staged,
    save_d,
    save_f,
    save_s,
    thin_d,
    thin_f,
    sums,
    left,
    given,
    sem_w,
    sem_in,
    sem_ff,
    sem_chunk,
    sem_out,
    sem_stage,
    sem_grad,
    sem_swap,
):
    del da_in, c_in
    place = z, x, c, y = my_place()
    loads = [
        pltpu.make_async_copy(attn_ref, wa, sem_w.at[0]),
        pltpu.make_async_copy(ffn_ref.at[0], wf.at[0], sem_w.at[1]),
        pltpu.make_async_copy(ffn_ref.at[1], wf.at[1], sem_w.at[2]),
    ]
    first_rows = lambda ref: ref.at[:, pl.ds(0, THIN)]
    saved = [
        pltpu.make_async_copy(saved_d_ref, save_d, sem_in.at[2]),
        pltpu.make_async_copy(saved_f_ref, save_f, sem_in.at[3]),
        pltpu.make_async_copy(saved_s_ref, save_s, sem_in.at[4]),
    ]
    reads = [
        pltpu.make_async_copy(src, dst, sem_in.at[5 + i])
        for i, (src, dst) in enumerate(
            ((q_ref, qb), (k_ref, kb), (v_ref, vb), (dc_ref, dcb), (c_ref, cb), (log_ref, logs))
        )
    ]
    merged = (da_ref, c_ref)
    tile_reads = [
        pltpu.make_async_copy(first_rows(ref), tiles.at[i], sem_in.at[i])
        for i, ref in enumerate(merged)
    ]
    rows_in = [
        pltpu.make_async_copy(df_ref, df, sem_ff.at[0]),
        pltpu.make_async_copy(h_ref, hid, sem_ff.at[1]),
    ]

    def chunk_reads(i):
        lanes = pl.ds(pl.multiple_of(CHUNK * i, CHUNK), CHUNK)
        slot = lax.rem(i, 2)
        return [
            pltpu.make_async_copy(src.at[:, :, lanes], dst.at[slot], sem_chunk.at[slot, j])
            for j, (src, dst) in enumerate(((g_ref, gb), (du_ref, dub)))
        ]

    @pl.when(y == 1)
    def _():
        for copy in reads + loads[:1] + saved + loads[:0:-1] + tile_reads:
            copy.start()
        for copy in rows_in + chunk_reads(0) + chunk_reads(1):
            copy.start()

    @pl.when(y == 0)
    def _():
        for copy in reads + saved + loads[:0:-1] + loads[:1] + tile_reads:
            copy.start()
        for copy in rows_in + chunk_reads(0) + chunk_reads(1):
            copy.start()

    pair_barrier(place)
    swap = place_rows(place, keep_ref, send_ref, rows_ref, sem_swap)
    for copy in swap:
        copy.start()
    handed = remote(left, given, sem_grad.at[0], sem_grad.at[1], device(z, x, c, 1 - y))

    sums[...] = jnp.zeros_like(sums)
    thin_d[...] = jnp.zeros_like(thin_d)
    thin_f[...] = jnp.zeros_like(thin_f)
    for buf in (dqb, dkb, dvb):
        buf[...] = jnp.zeros_like(buf)
    masks = head_masks()
    memory_row = lax.broadcasted_iota(jnp.int32, (THIN, 1), 0) < MEM
    row = lambda r: table_ref[r : r + 1, :]

    def add(r, value):
        sums[r : r + 1, :] += value

    def attend_at(i, carry):
        s, h = i // (HEADS // 2), lax.rem(i, HEADS // 2)
        lanes = pl.ds(pl.multiple_of(h * 2 * DH, 2 * DH), 2 * DH)
        pair = (buf[s, :, lanes] for buf in (qb, kb, vb, dcb))
        dq, dk, dv = attend_back_pair(*pair, logs[s, h])
        dqb[s, THIN:, lanes] = dq[THIN:]
        dqb[s, 0:THIN, lanes] = jnp.where(memory_row, dqb[s, 0:THIN, lanes], dq[0:THIN])
        dkb[s, :, lanes] = (dk + dkb[s, :, lanes].astype(F32)).astype(BF16)
        dvb[s, :, lanes] = (dv + dvb[s, :, lanes].astype(F32)).astype(BF16)
        return carry

    pairs = LOCAL * HEADS // 2

    def key_gradient(s):
        rows = jnp.concatenate([logs[s, h] for h in range(HEADS // 2)], axis=0)
        return memory_key_gradient(
            qb[s], kb[s, 0:THIN], vb[s, 0:THIN], dcb[s], cb[s], rows, masks
        )

    def slots(turn, grad):
        waited = set()

        def need(*copies):
            for copy in copies:
                if id(copy) not in waited:
                    waited.add(id(copy))
                    copy.wait()

        for s in reversed(range(LOCAL)):
            if turn == 1 and s == LOCAL - 1:
                grad = jnp.zeros((THIN, D), F32)
            else:
                after = place_ref[LOCAL * turn + s + 1]
                grad = jnp.where(memory_row, jnp.where(after > 0, grad, 0.0), 0.0)
                need(*saved)
                unit1, unit2 = save_d[s, 1].astype(F32), save_d[s, 2].astype(F32)
                base = HEADS * THIN
                log_total = save_s[s, 0:base, 0:1]
                inverse1 = save_s[s, base : base + THIN, 0:1]
                inverse2 = save_s[s, base + THIN :, 0:1]
                add(GAIN2, row_sum(grad * unit2))
                add(SHIFT2, row_sum(grad))
                second_grad = normalized_back(grad * row(GAIN2), unit2, inverse2)
                down_grad = second_grad.astype(BF16)
                add(DOWN_BIAS, row_sum(down_grad.astype(F32)))
                need(loads[2])
                up_grad = (nt(down_grad, wf[1]) * save_f[s, 1].astype(F32)).astype(BF16)
                up_sum = row_sum(up_grad.astype(F32))
                for i in range(FF // D):
                    add(UP_BIAS + i, up_sum[:, D * i : D * (i + 1)])
                need(loads[1])
                hidden_grad = second_grad + nn(up_grad, wf[0])
                add(GAIN1, row_sum(hidden_grad * unit1))
                add(SHIFT1, row_sum(hidden_grad))
                pre_grad = normalized_back(hidden_grad * row(GAIN1), unit1, inverse1)
                branch_grad = pre_grad.astype(BF16)
                add(OUT_BIAS, row_sum(branch_grad.astype(F32)))
                need(loads[0])
                context_grad = nn(branch_grad, wa[3]).astype(BF16)
                dc_heads = by_head(context_grad, masks)
                q_heads = by_head(qb[s, 0:THIN], masks)
                score = nt(q_heads, kb[s])
                share = jnp.exp(score - log_total) * copies_of(score.shape)
                share_grad = nt(dc_heads, vb[s])
                inner = jnp.sum(share_grad * share, axis=-1, keepdims=True)
                score_grad = (share * (share_grad - inner)).astype(BF16)
                query_grad = (own_columns(nn(score_grad, kb[s]), masks) * SCALE).astype(BF16)
                dkb[s] = (dkb[s].astype(F32) + tn(score_grad, q_heads)).astype(BF16)
                dvb[s] = (dvb[s].astype(F32) + tn(share.astype(BF16), dc_heads)).astype(BF16)
                dqb[s, 0:THIN] = jnp.where(memory_row, query_grad, dqb[s, 0:THIN])
                thin_d[s, 0] = down_grad
                thin_d[s, 1] = save_d[s, 0]
                thin_f[s, 0] = up_grad
                thin_f[s, 1] = save_f[s, 0]
                need(*tile_reads)
                for i, value in enumerate((branch_grad, save_d[s, 3])):
                    tiles[i, s] = jnp.where(memory_row, value, tiles[i, s])
                grad = pre_grad + nt(query_grad, wa[0])
            need(loads[0])
            dk, dv = dkb[s, 0:THIN], dvb[s, 0:THIN]
            if turn == 1:
                early_k, early_v = key_gradient(s)
                dk = (dk.astype(F32) + early_k).astype(BF16)
                dv = (dv.astype(F32) + early_v).astype(BF16)
            grad = grad + nt(dk, wa[1]) + nt(dv, wa[2])
            first = jnp.where(place_ref[LOCAL * turn + s] == 0, grad, 0.0)
            sums[FIRST_MEMORY : FIRST_MEMORY + THIN, :] += first
        return grad

    @pl.when(y == 1)
    def _():
        for copy in reads:
            copy.wait()
        left[...] = slots(1, None)
        handed.start()
        lax.fori_loop(0, pairs, attend_at, 0)

    @pl.when(y == 0)
    def _():
        for copy in reads:
            copy.wait()
        lax.fori_loop(0, pairs, attend_at, 0)
        handed.wait_recv()
        slots(0, given[...])

    writes = [
        pltpu.make_async_copy(dqb, dq_ref, sem_out.at[0]),
        pltpu.make_async_copy(dkb, dk_ref, sem_out.at[1]),
        pltpu.make_async_copy(dvb, dv_ref, sem_out.at[2]),
        pltpu.make_async_copy(sums, sums_ref, sem_out.at[3]),
        *[
            pltpu.make_async_copy(tiles.at[i], first_rows(ref), sem_out.at[5 + i])
            for i, ref in enumerate(merged)
        ],
    ]
    for copy in writes:
        copy.start()

    for copy in rows_in:
        copy.wait()
    for s in range(LOCAL):
        df[s, 0:THIN] = jnp.where(memory_row, thin_d[s, 0], df[s, 0:THIN])
        hid[s, 0:THIN] = jnp.where(memory_row, thin_d[s, 1], hid[s, 0:THIN])
    chunks = FF // CHUNK

    def store(i):
        lanes = pl.ds(pl.multiple_of(CHUNK * i, CHUNK), CHUNK)
        slot = lax.rem(i, 2)
        return pltpu.make_async_copy(
            staged.at[slot], terms_ref.at[:, lanes], sem_stage.at[slot]
        )

    def chunk(i, carry):
        slot = lax.rem(i, 2)
        for copy in chunk_reads(i):
            copy.wait()
        lanes = pl.ds(pl.multiple_of(CHUNK * i, CHUNK), CHUNK)
        for s in range(LOCAL):
            for j, buf in ((1, gb), (0, dub)):
                old = buf[slot, s, 0:THIN]
                buf[slot, s, 0:THIN] = jnp.where(memory_row, thin_f[s, j, :, lanes], old)

        @pl.when(i >= 2)
        def _():
            store(i - 2).wait()

        for j, (buf, rows) in enumerate(((dub, hid), (gb, df))):
            terms = tn(
                buf[slot].reshape(LOCAL * SEG, CHUNK), rows[...].reshape(LOCAL * SEG, D)
            )
            staged[slot, j] = terms.astype(BF16)
        store(i).start()

        @pl.when(i + 2 < chunks)
        def _():
            for copy in chunk_reads(i + 2):
                copy.start()

        return carry

    lax.fori_loop(0, chunks, chunk, 0)

    @pl.when(y == 1)
    def _():
        handed.wait_send()

    for copy in [*writes, store(chunks - 2), store(chunks - 1)]:
        copy.wait()
    for copy in swap:
        copy.wait()


THIN_SHAPES = (
    sds((LOCAL, 2, THIN, D), BF16),
    sds((LOCAL, 2, THIN, FF), BF16),
    sds((FIRST_MEMORY + THIN, D), F32),
)


def chain_back(place, table, attn, ffn, q, k, v, saved, g, du, df, h, halves, dc, logs, da, c):
    whole = sds((LOCAL, SEG, D), BF16)
    rows = pltpu.VMEM(whole.shape, BF16)
    dma = lambda *shape: pltpu.SemaphoreType.DMA(shape)
    outs = pl.pallas_call(
        chain_back_kernel,
        in_specs=[SMEM, VMEM] + [ANY] * 18,
        out_specs=[ANY] * 8,
        out_shape=[whole] * 5
        + [THIN_SHAPES[2]]
        + [sds((2, FF, D), BF16), sds((2 * LOCAL, *halves[0].shape[1:]), BF16)],
        input_output_aliases={18: 0, 19: 1},
        scratch_shapes=[
            pltpu.VMEM((4, D, D), BF16),
            pltpu.VMEM((2, FF, D), BF16),
            *[rows] * 5,
            pltpu.VMEM(logs.shape, F32),
            rows,
            rows,
            rows,
            pltpu.VMEM((2, LOCAL, THIN, D), BF16),
            rows,
            rows,
            pltpu.VMEM((2, LOCAL, SEG, CHUNK), BF16),
            pltpu.VMEM((2, LOCAL, SEG, CHUNK), BF16),
            pltpu.VMEM((2, 2, CHUNK, D), BF16),
            *[pltpu.VMEM(s.shape, s.dtype) for s in SAVED + THIN_SHAPES],
            pltpu.VMEM((THIN, D), F32),
            pltpu.VMEM((THIN, D), F32),
            dma(3),
            dma(11),
            dma(2),
            dma(2, 2),
            dma(8),
            dma(2),
            dma(2),
            dma(3),
        ],
        name="chain_back",
        compiler_params=params(collective_id=3, has_side_effects=True),
    )(place, table, attn, ffn, q, k, v, *saved, g, du, df, h, *halves, dc, logs, da, c)
    return outs


def table_row(ref, index, entries):
    blocks = []
    lane = lax.broadcasted_iota(jnp.int32, (1, 128), 1)
    for block in range(D // 128):
        at, end = index * D + 128 * block, index * D + 128 * (block + 1)
        target, value = 0, jnp.zeros((1, 128), F32)
        while at < end:
            shard, inner = at // entries, at % entries
            count = min(end - at, entries - inner, 128 - inner % 128)
            place = (shard // 8, shard // 4 % 2, shard // 2 % 2, shard % 2)
            source = ref[place][inner // 128 : inner // 128 + 1]
            shift = (target - inner) % 128
            if shift:
                source = pltpu.roll(source, shift, 1)
            value = jnp.where((lane >= target) & (lane < target + count), source, value)
            at, target = at + count, target + count
        blocks.append(value)
    return jnp.concatenate(blocks, axis=1)


def head_kernel(
    nz,
    entries,
    attn_src,
    ffn_src,
    vec_src,
    tokens,
    attn_ref,
    ffn_ref,
    table_ref,
    x_ref,
    q_ref,
    k_ref,
    v_ref,
    c_ref,
    log_ref,
    wa,
    vec,
    table,
    mine,
    other,
    xb,
    qb,
    kb,
    vb,
    cb,
    logs,
    send_sem,
    recv_sem,
    own_sem,
    swap_sem,
    out_sem,
):
    place = my_place()
    side = place[3]
    halves = swap_halves(place, tokens, other, swap_sem)
    own = [
        pltpu.make_async_copy(attn_src, attn_view(wa, *place), own_sem.at[0]),
        pltpu.make_async_copy(vec_src, vec_view(vec, *place), own_sem.at[1]),
        pltpu.make_async_copy(ffn_src, ffn_view(ffn_ref, *place), own_sem.at[2]),
        pltpu.make_async_copy(tokens.at[pl.ds(LOCAL * side, LOCAL)], mine, own_sem.at[3]),
    ]
    for copy in own:
        copy.start()
    entry_barrier(nz)
    steps = functools.partial(gather_steps, nz, place, send_sem=send_sem, recv_sem=recv_sem)
    begin, step, end_arrive, end_send = steps(
        1, True, [(0, wa, attn_view), (1, vec, vec_view)]
    )
    late = [
        steps(place[2], bool(i), [(2 + i, ffn_ref.at[i], hidden_view)]) for i in range(2)
    ]
    own[0].wait()
    own[1].wait()
    begin()
    step(1)
    halves.start()

    def loop(t, carry):
        step(t)
        return carry

    lax.fori_loop(2, nz + 2, loop, 0)
    own[2].wait()
    for begin2, _, _, _ in late:
        begin2()
    own[3].wait()
    halves.wait()
    end_arrive()
    for index in range(NVEC):
        table[index : index + 1] = table_row(vec, index, entries)
    outs = [
        pltpu.make_async_copy(wa, attn_ref, out_sem.at[0]),
        pltpu.make_async_copy(table, table_ref, out_sem.at[1]),
    ]
    for copy in outs:
        copy.start()

    weight = lambda i: wa[i].reshape(D, D)

    def project_slot(s):
        x = whole_rows(side, mine[s], other[s]).astype(BF16)
        xb[s] = x
        qb[s] = ((nn(x, weight(0)) + table[QUERY_BIAS : QUERY_BIAS + 1]) * SCALE).astype(BF16)
        kb[s] = nn(x, weight(1)).astype(BF16)
        vb[s] = (nn(x, weight(2)) + table[VALUE_BIAS : VALUE_BIAS + 1]).astype(BF16)
        for i, (buf, out) in enumerate(((xb, x_ref), (qb, q_ref), (kb, k_ref), (vb, v_ref))):
            outs.append(pltpu.make_async_copy(buf.at[s], out.at[s], out_sem.at[2 + 4 * s + i]))
            outs[-1].start()

    def attend_at(i, carry):
        s, h = i // (HEADS // 2), i % (HEADS // 2)
        lanes = pl.ds(pl.multiple_of(h * 2 * DH, 2 * DH), 2 * DH)
        context, log_rows = attend_pair(qb[s, :, lanes], kb[s, :, lanes], vb[s, :, lanes])
        cb[s, :, lanes] = context
        for head in range(2):
            logs[s, h, head : head + 1] = log_rows[head]
        return carry

    project_slot(0)
    project_slot(1)
    pairs = LOCAL * HEADS // 2
    done = 0
    for t in range(1, nz + 2):
        for _, step2, _, _ in late:
            step2(t)
        upto = pairs * t // (nz + 1)
        lax.fori_loop(done, upto, attend_at, 0)
        done = upto
    outs.append(pltpu.make_async_copy(cb, c_ref, out_sem.at[2 + 4 * LOCAL]))
    outs.append(pltpu.make_async_copy(logs, log_ref, out_sem.at[3 + 4 * LOCAL]))
    outs[-1].start()
    outs[-2].start()
    end_send()
    for _, _, end_arrive2, end_send2 in late:
        end_send2()
        end_arrive2()
    for copy in outs:
        copy.wait()


def head(nz, attention, hidden_major, vec, tokens, entries):
    rows, hidden = attention.shape[1], hidden_major.shape[1]
    whole = sds((LOCAL, SEG, D), BF16)
    logs = (LOCAL, HEADS // 2, 2, SEG)
    attn_shape, vec_shape = (4, nz, 2, 2, rows, D), (nz, 2, 2, 2, *VEC_TILE)
    half = pltpu.VMEM((LOCAL, *tokens.shape[1:]), BF16)
    return pl.pallas_call(
        functools.partial(head_kernel, nz, entries),
        in_specs=[ANY] * 4,
        out_specs=[ANY] * 9,
        out_shape=[
            sds(attn_shape, BF16),
            sds((2, nz, 2, 2, 2, hidden, D), BF16),
            sds((NVEC, D), F32),
            *[whole] * 5,
            sds(logs, F32),
        ],
        scratch_shapes=[
            pltpu.VMEM(attn_shape, BF16),
            pltpu.VMEM(vec_shape, F32),
            pltpu.VMEM((NVEC, D), F32),
            half,
            half,
            *[pltpu.VMEM(whole.shape, BF16)] * 5,
            pltpu.VMEM(logs, F32),
            pltpu.SemaphoreType.DMA((11, nz, 4)),
            pltpu.SemaphoreType.DMA((8, nz, 4)),
            pltpu.SemaphoreType.DMA((4,)),
            pltpu.SemaphoreType.DMA((2,)),
            pltpu.SemaphoreType.DMA((4 + 4 * LOCAL,)),
        ],
        name="head",
        compiler_params=params(collective_id=0, has_side_effects=True),
    )(attention, hidden_major, vec, tokens)


def token_grad_kernel(place_ref, da_ref, dq_ref, dk_ref, dv_ref, w_ref, keep_ref, send_ref):
    side = lax.axis_index("tensor")
    total = da_ref[0].astype(F32)
    for i, ref in enumerate((dq_ref, dk_ref, dv_ref)):
        total = total + nt(ref[0], w_ref[i])
    live = place_ref[LOCAL * side + pl.program_id(0)] >= 0
    keep, send = split_rows(side, jnp.where(live, total, 0.0))
    keep_ref[0] = keep.astype(BF16)
    send_ref[0] = send.astype(BF16)


def token_gradient(place, da, dq, dk, dv, attn):
    half = (SEG - MEM) // 2
    return pl.pallas_call(
        token_grad_kernel,
        grid=(LOCAL,),
        in_specs=[SMEM] + [slot_rows()] * 4 + [once((3, D, D), (0, 0, 0))],
        out_specs=[half_rows(half)] * 2,
        out_shape=[sds((LOCAL, half, D), BF16)] * 2,
        name="token_gradient",
        compiler_params=params(),
    )(place, da, dq, dk, dv, attn)


def flat(ref):
    return ref[...].reshape(LOCAL * ref.shape[1], ref.shape[2])


def attn_grad_kernel(
    x_ref, da_ref, dq_ref, dk_ref, dv_ref, c_ref, sums_ref, thin_sums_ref, out_ref, vec_ref
):
    x = flat(x_ref)
    dq, dv = flat(dq_ref), flat(dv_ref)
    out_ref[0] = tn(x, dq).astype(BF16)
    out_ref[1] = tn(x, flat(dk_ref)).astype(BF16)
    out_ref[2] = tn(x, dv).astype(BF16)
    out_ref[3] = tn(flat(da_ref), flat(c_ref)).astype(BF16)
    vec_ref[...] = thin_sums_ref[...]
    vec_ref[0:FIRST_MEMORY] = thin_sums_ref[0:FIRST_MEMORY] + sums_ref[0:FIRST_MEMORY]
    vec_ref[QUERY_BIAS : QUERY_BIAS + 1] = row_sum(dq.astype(F32))
    vec_ref[VALUE_BIAS : VALUE_BIAS + 1] = row_sum(dv.astype(F32))


def attn_gradient(x, da, dq, dk, dv, c, sums, thin_sums, chunk=256):
    part = pl.BlockSpec((LOCAL, SEG, chunk), lambda i: (0, 0, i))
    full = once((LOCAL, SEG, D), (0, 0, 0))
    lanes = lambda rows: pl.BlockSpec((rows, chunk), lambda i: (0, i))
    return pl.pallas_call(
        attn_grad_kernel,
        grid=(D // chunk,),
        in_specs=[full, full, part, part, part, part, lanes(THIN), lanes(FIRST_MEMORY + THIN)],
        out_specs=[
            pl.BlockSpec((4, D, chunk), lambda i: (0, 0, i)),
            lanes(FIRST_MEMORY + THIN),
        ],
        out_shape=[sds((4, D, D), BF16), sds((FIRST_MEMORY + THIN, D), F32)],
        name="attn_gradient",
        compiler_params=params(),
    )(x, da, dq, dk, dv, c, sums, thin_sums)


def scatter_steps(nz, place, lead, z_second, pieces, send_sem, recv_sem):
    z, x, c, y = place
    first, second, both = partners(place, lead)
    to_first = device(z, first[0], c, first[1])
    to_second = device(z, second[0], c, second[1])
    to_core = device(z, x, 1 - c, y)
    f_first, f_second = 2 - lead, 1 + lead

    def at(f):
        fx, fy = f // 2, f % 2
        return x + fx * (1 - 2 * x), y + fy * (1 - 2 * y)

    def term(piece, zz, core, f):
        xx, yy = at(f)
        return piece[2](piece[1], zz, xx, core, yy)

    def copies(kind, zz, target, src, dst):
        return [
            remote(src(p), dst(p), send_sem.at[kind, zz, p[0]], recv_sem.at[kind, zz, p[0]], target)
            for p in pieces
        ]

    def core_copies(zz, f):
        return copies(
            f, zz, to_core, lambda p: term(p, zz, 1 - c, f), lambda p: p[3].at[zz, f]
        )

    def second_copies(zz, across):
        f = 3 if across else f_second
        return copies(
            4 + across, zz, to_second, lambda p: p[3].at[zz, f], lambda p: p[4].at[zz, across]
        )

    def first_copies(zz):
        slot = 0 if z_second else zz
        return copies(6, zz, to_first, lambda p: p[4].at[zz, 1], lambda p: p[5].at[slot])

    def partial(p, zz, f):
        return p[4].at[zz, f] if z_second else p[5].at[zz]

    def beside(p, above, zz, f):
        return p[6 + above].at[zz, f] if z_second else p[6 + above].at[zz]

    def up_copies(zz, f):
        return copies(
            7 + 2 * f,
            zz,
            device(z + 1, x, c, y),
            lambda p: partial(p, zz, f),
            lambda p: beside(p, 0, zz, f),
        )

    def down_copies(zz, f):
        return copies(
            8 + 2 * f,
            zz,
            device(z - 1, x, c, y),
            lambda p: partial(p, zz, f),
            lambda p: beside(p, 1, zz, f),
        )

    def run(group, what):
        for copy in group:
            getattr(copy, what)()

    def add(into, other):
        for p in pieces:
            a, b = into(p), other(p)
            a[...] = (a[...].astype(F32) + b[...].astype(F32)).astype(a.dtype)

    def turn(k):
        upper = z // (nz // 2)
        return (1 - upper) * (nz - 1 - k) + upper * k

    def start(zz):
        for f in (3, 1, 2, 0):
            run(core_copies(zz, f), "start")

    def stage0(zz):
        for f in (3, 1, 2, 0):
            run(core_copies(zz, f), "wait_recv")
            add(lambda p: p[3].at[zz, f], lambda p: term(p, zz, c, f))
        run(second_copies(zz, 1), "start")
        run(second_copies(zz, 0), "start")

    def from_below(zz, f):
        run(up_copies(zz, f), "wait_recv")
        add(lambda p: partial(p, zz, f), lambda p: beside(p, 0, zz, f))

    def from_above(zz, f):
        run(down_copies(zz, f), "wait_recv")
        add(lambda p: partial(p, zz, f), lambda p: beside(p, 1, zz, f))

    def from_end(zz, f):
        @pl.when((zz > z) & (z == 0))
        def _():
            run(up_copies(zz, f), "start")

        @pl.when((zz < z) & (z == nz - 1))
        def _():
            run(down_copies(zz, f), "start")

    def along(zz, f):
        @pl.when((zz > z) & (z > 0))
        def _():
            from_below(zz, f)
            run(up_copies(zz, f), "start")

        @pl.when((zz < z) & (z < nz - 1))
        def _():
            from_above(zz, f)
            run(down_copies(zz, f), "start")

    def stage1(zz):
        run(second_copies(zz, 1), "wait_recv")
        add(lambda p: p[4].at[zz, 1], lambda p: p[3].at[zz, f_first])
        if z_second:
            from_end(zz, 1)
        else:
            run(first_copies(zz), "start")

    def stage2(zz):
        run(second_copies(zz, 0), "wait_recv")
        add(lambda p: p[4].at[zz, 0], lambda p: p[3].at[zz, 0])
        if not z_second:
            run(first_copies(zz), "wait_recv")
            add(lambda p: p[5].at[zz], lambda p: p[4].at[zz, 0])
        from_end(zz, 0)
        if z_second:
            along(zz, 1)

    def stage3(zz):
        along(zz, 0)

    def staged(stage):
        return lambda k: stage(turn(k))

    def at_owner(f):
        @pl.when(z > 0)
        def _():
            from_below(z, f)

        @pl.when(z < nz - 1)
        def _():
            from_above(z, f)

    def end(outs):
        if z_second:
            at_owner(1)
            run(first_copies(z), "start")
        at_owner(0)
        if z_second:
            run(first_copies(z), "wait_recv")
            add(lambda p: p[4].at[z, 0], lambda p: p[5].at[0])
        for p, out in zip(pieces, outs):
            out[...] = partial(p, z, 0)[...]

    def sent(zz, carry):
        for f in range(4):
            run(core_copies(zz, f), "wait_send")
        run(second_copies(zz, 1), "wait_send")
        run(second_copies(zz, 0), "wait_send")
        for f in range(2 if z_second else 1):

            @pl.when(zz > z)
            def _():
                run(up_copies(zz, f), "wait_send")

            @pl.when(zz < z)
            def _():
                run(down_copies(zz, f), "wait_send")

        if z_second:

            @pl.when(zz == z)
            def _():
                run(first_copies(zz), "wait_send")

        else:
            run(first_copies(zz), "wait_send")
        return carry

    stages = [staged(stage) for stage in (stage0, stage1, stage2, stage3)]
    return start, stages, turn, end, lambda: lax.fori_loop(0, nz, sent, 0)


def scatter_places(nz, shape, z_second):
    lead = (nz, 2) if z_second else (nz,)
    return [
        pltpu.VMEM((nz, 4, *shape), BF16),
        pltpu.VMEM((nz, 2, *shape), BF16),
        pltpu.VMEM((1 if z_second else nz, *shape), BF16),
        pltpu.VMEM((*lead, *shape), BF16),
        pltpu.VMEM((*lead, *shape), BF16),
    ]


VEC_ROWS = FIRST_MEMORY + THIN


def tail_kernel(nz, *refs):
    (
        place_ref,
        sums_ref,
        thin_sums_ref,
        ffn_terms,
        *rows_refs,
        w_ref,
        attn_out,
        ffn_out,
        vec_out,
        grad_ref,
        terms_f,
        terms_a,
        rows,
        wb,
        keep,
        send,
    ) = refs[:21]
    places = [refs[21 + 5 * i : 26 + 5 * i] for i in range(3)]
    vec_mine, vec_given, vec_z, send_sem, recv_sem, block_sem, in_sem, swap_sem, vec_sem = refs[36:]
    place = z, x, c, y = my_place()
    blocks = lambda zz: pltpu.make_async_copy(
        ffn_terms.at[:, zz], terms_f.at[:, zz], block_sem.at[zz]
    )
    rows_in = [
        pltpu.make_async_copy(src, rows.at[i], in_sem.at[2 + i]) for i, src in enumerate(rows_refs)
    ]
    rows_in.append(pltpu.make_async_copy(w_ref.at[pl.ds(0, 3)], wb, in_sem.at[8]))
    steps = functools.partial(scatter_steps, nz, place, send_sem=send_sem, recv_sem=recv_sem)
    up = steps(c, True, [(0, terms_f.at[0], hidden_view, *places[0])])
    down = steps(1 - c, True, [(1, terms_f.at[1], hidden_view, *places[1])])
    attn = steps(1, False, [(2, terms_a, attn_view, *places[2])])
    turn = up[2]
    for k in range(nz):
        blocks(turn(k)).start()
    for copy in rows_in:
        copy.start()

    barrier = pltpu.get_barrier_semaphore()
    others = [device(lax.rem(z + dz, nz), x, c, y) for dz in range(1, nz)]
    for other in [device(z, 1 - x, c, y), device(z, x, 1 - c, y), device(z, x, c, 1 - y), *others]:
        pl.semaphore_signal(
            barrier, inc=1, device_id=other, device_id_type=pl.DeviceIdType.MESH
        )
    pl.semaphore_wait(barrier, 2 + nz)

    def begin(k, carry):
        zz = turn(k)
        blocks(zz).wait()
        up[0](zz)
        down[0](zz)
        return carry

    def attn_terms(i, carry):
        left, right = rows[i // 3], rows[i + 2]
        value = tn(left.reshape(LOCAL * SEG, D), right.reshape(LOCAL * SEG, D))
        terms_a[i] = value.astype(BF16).reshape(terms_a.shape[1:])
        return carry

    def token_rows(s):
        total = rows[1, s].astype(F32)
        for i in range(3):
            total = total + nt(rows[2 + i, s], wb[i])
        live = place_ref[LOCAL * y + s] >= 0
        stay, go = split_rows(y, jnp.where(live, total, 0.0))
        keep[s] = stay.astype(BF16)
        send[s] = go.astype(BF16)

    def vec_copies(phase):
        if phase < 3:
            target = (device(z, x, 1 - c, y), device(z, x, c, 1 - y), device(z, 1 - x, c, y))[phase]
            sems = vec_sem.at[0, phase], vec_sem.at[1, phase]
            return [remote(vec_mine.at[phase], vec_given.at[phase], *sems, target)]
        return [
            remote(
                vec_mine.at[3], vec_z.at[dz], vec_sem.at[0, 3 + dz], vec_sem.at[1, 3 + dz], target
            )
            for dz, target in enumerate(others)
        ]

    def vec_start(phase):
        if phase == 0:
            vec_mine[0] = thin_sums_ref[...]
            vec_mine[0, 0:FIRST_MEMORY] = (
                thin_sums_ref[0:FIRST_MEMORY] + sums_ref[0:FIRST_MEMORY]
            )
            for r, i in ((QUERY_BIAS, 2), (VALUE_BIAS, 4)):
                total = row_sum(rows[i].reshape(LOCAL * SEG, D).astype(F32))
                vec_mine[0, r : r + 1] = total
        else:
            for copy in vec_copies(phase - 1):
                copy.wait_recv()
            vec_mine[phase] = vec_mine[phase - 1] + vec_given[phase - 1]
        for copy in vec_copies(phase):
            copy.start()

    swap = place_rows(place, keep, send, grad_ref, swap_sem)

    def stage(i, *groups):
        for k in groups[-1]:
            for group in groups[:-1]:
                group[1][i](k)

    def step(k, *groups):
        for lag in range(4):
            if 0 <= k - lag < nz:
                stage(lag, *groups, (k - lag,))

    lax.fori_loop(0, 2, begin, 0)
    step(0, up, down)
    for copy in rows_in:
        copy.wait()
    lax.fori_loop(0, 2, attn_terms, 0)
    lax.fori_loop(2, 3, begin, 0)
    step(1, up, down)
    lax.fori_loop(2, 4, attn_terms, 0)
    vec_start(0)
    lax.fori_loop(3, 4, begin, 0)
    attn[0](turn(0))
    step(2, up, down)
    step(0, attn)
    attn[0](turn(1))
    token_rows(0)
    vec_start(1)
    step(3, up, down)
    step(1, attn)
    attn[0](turn(2))
    token_rows(1)
    for copy in swap:
        copy.start()
    step(4, up, down)
    step(2, attn)
    attn[0](turn(3))
    vec_start(2)
    step(5, up, down)
    step(3, attn)
    vec_start(3)
    step(6, up, down)
    step(4, attn)
    up[3]([ffn_out.at[0]])
    step(5, attn)
    down[3]([ffn_out.at[1]])
    step(6, attn)
    attn[3]([attn_out])
    total = vec_mine[3]
    for dz, copy in enumerate(vec_copies(3)):
        copy.wait_recv()
        total = total + vec_z[dz]
    vec_out[...] = total
    for phase in range(4):
        for copy in vec_copies(phase):
            copy.wait_send()
    for group in (up, down, attn):
        group[4]()
    for copy in swap:
        copy.wait()


def tail(place, sums, thin_sums, ffn_terms, x, da, dq, dk, dv, c, attn, shapes):
    nz = lax.axis_size("dp") // 4
    rows, hidden, half = shapes
    attn_shape, ffn_shape = (4, nz, 2, 2, rows, D), (2, nz, 2, 2, 2, hidden, D)
    part = pltpu.VMEM((LOCAL, half, D), BF16)
    dma = lambda *shape: pltpu.SemaphoreType.DMA(shape)
    return pl.pallas_call(
        functools.partial(tail_kernel, nz),
        in_specs=[SMEM, VMEM, VMEM] + [ANY] * 8,
        out_specs=[VMEM] * 3 + [ANY],
        out_shape=[
            sds((4, rows, HALF), BF16),
            sds((2, hidden, D), BF16),
            sds((VEC_ROWS, D), F32),
            sds((2 * LOCAL, half, D), BF16),
        ],
        scratch_shapes=[
            pltpu.VMEM(ffn_shape, BF16),
            pltpu.VMEM(attn_shape, BF16),
            pltpu.VMEM((6, LOCAL, SEG, D), BF16),
            pltpu.VMEM((3, D, D), BF16),
            part,
            part,
            *scatter_places(nz, (hidden, D), True),
            *scatter_places(nz, (hidden, D), True),
            *scatter_places(nz, (4, rows, HALF), False),
            pltpu.VMEM((4, VEC_ROWS, D), F32),
            pltpu.VMEM((3, VEC_ROWS, D), F32),
            pltpu.VMEM((nz - 1, VEC_ROWS, D), F32),
            dma(11, nz, 3),
            dma(11, nz, 3),
            dma(nz),
            dma(9),
            dma(3),
            dma(2, 2 + nz),
        ],
        name="tail",
        compiler_params=params(62, collective_id=1, has_side_effects=True),
    )(place, sums, thin_sums, ffn_terms.reshape(ffn_shape), x, da, dq, dk, dv, c, attn)


def update(gradient, momentum, weight, average, rate, grad_scale):
    scaled = gradient * grad_scale
    moment = MOMENTUM * momentum + scaled
    weight_new = weight - rate * (scaled + MOMENTUM * moment)
    return (moment, weight_new, AVERAGE_DECAY * average + (1.0 - AVERAGE_DECAY) * weight_new)


VEC_TILE = (8, 128)


def in_tiles(rows):
    size = VEC_TILE[0] * VEC_TILE[1]
    padded = jnp.pad(rows, [(0, 0)] * (rows.ndim - 1) + [(0, size - rows.shape[-1])])
    return padded.reshape(*rows.shape[:-1], *VEC_TILE)


def start(attention, feedforward, vectors, tokens):
    nz = lax.axis_size("dp") // 4
    rows, hidden, entries = attention.shape[1], feedforward.shape[2], vectors.shape[0]
    attention = attention.astype(BF16)
    hidden_major = jnp.swapaxes(feedforward.astype(BF16), 1, 2)
    vec = in_tiles(vectors.astype(BF16).astype(F32))
    aligned = rows % THIN == 0
    if aligned:
        attn, ffn, table, *work = head(nz, attention, hidden_major, vec, tokens, entries)
    else:
        attn, ffn, table, other = gather(
            nz,
            0,
            [
                (attention, (4, nz, 2, 2, rows, D), attn_view),
                (hidden_major, (2, nz, 2, 2, 2, hidden, D), ffn_view),
                (vec, (nz, 2, 2, 2, *VEC_TILE), vec_view),
            ],
            tokens,
        )
    attn, ffn = attn.reshape(4, D, D), ffn.reshape(2, FF, D)
    if not aligned:
        table = table.reshape(nz * 8, VEC_TILE[0] * VEC_TILE[1])[:, :entries].reshape(NVEC, D)
        work = project(tokens, other, attn, table)
        work = [*work, *attend(*work[1:])]
    return attn, ffn, table, work


def scatter_gradients(attn_terms, ffn_terms, vec_terms, shapes):
    nz = lax.axis_size("dp") // 4
    rows, hidden, entries = shapes
    attn, ffn, vec = scatter(
        nz,
        1,
        [
            (attn_terms.reshape(4, nz, 2, 2, rows, D), (4, rows, HALF), attn_view),
            (ffn_terms.reshape(2, nz, 2, 2, 2, hidden, D), (2, hidden, D), ffn_view),
            (in_tiles(vec_terms.reshape(nz, 2, 2, 2, entries)), VEC_TILE, vec_view),
        ],
    )
    return attn.astype(F32), jnp.swapaxes(ffn, 1, 2).astype(F32), vec.reshape(-1)[:entries]


def swap(value):
    return lax.ppermute(value, "tensor", [(0, 1), (1, 0)])


def joined_kernel(keep_ref, other_ref, out_ref, sem):
    side = lax.axis_index("tensor")
    copies = [
        pltpu.make_async_copy(keep_ref, out_ref.at[pl.ds(LOCAL * side, LOCAL)], sem.at[0]),
        pltpu.make_async_copy(other_ref, out_ref.at[pl.ds(LOCAL * (1 - side), LOCAL)], sem.at[1]),
    ]
    for c in copies:
        c.start()
    for c in copies:
        c.wait()


def joined(keep, other):
    return pl.pallas_call(
        joined_kernel,
        in_specs=[ANY] * 2,
        out_specs=ANY,
        out_shape=sds((2 * LOCAL, *keep.shape[1:]), keep.dtype),
        scratch_shapes=[pltpu.SemaphoreType.DMA((2,))],
        name="joined",
        compiler_params=params(16),
    )(keep, other)


def on_device(
    tokens,
    slot_position,
    cotangent,
    attention,
    feedforward,
    vectors,
    attn_momentum,
    ffn_momentum,
    vec_momentum,
    attn_average,
    ffn_average,
    vec_average,
):
    place = slot_position
    attn, ffn, table, work = start(attention, feedforward, vectors, tokens)
    x, q, k, v, c, log_tokens = work

    (x, q, k, v), saved, cot_other = chain(place, table, attn, ffn, x, q, k, v, cotangent)
    keep, send, h, g, du, df, da, dc, c, log_total, sums = rows_part(
        place, x, q, k, v, c, log_tokens, cotangent, cot_other, attn, ffn, table
    )
    da, c, dq, dk, dv, thin_sums, ffn_terms, activations = chain_back(
        place, table, attn, ffn, q, k, v, saved, g, du, df, h, (keep, send), dc, log_total, da, c
    )
    rows, hidden, entries = attention.shape[1], feedforward.shape[2], vectors.shape[0]
    if rows % THIN == 0:
        shapes = (rows, hidden, tokens.shape[1])
        attn_grad, ffn_grad, vec_sums, token_grad = tail(
            place, sums, thin_sums, ffn_terms, x, da, dq, dk, dv, c, attn, shapes
        )
        attn_grad = attn_grad.astype(F32)
        ffn_grad = jnp.swapaxes(ffn_grad, 1, 2).astype(F32)
        index = lax.axis_index("dp") * 2 + lax.axis_index("tensor")
        vec_grad = lax.dynamic_slice_in_dim(
            vec_sums[:NVEC].reshape(-1), index * entries, entries
        )
    else:
        keep, send = token_gradient(place, da, dq, dk, dv, attn)
        token_grad = joined(keep, swap(send))
        attn_terms, vec_terms = attn_gradient(x, da, dq, dk, dv, c, sums, thin_sums)
        attn_grad, ffn_grad, vec_grad = scatter_gradients(
            attn_terms, ffn_terms, vec_terms[:NVEC], (rows, hidden, entries)
        )
    grad_scale = 1.0 / math.sqrt(lax.axis_size("dp") * SLOTS * ROWS)
    attn_new = update(attn_grad, attn_momentum, attention, attn_average, ATTENTION_RATE, grad_scale)
    ffn_new = update(ffn_grad, ffn_momentum, feedforward, ffn_average, FEEDFORWARD_RATE, grad_scale)
    vec_new = update(vec_grad, vec_momentum, vectors, vec_average, VECTOR_RATE, grad_scale)
    return (
        activations,
        token_grad,
        attn_new[0],
        ffn_new[0],
        vec_new[0],
        attn_new[1],
        ffn_new[1],
        vec_new[1],
        attn_new[2],
        ffn_new[2],
        vec_new[2],
    )


def solution(mesh):
    attn_spec = P(None, "dp", "tensor")
    ffn_spec = P(None, None, ("dp", "tensor"))
    vec_spec = P(("dp", "tensor"))
    rows_spec = P("dp", "tensor", None)
    states = (attn_spec, ffn_spec, vec_spec)
    return jax.shard_map(
        on_device,
        mesh=mesh,
        in_specs=(rows_spec, P("dp"), rows_spec) + states * 3,
        out_specs=(rows_spec, rows_spec) + states * 3,
        check_vma=False,
    )
```
